32 devices in a mesh: dp: 16 (over z, y, core), tensor: 2 (over x).
Axes of the slice: x: 2, y: 2, z: 4, core: 2. Of those that a mesh axis runs over, the one named last changes fastest.
Arguments:
- block_input: bfloat16 [2, 16, 576, 1280], P(None, 'dp', 'tensor'), may hold values from -6 to 6
- out_cotangent: bfloat16 [2, 16, 576, 1280], P(None, 'dp', 'tensor'), may hold values from -6 to 6
- picture_ids: int32 [2, 16, 576], P(None, 'dp'), may hold values from 0 to 3, as said below
- patch_positions: int32 [2, 2, 16, 576], P(None, None, 'dp'), may hold values from 0 to 23, as said below
- picture_lengths: int32 [2, 16, 4], P(None, 'dp'), may hold values from 0 to 576, as said below
- pad_mask: int32 [2, 16, 576], P(None, 'dp'), may hold values from 0 to 1, as said below
- qkv_weight: float32 [1280, 3, 1280], P('dp', None, 'tensor')
- proj_weight: float32 [1280, 1280], P('tensor', 'dp')
- fc1_weight: float32 [1280, 5120], P('dp', 'tensor')
- fc2_weight: float32 [5120, 1280], P('tensor', 'dp')
- qkv_bias: float32 [3, 1280], P(None, 'tensor'), may hold values from -3 to 3
- fc1_bias: float32 [5120], P('tensor'), may hold values from -3 to 3
- vectors: float32 [6, 1280], replicated
- qkv_moments: float32 [2, 1280, 3, 1280], P(None, 'dp', None, 'tensor')
- proj_moments: float32 [2, 1280, 1280], P(None, 'tensor', 'dp')
- fc1_moments: float32 [2, 1280, 5120], P(None, 'dp', 'tensor')
- fc2_moments: float32 [2, 5120, 1280], P(None, 'tensor', 'dp')
- qkv_bias_moments: float32 [2, 3, 1280], P(None, None, 'tensor')
- fc1_bias_moments: float32 [2, 5120], P(None, 'tensor')
- vector_moments: float32 [2, 6, 1280], replicated
Outputs:
- block_output: bfloat16 [2, 16, 576, 1280], P(None, 'dp', 'tensor')
- input_grad: bfloat16 [2, 16, 576, 1280], P(None, 'dp', 'tensor')
- qkv_new: float32 [1280, 3, 1280], P('dp', None, 'tensor')
- proj_new: float32 [1280, 1280], P('tensor', 'dp')
- fc1_new: float32 [1280, 5120], P('dp', 'tensor')
- fc2_new: float32 [5120, 1280], P('tensor', 'dp')
- qkv_bias_new: float32 [3, 1280], P(None, 'tensor')
- fc1_bias_new: float32 [5120], P('tensor')
- vectors_new: float32 [6, 1280], replicated
- qkv_moments_new: float32 [2, 1280, 3, 1280], P(None, 'dp', None, 'tensor')
- proj_moments_new: float32 [2, 1280, 1280], P(None, 'tensor', 'dp')
- fc1_moments_new: float32 [2, 1280, 5120], P(None, 'dp', 'tensor')
- fc2_moments_new: float32 [2, 5120, 1280], P(None, 'tensor', 'dp')
- qkv_bias_moments_new: float32 [2, 3, 1280], P(None, None, 'tensor')
- fc1_bias_moments_new: float32 [2, 5120], P(None, 'tensor')
- vector_moments_new: float32 [2, 6, 1280], replicated
- qkv_copy: bfloat16 [1280, 3, 1280], P('dp', None, 'tensor')
- proj_copy: bfloat16 [1280, 1280], P('tensor', 'dp')
- fc1_copy: bfloat16 [1280, 5120], P('dp', 'tensor')
- fc2_copy: bfloat16 [5120, 1280], P('tensor', 'dp')
- norms: float32 [2, 7], replicated
- trust: float32 [7], replicated
The draws below stay inside these ranges and needn't reach their ends.
Inputs may be any that keep to these rules, and one draw needn't show every extreme that they name: `picture_ids`: within a row the picture number never falls; the patches after a row's last picture are padding and carry that picture's number. `patch_positions`: A picture of height h and width w, both from 10 to 24, lists its h * w patches row by row; [0] is the row and [1] the column inside it; padding has 0 and 0. `picture_lengths`: the pictures fill a row's first patches in slot order; a used slot holds h * w, unused slots at the end hold 0; a row's lengths sum to at most 576. `pad_mask`: 1 exactly on a row's first (sum of its picture_lengths) patches.
All inputs are finite; a program needn't handle non-finite values.
Results may differ from the reference program's by a relative error of at most 0.013.
The reference program's roundings to bfloat16 on the way count: a program that leaves them out, or rounds other values in their place, can miss the bound.
Values may be sent and summed in bfloat16 or wider, within the bound.
No kernel may reach another device: no remote copies, remote signals or barrier semaphores. Data moves between devices by JAX's collectives and lax.ppermute only.
A program may use at most 256 MiB of HBM per device.

```python
import math
import jax
import jax.numpy as jnp
from jax import lax

D = 1280
HEADS = 16
HD = 80
FF = 5120
MB = 2
SIDE = 24
SMIN = 10
SLOTS = 4
LEN = 576
SEQS = 16


def base_normal(key, array_shape):
    return jnp.clip(jax.random.normal(key, array_shape, jnp.float32), -5.0, 5.0)


def rising_weight(key, array_shape, fan_in, rise_axis, label):
    extent = array_shape[rise_axis]
    rising = (1.0 + 2.0 * jnp.arange(extent, dtype=jnp.float32) / max(extent - 1, 1)) / 2.0
    layout = [1] * len(array_shape)
    layout[rise_axis] = extent
    own_key = jax.random.fold_in(key, label)
    return base_normal(own_key, array_shape) * fan_in ** (-0.5) * rising.reshape(layout)


def moment_pair(key, array_shape, grad_scale, rise_axis, label):
    key_first, key_second = jax.random.split(jax.random.fold_in(key, label))
    first = grad_scale * base_normal(key_first, array_shape)
    spread = jnp.exp(jax.random.uniform(key_second, array_shape, jnp.float32, math.log(0.5), math.log(2.0)))
    if rise_axis >= 0:
        extent = array_shape[rise_axis]
        rising = 1.0 + 3.0 * jnp.arange(extent, dtype=jnp.float32) / max(extent - 1, 1)
        layout = [1] * len(array_shape)
        layout[rise_axis] = extent
        spread = spread * rising.reshape(layout)
    second = grad_scale * grad_scale * spread
    return jnp.stack([first, second])


def draw_qkv_weight(key, part):
    return rising_weight(key, (D, 3, D), D, 0, 101)


def draw_proj_weight(key, part):
    return rising_weight(key, (D, D), D * 16 // LEN, 1, 102)


def draw_fc1_weight(key, part):
    return rising_weight(key, (D, FF), D, 0, 103)


def draw_fc2_weight(key, part):
    return rising_weight(key, (FF, D), FF, 1, 104)


def draw_vectors(key, part):
    gains = jnp.array([1.0, 0.0, 0.0, 1.0, 0.0, 0.0], jnp.float32)[:, None]
    return gains + 0.3 * base_normal(jax.random.fold_in(key, 105), (6, D))


def draw_qkv_moments(key, part):
    return moment_pair(key, (D, 3, D), 0.5, 0, 201)


def draw_proj_moments(key, part):
    return moment_pair(key, (D, D), 3.0 / math.sqrt(LEN), 1, 202)


def draw_fc1_moments(key, part):
    return moment_pair(key, (D, FF), 0.5, 0, 203)


def draw_fc2_moments(key, part):
    return moment_pair(key, (FF, D), 1.0, 1, 204)


def draw_qkv_bias_moments(key, part):
    return moment_pair(key, (3, D), 0.5, -1, 205)


def draw_fc1_bias_moments(key, part):
    return moment_pair(key, (FF,), 0.5, -1, 206)


def draw_vector_moments(key, part):
    return moment_pair(key, (6, D), 2.0, -1, 207)


def picture_plan(key):
    base = jax.random.fold_in(key, 11)
    key_tall, key_broad = jax.random.split(base)
    array_shape = (MB, SEQS, SLOTS)
    heights = jax.random.randint(key_tall, array_shape, SMIN, SIDE + 1)
    widths = jax.random.randint(key_broad, array_shape, SMIN, SIDE + 1)
    batch_at = jnp.arange(MB)[:, None, None]
    row_at = jnp.arange(SEQS)[None, :, None]
    slot_at = jnp.arange(SLOTS)[None, None, :]
    whole = (batch_at == 0) & (row_at == 0) & (slot_at == 0)
    little = (batch_at == 0) & (row_at == 1)
    heights = jnp.where(whole, SIDE, jnp.where(little, SMIN, heights))
    widths = jnp.where(whole, SIDE, jnp.where(little, SMIN, widths))
    sizes = heights * widths
    picture_ends = jnp.cumsum(sizes, -1)
    retained = picture_ends <= LEN
    return (widths, sizes, picture_ends, retained)


def token_plan(key):
    widths, sizes, picture_ends, retained = picture_plan(key)
    places = jnp.arange(LEN)[None, None, :]
    passed = jnp.sum(((places[..., None] >= picture_ends[:, :, None, :]) & retained[:, :, None, :]).astype(jnp.int32), -1)
    retained_count = jnp.sum(retained.astype(jnp.int32), -1)
    picture = jnp.minimum(passed, retained_count[..., None] - 1)
    lengths = jnp.where(retained, sizes, 0)
    occupied = jnp.sum(lengths, -1)
    inside = places < occupied[..., None]
    choose = (picture[..., None] == jnp.arange(SLOTS)[None, None, None, :]).astype(jnp.int32)
    start_at = jnp.sum(choose * (picture_ends - sizes)[:, :, None, :], -1)
    widths_tok = jnp.sum(choose * widths[:, :, None, :], -1)
    offset = places - start_at
    rows_at = jnp.where(inside, offset // widths_tok, 0)
    cols_at = jnp.where(inside, offset % widths_tok, 0)
    return (picture.astype(jnp.int32), jnp.stack([rows_at, cols_at]).astype(jnp.int32), lengths.astype(jnp.int32), inside.astype(jnp.int32))


def draw_picture_ids(key, part):
    return token_plan(key)[0]


def draw_patch_positions(key, part):
    return token_plan(key)[1]


def draw_picture_lengths(key, part):
    return token_plan(key)[2]


def draw_pad_mask(key, part):
    return token_plan(key)[3]


def steps_of(rng, dims, cuts, least, largest):
    level, own = 1.0, jax.random.fold_in(rng, 6)
    for position, blocks in cuts:
        steps = jnp.exp(jax.random.uniform(jax.random.fold_in(own, position), (blocks,), jnp.float32, least / len(cuts), largest / len(cuts)))
        level = level * jnp.repeat(steps, dims[position] // blocks).reshape([-1 if axis == position else 1 for axis in range(len(dims))])
    return level


def noise(stream_key, dims, scale, limit, shards=(), kind=jnp.bfloat16):
    drawn = scale * jax.random.normal(stream_key, dims, jnp.float32)
    if shards:
        drawn = drawn * steps_of(stream_key, dims, shards, -0.22, 0.18)
    return jnp.clip(drawn, -limit, limit).astype(kind)


def setup_inputs(seed: int = 0) -> dict:
    arg_keys = jax.random.split(jax.random.key(seed), 21)
    block_input = noise(arg_keys[0], (MB, SEQS, LEN, D), 1.0, 6.0, ((1, 16), (2, 2)))
    out_cotangent = noise(arg_keys[1], (MB, SEQS, LEN, D), 1.0, 6.0, ((1, 16), (2, 2)))
    picture_ids = draw_picture_ids(jax.random.fold_in(arg_keys[20], 71), 0)
    patch_positions = draw_patch_positions(jax.random.fold_in(arg_keys[20], 71), 0)
    picture_lengths = draw_picture_lengths(jax.random.fold_in(arg_keys[20], 71), 0)
    pad_mask = draw_pad_mask(jax.random.fold_in(arg_keys[20], 71), 0)
    qkv_weight = draw_qkv_weight(jax.random.fold_in(arg_keys[20], 71), 0)
    proj_weight = draw_proj_weight(jax.random.fold_in(arg_keys[20], 71), 0)
    fc1_weight = draw_fc1_weight(jax.random.fold_in(arg_keys[20], 71), 0)
    fc2_weight = draw_fc2_weight(jax.random.fold_in(arg_keys[20], 71), 0)
    qkv_bias = noise(arg_keys[10], (3, D), 0.5, 3.0, ((1, 2),), jnp.float32)
    fc1_bias = noise(arg_keys[11], (FF,), 0.5, 3.0, ((0, 2),), jnp.float32)
    vectors = draw_vectors(jax.random.fold_in(arg_keys[20], 71), 0)
    qkv_moments = draw_qkv_moments(jax.random.fold_in(arg_keys[20], 71), 0)
    proj_moments = draw_proj_moments(jax.random.fold_in(arg_keys[20], 71), 0)
    fc1_moments = draw_fc1_moments(jax.random.fold_in(arg_keys[20], 71), 0)
    fc2_moments = draw_fc2_moments(jax.random.fold_in(arg_keys[20], 71), 0)
    qkv_bias_moments = draw_qkv_bias_moments(jax.random.fold_in(arg_keys[20], 71), 0)
    fc1_bias_moments = draw_fc1_bias_moments(jax.random.fold_in(arg_keys[20], 71), 0)
    vector_moments = draw_vector_moments(jax.random.fold_in(arg_keys[20], 71), 0)
    return dict(block_input=block_input, out_cotangent=out_cotangent, picture_ids=picture_ids, patch_positions=patch_positions, picture_lengths=picture_lengths, pad_mask=pad_mask, qkv_weight=qkv_weight, proj_weight=proj_weight, fc1_weight=fc1_weight, fc2_weight=fc2_weight, qkv_bias=qkv_bias, fc1_bias=fc1_bias, vectors=vectors, qkv_moments=qkv_moments, proj_moments=proj_moments, fc1_moments=fc1_moments, fc2_moments=fc2_moments, qkv_bias_moments=qkv_bias_moments, fc1_bias_moments=fc1_bias_moments, vector_moments=vector_moments)


@jax.custom_vjp
def low(v):
    return lax.optimization_barrier(v.astype(jnp.bfloat16)).astype(jnp.float32)

@jax.custom_vjp
def low_back(v):
    return v

def low_keep(v):
    return (low(v), None)

def low_pass(kept, grad):
    return (grad,)

def back_keep(v):
    return (v, None)

def back_low(kept, grad):
    return (low(grad),)
low.defvjp(low_keep, low_pass)
low_back.defvjp(back_keep, back_low)
HIGHEST = lax.Precision.HIGHEST
NEGATIVE = -1e+30
EPS_NORM = 1e-06
EPS_ADAM = 1e-06
WEIGHT_DECAY = 0.01
LEARN_RATE = 0.5
GELU_SLOPE = 1.702

def matmul_high(left, right):
    return jnp.dot(left, right, precision=HIGHEST, preferred_element_type=jnp.float32)

def layer_norm(values, gain, shift):
    center = values - lax.optimization_barrier(jnp.mean(values, -1, keepdims=True))
    variance = lax.optimization_barrier(jnp.mean(center * center, -1, keepdims=True))
    return center * lax.rsqrt(variance + EPS_NORM) * gain + shift

def rotary_tables(rows_at, cols_at):
    quarter = HD // 4
    frequency = 10000.0 ** (-jnp.arange(quarter, dtype=jnp.float32) / quarter)
    halves = jnp.concatenate([rows_at.astype(jnp.float32)[:, None] * frequency, cols_at.astype(jnp.float32)[:, None] * frequency], -1)
    angles = jnp.concatenate([halves, halves], -1)
    return (jnp.cos(angles), jnp.sin(angles))

def rotate_pairs(values, cosine, sine):
    middle = values.shape[-1] // 2
    turned = jnp.concatenate([-values[..., middle:], values[..., :middle]], -1)
    return values * cosine[:, None, :] + turned * sine[:, None, :]

def row_block(row, w_qkv, w_proj, w_up, w_down, b_qkv, b_up, vectors):
    row_values, row_ids, rows_at, cols_at, row_mask = row
    first_in = low(layer_norm(row_values, vectors[0], vectors[1]))
    mixed = low_back(jnp.einsum('td,dcf->tcf', first_in, w_qkv, precision=HIGHEST) + b_qkv[None])
    cosine, sine = rotary_tables(rows_at, cols_at)
    queries = low(rotate_pairs(mixed[:, 0].reshape(LEN, HEADS, HD), cosine, sine))
    keys_rot = low(rotate_pairs(mixed[:, 1].reshape(LEN, HEADS, HD), cosine, sine))
    head_values = low(mixed[:, 2].reshape(LEN, HEADS, HD))
    raw_scores = low_back(jnp.einsum('qhd,khd->hqk', queries, keys_rot, precision=HIGHEST))
    allowed = (row_ids[:, None] == row_ids[None, :]) & (row_mask[None, :] == 1)
    logits = jnp.where(allowed[None], raw_scores * HD ** (-0.5), NEGATIVE)
    row_top = lax.optimization_barrier(jnp.max(logits, -1, keepdims=True))
    exponent = jnp.exp(logits - row_top)
    prob = low(exponent / lax.optimization_barrier(jnp.sum(exponent, -1, keepdims=True)))
    attended = jnp.einsum('hqk,khd->qhd', prob, head_values, precision=HIGHEST).reshape(LEN, D)
    attended = low_back(low(attended))
    hidden1 = row_values + low_back(matmul_high(attended, w_proj) + vectors[2])
    second_in = low(layer_norm(hidden1, vectors[3], vectors[4]))
    upward = low_back(matmul_high(second_in, w_up) + b_up)
    activated = low(upward * jax.nn.sigmoid(GELU_SLOPE * upward))
    return hidden1 + low_back(matmul_high(activated, w_down) + vectors[5])

def block_rows(values, weights, picture_ids, patch_positions, pad_mask):
    w_qkv = low(weights[0])
    w_proj = low(weights[1])
    w_up = low(weights[2])
    w_down = low(weights[3])
    rows = (values.reshape(-1, LEN, D), picture_ids.reshape(-1, LEN), patch_positions[0].reshape(-1, LEN), patch_positions[1].reshape(-1, LEN), pad_mask.reshape(-1, LEN))

    def one_row(row):
        return row_block(row, w_qkv, w_proj, w_up, w_down, weights[4], weights[5], weights[6])
    result = lax.map(jax.checkpoint(one_row), rows)
    return result.reshape(values.shape)

def lamb_parts(master, moments, gradient):
    first = 0.5 * moments[0] + 0.5 * gradient
    second = 0.5 * moments[1] + 0.5 * gradient * gradient
    update = first / (jnp.sqrt(second) + EPS_ADAM) + WEIGHT_DECAY * master
    return (first, second, update)

def reference(block_input, out_cotangent, picture_ids, patch_positions, picture_lengths, pad_mask, qkv_weight, proj_weight, fc1_weight, fc2_weight, qkv_bias, fc1_bias, vectors, qkv_moments, proj_moments, fc1_moments, fc2_moments, qkv_bias_moments, fc1_bias_moments, vector_moments):
    inputs = block_input.astype(jnp.float32)
    params = (qkv_weight, proj_weight, fc1_weight, fc2_weight, qkv_bias, fc1_bias, vectors)

    def forward(values, weights):
        return block_rows(values, weights, picture_ids, patch_positions, pad_mask)
    output, pullback = jax.vjp(forward, inputs, params)
    slot_hit = (picture_ids[..., None] == jnp.arange(SLOTS, dtype=jnp.int32)).astype(jnp.float32)
    picture_size = lax.optimization_barrier(jnp.sum(slot_hit * picture_lengths.astype(jnp.float32)[:, :, None, :], -1))
    token_weight = pad_mask.astype(jnp.float32) * jnp.sqrt(LEN / picture_size)
    seed_grad = out_cotangent.astype(jnp.float32) * token_weight[..., None]
    input_grad, raw_gradients = pullback(seed_grad)
    grad_factor = float(MB * SEQS * LEN) ** (-0.5)
    gradients = tuple((gradient * grad_factor for gradient in raw_gradients))
    moment_list = (qkv_moments, proj_moments, fc1_moments, fc2_moments, qkv_bias_moments, fc1_bias_moments, vector_moments)
    new_params = []
    new_moments = []
    weight_sq = []
    update_sq = []
    updates = []
    for master, moments, gradient in zip(params, moment_list, gradients):
        first, second, update = lamb_parts(master, moments, gradient)
        new_moments.append(jnp.stack([first, second]))
        updates.append(update)
        weight_sq.append(jnp.sum(master * master))
        update_sq.append(jnp.sum(update * update))
    weight_sq = jnp.stack(weight_sq)
    update_sq = jnp.stack(update_sq)
    trust = jnp.sqrt(weight_sq) / jnp.sqrt(update_sq + 1e-12)
    for index in range(7):
        new_params.append(params[index] - LEARN_RATE * trust[index] * updates[index])
    norms = jnp.stack([jnp.sqrt(weight_sq), jnp.sqrt(update_sq)])
    return (output.astype(jnp.bfloat16), input_grad.astype(jnp.bfloat16), new_params[0], new_params[1], new_params[2], new_params[3], new_params[4], new_params[5], new_params[6], new_moments[0], new_moments[1], new_moments[2], new_moments[3], new_moments[4], new_moments[5], new_moments[6], new_params[0].astype(jnp.bfloat16), new_params[1].astype(jnp.bfloat16), new_params[2].astype(jnp.bfloat16), new_params[3].astype(jnp.bfloat16), norms, trust)
```

```python
import jax
import jax.numpy as jnp
from jax import lax
from jax.sharding import PartitionSpec as P

HD = 80
SLOTS = 4
LEN = 576


NEGATIVE = -1e30
EPS_NORM = 1e-06
EPS_ADAM = 1e-06
WEIGHT_DECAY = 0.01
LEARN_RATE = 0.5
GELU_SLOPE = 1.702
F32 = jnp.float32
LOW = jnp.bfloat16


def norm_parts(values):
    center = values - jnp.mean(values, -1, keepdims=True)
    inverse = lax.rsqrt(jnp.mean(center * center, -1, keepdims=True) + EPS_NORM)
    return (center * inverse, inverse)


def norm_back(out_grad, normed, inverse, gain):
    scaled = out_grad * gain
    return inverse * (
        scaled
        - jnp.mean(scaled, -1, keepdims=True)
        - normed * jnp.mean(scaled * normed, -1, keepdims=True)
    )


def rotary_tables(rows_at, cols_at):
    quarter = HD // 4
    frequency = 10000.0 ** (-jnp.arange(quarter, dtype=F32) / quarter)
    halves = jnp.concatenate(
        [
            rows_at.astype(F32)[:, None] * frequency,
            cols_at.astype(F32)[:, None] * frequency,
        ],
        -1,
    )
    angles = jnp.concatenate([halves, halves], -1)
    return (jnp.cos(angles), jnp.sin(angles))


def rotate_pairs(values, cosine, sine):
    middle = values.shape[-1] // 2
    turned = jnp.concatenate([-values[..., middle:], values[..., :middle]], -1)
    return values * cosine[:, None, :] + turned * sine[:, None, :]


def rotate_back(grads, cosine, sine):
    middle = grads.shape[-1] // 2
    weighted = grads * sine[:, None, :]
    return grads * cosine[:, None, :] + jnp.concatenate(
        [weighted[..., middle:], -weighted[..., :middle]], -1
    )


def attend(queries, keys_rot, values, allowed):
    score_scale = HD ** (-0.5)
    raw_scores = jnp.einsum("qhd,khd->hqk", queries, keys_rot, preferred_element_type=F32)
    logits = jnp.where(allowed[None], raw_scores * score_scale, NEGATIVE)
    row_top = jnp.max(logits, -1, keepdims=True)
    exponent = jnp.exp(logits - row_top)
    row_total = jnp.sum(exponent, -1, keepdims=True)
    prob_rows = (exponent / row_total).astype(LOW)
    mixed = jnp.einsum("hqk,khd->qhd", prob_rows, values, preferred_element_type=F32)
    return (mixed, row_top + jnp.log(row_total))


def attend_back(queries, keys_rot, values, allowed, log_total, grad_out):
    score_scale = HD ** (-0.5)
    raw_scores = jnp.einsum("qhd,khd->hqk", queries, keys_rot, preferred_element_type=F32)
    logits = jnp.where(allowed[None], raw_scores * score_scale, NEGATIVE)
    prob_rows = jnp.exp(logits - log_total)
    prob_grad = jnp.einsum("qhd,khd->hqk", grad_out, values, preferred_element_type=F32)
    inner_sum = jnp.sum(prob_rows * prob_grad, -1, keepdims=True)
    score_grad = (score_scale * prob_rows * (prob_grad - inner_sum)).astype(LOW)
    query_grad = jnp.einsum("hqk,khd->qhd", score_grad, keys_rot, preferred_element_type=F32)
    key_grad = jnp.einsum("hqk,qhd->khd", score_grad, queries, preferred_element_type=F32)
    value_grad = jnp.einsum(
        "hqk,qhd->khd", prob_rows.astype(LOW), grad_out, preferred_element_type=F32
    )
    return (query_grad, key_grad, value_grad)


def dot(left, right):
    return lax.dot_general(left, right, (((1,), (0,)), ((), ())), preferred_element_type=F32)


def dot_t(left, right):
    return lax.dot_general(left, right, (((1,), (1,)), ((), ())), preferred_element_type=F32)


def outer(left, right):
    return lax.dot_general(left, right, (((0,), (0,)), ((), ())), preferred_element_type=F32)


def lamb_parts(master, moments, gradient):
    first = 0.5 * moments[0] + 0.5 * gradient
    second = 0.5 * moments[1] + 0.5 * gradient * gradient
    update = first / (jnp.sqrt(second) + EPS_ADAM) + WEIGHT_DECAY * master
    return (first, second, update)


class Lanes:
    def __init__(self, dp):
        self.dp = dp
        self.ring = dp // 4

    def over_x(self, v):
        return lax.ppermute(v, "tensor", [(0, 1), (1, 0)])

    def over_core(self, v):
        return lax.ppermute(v, "dp", [(i, i ^ 1) for i in range(self.dp)])

    def over_y(self, v):
        return lax.ppermute(v, "dp", [(i, i ^ 2) for i in range(self.dp)])

    def down_z(self, v):
        return lax.ppermute(v, "dp", [(i, (i - 4) % self.dp) for i in range(self.dp)])

    def up_z(self, v):
        return lax.ppermute(v, "dp", [(i, (i + 4) % self.dp) for i in range(self.dp)])

    def order(self):
        i = lax.axis_index("dp")
        z, y, c = i // 4, (i // 2) % 2, i % 2
        blocks = []
        for dc in range(2):
            for dy in range(2):
                for dz in range(self.ring):
                    blocks.append(((z + dz) % self.ring) * 4 + (y ^ dy) * 2 + (c ^ dc))
        return jnp.stack(blocks)

    def ring_down(self, v):
        held = [v]
        for _ in range(self.ring - 1):
            held.append(self.down_z(held[-1]))
        return held

    def gather_a(self, own):
        wide = jnp.concatenate([own, self.over_x(own)], 1)
        held = jnp.concatenate(self.ring_down(wide), 0)
        across = self.over_y(held)
        return [held, across, self.over_core(held), self.over_core(across)]

    def gather_b(self, own):
        pair = jnp.stack([own, self.over_y(own)])
        held = jnp.stack(self.ring_down(pair), 1)
        held = held.reshape((-1,) + own.shape[1:])
        across = self.over_x(held)
        return [held, self.over_core(held)], [across, self.over_core(across)]

    def reduce_a(self, own, other):
        own = own + [self.over_x(total(other))]
        half = own[0].shape[0] // 2
        came = self.over_y(total([v[half:] for v in own]))
        own = [v[:half] for v in own] + [came]
        rows = half // self.ring
        came = None
        for step in range(self.ring - 1, -1, -1):
            part = [v[step * rows : (step + 1) * rows] for v in own]
            if came is not None:
                part = part + [came]
            if step:
                came = self.up_z(total(part))
        return wide_total(part)

    def reduce_b(self, own, other):
        half = own[0].shape[0] // 2
        came = self.over_y(
            jnp.stack([total([v[half:] for v in own]), total([v[half:] for v in other])])
        )
        own = [v[:half] for v in own] + [came[0]]
        other = [v[:half] for v in other] + [came[1]]
        rows = half // self.ring
        came = None
        for step in range(self.ring - 1, -1, -1):
            cut = slice(step * rows, (step + 1) * rows)
            parts = [[v[cut] for v in own], [v[cut] for v in other]]
            if came is not None:
                parts = [parts[0] + [came[0]], parts[1] + [came[1]]]
            if step:
                came = self.up_z(jnp.stack([total(parts[0]), total(parts[1])]))
        return wide_total(parts[0] + [self.over_x(total(parts[1]))])


def wide_total(parts):
    result = parts[0].astype(F32)
    for part in parts[1:]:
        result = result + part.astype(F32)
    return result


def total(parts):
    return wide_total(parts).astype(LOW)


class PlainLanes(Lanes):
    def order(self):
        return jnp.arange(self.dp)

    def gather_a(self, own):
        wide = jnp.concatenate([own, self.over_x(own)], 1)
        return [lax.all_gather(wide, "dp", axis=0, tiled=True)]

    def gather_b(self, own):
        held = lax.all_gather(own, "dp", axis=0, tiled=True)
        return [held], [self.over_x(held)]


def butterfly(value, dp):
    if dp & (dp - 1):
        return lax.psum(value, ("dp", "tensor"))
    value = value + lax.ppermute(value, "tensor", [(0, 1), (1, 0)])
    bit = 1
    while bit < dp:
        value = value + lax.ppermute(value, "dp", [(i, i ^ bit) for i in range(dp)])
        bit *= 2
    return value


def body(
    block_input,
    out_cotangent,
    picture_ids,
    patch_positions,
    picture_lengths,
    pad_mask,
    qkv_weight,
    proj_weight,
    fc1_weight,
    fc2_weight,
    qkv_bias,
    fc1_bias,
    vectors,
    qkv_moments,
    proj_moments,
    fc1_moments,
    fc2_moments,
    qkv_bias_moments,
    fc1_bias_moments,
    vector_moments,
):
    dp = lax.axis_size("dp")
    relative = dp == 16
    lanes = Lanes(dp) if relative else PlainLanes(dp)
    slot = lax.axis_index("tensor")
    lead_dp = (lax.axis_index("dp") == 0).astype(F32)
    lead_all = lead_dp * (slot == 0).astype(F32)
    width = block_input.shape[3]
    rows_own = width // dp
    half_heads = qkv_weight.shape[2] // HD // 2
    quarter = half_heads * HD
    hidden = fc1_weight.shape[1] // 2
    grad_factor = float(block_input.shape[0] * block_input.shape[1] * dp * LEN) ** (-0.5)

    def own_row(both):
        mine = lax.dynamic_index_in_dim(both[:, 0], slot, 0, keepdims=False)
        theirs = lax.dynamic_index_in_dim(both[:, 0], 1 - slot, 0, keepdims=False)
        return jnp.concatenate([mine, lanes.over_x(theirs)], 0)

    local_rows = block_input.shape[2]
    biases = jnp.concatenate([qkv_bias.reshape(-1), fc1_bias])
    other_biases = lanes.over_x(biases)

    def pick(array, axis=0):
        return lax.dynamic_index_in_dim(array, slot, axis, keepdims=False)

    def turn(values):
        return jnp.roll(values, -slot * local_rows, axis=-1)

    ids_row = turn(pick(picture_ids[:, 0]))
    rows_at = turn(pick(patch_positions[0, :, 0]))
    cols_at = turn(pick(patch_positions[1, :, 0]))
    mask_row = turn(pick(pad_mask[:, 0]))
    length_row = pick(picture_lengths[:, 0])

    q_low = qkv_weight.astype(LOW)
    p_low = proj_weight.astype(LOW).T
    group_1 = [
        jnp.concatenate(
            [
                q_low[:, :, k * quarter : (k + 1) * quarter].reshape(rows_own, 3 * quarter),
                p_low[:, k * quarter : (k + 1) * quarter],
            ],
            1,
        )
        for k in range(2)
    ]
    f1_low = fc1_weight.astype(LOW)
    f2_low = fc2_weight.astype(LOW).T
    group_2 = [f1_low[:, k * hidden : (k + 1) * hidden] for k in range(2)]
    group_3 = [f2_low[:, k * hidden : (k + 1) * hidden] for k in range(2)]

    def gather(group):
        wide = lanes.gather_a(group[0])
        own, other = lanes.gather_b(group[1])
        return wide, own, other

    g1, g2, g3 = gather(group_1), gather(group_2), gather(group_3)

    def rows_of(pieces, start, stop):
        return jnp.concatenate([v[:, start:stop] for v in pieces], 0)

    n1 = 4 * quarter
    w_qkv = [
        rows_of(g1[0], 0, 3 * quarter),
        rows_of(g1[0], n1, n1 + 3 * quarter),
        rows_of(g1[1], 0, 3 * quarter),
        rows_of(g1[2], 0, 3 * quarter),
    ]
    w_proj = [
        rows_of(g1[0], 3 * quarter, n1),
        rows_of(g1[0], n1 + 3 * quarter, 2 * n1),
        rows_of(g1[1], 3 * quarter, n1),
        rows_of(g1[2], 3 * quarter, n1),
    ]

    def three(group):
        return [jnp.concatenate(v, 0) for v in group]

    w_up = three(g2)
    w_down = three(g3)

    order = lanes.order()
    column = (order[:, None] * rows_own + jnp.arange(rows_own)[None, :]).reshape(-1)
    shuffle = (jnp.arange(width)[:, None] == column[None, :]).astype(LOW)
    if relative:
        vec = lax.dot_general(
            vectors,
            shuffle.astype(F32),
            (((1,), (0,)), ((), ())),
            precision=lax.Precision.HIGHEST,
            preferred_element_type=F32,
        )
        row_low = dot(own_row(block_input), shuffle).astype(LOW)
        cot_low = dot(own_row(out_cotangent), shuffle).astype(LOW)
    else:
        vec = vectors
        row_low = own_row(block_input)
        cot_low = own_row(out_cotangent)

    def quarters(own, other):
        half = own.shape[-1] // 2
        return [own[..., :half], other[..., :half], own[..., half:], other[..., half:]]

    bq = quarters(
        qkv_bias, other_biases[: qkv_bias.size].reshape(qkv_bias.shape)
    )
    bu = quarters(fc1_bias, other_biases[qkv_bias.size :])

    row_values = row_low.astype(F32)
    normed1, inverse1 = norm_parts(row_values)
    first_in = (normed1 * vec[0] + vec[1]).astype(LOW)
    mixed = [
        (dot(first_in, w) + b.reshape(-1)).reshape(LEN, 3, half_heads, HD)
        for w, b in zip(w_qkv, bq)
    ]
    mixed = jnp.concatenate(mixed, 2)
    heads = 4 * half_heads
    cosine, sine = rotary_tables(rows_at, cols_at)
    queries = rotate_pairs(mixed[:, 0], cosine, sine).astype(LOW)
    keys_rot = rotate_pairs(mixed[:, 1], cosine, sine).astype(LOW)
    head_values = mixed[:, 2].astype(LOW)
    allowed = (ids_row[:, None] == ids_row[None, :]) & (mask_row[None, :] == 1)
    attended, log_total = attend(queries, keys_rot, head_values, allowed)
    attended_low = attended.reshape(LEN, -1).astype(LOW)
    att_parts = [attended_low[:, k * quarter : (k + 1) * quarter] for k in range(4)]
    hidden1 = row_values + (sum(dot_t(a, w) for a, w in zip(att_parts, w_proj)) + vec[2])
    normed2, inverse2 = norm_parts(hidden1)
    second_in = (normed2 * vec[3] + vec[4]).astype(LOW)
    bu3 = [jnp.concatenate(bu[:2]), bu[2], bu[3]]
    upward = [dot(second_in, w) + b for w, b in zip(w_up, bu3)]
    activated = [(u * jax.nn.sigmoid(GELU_SLOPE * u)).astype(LOW) for u in upward]
    result = hidden1 + (sum(dot_t(a, w) for a, w in zip(activated, w_down)) + vec[5])

    def give_back(values_low):
        if relative:
            values_low = dot_t(values_low, shuffle).astype(LOW)
        mine, theirs = values_low[:local_rows], lanes.over_x(values_low[local_rows:])
        swap = slot == 0
        return jnp.stack([jnp.where(swap, mine, theirs), jnp.where(swap, theirs, mine)])[:, None]

    block_output = give_back(result.astype(LOW))

    slot_hit = (ids_row[:, None] == jnp.arange(SLOTS, dtype=jnp.int32)[None, :]).astype(F32)
    picture_size = jnp.sum(slot_hit * length_row.astype(F32)[None, :], -1)
    token_weight = mask_row.astype(F32) * jnp.sqrt(LEN / picture_size)
    grad_y = cot_low.astype(F32) * token_weight[:, None]
    down_grad = grad_y.astype(LOW)

    middle = width // 2

    def weight_grads(left, rights):
        kept = [outer(left[:, :middle], r).astype(LOW) for r in rights]
        sent = [outer(left[:, middle:], r).astype(LOW) for r in rights]
        return [[k, lanes.over_core(s)] for k, s in zip(kept, sent)]

    def columns(addends, start, stop):
        return [v[:, start:stop] for v in addends]

    def reduce_plain(parts):
        own = jnp.concatenate([parts[0], parts[2]], 1).astype(LOW)
        other = jnp.concatenate([parts[1], parts[3]], 1).astype(LOW)
        both = wide_total([own, lanes.over_x(other)])
        return lax.psum_scatter(both, "dp", scatter_dimension=0, tiled=True)

    def reduce_wide(left, rights):
        if not relative:
            a = outer(left, rights[0])
            return reduce_plain(
                [a[:, :hidden], a[:, hidden:], outer(left, rights[1]), outer(left, rights[2])]
            )
        a, b_own, b_other = weight_grads(left, rights)
        first = lanes.reduce_a(columns(a, 0, hidden), columns(a, hidden, 2 * hidden))
        second = lanes.reduce_b(b_own, b_other)
        return jnp.concatenate([first, second], 1)

    grad_down = reduce_wide(down_grad, activated).T
    act_grad = [dot(down_grad, w) for w in w_down]
    up_grad = []
    for g, u in zip(act_grad, upward):
        sigma = jax.nn.sigmoid(GELU_SLOPE * u)
        up_grad.append((g * (sigma + GELU_SLOPE * u * sigma * (1.0 - sigma))).astype(LOW))
    grad_up = reduce_wide(second_in, up_grad)
    sum_up = [jnp.sum(g.astype(F32), 0) for g in up_grad]
    norm2_grad = sum(dot_t(g, w) for g, w in zip(up_grad, w_up))
    hidden1_grad = grad_y + norm_back(norm2_grad, normed2, inverse2, vec[3])
    branch_grad = hidden1_grad.astype(LOW)
    attn_grad = jnp.concatenate([dot(branch_grad, w) for w in w_proj], 1).astype(LOW)
    attn_grad = attn_grad.reshape(LEN, heads, HD)
    query_grad, key_grad, value_grad = attend_back(
        queries, keys_rot, head_values, allowed, log_total, attn_grad
    )
    mixed_grad = jnp.stack(
        [rotate_back(query_grad, cosine, sine), rotate_back(key_grad, cosine, sine), value_grad], 1
    ).astype(LOW)
    mixed_parts = [
        mixed_grad[:, :, k * half_heads : (k + 1) * half_heads].reshape(LEN, 3 * quarter)
        for k in range(4)
    ]
    sum_qkv = [jnp.sum(g.astype(F32), 0).reshape(3, quarter) for g in mixed_parts]
    if relative:
        q_grads = weight_grads(first_in, mixed_parts)
        p_grads = weight_grads(branch_grad, att_parts)
        joined = [
            [jnp.concatenate([a, b], 1) for a, b in zip(q, p)] for q, p in zip(q_grads, p_grads)
        ]
        halves = [lanes.reduce_a(joined[0], joined[1]), lanes.reduce_b(joined[2], joined[3])]
        grad_qkv = jnp.concatenate(
            [h[:, : 3 * quarter].reshape(rows_own, 3, quarter) for h in halves], 2
        )
        grad_proj = jnp.concatenate([h[:, 3 * quarter :] for h in halves], 1).T
    else:
        q_parts = [outer(first_in, g).reshape(width, 3, quarter) for g in mixed_parts]
        own = jnp.concatenate([q_parts[0], q_parts[2]], 2)
        other = jnp.concatenate([q_parts[1], q_parts[3]], 2)
        grad_qkv = lax.psum_scatter(
            own + lanes.over_x(other), "dp", scatter_dimension=0, tiled=True
        )
        grad_proj = reduce_plain([outer(branch_grad, a) for a in att_parts]).T
    norm1_grad = sum(dot_t(g, w) for g, w in zip(mixed_parts, w_qkv))
    input_rows = hidden1_grad + norm_back(norm1_grad, normed1, inverse1, vec[0])
    input_grad = give_back(input_rows.astype(LOW))
    vector_terms = jnp.stack(
        [
            jnp.sum(norm1_grad * normed1, 0),
            jnp.sum(norm1_grad, 0),
            jnp.sum(branch_grad.astype(F32), 0),
            jnp.sum(norm2_grad * normed2, 0),
            jnp.sum(norm2_grad, 0),
            jnp.sum(down_grad.astype(F32), 0),
        ]
    )
    if relative:
        vector_terms = lax.dot_general(
            vector_terms,
            shuffle.astype(F32),
            (((1,), (1,)), ((), ())),
            precision=lax.Precision.HIGHEST,
            preferred_element_type=F32,
        )
    own_small = jnp.concatenate(
        [
            jnp.concatenate([sum_qkv[0], sum_qkv[2]], 1).reshape(-1),
            sum_up[0][:hidden],
            sum_up[1],
        ]
    )
    other_small = jnp.concatenate(
        [
            jnp.concatenate([sum_qkv[1], sum_qkv[3]], 1).reshape(-1),
            sum_up[0][hidden:],
            sum_up[2],
        ]
    )
    first_half = slot == 0
    small = jnp.concatenate(
        [
            jnp.where(first_half, own_small, other_small),
            jnp.where(first_half, other_small, own_small),
            vector_terms.reshape(-1),
        ]
    )
    small = butterfly(small.reshape(-1, 128), dp).reshape(-1)
    size = own_small.shape[0]
    bias_sum = jnp.where(first_half, small[:size], small[size : 2 * size])
    grad_qkv_bias = bias_sum[: qkv_bias.size].reshape(qkv_bias.shape)
    grad_up_bias = bias_sum[qkv_bias.size :]
    grad_vectors = small[2 * size :].reshape(vectors.shape)

    params = (qkv_weight, proj_weight, fc1_weight, fc2_weight, qkv_bias, fc1_bias, vectors)
    moment_list = (
        qkv_moments,
        proj_moments,
        fc1_moments,
        fc2_moments,
        qkv_bias_moments,
        fc1_bias_moments,
        vector_moments,
    )
    shares = (1.0, 1.0, 1.0, 1.0, lead_dp, lead_dp, lead_all)
    summed = (grad_qkv, grad_proj, grad_up, grad_down, grad_qkv_bias, grad_up_bias, grad_vectors)
    new_moments = []
    updates = []
    terms = []
    for master, moments, gradient, factor in zip(params, moment_list, summed, shares):
        first, second, update = lamb_parts(master, moments, gradient * grad_factor)
        new_moments.append(jnp.stack([first, second]))
        updates.append(update)
        terms.append(jnp.sum(update * update) * factor)
    terms = [
        jnp.sum(master * master) * factor for master, factor in zip(params, shares)
    ] + terms
    terms = jnp.pad(jnp.stack(terms), (0, 114)).reshape(1, 128)
    terms = butterfly(terms, dp)[0]
    weight_sq, update_sq = terms[:7], terms[7:14]
    trust = jnp.sqrt(weight_sq) / jnp.sqrt(update_sq + 1e-12)
    new_params = [params[k] - LEARN_RATE * trust[k] * updates[k] for k in range(7)]
    norms = jnp.stack([jnp.sqrt(weight_sq), jnp.sqrt(update_sq)])
    return (
        block_output,
        input_grad,
        *new_params,
        *new_moments,
        *[p.astype(LOW) for p in new_params[:4]],
        norms,
        trust,
    )


def solution(mesh):
    in_specs = (
        P(None, "dp", "tensor", None),
        P(None, "dp", "tensor", None),
        P(None, "dp", None),
        P(None, None, "dp", None),
        P(None, "dp", None),
        P(None, "dp", None),
        P("dp", None, "tensor"),
        P("tensor", "dp"),
        P("dp", "tensor"),
        P("tensor", "dp"),
        P(None, "tensor"),
        P("tensor"),
        P(),
        P(None, "dp", None, "tensor"),
        P(None, "tensor", "dp"),
        P(None, "dp", "tensor"),
        P(None, "tensor", "dp"),
        P(None, None, "tensor"),
        P(None, "tensor"),
        P(),
    )
    out_specs = (
        P(None, "dp", "tensor", None),
        P(None, "dp", "tensor", None),
        P("dp", None, "tensor"),
        P("tensor", "dp"),
        P("dp", "tensor"),
        P("tensor", "dp"),
        P(None, "tensor"),
        P("tensor"),
        P(),
        P(None, "dp", None, "tensor"),
        P(None, "tensor", "dp"),
        P(None, "dp", "tensor"),
        P(None, "tensor", "dp"),
        P(None, None, "tensor"),
        P(None, "tensor"),
        P(),
        P("dp", None, "tensor"),
        P("tensor", "dp"),
        P("dp", "tensor"),
        P("tensor", "dp"),
        P(),
        P(),
    )
    return jax.shard_map(body, mesh=mesh, in_specs=in_specs, out_specs=out_specs, check_vma=False)
```

```python
import jax
import jax.numpy as jnp
from jax import lax
from jax.experimental import pallas as pl
from jax.experimental.pallas import tpu as pltpu
from jax.sharding import PartitionSpec as P

HD = 80
SLOTS = 4
LEN = 576


NEGATIVE = -1e30
EPS_NORM = 1e-06
EPS_ADAM = 1e-06
WEIGHT_DECAY = 0.01
LEARN_RATE = 0.5
GELU_SLOPE = 1.702
F32 = jnp.float32
LOW = jnp.bfloat16


def norm_parts(values):
    center = values - jnp.mean(values, -1, keepdims=True)
    inverse = lax.rsqrt(jnp.mean(center * center, -1, keepdims=True) + EPS_NORM)
    return (center * inverse, inverse)


def norm_back(out_grad, normed, inverse, gain):
    scaled = out_grad * gain
    return inverse * (
        scaled
        - jnp.mean(scaled, -1, keepdims=True)
        - normed * jnp.mean(scaled * normed, -1, keepdims=True)
    )


def rotary_tables(rows_at, cols_at):
    quarter = HD // 4
    frequency = 10000.0 ** (-jnp.arange(quarter, dtype=F32) / quarter)
    halves = jnp.concatenate(
        [
            rows_at.astype(F32)[:, None] * frequency,
            cols_at.astype(F32)[:, None] * frequency,
        ],
        -1,
    )
    angles = jnp.concatenate([halves, halves], -1)
    return (jnp.cos(angles), jnp.sin(angles))


def dot(left, right):
    return lax.dot_general(left, right, (((1,), (0,)), ((), ())), preferred_element_type=F32)


def dot_t(left, right):
    return lax.dot_general(left, right, (((1,), (1,)), ((), ())), preferred_element_type=F32)


def outer(left, right):
    return lax.dot_general(left, right, (((0,), (0,)), ((), ())), preferred_element_type=F32)


def lamb_parts(master, moments, gradient):
    first = 0.5 * moments[0] + 0.5 * gradient
    second = 0.5 * moments[1] + 0.5 * gradient * gradient
    update = first / (jnp.sqrt(second) + EPS_ADAM) + WEIGHT_DECAY * master
    return (first, second, update)


VMEM_LIMIT = 56 * 1024 * 1024


class Order:
    def __init__(self):
        self.last = None


ORDER = Order()


def call(kernel, grid, in_specs, out_specs, out_shape, scratch=(), flops=0, moved=0, after=()):
    if ORDER.last is not None:
        after = [*after, ORDER.last]
    count, extra = len(in_specs), len(after)

    def ordered(*refs):
        kernel(*refs[:count], *refs[count + extra :])

    run = pl.pallas_call(
        ordered,
        grid=grid,
        in_specs=list(in_specs) + [pl.BlockSpec(memory_space=pl.ANY)] * extra,
        out_specs=out_specs,
        out_shape=out_shape,
        scratch_shapes=list(scratch),
        compiler_params=pltpu.CompilerParams(
            dimension_semantics=("arbitrary",) * len(grid), vmem_limit_bytes=VMEM_LIMIT
        ),
        cost_estimate=pl.CostEstimate(flops=flops, bytes_accessed=moved, transcendentals=0),
    )

    def start(*operands):
        result = run(*operands, *after)
        ORDER.last = result[0] if isinstance(result, (list, tuple)) else result
        return result

    return start


def whole(shape):
    return pl.BlockSpec(shape, lambda *_: (0,) * len(shape))


def lookup(table):
    def column(j):
        found = table[0]
        for k in range(1, len(table)):
            found = jnp.where(j == k, table[k], found)
        return found

    return column


class Parts:
    def __init__(self, sets, block):
        self.sets, self.block = sets, block
        self.steps = sum(s[2] for s in sets)
        self.width = sum(piece.shape[0] for piece, _ in sets[0][0])
        self.arrays, self.specs = [], []
        base = 0
        for pieces, _, count in sets:
            for piece, first in pieces:
                self.arrays.append(piece)
                self.specs.append(
                    pl.BlockSpec(
                        (piece.shape[0], block),
                        lambda j, first=first, base=base, count=count: (
                            0,
                            first + jnp.clip(j - base, 0, count - 1),
                        ),
                    )
                )
            base += count

    def each(self, refs, work):
        j = pl.program_id(0)
        base, at = 0, 0
        for pieces, cuts, count in self.sets:
            mine = refs[at : at + len(pieces)]

            @pl.when((j >= base) & (j < base + count))
            def _(mine=mine, cuts=cuts):
                if cuts is None:
                    values = [r[...] for r in mine]
                else:
                    values = [mine[p][r : r + n, :] for p, r, n in cuts]
                work(values[0] if len(values) == 1 else jnp.concatenate(values, 0))

            base += count
            at += len(pieces)

    @property
    def volume(self):
        return self.steps * self.block * self.width


ROWS = 96


def row_loop(rows, work):
    def step(k, carry):
        work(pl.ds(pl.multiple_of(k * ROWS, ROWS), ROWS))
        return carry

    lax.fori_loop(0, rows // ROWS, step, 0)


def times_weight(left, parts, table, ins, in_specs, outs, out_specs, finish, after=()):
    count = len(parts.arrays)

    def kernel(*refs):
        left_ref, w_refs, rest = refs[0], refs[1 : 1 + count], refs[1 + count :]

        def work(w):
            y = jnp.dot(left_ref[...], w, preferred_element_type=F32)
            finish(y, rest[: len(ins)], rest[len(ins) :])

        parts.each(w_refs, work)

    return call(
        kernel,
        (parts.steps,),
        [whole(left.shape)] + parts.specs + in_specs,
        out_specs,
        outs,
        flops=2 * left.shape[0] * parts.volume,
        moved=2 * parts.volume + 6 * left.shape[0] * parts.steps * parts.block,
        after=after,
    )(left, *parts.arrays, *ins)


def times_turned(left, parts, table, ins, in_specs, outs, out_specs, finish, after=()):
    count = len(parts.arrays)
    rows, width = left.shape[0], parts.width
    column = lookup(table)

    def kernel(*refs):
        left_ref, w_refs, rest = refs[0], refs[1 : 1 + count], refs[1 + count :]
        acc = rest[-1]
        rest = rest[:-1]

        def work(w):
            y = lax.dot_general(
                left_ref[...], w, (((1,), (1,)), ((), ())), preferred_element_type=F32
            )

            @pl.when(pl.program_id(0) == 0)
            def _():
                acc[...] = y

            @pl.when(pl.program_id(0) > 0)
            def _():
                acc[...] += y

        parts.each(w_refs, work)

        @pl.when(pl.program_id(0) == parts.steps - 1)
        def _():
            finish(acc, rest[: len(ins)], rest[len(ins) :])

    return call(
        kernel,
        (parts.steps,),
        [pl.BlockSpec((rows, parts.block), lambda j: (0, column(j)))] + parts.specs + in_specs,
        out_specs,
        outs,
        scratch=[pltpu.VMEM((rows, width), F32)],
        flops=2 * rows * parts.volume,
        moved=2 * parts.volume + 2 * left.size + 8 * rows * width,
        after=after,
    )(left, *parts.arrays, *ins)


def qkv_forward(first_in, parts, bias, table, after=()):
    column = lookup(table)
    block = parts.block

    def finish(y, ins, outs):
        outs[0][...] = y + ins[0][...]

    total_columns = parts.steps * block
    return times_weight(
        first_in,
        parts,
        table,
        [bias],
        [pl.BlockSpec((1, block), lambda j: (0, column(j)))],
        [jax.ShapeDtypeStruct((first_in.shape[0], total_columns), F32)],
        [pl.BlockSpec((first_in.shape[0], block), lambda j: (0, column(j)))],
        finish,
        after,
    )[0]


def proj_forward(attended, parts, row_low, vec, after=()):
    rows, width = row_low.shape

    def finish(acc, ins, outs):
        row_ref, vec_ref = ins
        hidden_ref, second_ref = outs

        def work(cut):
            hidden = row_ref[cut, :].astype(F32) + (acc[cut, :] + vec_ref[2:3, :])
            hidden_ref[cut, :] = hidden
            normed, _ = norm_parts(hidden)
            second_ref[cut, :] = (normed * vec_ref[3:4, :] + vec_ref[4:5, :]).astype(LOW)

        row_loop(rows, work)

    return times_turned(
        attended,
        parts,
        list(range(parts.steps)),
        [row_low, vec],
        [whole(row_low.shape), whole(vec.shape)],
        [jax.ShapeDtypeStruct((rows, width), F32), jax.ShapeDtypeStruct((rows, width), LOW)],
        [whole((rows, width))] * 2,
        finish,
        after,
    )


def up_forward(second_in, parts, bias, after=()):
    rows, block = second_in.shape[0], parts.block
    total_columns = parts.steps * block

    def finish(y, ins, outs):
        outs[0][...] = y + ins[0][...]

        def work(cut):
            u = outs[0][cut, :]
            outs[1][cut, :] = (u * jax.nn.sigmoid(GELU_SLOPE * u)).astype(LOW)

        row_loop(rows, work)

    spec = pl.BlockSpec((rows, block), lambda j: (0, j))
    return times_weight(
        second_in,
        parts,
        None,
        [bias],
        [pl.BlockSpec((1, block), lambda j: (0, j))],
        [
            jax.ShapeDtypeStruct((rows, total_columns), F32),
            jax.ShapeDtypeStruct((rows, total_columns), LOW),
        ],
        [spec, spec],
        finish,
        after,
    )


def down_forward(activated, parts, hidden1, vec, after=()):
    rows, width = hidden1.shape

    def finish(acc, ins, outs):
        def work(cut):
            outs[0][cut, :] = (ins[0][cut, :] + (acc[cut, :] + ins[1][5:6, :])).astype(LOW)

        row_loop(rows, work)

    return times_turned(
        activated,
        parts,
        list(range(parts.steps)),
        [hidden1, vec],
        [whole(hidden1.shape), whole(vec.shape)],
        [jax.ShapeDtypeStruct((rows, width), LOW)],
        [whole((rows, width))],
        finish,
        after,
    )[0]


def down_backward(down_grad, parts, upward, after=()):
    rows, block = down_grad.shape[0], parts.block
    total_columns = parts.steps * block

    def finish(y, ins, outs):
        total_ref = outs[1]
        total_ref[...] = jnp.zeros_like(total_ref)
        scratch = outs[2]
        scratch[...] = y

        def work(cut):
            u = ins[0][cut, :]
            sigma = jax.nn.sigmoid(GELU_SLOPE * u)
            g = (scratch[cut, :] * (sigma + GELU_SLOPE * u * sigma * (1.0 - sigma))).astype(LOW)
            outs[0][cut, :] = g
            total_ref[...] += jnp.sum(g.astype(F32), 0, keepdims=True)

        row_loop(rows, work)

    count = len(parts.arrays)

    def kernel(*refs):
        left_ref, w_refs, rest = refs[0], refs[1 : 1 + count], refs[1 + count :]

        def work(w):
            y = jnp.dot(left_ref[...], w, preferred_element_type=F32)
            finish(y, rest[:1], rest[1:])

        parts.each(w_refs, work)

    spec = pl.BlockSpec((rows, block), lambda j: (0, j))
    return call(
        kernel,
        (parts.steps,),
        [whole(down_grad.shape)] + parts.specs + [spec],
        [spec, pl.BlockSpec((1, block), lambda j: (0, j))],
        [
            jax.ShapeDtypeStruct((rows, total_columns), LOW),
            jax.ShapeDtypeStruct((1, total_columns), F32),
        ],
        scratch=[pltpu.VMEM((rows, block), F32)],
        flops=2 * rows * parts.volume,
        moved=2 * parts.volume + 6 * rows * total_columns,
        after=after,
    )(down_grad, *parts.arrays, upward)


def up_backward(up_grad, parts, hidden1, cot_low, token_weight, vec, after=()):
    rows, width = hidden1.shape

    def finish(acc, ins, outs):
        hidden_ref, cot_ref, weight_ref, vec_ref = ins
        grad_ref, branch_ref, sums_ref = outs
        sums_ref[...] = jnp.zeros_like(sums_ref)

        def work(cut):
            e = acc[cut, :]
            normed, inverse = norm_parts(hidden_ref[cut, :])
            grad_y = cot_ref[cut, :].astype(F32) * weight_ref[cut, :]
            grad = grad_y + norm_back(e, normed, inverse, vec_ref[3:4, :])
            branch = grad.astype(LOW)
            grad_ref[cut, :] = grad
            branch_ref[cut, :] = branch
            sums_ref[0:1, :] += jnp.sum(e * normed, 0, keepdims=True)
            sums_ref[1:2, :] += jnp.sum(e, 0, keepdims=True)
            sums_ref[2:3, :] += jnp.sum(branch.astype(F32), 0, keepdims=True)
            sums_ref[3:4, :] += jnp.sum(grad_y.astype(LOW).astype(F32), 0, keepdims=True)

        row_loop(rows, work)

    return times_turned(
        up_grad,
        parts,
        list(range(parts.steps)),
        [hidden1, cot_low, token_weight, vec],
        [whole(hidden1.shape), whole(cot_low.shape), whole(token_weight.shape), whole(vec.shape)],
        [
            jax.ShapeDtypeStruct((rows, width), F32),
            jax.ShapeDtypeStruct((rows, width), LOW),
            jax.ShapeDtypeStruct((8, width), F32),
        ],
        [whole((rows, width)), whole((rows, width)), whole((8, width))],
        finish,
        after,
    )


def proj_backward(branch_grad, parts, after=()):
    rows, block = branch_grad.shape[0], parts.block

    def finish(y, ins, outs):
        outs[0][...] = y.astype(LOW)

    return times_weight(
        branch_grad,
        parts,
        None,
        [],
        [],
        [jax.ShapeDtypeStruct((rows, parts.steps * block), LOW)],
        [pl.BlockSpec((rows, block), lambda j: (0, j))],
        finish,
        after,
    )[0]


def qkv_backward(mixed_grad, parts, table, row_low, hidden1_grad, vec, after=()):
    rows, width = row_low.shape

    def finish(acc, ins, outs):
        row_ref, grad_ref, vec_ref = ins
        sums_ref = outs[1]
        sums_ref[...] = jnp.zeros_like(sums_ref)

        def work(cut):
            e = acc[cut, :]
            normed, inverse = norm_parts(row_ref[cut, :].astype(F32))
            grad = grad_ref[cut, :] + norm_back(e, normed, inverse, vec_ref[0:1, :])
            outs[0][cut, :] = grad.astype(LOW)
            sums_ref[0:1, :] += jnp.sum(e * normed, 0, keepdims=True)
            sums_ref[1:2, :] += jnp.sum(e, 0, keepdims=True)

        row_loop(rows, work)

    return times_turned(
        mixed_grad,
        parts,
        table,
        [row_low, hidden1_grad, vec],
        [whole(row_low.shape), whole(hidden1_grad.shape), whole(vec.shape)],
        [jax.ShapeDtypeStruct((rows, width), LOW), jax.ShapeDtypeStruct((8, width), F32)],
        [whole((rows, width)), whole((8, width))],
        finish,
        after,
    )


def grad_kernel(pairs, block, kind, half, came, after=()):
    rows, width = pairs[0][0].shape
    middle = width // 2
    low = middle // 2
    steps = len(kind)
    near = steps // 2
    count = len(pairs)

    def kernel(*refs):
        lefts, rights = refs[:count], refs[count : 2 * count]
        rest = refs[2 * count :]
        turned = rest[-count:]
        j = pl.program_id(0)

        @pl.when(j == 0)
        def _():
            for k in range(count):
                turned[k][...] = lefts[k][:, half * middle : (half + 1) * middle].T

        for k in range(count):
            hits = [s for s in range(steps) if kind[s][0] == k]
            hit = j == hits[0]
            for s in hits[1:]:
                hit = hit | (j == s)

            @pl.when(hit)
            def _(k=k):
                right = rights[k][...]
                if came is None:
                    rest[0][...] = jnp.dot(
                        turned[k][...], right, preferred_element_type=F32
                    ).astype(LOW)
                    return
                came_ref, own0, own1, other0, far_a, far_b = rest[:6]
                y0 = jnp.dot(turned[k][:low, :], right, preferred_element_type=F32)
                y0 = (y0 + came_ref[:low, :].astype(F32)).astype(LOW)
                y1 = jnp.dot(turned[k][low:, :], right, preferred_element_type=F32)
                y1 = (y1 + came_ref[low:, :].astype(F32)).astype(LOW)

                @pl.when(j < near)
                def _():
                    own0[...] = y0
                    own1[...] = y1

                @pl.when(j >= near)
                def _():
                    other0[...] = y0

                @pl.when((j >= near) & (j < near + near // 2))
                def _():
                    far_a[...] = y1

                @pl.when(j >= near + near // 2)
                def _():
                    far_b[...] = y1

    right_specs = []
    for k in range(count):
        table, last = [], 0
        for s in range(steps):
            if kind[s][0] == k:
                last = kind[s][1]
            table.append(last)
        column = lookup(table)
        right_specs.append(pl.BlockSpec((rows, block), lambda j, column=column: (0, column(j))))

    def clipped(base, number, height):
        spec = pl.BlockSpec((height, block), lambda j: (0, jnp.clip(j - base, 0, number - 1)))
        return spec, jax.ShapeDtypeStruct((height, number * block), LOW)

    if came is None:
        outs = [clipped(0, steps, middle)]
    else:
        outs = [
            clipped(0, near, low),
            clipped(0, near, low),
            clipped(near, near, low),
            clipped(near, near // 2, low),
            clipped(near + near // 2, near // 2, low),
        ]
    extra = [] if came is None else [came]
    return call(
        kernel,
        (steps,),
        [whole(left.shape) for left, _ in pairs]
        + right_specs
        + [pl.BlockSpec((middle, block), lambda j: (0, j)) for _ in extra],
        [s for s, _ in outs],
        [s for _, s in outs],
        scratch=[pltpu.VMEM((middle, rows), LOW) for _ in pairs],
        flops=rows * width * steps * block,
        moved=2 * (middle + rows) * steps * block,
        after=after,
    )(*[left for left, _ in pairs], *[right for _, right in pairs], *extra)


def add_far(other0, own1, far_a, far_b):
    rows, columns = other0.shape
    block = columns // 2

    def kernel(other_ref, own_ref, a_ref, b_ref, x_ref, y_ref):
        j = pl.program_id(0)

        @pl.when(j == 0)
        def _():
            x_ref[...] = (other_ref[...].astype(F32) + a_ref[...].astype(F32)).astype(LOW)
            y_ref[...] = own_ref[...]

        @pl.when(j == 1)
        def _():
            x_ref[...] = other_ref[...]
            y_ref[...] = (own_ref[...].astype(F32) + b_ref[...].astype(F32)).astype(LOW)

    spec = pl.BlockSpec((rows, block), lambda j: (0, j))
    shape = jax.ShapeDtypeStruct((rows, columns), LOW)
    return call(
        kernel,
        (2,),
        [spec, spec, whole(far_a.shape), whole(far_b.shape)],
        [spec, spec],
        [shape, shape],
        flops=2 * rows * columns,
        moved=10 * rows * columns,
    )(other0, own1, far_a, far_b)


def stack_rows(pieces):
    rows, columns = pieces[0].shape
    count = len(pieces)
    block = columns // 2

    def kernel(*refs):
        for k in range(count):
            refs[-1][k * rows : (k + 1) * rows, :] = refs[k][...]

    return call(
        kernel,
        (2,),
        [pl.BlockSpec((rows, block), lambda j: (0, j))] * count,
        pl.BlockSpec((count * rows, block), lambda j: (0, j)),
        jax.ShapeDtypeStruct((count * rows, columns), pieces[0].dtype),
        moved=4 * count * rows * columns,
    )(*pieces)


def add_cuts(arrays, rows, columns, block_rows, block_columns, kind, after=()):
    def kernel(*refs):
        value = refs[0][...].astype(F32)
        for ref in refs[1:-1]:
            value = value + ref[...].astype(F32)
        refs[-1][...] = value.astype(kind)

    specs = [
        pl.BlockSpec(
            (block_rows, block_columns),
            lambda i, j, r=r // block_rows, c=c // block_columns: (r + i, c + j),
        )
        for _, r, c in arrays
    ]
    return call(
        kernel,
        (rows // block_rows, columns // block_columns),
        specs,
        pl.BlockSpec((block_rows, block_columns), lambda i, j: (i, j)),
        jax.ShapeDtypeStruct((rows, columns), kind),
        flops=rows * columns * len(arrays),
        moved=2 * rows * columns * (len(arrays) + 1),
        after=after,
    )(*[a for a, _, _ in arrays])


def turn_pairs(v, heads_lanes):
    middle = HD // 2
    lanes = lax.broadcasted_iota(jnp.int32, v.shape, 1)
    early = lanes % HD < middle
    width = v.shape[1]
    return jnp.where(early, -pltpu.roll(v, width - middle, 1), pltpu.roll(v, middle, 1))


def head_cut(h):
    return slice(h * HD, (h + 1) * HD)


def attention_forward(mixed, cosine, sine, key_code, query_code, groups, after=()):
    rows, columns = mixed.shape
    lanes = columns // (3 * groups)
    heads = lanes // HD
    scale = HD ** (-0.5)

    def kernel(mixed_ref, cos_ref, sin_ref, key_ref, query_ref, qkv_ref, att_ref, lse_ref, out_t):
        cos, sin = cos_ref[...], sin_ref[...]
        for part in range(2):
            cut = slice(part * lanes, (part + 1) * lanes)
            v = mixed_ref[:, cut]
            qkv_ref[:, cut] = (v * cos + turn_pairs(v, lanes) * sin).astype(LOW)
        qkv_ref[:, 2 * lanes :] = mixed_ref[:, 2 * lanes :].astype(LOW)
        query_t = qkv_ref[:, :lanes].T
        keys = qkv_ref[:, lanes : 2 * lanes]
        value_t = qkv_ref[:, 2 * lanes :].T
        allowed = key_ref[...] == query_ref[...]
        for h in range(heads):
            cut = head_cut(h)
            logits = jnp.dot(keys[:, cut], query_t[cut, :], preferred_element_type=F32)
            logits = jnp.where(allowed, logits * scale, NEGATIVE)
            top = jnp.max(logits, 0, keepdims=True)
            exponent = jnp.exp(logits - top)
            total_ = jnp.sum(exponent, 0, keepdims=True)
            prob = (exponent / total_).astype(LOW)
            out_t[cut, :] = jnp.dot(value_t[cut, :], prob, preferred_element_type=F32)
            lse_ref[0, h : h + 1, :] = top + jnp.log(total_)
        att_ref[...] = out_t[...].T.astype(LOW)

    return call(
        kernel,
        (groups,),
        [
            pl.BlockSpec((rows, 3 * lanes), lambda g: (0, g)),
            whole(cosine.shape),
            whole(sine.shape),
            whole(key_code.shape),
            whole(query_code.shape),
        ],
        [
            pl.BlockSpec((rows, 3 * lanes), lambda g: (0, g)),
            pl.BlockSpec((rows, lanes), lambda g: (0, g)),
            pl.BlockSpec((1, heads, rows), lambda g: (g, 0, 0)),
        ],
        [
            jax.ShapeDtypeStruct((rows, columns), LOW),
            jax.ShapeDtypeStruct((rows, groups * lanes), LOW),
            jax.ShapeDtypeStruct((groups, heads, rows), F32),
        ],
        scratch=[pltpu.VMEM((lanes, rows), F32)],
        flops=4 * rows * rows * lanes * groups * 3,
        moved=6 * rows * columns,
        after=after,
    )(mixed, cosine, sine, key_code, query_code)


def attention_backward(qkv, lse, attn_grad, cosine, sine, key_code, query_code, groups, after=()):
    rows, columns = qkv.shape
    lanes = columns // (3 * groups)
    heads = lanes // HD
    scale = HD ** (-0.5)

    def kernel(
        qkv_ref, lse_ref, grad_ref, cos_ref, sin_ref, key_ref, query_ref, out_ref, sum_ref, q_t, k_n, v_n
    ):
        query_t = qkv_ref[:, :lanes].T
        key_t = qkv_ref[:, lanes : 2 * lanes].T
        grad_t = grad_ref[...].T
        queries = qkv_ref[:, :lanes]
        keys = qkv_ref[:, lanes : 2 * lanes]
        values = qkv_ref[:, 2 * lanes :]
        grads = grad_ref[...]
        allowed = key_ref[...] == query_ref[...]
        for h in range(heads):
            cut = head_cut(h)
            logits = jnp.dot(keys[:, cut], query_t[cut, :], preferred_element_type=F32)
            logits = jnp.where(allowed, logits * scale, NEGATIVE)
            prob = jnp.exp(logits - lse_ref[0, h : h + 1, :])
            prob_grad = jnp.dot(values[:, cut], grad_t[cut, :], preferred_element_type=F32)
            inner = jnp.sum(prob * prob_grad, 0, keepdims=True)
            score_grad = (scale * prob * (prob_grad - inner)).astype(LOW)
            q_t[cut, :] = jnp.dot(key_t[cut, :], score_grad, preferred_element_type=F32)
            k_n[:, cut] = jnp.dot(score_grad, queries[:, cut], preferred_element_type=F32)
            v_n[:, cut] = jnp.dot(prob.astype(LOW), grads[:, cut], preferred_element_type=F32)
        cos, sin = cos_ref[...], sin_ref[...]
        for part, w in enumerate((q_t[...].T, k_n[...], v_n[...])):
            cut = slice(part * lanes, (part + 1) * lanes)
            if part < 2:
                w = w * cos - turn_pairs(w, lanes) * sin
            w = w.astype(LOW)
            out_ref[:, cut] = w
            sum_ref[:, cut] = jnp.sum(w.astype(F32), 0, keepdims=True)

    return call(
        kernel,
        (groups,),
        [
            pl.BlockSpec((rows, 3 * lanes), lambda g: (0, g)),
            pl.BlockSpec((1, heads, rows), lambda g: (g, 0, 0)),
            pl.BlockSpec((rows, lanes), lambda g: (0, g)),
            whole(cosine.shape),
            whole(sine.shape),
            whole(key_code.shape),
            whole(query_code.shape),
        ],
        [
            pl.BlockSpec((rows, 3 * lanes), lambda g: (0, g)),
            pl.BlockSpec((1, 3 * lanes), lambda g: (0, g)),
        ],
        [
            jax.ShapeDtypeStruct((rows, columns), LOW),
            jax.ShapeDtypeStruct((1, columns), F32),
        ],
        scratch=[
            pltpu.VMEM((lanes, rows), F32),
            pltpu.VMEM((rows, lanes), F32),
            pltpu.VMEM((rows, lanes), F32),
        ],
        flops=10 * rows * rows * lanes * groups * 3,
        moved=6 * rows * columns,
        after=after,
    )(qkv, lse, attn_grad, cosine, sine, key_code, query_code)
class Lanes:
    def __init__(self, dp):
        self.dp = dp
        self.ring = dp // 4

    def over_x(self, v):
        return lax.ppermute(v, "tensor", [(0, 1), (1, 0)])

    def over_core(self, v):
        return lax.ppermute(v, "dp", [(i, i ^ 1) for i in range(self.dp)])

    def over_y(self, v):
        return lax.ppermute(v, "dp", [(i, i ^ 2) for i in range(self.dp)])

    def down_z(self, v):
        return lax.ppermute(v, "dp", [(i, (i - 4) % self.dp) for i in range(self.dp)])

    def up_z(self, v):
        return lax.ppermute(v, "dp", [(i, (i + 4) % self.dp) for i in range(self.dp)])

    def order(self):
        i = lax.axis_index("dp")
        z, y, c = i // 4, (i // 2) % 2, i % 2
        blocks = []
        for dc in range(2):
            for dy in range(2):
                for dz in range(self.ring):
                    blocks.append(((z + dz) % self.ring) * 4 + (y ^ dy) * 2 + (c ^ dc))
        return jnp.stack(blocks)

    def ring_down(self, v):
        held = [v]
        for _ in range(self.ring - 1):
            held.append(self.down_z(held[-1]))
        return held

    def gather_z(self, shard):
        return stack_rows(self.ring_down(shard))

    def gather_xy(self, held):
        middle = held.shape[1] // 2
        side, across = self.over_x(held), self.over_y(held)
        far_a, far_b = self.over_y(side[:, :middle]), self.over_x(across[:, middle:])
        core = self.over_core
        own = [held, across, core(held), core(across)]
        side_core = core(side)
        other_a = [side, far_a, side_core, core(far_a)]
        other_b = [side, far_b, side_core, core(far_b)]
        return Gathered(own, other_a, other_b)

    def gather_early(self, shard):
        side, across = self.over_x(shard), self.over_y(shard)
        far = self.over_y(side)
        return jnp.concatenate(
            [jnp.concatenate([shard, side], 1), jnp.concatenate([across, far], 1)], 0
        )

    def gather_late(self, both):
        held = self.ring_down(both)
        held = held + [self.over_core(v) for v in held]
        rows = both.shape[0] // 2
        cuts = [
            (dc * self.ring + dz, dy * rows, rows)
            for dc in range(2)
            for dy in range(2)
            for dz in range(self.ring)
        ]
        return Stacked(held, cuts)

    def reduce_xy(self, kept):
        own0, own1, other0, far_a, far_b = kept
        return self.over_y(far_a), self.over_x(far_b)


class Gathered:
    def __init__(self, own, other_a, other_b):
        self.own, self.other_a, self.other_b = own, other_a, other_b

    def parts(self, block, ranges):
        half = self.own[0].shape[1] // 2 // block
        sets = []
        (first, count), (first_a, count_a), (first_b, count_b) = ranges
        if count:
            sets.append(([(v, first) for v in self.own], None, count))
        if count_a:
            sets.append(([(v, first_a) for v in self.other_a], None, count_a))
        if count_b:
            wide = [v.shape[1] // block > half for v in self.other_b]
            sets.append(
                (
                    [(v, first_b + half * w) for v, w in zip(self.other_b, wide)],
                    None,
                    count_b,
                )
            )
        return Parts(sets, block)


class Stacked:
    def __init__(self, pieces, cuts):
        self.pieces, self.cuts = pieces, cuts

    def parts(self, block):
        count = self.pieces[0].shape[1] // block
        return Parts([([(v, 0) for v in self.pieces], self.cuts, count)], block)


def butterfly(value, dp):
    if dp & (dp - 1):
        return lax.psum(value, ("dp", "tensor"))
    value = value + lax.ppermute(value, "tensor", [(0, 1), (1, 0)])
    bit = 1
    while bit < dp:
        value = value + lax.ppermute(value, "dp", [(i, i ^ bit) for i in range(dp)])
        bit *= 2
    return value


def body(
    block_input,
    out_cotangent,
    picture_ids,
    patch_positions,
    picture_lengths,
    pad_mask,
    qkv_weight,
    proj_weight,
    fc1_weight,
    fc2_weight,
    qkv_bias,
    fc1_bias,
    vectors,
    qkv_moments,
    proj_moments,
    fc1_moments,
    fc2_moments,
    qkv_bias_moments,
    fc1_bias_moments,
    vector_moments,
):
    ORDER.last = None
    dp = lax.axis_size("dp")
    relative = dp == 16
    lanes = Lanes(dp)
    slot = lax.axis_index("tensor")
    lead_dp = (lax.axis_index("dp") == 0).astype(F32)
    lead_all = lead_dp * (slot == 0).astype(F32)
    width = block_input.shape[3]
    rows_own = width // dp
    lane_columns = qkv_weight.shape[2]
    hidden = fc1_weight.shape[1]
    grad_factor = float(block_input.shape[0] * block_input.shape[1] * dp * LEN) ** (-0.5)

    shard_1 = jnp.concatenate(
        [qkv_weight.reshape(rows_own, 3 * lane_columns), proj_weight.T], 1
    ).astype(LOW)
    shard_2 = fc1_weight.astype(LOW)
    shard_3 = fc2_weight.astype(LOW).T
    if relative:
        early_3 = lanes.gather_early(shard_3)
        held_1 = lanes.gather_z(shard_1)
        held_2 = lanes.gather_z(shard_2)
        w1, w2 = lanes.gather_xy(held_1), lanes.gather_xy(held_2)
        w3 = lanes.gather_late(early_3)
        w_down = w3.parts(hidden // 2)
    else:

        def plain(shard):
            held = lax.all_gather(shard, "dp", axis=0, tiled=True)
            side = lanes.over_x(held)
            return Gathered([held], [side], [side])

        w1, w2, w3 = plain(shard_1), plain(shard_2), plain(shard_3)
        w_down = w3.parts(hidden // 2, [(0, 2), (0, 1), (0, 1)])
    w_qkv = w1.parts(lane_columns, [(0, 3), (0, 2), (0, 1)])
    w_proj = w1.parts(lane_columns, [(3, 1), (0, 0), (1, 1)])
    w_up = w2.parts(hidden // 2, [(0, 2), (0, 1), (0, 1)])

    def own_row(both):
        mine = lax.dynamic_index_in_dim(both[:, 0], slot, 0, keepdims=False)
        theirs = lax.dynamic_index_in_dim(both[:, 0], 1 - slot, 0, keepdims=False)
        return jnp.concatenate([mine, lanes.over_x(theirs)], 0)

    local_rows = block_input.shape[2]
    biases = jnp.concatenate([qkv_bias.reshape(-1), fc1_bias])
    other_biases = lanes.over_x(biases)
    cut = qkv_bias.size
    bias_qkv = jnp.concatenate([biases[:cut], other_biases[:cut]])[None]
    bias_up = jnp.concatenate([biases[cut:], other_biases[cut:]])[None]

    def pick(array, axis=0):
        return lax.dynamic_index_in_dim(array, slot, axis, keepdims=False)

    def turn(values):
        return jnp.roll(values, -slot * local_rows, axis=-1)

    ids_row = turn(pick(picture_ids[:, 0]))
    rows_at = turn(pick(patch_positions[0, :, 0]))
    cols_at = turn(pick(patch_positions[1, :, 0]))
    mask_row = turn(pick(pad_mask[:, 0]))
    length_row = pick(picture_lengths[:, 0])
    cosine, sine = rotary_tables(rows_at, cols_at)
    groups = 2
    heads = lane_columns // HD
    cosine, sine = jnp.tile(cosine, (1, heads)), jnp.tile(sine, (1, heads))
    key_code = jnp.where(mask_row == 1, ids_row, -1)[:, None]
    query_code = ids_row[None, :]
    slot_hit = (ids_row[:, None] == jnp.arange(SLOTS, dtype=jnp.int32)[None, :]).astype(F32)
    picture_size = jnp.sum(slot_hit * length_row.astype(F32)[None, :], -1)
    token_weight = (mask_row.astype(F32) * jnp.sqrt(LEN / picture_size))[:, None]

    if relative:
        order = lanes.order()
        column = (order[:, None] * rows_own + jnp.arange(rows_own)[None, :]).reshape(-1)
        shuffle = (jnp.arange(width)[:, None] == column[None, :]).astype(LOW)
        vec = lax.dot_general(
            vectors,
            shuffle.astype(F32),
            (((1,), (0,)), ((), ())),
            precision=lax.Precision.HIGHEST,
            preferred_element_type=F32,
        )
        row_low = dot(own_row(block_input), shuffle).astype(LOW)
        cot_low = dot(own_row(out_cotangent), shuffle).astype(LOW)
    else:
        vec = vectors
        row_low = own_row(block_input)
        cot_low = own_row(out_cotangent)

    def give_back(values_low):
        if relative:
            values_low = dot_t(values_low, shuffle).astype(LOW)
        mine, theirs = values_low[:local_rows], lanes.over_x(values_low[local_rows:])
        swap = slot == 0
        return jnp.stack([jnp.where(swap, mine, theirs), jnp.where(swap, theirs, mine)])[:, None]

    wide_kind = [(0, j) for j in range(4)]
    first_kind = [(0, 0), (0, 1), (0, 2), (1, 0), (0, 3), (0, 4), (0, 5), (1, 1)]

    def send_grads(pairs, block, kind):
        (sent,) = grad_kernel(pairs, block, kind, 1, None)
        return lanes.over_core(sent) if relative else sent

    def keep_grads(pairs, block, kind, came):
        return grad_kernel(pairs, block, kind, 0, came)

    def send_far(kept):
        return lanes.over_y(kept[3]), lanes.over_x(kept[4])

    def send_sides(kept, far):
        to_x, to_y = add_far(kept[2], kept[1], *far)
        return lanes.over_x(to_x), lanes.over_y(to_y)

    def ring_step(kept, sides, came, place):
        arrays = [(v, place * rows_own, 0) for v in (kept[0], *sides)]
        if came is not None:
            arrays.append((came, 0, 0))
        kind = LOW if place else F32
        total = add_cuts(arrays, rows_own, hidden, rows_own, hidden, kind)
        return lanes.up_z(total) if place else total

    def plain_grads(pairs, block, kind):
        whole_grad = jnp.concatenate(
            [
                outer(pairs[p][0], pairs[p][1][:, c * block : (c + 1) * block])
                for p, c in kind
            ],
            1,
        )
        both = whole_grad[:, :hidden] + lanes.over_x(whole_grad[:, hidden:])
        return lax.psum_scatter(both, "dp", scatter_dimension=0, tiled=True)

    normed1, _ = norm_parts(row_low.astype(F32))
    first_in = (normed1 * vec[0] + vec[1]).astype(LOW)
    down_grad = (cot_low.astype(F32) * token_weight).astype(LOW)
    mixed = qkv_forward(first_in, w_qkv, bias_qkv, list(range(6)))
    qkv, attended, lse = attention_forward(mixed, cosine, sine, key_code, query_code, groups)
    hidden1, second_in = proj_forward(attended, w_proj, row_low, vec)
    upward, activated = up_forward(second_in, w_up, bias_up)
    pair_3 = [(down_grad, activated)]
    half = hidden // 2
    if relative:
        came_3 = send_grads(pair_3, half, wide_kind)
    result = down_forward(activated, w_down, hidden1, vec)

    if relative:
        kept_3 = keep_grads(pair_3, half, wide_kind, came_3)
        far_3 = send_far(kept_3)
    up_grad, sum_up = down_backward(down_grad, w_down, upward)
    pair_2 = [(second_in, up_grad)]
    if relative:
        sides_3 = send_sides(kept_3, far_3)
        came_2 = send_grads(pair_2, half, wide_kind)
    hidden1_grad, branch_grad, sums_2 = up_backward(
        up_grad, w_up, hidden1, cot_low, token_weight, vec
    )
    if relative:
        kept_2 = keep_grads(pair_2, half, wide_kind, came_2)
        far_2 = send_far(kept_2)
    attn_grad = proj_backward(branch_grad, w_proj)
    if relative:
        ring_3 = ring_step(kept_3, sides_3, None, 3)
    mixed_grad, sum_qkv = attention_backward(
        qkv, lse, attn_grad, cosine, sine, key_code, query_code, groups
    )
    pair_1 = [(first_in, mixed_grad), (branch_grad, attended)]
    if relative:
        ring_3 = ring_step(kept_3, sides_3, ring_3, 2)
        sides_2 = send_sides(kept_2, far_2)
        came_1 = send_grads(pair_1, lane_columns, first_kind)
        ring_3 = ring_step(kept_3, sides_3, ring_3, 1)
        kept_1 = keep_grads(pair_1, lane_columns, first_kind, came_1)
        far_1 = send_far(kept_1)
    input_low, sums_1 = qkv_backward(
        mixed_grad, w_qkv, list(range(6)), row_low, hidden1_grad, vec
    )
    if relative:
        sides_1 = send_sides(kept_1, far_1)
        grad_3 = ring_step(kept_3, sides_3, ring_3, 0)
        ring_2 = ring_step(kept_2, sides_2, None, 3)
        ring_2 = ring_step(kept_2, sides_2, ring_2, 2)
        ring_2 = ring_step(kept_2, sides_2, ring_2, 1)
        grad_2 = ring_step(kept_2, sides_2, ring_2, 0)
        ring_1 = ring_step(kept_1, sides_1, None, 3)
        ring_1 = ring_step(kept_1, sides_1, ring_1, 2)
        ring_1 = ring_step(kept_1, sides_1, ring_1, 1)
        grad_1 = ring_step(kept_1, sides_1, ring_1, 0)
    else:
        grad_3 = plain_grads(pair_3, half, wide_kind)
        grad_2 = plain_grads(pair_2, half, wide_kind)
        grad_1 = plain_grads(pair_1, lane_columns, first_kind)
    block_output = give_back(result)
    input_grad = give_back(input_low)

    grad_qkv = grad_1[:, : 3 * lane_columns].reshape(rows_own, 3, lane_columns)
    grad_proj = grad_1[:, 3 * lane_columns :].T
    grad_up = grad_2
    grad_down = grad_3.T
    vector_terms = jnp.concatenate([sums_1[0:2], sums_2[2:3], sums_2[0:2], sums_2[3:4]], 0)
    if relative:
        vector_terms = lax.dot_general(
            vector_terms,
            shuffle.astype(F32),
            (((1,), (1,)), ((), ())),
            precision=lax.Precision.HIGHEST,
            preferred_element_type=F32,
        )
    qkv_columns = 3 * lane_columns
    own_small = jnp.concatenate([sum_qkv[0, :qkv_columns], sum_up[0, :hidden]])
    other_small = jnp.concatenate([sum_qkv[0, qkv_columns:], sum_up[0, hidden:]])
    first_half = slot == 0
    small = jnp.concatenate(
        [
            jnp.where(first_half, own_small, other_small),
            jnp.where(first_half, other_small, own_small),
            vector_terms.reshape(-1),
        ]
    )
    small = butterfly(small.reshape(-1, 128), dp).reshape(-1)
    size = own_small.shape[0]
    bias_sum = jnp.where(first_half, small[:size], small[size : 2 * size])
    grad_qkv_bias = bias_sum[: qkv_bias.size].reshape(qkv_bias.shape)
    grad_up_bias = bias_sum[qkv_bias.size :]
    grad_vectors = small[2 * size :].reshape(vectors.shape)

    params = (qkv_weight, proj_weight, fc1_weight, fc2_weight, qkv_bias, fc1_bias, vectors)
    moment_list = (
        qkv_moments,
        proj_moments,
        fc1_moments,
        fc2_moments,
        qkv_bias_moments,
        fc1_bias_moments,
        vector_moments,
    )
    shares = (1.0, 1.0, 1.0, 1.0, lead_dp, lead_dp, lead_all)
    summed = (grad_qkv, grad_proj, grad_up, grad_down, grad_qkv_bias, grad_up_bias, grad_vectors)
    new_moments = []
    updates = []
    terms = []
    for master, moments, gradient, factor in zip(params, moment_list, summed, shares):
        first, second, update = lamb_parts(master, moments, gradient * grad_factor)
        new_moments.append(jnp.stack([first, second]))
        updates.append(update)
        terms.append(jnp.sum(update * update) * factor)
    terms = [
        jnp.sum(master * master) * factor for master, factor in zip(params, shares)
    ] + terms
    terms = jnp.pad(jnp.stack(terms), (0, 114)).reshape(1, 128)
    terms = butterfly(terms, dp)[0]
    weight_sq, update_sq = terms[:7], terms[7:14]
    trust = jnp.sqrt(weight_sq) / jnp.sqrt(update_sq + 1e-12)
    new_params = [params[k] - LEARN_RATE * trust[k] * updates[k] for k in range(7)]
    norms = jnp.stack([jnp.sqrt(weight_sq), jnp.sqrt(update_sq)])
    return (
        block_output,
        input_grad,
        *new_params,
        *new_moments,
        *[p.astype(LOW) for p in new_params[:4]],
        norms,
        trust,
    )


def solution(mesh):
    in_specs = (
        P(None, "dp", "tensor", None),
        P(None, "dp", "tensor", None),
        P(None, "dp", None),
        P(None, None, "dp", None),
        P(None, "dp", None),
        P(None, "dp", None),
        P("dp", None, "tensor"),
        P("tensor", "dp"),
        P("dp", "tensor"),
        P("tensor", "dp"),
        P(None, "tensor"),
        P("tensor"),
        P(),
        P(None, "dp", None, "tensor"),
        P(None, "tensor", "dp"),
        P(None, "dp", "tensor"),
        P(None, "tensor", "dp"),
        P(None, None, "tensor"),
        P(None, "tensor"),
        P(),
    )
    out_specs = (
        P(None, "dp", "tensor", None),
        P(None, "dp", "tensor", None),
        P("dp", None, "tensor"),
        P("tensor", "dp"),
        P("dp", "tensor"),
        P("tensor", "dp"),
        P(None, "tensor"),
        P("tensor"),
        P(),
        P(None, "dp", None, "tensor"),
        P(None, "tensor", "dp"),
        P(None, "dp", "tensor"),
        P(None, "tensor", "dp"),
        P(None, None, "tensor"),
        P(None, "tensor"),
        P(),
        P("dp", None, "tensor"),
        P("tensor", "dp"),
        P("dp", "tensor"),
        P("tensor", "dp"),
        P(),
        P(),
    )
    return jax.shard_map(body, mesh=mesh, in_specs=in_specs, out_specs=out_specs, check_vma=False)
```

```python
import jax
import jax.numpy as jnp
from jax import lax
from jax.experimental import pallas as pl
from jax.experimental.pallas import tpu as pltpu
from jax.sharding import PartitionSpec as P

HD = 80
SLOTS = 4
LEN = 576


NEGATIVE = -1e30
EPS_NORM = 1e-06
EPS_ADAM = 1e-06
WEIGHT_DECAY = 0.01
LEARN_RATE = 0.5
GELU_SLOPE = 1.702
F32 = jnp.float32
LOW = jnp.bfloat16


def norm_parts(values):
    center = values - jnp.mean(values, -1, keepdims=True)
    inverse = lax.rsqrt(jnp.mean(center * center, -1, keepdims=True) + EPS_NORM)
    return (center * inverse, inverse)


def norm_back(out_grad, normed, inverse, gain):
    scaled = out_grad * gain
    return inverse * (
        scaled
        - jnp.mean(scaled, -1, keepdims=True)
        - normed * jnp.mean(scaled * normed, -1, keepdims=True)
    )


def rotary_tables(rows_at, cols_at):
    quarter = HD // 4
    frequency = 10000.0 ** (-jnp.arange(quarter, dtype=F32) / quarter)
    halves = jnp.concatenate(
        [
            rows_at.astype(F32)[:, None] * frequency,
            cols_at.astype(F32)[:, None] * frequency,
        ],
        -1,
    )
    angles = jnp.concatenate([halves, halves], -1)
    return (jnp.cos(angles), jnp.sin(angles))


def dot(left, right):
    return lax.dot_general(left, right, (((1,), (0,)), ((), ())), preferred_element_type=F32)


def dot_t(left, right):
    return lax.dot_general(left, right, (((1,), (1,)), ((), ())), preferred_element_type=F32)


def outer(left, right):
    return lax.dot_general(left, right, (((0,), (0,)), ((), ())), preferred_element_type=F32)


def lamb_parts(master, moments, gradient):
    first = 0.5 * moments[0] + 0.5 * gradient
    second = 0.5 * moments[1] + 0.5 * gradient * gradient
    update = first / (jnp.sqrt(second) + EPS_ADAM) + WEIGHT_DECAY * master
    return (first, second, update)


VMEM_LIMIT = 56 * 1024 * 1024
COST = int(8 * 1.15e9)


class Order:
    def __init__(self):
        self.last = None


ORDER = Order()


def call(
    kernel, grid, in_specs, out_specs, out_shape, scratch=(), us=2.4, after=()
):
    if ORDER.last is not None:
        after = [*after, ORDER.last]
    count, extra = len(in_specs), len(after)

    def ordered(*refs):
        kernel(*refs[:count], *refs[count + extra :])

    run = pl.pallas_call(
        ordered,
        grid=grid,
        in_specs=list(in_specs) + [pl.BlockSpec(memory_space=pl.ANY)] * extra,
        out_specs=out_specs,
        out_shape=out_shape,
        scratch_shapes=list(scratch),
        compiler_params=pltpu.CompilerParams(
            dimension_semantics=("arbitrary",) * len(grid), vmem_limit_bytes=VMEM_LIMIT
        ),
        cost_estimate=pl.CostEstimate(
            flops=int(COST * us), bytes_accessed=0, transcendentals=0
        ),
    )

    def start(*operands):
        result = run(*operands, *after)
        ORDER.last = result[0] if isinstance(result, (list, tuple)) else result
        return result

    return start


def whole(shape):
    return pl.BlockSpec(shape, lambda *_: (0,) * len(shape))


def lookup(table):
    def column(j):
        found = table[0]
        for k in range(1, len(table)):
            found = jnp.where(j == k, table[k], found)
        return found

    return column


class Parts:
    def __init__(self, sets, block):
        self.sets, self.block = sets, block
        self.steps = sum(s[2] for s in sets)
        self.width = sum(piece.shape[0] for piece, _ in sets[0][0])
        self.arrays, self.specs = [], []
        base = 0
        for pieces, _, count in sets:
            for piece, first in pieces:
                self.arrays.append(piece)
                self.specs.append(
                    pl.BlockSpec(
                        (piece.shape[0], block),
                        lambda j, first=first, base=base, count=count: (
                            0,
                            first + jnp.clip(j - base, 0, count - 1),
                        ),
                    )
                )
            base += count

    def each(self, refs, work):
        j = pl.program_id(0)
        base, at = 0, 0
        for pieces, cuts, count in self.sets:
            mine = refs[at : at + len(pieces)]

            @pl.when((j >= base) & (j < base + count))
            def _(mine=mine, cuts=cuts):
                if cuts is None:
                    values = [r[...] for r in mine]
                else:
                    values = [mine[p][r : r + n, :] for p, r, n in cuts]
                work(values[0] if len(values) == 1 else jnp.concatenate(values, 0))

            base += count
            at += len(pieces)


ROWS = 96


def row_loop(rows, work):
    def step(k, carry):
        work(pl.ds(pl.multiple_of(k * ROWS, ROWS), ROWS))
        return carry

    lax.fori_loop(0, rows // ROWS, step, 0)


def times_weight(left, parts, table, ins, in_specs, outs, out_specs, finish, us, after=()):
    count = len(parts.arrays)

    def kernel(*refs):
        left_ref, w_refs, rest = refs[0], refs[1 : 1 + count], refs[1 + count :]

        def work(w):
            y = jnp.dot(left_ref[...], w, preferred_element_type=F32)
            finish(y, rest[: len(ins)], rest[len(ins) :])

        parts.each(w_refs, work)

    return call(
        kernel,
        (parts.steps,),
        [whole(left.shape)] + parts.specs + in_specs,
        out_specs,
        outs,
        us=us,
        after=after,
    )(left, *parts.arrays, *ins)


def times_turned(left, parts, table, ins, in_specs, outs, out_specs, finish, us, after=()):
    count = len(parts.arrays)
    rows, width = left.shape[0], parts.width
    column = lookup(table)

    def kernel(*refs):
        left_ref, w_refs, rest = refs[0], refs[1 : 1 + count], refs[1 + count :]
        acc = rest[-1]
        rest = rest[:-1]

        def work(w):
            y = lax.dot_general(
                left_ref[...], w, (((1,), (1,)), ((), ())), preferred_element_type=F32
            )

            @pl.when(pl.program_id(0) == 0)
            def _():
                acc[...] = y

            @pl.when(pl.program_id(0) > 0)
            def _():
                acc[...] += y

        parts.each(w_refs, work)

        @pl.when(pl.program_id(0) == parts.steps - 1)
        def _():
            finish(acc, rest[: len(ins)], rest[len(ins) :])

    return call(
        kernel,
        (parts.steps,),
        [pl.BlockSpec((rows, parts.block), lambda j: (0, column(j)))] + parts.specs + in_specs,
        out_specs,
        outs,
        scratch=[pltpu.VMEM((rows, width), F32)],
        us=us,
        after=after,
    )(left, *parts.arrays, *ins)


def qkv_forward(first_in, parts, bias, table, after=()):
    column = lookup(table)
    block = parts.block

    def finish(y, ins, outs):
        outs[0][...] = y + ins[0][...]

    total_columns = parts.steps * block
    return times_weight(
        first_in,
        parts,
        table,
        [bias],
        [pl.BlockSpec((1, block), lambda j: (0, column(j)))],
        [jax.ShapeDtypeStruct((first_in.shape[0], total_columns), F32)],
        [pl.BlockSpec((first_in.shape[0], block), lambda j: (0, column(j)))],
        finish,
        14,
        after,
    )[0]


def proj_forward(attended, parts, row_low, vec, after=()):
    rows, width = row_low.shape

    def finish(acc, ins, outs):
        row_ref, vec_ref = ins
        hidden_ref, second_ref = outs

        def work(cut):
            hidden = row_ref[cut, :].astype(F32) + (acc[cut, :] + vec_ref[2:3, :])
            hidden_ref[cut, :] = hidden
            normed, _ = norm_parts(hidden)
            second_ref[cut, :] = (normed * vec_ref[3:4, :] + vec_ref[4:5, :]).astype(LOW)

        row_loop(rows, work)

    return times_turned(
        attended,
        parts,
        list(range(parts.steps)),
        [row_low, vec],
        [whole(row_low.shape), whole(vec.shape)],
        [jax.ShapeDtypeStruct((rows, width), F32), jax.ShapeDtypeStruct((rows, width), LOW)],
        [whole((rows, width))] * 2,
        finish,
        9.8,
        after,
    )


def up_forward(second_in, parts, bias, after=()):
    rows, block = second_in.shape[0], parts.block
    total_columns = parts.steps * block

    def finish(y, ins, outs):
        outs[0][...] = y + ins[0][...]

        def work(cut):
            u = outs[0][cut, :]
            outs[1][cut, :] = (u * jax.nn.sigmoid(GELU_SLOPE * u)).astype(LOW)

        row_loop(rows, work)

    spec = pl.BlockSpec((rows, block), lambda j: (0, j))
    return times_weight(
        second_in,
        parts,
        None,
        [bias],
        [pl.BlockSpec((1, block), lambda j: (0, j))],
        [
            jax.ShapeDtypeStruct((rows, total_columns), F32),
            jax.ShapeDtypeStruct((rows, total_columns), LOW),
        ],
        [spec, spec],
        finish,
        17.8,
        after,
    )


def down_forward(activated, parts, hidden1, vec, after=()):
    rows, width = hidden1.shape

    def finish(acc, ins, outs):
        def work(cut):
            outs[0][cut, :] = (ins[0][cut, :] + (acc[cut, :] + ins[1][5:6, :])).astype(LOW)

        row_loop(rows, work)

    return times_turned(
        activated,
        parts,
        list(range(parts.steps)),
        [hidden1, vec],
        [whole(hidden1.shape), whole(vec.shape)],
        [jax.ShapeDtypeStruct((rows, width), LOW)],
        [whole((rows, width))],
        finish,
        15,
        after,
    )[0]


def down_backward(down_grad, parts, upward, after=()):
    rows, block = down_grad.shape[0], parts.block
    total_columns = parts.steps * block

    def finish(y, ins, outs):
        total_ref = outs[1]
        total_ref[...] = jnp.zeros_like(total_ref)
        scratch = outs[2]
        scratch[...] = y

        def work(cut):
            u = ins[0][cut, :]
            sigma = jax.nn.sigmoid(GELU_SLOPE * u)
            g = (scratch[cut, :] * (sigma + GELU_SLOPE * u * sigma * (1.0 - sigma))).astype(LOW)
            outs[0][cut, :] = g
            total_ref[...] += jnp.sum(g.astype(F32), 0, keepdims=True)

        row_loop(rows, work)

    count = len(parts.arrays)

    def kernel(*refs):
        left_ref, w_refs, rest = refs[0], refs[1 : 1 + count], refs[1 + count :]

        def work(w):
            y = jnp.dot(left_ref[...], w, preferred_element_type=F32)
            finish(y, rest[:1], rest[1:])

        parts.each(w_refs, work)

    spec = pl.BlockSpec((rows, block), lambda j: (0, j))
    return call(
        kernel,
        (parts.steps,),
        [whole(down_grad.shape)] + parts.specs + [spec],
        [spec, pl.BlockSpec((1, block), lambda j: (0, j))],
        [
            jax.ShapeDtypeStruct((rows, total_columns), LOW),
            jax.ShapeDtypeStruct((1, total_columns), F32),
        ],
        scratch=[pltpu.VMEM((rows, block), F32)],
        us=19,
        after=after,
    )(down_grad, *parts.arrays, upward)


def up_backward(up_grad, parts, hidden1, cot_low, token_weight, vec, after=()):
    rows, width = hidden1.shape

    def finish(acc, ins, outs):
        hidden_ref, cot_ref, weight_ref, vec_ref = ins
        grad_ref, branch_ref, sums_ref = outs
        sums_ref[...] = jnp.zeros_like(sums_ref)

        def work(cut):
            e = acc[cut, :]
            normed, inverse = norm_parts(hidden_ref[cut, :])
            grad_y = cot_ref[cut, :].astype(F32) * weight_ref[cut, :]
            grad = grad_y + norm_back(e, normed, inverse, vec_ref[3:4, :])
            branch = grad.astype(LOW)
            grad_ref[cut, :] = grad
            branch_ref[cut, :] = branch
            sums_ref[0:1, :] += jnp.sum(e * normed, 0, keepdims=True)
            sums_ref[1:2, :] += jnp.sum(e, 0, keepdims=True)
            sums_ref[2:3, :] += jnp.sum(branch.astype(F32), 0, keepdims=True)
            sums_ref[3:4, :] += jnp.sum(grad_y.astype(LOW).astype(F32), 0, keepdims=True)

        row_loop(rows, work)

    return times_turned(
        up_grad,
        parts,
        list(range(parts.steps)),
        [hidden1, cot_low, token_weight, vec],
        [whole(hidden1.shape), whole(cot_low.shape), whole(token_weight.shape), whole(vec.shape)],
        [
            jax.ShapeDtypeStruct((rows, width), F32),
            jax.ShapeDtypeStruct((rows, width), LOW),
            jax.ShapeDtypeStruct((8, width), F32),
        ],
        [whole((rows, width)), whole((rows, width)), whole((8, width))],
        finish,
        21.7,
        after,
    )


def proj_backward(branch_grad, parts, after=()):
    rows, block = branch_grad.shape[0], parts.block

    def finish(y, ins, outs):
        outs[0][...] = y.astype(LOW)

    return times_weight(
        branch_grad,
        parts,
        None,
        [],
        [],
        [jax.ShapeDtypeStruct((rows, parts.steps * block), LOW)],
        [pl.BlockSpec((rows, block), lambda j: (0, j))],
        finish,
        6,
        after,
    )[0]


def qkv_backward(mixed_grad, parts, table, row_low, hidden1_grad, vec, after=()):
    rows, width = row_low.shape

    def finish(acc, ins, outs):
        row_ref, grad_ref, vec_ref = ins
        sums_ref = outs[1]
        sums_ref[...] = jnp.zeros_like(sums_ref)

        def work(cut):
            e = acc[cut, :]
            normed, inverse = norm_parts(row_ref[cut, :].astype(F32))
            grad = grad_ref[cut, :] + norm_back(e, normed, inverse, vec_ref[0:1, :])
            outs[0][cut, :] = grad.astype(LOW)
            sums_ref[0:1, :] += jnp.sum(e * normed, 0, keepdims=True)
            sums_ref[1:2, :] += jnp.sum(e, 0, keepdims=True)

        row_loop(rows, work)

    return times_turned(
        mixed_grad,
        parts,
        table,
        [row_low, hidden1_grad, vec],
        [whole(row_low.shape), whole(hidden1_grad.shape), whole(vec.shape)],
        [jax.ShapeDtypeStruct((rows, width), LOW), jax.ShapeDtypeStruct((8, width), F32)],
        [whole((rows, width)), whole((8, width))],
        finish,
        18,
        after,
    )


def grad_kernel(pairs, block, kind, half, came, after=()):
    rows, width = pairs[0][0].shape
    middle = width // 2
    low = middle // 2
    steps = len(kind)
    near = steps // 2
    fourth = near // 2
    count = len(pairs)

    def kernel(*refs):
        lefts, rights = refs[:count], refs[count : 2 * count]
        rest = refs[2 * count :]
        turned = rest[-count:]
        j = pl.program_id(0)

        @pl.when(j == 0)
        def _():
            for k in range(count):
                turned[k][...] = lefts[k][:, half * middle : (half + 1) * middle].T

        for k in range(count):
            hits = [s for s in range(steps) if kind[s][0] == k]
            hit = j == hits[0]
            for s in hits[1:]:
                hit = hit | (j == s)

            @pl.when(hit)
            def _(k=k):
                right = rights[k][...]
                if came is None:
                    rest[0][...] = jnp.dot(
                        turned[k][...], right, preferred_element_type=F32
                    ).astype(LOW)
                    return
                came_ref, own0, to_y, to_x, other_a, own_b = rest[:6]
                y0 = jnp.dot(turned[k][:low, :], right, preferred_element_type=F32)
                y0 = (y0 + came_ref[:low, :].astype(F32)).astype(LOW)
                y1 = jnp.dot(turned[k][low:, :], right, preferred_element_type=F32)
                y1 = (y1 + came_ref[low:, :].astype(F32)).astype(LOW)

                @pl.when(j < near)
                def _():
                    own0[...] = y0

                @pl.when(j % near < fourth)
                def _():
                    to_y[...] = y1

                @pl.when((j >= fourth) & (j < near))
                def _():
                    own_b[...] = y1

                @pl.when((j >= near) & (j < near + fourth))
                def _():
                    other_a[...] = y0

                @pl.when(j >= near + fourth)
                def _():
                    to_x[:low, :] = y0
                    to_x[low:, :] = y1

    right_specs = []
    for k in range(count):
        table, last = [], 0
        for s in range(steps):
            if kind[s][0] == k:
                last = kind[s][1]
            table.append(last)
        column = lookup(table)
        right_specs.append(pl.BlockSpec((rows, block), lambda j, column=column: (0, column(j))))

    def clipped(base, number, height):
        spec = pl.BlockSpec((height, block), lambda j: (0, jnp.clip(j - base, 0, number - 1)))
        return spec, jax.ShapeDtypeStruct((height, number * block), LOW)

    if came is None:
        outs = [clipped(0, steps, middle)]
    else:
        turn_spec = pl.BlockSpec(
            (low, block), lambda j: (j // near, jnp.clip(j % near, 0, fourth - 1))
        )
        outs = [
            clipped(0, near, low),
            (turn_spec, jax.ShapeDtypeStruct((middle, fourth * block), LOW)),
            clipped(near + fourth, fourth, middle),
            clipped(near, fourth, low),
            clipped(fourth, fourth, low),
        ]
    extra = [] if came is None else [came]
    return call(
        kernel,
        (steps,),
        [whole(left.shape) for left, _ in pairs]
        + right_specs
        + [pl.BlockSpec((middle, block), lambda j: (0, j)) for _ in extra],
        [s for s, _ in outs],
        [s for _, s in outs],
        scratch=[pltpu.VMEM((middle, rows), LOW) for _ in pairs],
        us=10 if came is None else 12,
        after=after,
    )(*[left for left, _ in pairs], *[right for _, right in pairs], *extra)


def add_second(other_a, own_b, from_y, from_x):
    rows, columns = other_a.shape

    def kernel(a_ref, b_ref, y_ref, x_ref, to_x, to_y):
        to_x[...] = (a_ref[...].astype(F32) + y_ref[...].astype(F32)).astype(LOW)
        to_y[...] = (b_ref[...].astype(F32) + x_ref[...].astype(F32)).astype(LOW)

    shape = jax.ShapeDtypeStruct((rows, columns), LOW)
    block = columns // 2
    spec = pl.BlockSpec((rows, block), lambda j: (0, j))
    later = pl.BlockSpec((rows, block), lambda j: (1, j))
    return call(
        kernel,
        (2,),
        [spec, spec, later, later],
        [spec, spec],
        [shape, shape],
    )(other_a, own_b, from_y, from_x)


def add_ring(own0, from_y, from_x, second_x, second_y, came, place, rows, kind):
    columns = own0.shape[1]
    half = columns // 2

    def kernel(*refs):
        own, y, x, x2, y2 = refs[:5]
        out = refs[-1]
        a = own[:, :half].astype(F32) + y[...].astype(F32) + x2[...].astype(F32)
        b = own[:, half:].astype(F32) + x[...].astype(F32) + y2[...].astype(F32)
        if came is not None:
            a = a + refs[5][:, :half].astype(F32)
            b = b + refs[5][:, half:].astype(F32)
        out[:, :half] = a.astype(kind)
        out[:, half:] = b.astype(kind)

    side = pl.BlockSpec((rows, half), lambda j: (place, 0))
    extra = [] if came is None else [came]
    return call(
        kernel,
        (1,),
        [pl.BlockSpec((rows, columns), lambda j: (place, 0)), side, side, side, side]
        + [whole(v.shape) for v in extra],
        whole((rows, columns)),
        jax.ShapeDtypeStruct((rows, columns), kind),
    )(own0, from_y, from_x, second_x, second_y, *extra)


def cut_far(side, across):
    rows, columns = side.shape
    half = columns // 2

    def kernel(a, b, out_a, out_b):
        out_a[...] = a[...]
        out_b[...] = b[...]

    shape = jax.ShapeDtypeStruct((rows, half), side.dtype)
    return call(
        kernel,
        (1,),
        [
            pl.BlockSpec((rows, half), lambda j: (0, 0)),
            pl.BlockSpec((rows, half), lambda j: (0, 1)),
        ],
        [whole((rows, half))] * 2,
        [shape, shape],
    )(side, across)


def hold(values):
    def kernel(in_ref, out_ref):
        out_ref[...] = in_ref[...]

    return call(
        kernel,
        (1,),
        [whole(values.shape)],
        whole(values.shape),
        jax.ShapeDtypeStruct(values.shape, values.dtype),
        us=1,
    )(values)


def stack_early(shard, side, across, far, after=()):
    rows, columns = shard.shape

    def kernel(a, b, c, d, out):
        out[:rows, :columns] = a[...]
        out[:rows, columns:] = b[...]
        out[rows:, :columns] = c[...]
        out[rows:, columns:] = d[...]

    return call(
        kernel,
        (1,),
        [whole(shard.shape)] * 4,
        whole((2 * rows, 2 * columns)),
        jax.ShapeDtypeStruct((2 * rows, 2 * columns), shard.dtype),
        after=after,
    )(shard, side, across, far)


def stack_rows(pieces, after=()):
    rows, columns = pieces[0].shape
    count = len(pieces)
    block = columns // 2

    def kernel(*refs):
        for k in range(count):
            refs[-1][k * rows : (k + 1) * rows, :] = refs[k][...]

    return call(
        kernel,
        (2,),
        [pl.BlockSpec((rows, block), lambda j: (0, j))] * count,
        pl.BlockSpec((count * rows, block), lambda j: (0, j)),
        jax.ShapeDtypeStruct((count * rows, columns), pieces[0].dtype),
        after=after,
    )(*pieces)


def turn_pairs(v, heads_lanes):
    middle = HD // 2
    lanes = lax.broadcasted_iota(jnp.int32, v.shape, 1)
    early = lanes % HD < middle
    width = v.shape[1]
    return jnp.where(early, -pltpu.roll(v, width - middle, 1), pltpu.roll(v, middle, 1))


def head_cut(h):
    return slice(h * HD, (h + 1) * HD)


def attention_forward(mixed, cosine, sine, key_code, query_code, groups, after=()):
    rows, columns = mixed.shape
    lanes = columns // (3 * groups)
    heads = lanes // HD
    scale = HD ** (-0.5)

    def kernel(mixed_ref, cos_ref, sin_ref, key_ref, query_ref, qkv_ref, att_ref, lse_ref, out_t):
        cos, sin = cos_ref[...], sin_ref[...]
        for part in range(2):
            cut = slice(part * lanes, (part + 1) * lanes)
            v = mixed_ref[:, cut]
            qkv_ref[:, cut] = (v * cos + turn_pairs(v, lanes) * sin).astype(LOW)
        qkv_ref[:, 2 * lanes :] = mixed_ref[:, 2 * lanes :].astype(LOW)
        query_t = qkv_ref[:, :lanes].T
        keys = qkv_ref[:, lanes : 2 * lanes]
        value_t = qkv_ref[:, 2 * lanes :].T
        allowed = key_ref[...] == query_ref[...]
        for h in range(heads):
            cut = head_cut(h)
            logits = jnp.dot(keys[:, cut], query_t[cut, :], preferred_element_type=F32)
            logits = jnp.where(allowed, logits * scale, NEGATIVE)
            top = jnp.max(logits, 0, keepdims=True)
            exponent = jnp.exp(logits - top)
            total_ = jnp.sum(exponent, 0, keepdims=True)
            prob = (exponent / total_).astype(LOW)
            out_t[cut, :] = jnp.dot(value_t[cut, :], prob, preferred_element_type=F32)
            lse_ref[0, h : h + 1, :] = top + jnp.log(total_)
        att_ref[...] = out_t[...].T.astype(LOW)

    return call(
        kernel,
        (groups,),
        [
            pl.BlockSpec((rows, 3 * lanes), lambda g: (0, g)),
            whole(cosine.shape),
            whole(sine.shape),
            whole(key_code.shape),
            whole(query_code.shape),
        ],
        [
            pl.BlockSpec((rows, 3 * lanes), lambda g: (0, g)),
            pl.BlockSpec((rows, lanes), lambda g: (0, g)),
            pl.BlockSpec((1, heads, rows), lambda g: (g, 0, 0)),
        ],
        [
            jax.ShapeDtypeStruct((rows, columns), LOW),
            jax.ShapeDtypeStruct((rows, groups * lanes), LOW),
            jax.ShapeDtypeStruct((groups, heads, rows), F32),
        ],
        scratch=[pltpu.VMEM((lanes, rows), F32)],
        us=19.6,
        after=after,
    )(mixed, cosine, sine, key_code, query_code)


def attention_backward(qkv, lse, attn_grad, cosine, sine, key_code, query_code, groups, after=()):
    rows, columns = qkv.shape
    lanes = columns // (3 * groups)
    heads = lanes // HD
    scale = HD ** (-0.5)

    def kernel(
        qkv_ref, lse_ref, grad_ref, cos_ref, sin_ref, key_ref, query_ref, out_ref, sum_ref, q_t, k_n, v_n
    ):
        query_t = qkv_ref[:, :lanes].T
        key_t = qkv_ref[:, lanes : 2 * lanes].T
        grad_t = grad_ref[...].T
        queries = qkv_ref[:, :lanes]
        keys = qkv_ref[:, lanes : 2 * lanes]
        values = qkv_ref[:, 2 * lanes :]
        grads = grad_ref[...]
        allowed = key_ref[...] == query_ref[...]
        for h in range(heads):
            cut = head_cut(h)
            logits = jnp.dot(keys[:, cut], query_t[cut, :], preferred_element_type=F32)
            logits = jnp.where(allowed, logits * scale, NEGATIVE)
            prob = jnp.exp(logits - lse_ref[0, h : h + 1, :])
            prob_grad = jnp.dot(values[:, cut], grad_t[cut, :], preferred_element_type=F32)
            inner = jnp.sum(prob * prob_grad, 0, keepdims=True)
            score_grad = (scale * prob * (prob_grad - inner)).astype(LOW)
            q_t[cut, :] = jnp.dot(key_t[cut, :], score_grad, preferred_element_type=F32)
            k_n[:, cut] = jnp.dot(score_grad, queries[:, cut], preferred_element_type=F32)
            v_n[:, cut] = jnp.dot(prob.astype(LOW), grads[:, cut], preferred_element_type=F32)
        cos, sin = cos_ref[...], sin_ref[...]
        for part, w in enumerate((q_t[...].T, k_n[...], v_n[...])):
            cut = slice(part * lanes, (part + 1) * lanes)
            if part < 2:
                w = w * cos - turn_pairs(w, lanes) * sin
            w = w.astype(LOW)
            out_ref[:, cut] = w
            sum_ref[:, cut] = jnp.sum(w.astype(F32), 0, keepdims=True)

    return call(
        kernel,
        (groups,),
        [
            pl.BlockSpec((rows, 3 * lanes), lambda g: (0, g)),
            pl.BlockSpec((1, heads, rows), lambda g: (g, 0, 0)),
            pl.BlockSpec((rows, lanes), lambda g: (0, g)),
            whole(cosine.shape),
            whole(sine.shape),
            whole(key_code.shape),
            whole(query_code.shape),
        ],
        [
            pl.BlockSpec((rows, 3 * lanes), lambda g: (0, g)),
            pl.BlockSpec((1, 3 * lanes), lambda g: (0, g)),
        ],
        [
            jax.ShapeDtypeStruct((rows, columns), LOW),
            jax.ShapeDtypeStruct((1, columns), F32),
        ],
        scratch=[
            pltpu.VMEM((lanes, rows), F32),
            pltpu.VMEM((rows, lanes), F32),
            pltpu.VMEM((rows, lanes), F32),
        ],
        us=27.3,
        after=after,
    )(qkv, lse, attn_grad, cosine, sine, key_code, query_code)
class Lanes:
    def __init__(self, dp):
        self.dp = dp
        self.ring = dp // 4

    def over_x(self, v):
        return lax.ppermute(v, "tensor", [(0, 1), (1, 0)])

    def over_core(self, v):
        return lax.ppermute(v, "dp", [(i, i ^ 1) for i in range(self.dp)])

    def over_y(self, v):
        return lax.ppermute(v, "dp", [(i, i ^ 2) for i in range(self.dp)])

    def down_z(self, v):
        return lax.ppermute(v, "dp", [(i, (i - 4) % self.dp) for i in range(self.dp)])

    def up_z(self, v):
        return lax.ppermute(v, "dp", [(i, (i + 4) % self.dp) for i in range(self.dp)])

    def order(self):
        i = lax.axis_index("dp")
        z, y, c = i // 4, (i // 2) % 2, i % 2
        blocks = []
        for dc in range(2):
            for dy in range(2):
                for dz in range(self.ring):
                    blocks.append(((z + dz) % self.ring) * 4 + (y ^ dy) * 2 + (c ^ dc))
        return jnp.stack(blocks)

    def ring_down(self, v):
        held = [v]
        for _ in range(self.ring - 1):
            held.append(self.down_z(held[-1]))
        return held

    def corners(self, held):
        side, across = self.over_x(held), self.over_y(held)
        return side, across, *self.far(side, across)

    def far(self, side, across):
        a, b = cut_far(side, across)
        return self.over_y(a), self.over_x(b)

    def gathered(self, held, corners):
        side, across, far_a, far_b = corners
        core = self.over_core
        side_core = core(side)
        return Gathered(
            [held, across, core(held), core(across)],
            [side, far_a, side_core, core(far_a)],
            [side, far_b, side_core, core(far_b)],
        )

    def stacked(self, held):
        rows = held[0].shape[0] // 2
        held = held + [self.over_core(v) for v in held]
        cuts = [
            (dc * self.ring + dz, dy * rows, rows)
            for dc in range(2)
            for dy in range(2)
            for dz in range(self.ring)
        ]
        return Stacked(held, cuts)


class Gathered:
    def __init__(self, own, other_a, other_b):
        self.own, self.other_a, self.other_b = own, other_a, other_b

    def parts(self, block, ranges):
        half = self.own[0].shape[1] // 2 // block
        sets = []
        (first, count), (first_a, count_a), (first_b, count_b) = ranges
        if count:
            sets.append(([(v, first) for v in self.own], None, count))
        if count_a:
            sets.append(([(v, first_a) for v in self.other_a], None, count_a))
        if count_b:
            wide = [v.shape[1] // block > half for v in self.other_b]
            sets.append(
                (
                    [(v, first_b + half * w) for v, w in zip(self.other_b, wide)],
                    None,
                    count_b,
                )
            )
        return Parts(sets, block)


class Stacked:
    def __init__(self, pieces, cuts):
        self.pieces, self.cuts = pieces, cuts

    def parts(self, block):
        count = self.pieces[0].shape[1] // block
        return Parts([([(v, 0) for v in self.pieces], self.cuts, count)], block)


def butterfly(value, dp):
    if dp & (dp - 1):
        return lax.psum(value, ("dp", "tensor"))
    value = value + lax.ppermute(value, "tensor", [(0, 1), (1, 0)])
    bit = 1
    while bit < dp:
        value = value + lax.ppermute(value, "dp", [(i, i ^ bit) for i in range(dp)])
        bit *= 2
    return value


def body(
    block_input,
    out_cotangent,
    picture_ids,
    patch_positions,
    picture_lengths,
    pad_mask,
    qkv_weight,
    proj_weight,
    fc1_weight,
    fc2_weight,
    qkv_bias,
    fc1_bias,
    vectors,
    qkv_moments,
    proj_moments,
    fc1_moments,
    fc2_moments,
    qkv_bias_moments,
    fc1_bias_moments,
    vector_moments,
):
    ORDER.last = None
    dp = lax.axis_size("dp")
    relative = dp == 16
    lanes = Lanes(dp)
    slot = lax.axis_index("tensor")
    lead_dp = (lax.axis_index("dp") == 0).astype(F32)
    lead_all = lead_dp * (slot == 0).astype(F32)
    width = block_input.shape[3]
    rows_own = width // dp
    lane_columns = qkv_weight.shape[2]
    hidden = fc1_weight.shape[1]
    grad_factor = float(block_input.shape[0] * block_input.shape[1] * dp * LEN) ** (-0.5)

    shard_1 = jnp.concatenate(
        [qkv_weight.reshape(rows_own, 3 * lane_columns), proj_weight.T], 1
    ).astype(LOW)
    shard_2 = fc1_weight.astype(LOW)
    shard_3 = fc2_weight.astype(LOW).T
    if relative:
        ring_1 = lanes.ring_down(shard_1)
        side_3, across_3 = lanes.over_x(shard_3), lanes.over_y(shard_3)
        far_3 = lanes.over_y(side_3)
        late_3 = [stack_early(shard_3, side_3, across_3, far_3, after=[ring_1[2]])]
        held_1 = stack_rows(ring_1)
        corners_1 = lanes.corners(held_1)
        w1 = lanes.gathered(held_1, corners_1)
        for _ in range(3):
            late_3.append(lanes.down_z(late_3[-1]))
        ring_2 = lanes.ring_down(shard_2)
        held_2 = stack_rows(ring_2, after=[corners_1[2], corners_1[3], late_3[1]])
        sides_up = lanes.over_x(held_2), lanes.over_y(held_2)
        w3 = lanes.stacked(late_3)
        w_down = w3.parts(hidden // 2)
    else:

        def plain(shard):
            held = lax.all_gather(shard, "dp", axis=0, tiled=True)
            side = lanes.over_x(held)
            return Gathered([held], [side], [side])

        w1, w2, w3 = plain(shard_1), plain(shard_2), plain(shard_3)
        w_up = w2.parts(hidden // 2, [(0, 2), (0, 1), (0, 1)])
        w_down = w3.parts(hidden // 2, [(0, 2), (0, 1), (0, 1)])
    w_qkv = w1.parts(lane_columns, [(0, 3), (0, 2), (0, 1)])
    w_proj = w1.parts(lane_columns, [(3, 1), (0, 0), (1, 1)])

    def own_row(both):
        mine = lax.dynamic_index_in_dim(both[:, 0], slot, 0, keepdims=False)
        theirs = lax.dynamic_index_in_dim(both[:, 0], 1 - slot, 0, keepdims=False)
        return jnp.concatenate([mine, lanes.over_x(theirs)], 0)

    local_rows = block_input.shape[2]
    biases = jnp.concatenate([qkv_bias.reshape(-1), fc1_bias])
    other_biases = lanes.over_x(biases)
    cut = qkv_bias.size
    bias_qkv = jnp.concatenate([biases[:cut], other_biases[:cut]])[None]
    bias_up = jnp.concatenate([biases[cut:], other_biases[cut:]])[None]

    def pick(array, axis=0):
        return lax.dynamic_index_in_dim(array, slot, axis, keepdims=False)

    def turn(values):
        return jnp.roll(values, -slot * local_rows, axis=-1)

    ids_row = turn(pick(picture_ids[:, 0]))
    rows_at = turn(pick(patch_positions[0, :, 0]))
    cols_at = turn(pick(patch_positions[1, :, 0]))
    mask_row = turn(pick(pad_mask[:, 0]))
    length_row = pick(picture_lengths[:, 0])
    cosine, sine = rotary_tables(rows_at, cols_at)
    groups = 2
    heads = lane_columns // HD
    cosine, sine = jnp.tile(cosine, (1, heads)), jnp.tile(sine, (1, heads))
    key_code = jnp.where(mask_row == 1, ids_row, -1)[:, None]
    query_code = ids_row[None, :]
    slot_hit = (ids_row[:, None] == jnp.arange(SLOTS, dtype=jnp.int32)[None, :]).astype(F32)
    picture_size = jnp.sum(slot_hit * length_row.astype(F32)[None, :], -1)
    token_weight = (mask_row.astype(F32) * jnp.sqrt(LEN / picture_size))[:, None]

    if relative:
        order = lanes.order()
        column = (order[:, None] * rows_own + jnp.arange(rows_own)[None, :]).reshape(-1)
        shuffle = (jnp.arange(width)[:, None] == column[None, :]).astype(LOW)
        vec = lax.dot_general(
            vectors,
            shuffle.astype(F32),
            (((1,), (0,)), ((), ())),
            precision=lax.Precision.HIGHEST,
            preferred_element_type=F32,
        )
        row_low = dot(own_row(block_input), shuffle).astype(LOW)
        cot_low = dot(own_row(out_cotangent), shuffle).astype(LOW)
    else:
        vec = vectors
        row_low = own_row(block_input)
        cot_low = own_row(out_cotangent)

    def give_back(values_low):
        if relative:
            values_low = dot_t(values_low, shuffle).astype(LOW)
        mine, theirs = values_low[:local_rows], lanes.over_x(values_low[local_rows:])
        swap = slot == 0
        return jnp.stack([jnp.where(swap, mine, theirs), jnp.where(swap, theirs, mine)])[:, None]

    wide_kind = [(0, j) for j in range(4)]
    first_kind = [(0, 0), (0, 1), (0, 2), (1, 0), (0, 3), (0, 4), (0, 5), (1, 1)]

    def send_grads(pairs, block, kind):
        (sent,) = grad_kernel(pairs, block, kind, 1, None)
        return lanes.over_core(sent) if relative else sent

    def keep_grads(pairs, block, kind, came, after=()):
        return grad_kernel(pairs, block, kind, 0, came, after)

    def send_first(kept):
        return lanes.over_y(kept[1]), lanes.over_x(kept[2])

    def send_second(kept, first):
        to_x, to_y = add_second(kept[3], kept[4], *first)
        return (*first, lanes.over_x(to_x), lanes.over_y(to_y))

    def ring_step(kept, sides, came, place):
        kind = LOW if place else F32
        total = add_ring(kept[0], *sides, came, place, rows_own, kind)
        return lanes.up_z(total) if place else total

    def plain_grads(pairs, block, kind):
        whole_grad = jnp.concatenate(
            [
                outer(pairs[p][0], pairs[p][1][:, c * block : (c + 1) * block])
                for p, c in kind
            ],
            1,
        )
        both = whole_grad[:, :hidden] + lanes.over_x(whole_grad[:, hidden:])
        return lax.psum_scatter(both, "dp", scatter_dimension=0, tiled=True)

    normed1, _ = norm_parts(row_low.astype(F32))
    first_in = (normed1 * vec[0] + vec[1]).astype(LOW)
    down_grad = (cot_low.astype(F32) * token_weight).astype(LOW)
    mixed = qkv_forward(first_in, w_qkv, bias_qkv, list(range(6)))
    qkv, attended, lse = attention_forward(mixed, cosine, sine, key_code, query_code, groups)
    before_proj = []
    if relative:
        corners_2 = (*sides_up, *lanes.far(*sides_up))
        before_proj = [late_3[2]]
    hidden1, second_in = proj_forward(attended, w_proj, row_low, vec, after=before_proj)
    if relative:
        w_up = lanes.gathered(held_2, corners_2).parts(
            hidden // 2, [(0, 2), (0, 1), (0, 1)]
        )
    upward, activated = up_forward(second_in, w_up, bias_up)
    pair_3 = [(down_grad, activated)]
    half = hidden // 2
    if relative:
        came_3 = send_grads(pair_3, half, wide_kind)
    result = down_forward(activated, w_down, hidden1, vec)
    block_output = give_back(result)

    if relative:
        kept_3 = keep_grads(pair_3, half, wide_kind, came_3)
        first_3 = send_first(kept_3)
    up_grad, sum_up = down_backward(down_grad, w_down, upward)
    pair_2 = [(second_in, up_grad)]
    if relative:
        sides_3 = send_second(kept_3, first_3)
        came_2 = send_grads(pair_2, half, wide_kind)
    hidden1_grad, branch_grad, sums_2 = up_backward(
        up_grad, w_up, hidden1, cot_low, token_weight, vec
    )
    if relative:
        kept_2 = keep_grads(pair_2, half, wide_kind, came_2, after=[block_output])
        first_2 = send_first(kept_2)
        ring_3 = ring_step(kept_3, sides_3, None, 3)
    attn_grad = proj_backward(branch_grad, w_proj)
    if relative:
        ring_3 = ring_step(kept_3, sides_3, ring_3, 2)
    mixed_grad, sum_qkv = attention_backward(
        qkv, lse, attn_grad, cosine, sine, key_code, query_code, groups
    )
    pair_1 = [(first_in, mixed_grad), (branch_grad, attended)]
    if relative:
        sides_2 = send_second(kept_2, first_2)
        ring_3 = ring_step(kept_3, sides_3, ring_3, 1)
        came_1 = send_grads(pair_1, lane_columns, first_kind)
        ring_2 = ring_step(kept_2, sides_2, None, 3)
        kept_1 = keep_grads(pair_1, lane_columns, first_kind, came_1)
        first_1 = send_first(kept_1)
        ring_2 = ring_step(kept_2, sides_2, ring_2, 2)
        grad_3 = ring_step(kept_3, sides_3, ring_3, 0)
    input_low, sums_1 = qkv_backward(
        mixed_grad, w_qkv, list(range(6)), row_low, hidden1_grad, vec
    )
    if relative:
        ring_2 = ring_step(kept_2, sides_2, ring_2, 1)
        sides_1 = send_second(kept_1, first_1)
        sums_1 = hold(sums_1)
        grad_2 = ring_step(kept_2, sides_2, ring_2, 0)
        ring_1 = ring_step(kept_1, sides_1, None, 3)
        ring_1 = ring_step(kept_1, sides_1, ring_1, 2)
        ring_1 = ring_step(kept_1, sides_1, ring_1, 1)
        grad_1 = ring_step(kept_1, sides_1, ring_1, 0)
    else:
        grad_3 = plain_grads(pair_3, half, wide_kind)
        grad_2 = plain_grads(pair_2, half, wide_kind)
        grad_1 = plain_grads(pair_1, lane_columns, first_kind)
    input_grad = give_back(input_low)

    grad_qkv = grad_1[:, : 3 * lane_columns].reshape(rows_own, 3, lane_columns)
    grad_proj = grad_1[:, 3 * lane_columns :].T
    grad_up = grad_2
    grad_down = grad_3.T
    vector_terms = jnp.concatenate([sums_1[0:2], sums_2[2:3], sums_2[0:2], sums_2[3:4]], 0)
    if relative:
        vector_terms = lax.dot_general(
            vector_terms,
            shuffle.astype(F32),
            (((1,), (1,)), ((), ())),
            precision=lax.Precision.HIGHEST,
            preferred_element_type=F32,
        )
    qkv_columns = 3 * lane_columns
    own_small = jnp.concatenate([sum_qkv[0, :qkv_columns], sum_up[0, :hidden]])
    other_small = jnp.concatenate([sum_qkv[0, qkv_columns:], sum_up[0, hidden:]])
    first_half = slot == 0
    small = jnp.concatenate(
        [
            jnp.where(first_half, own_small, other_small),
            jnp.where(first_half, other_small, own_small),
            vector_terms.reshape(-1),
        ]
    )
    small = butterfly(small.reshape(-1, 128), dp).reshape(-1)
    size = own_small.shape[0]
    bias_sum = jnp.where(first_half, small[:size], small[size : 2 * size])
    grad_qkv_bias = bias_sum[: qkv_bias.size].reshape(qkv_bias.shape)
    grad_up_bias = bias_sum[qkv_bias.size :]
    grad_vectors = small[2 * size :].reshape(vectors.shape)

    params = (qkv_weight, proj_weight, fc1_weight, fc2_weight, qkv_bias, fc1_bias, vectors)
    moment_list = (
        qkv_moments,
        proj_moments,
        fc1_moments,
        fc2_moments,
        qkv_bias_moments,
        fc1_bias_moments,
        vector_moments,
    )
    shares = (1.0, 1.0, 1.0, 1.0, lead_dp, lead_dp, lead_all)
    summed = (grad_qkv, grad_proj, grad_up, grad_down, grad_qkv_bias, grad_up_bias, grad_vectors)
    new_moments = []
    updates = []
    terms = []
    for master, moments, gradient, factor in zip(params, moment_list, summed, shares):
        first, second, update = lamb_parts(master, moments, gradient * grad_factor)
        new_moments.append(jnp.stack([first, second]))
        updates.append(update)
        terms.append(jnp.sum(update * update) * factor)
    terms = [
        jnp.sum(master * master) * factor for master, factor in zip(params, shares)
    ] + terms
    terms = jnp.pad(jnp.stack(terms), (0, 114)).reshape(1, 128)
    terms = butterfly(terms, dp)[0]
    weight_sq, update_sq = terms[:7], terms[7:14]
    trust = jnp.sqrt(weight_sq) / jnp.sqrt(update_sq + 1e-12)
    new_params = [params[k] - LEARN_RATE * trust[k] * updates[k] for k in range(7)]
    norms = jnp.stack([jnp.sqrt(weight_sq), jnp.sqrt(update_sq)])
    return (
        block_output,
        input_grad,
        *new_params,
        *new_moments,
        *[p.astype(LOW) for p in new_params[:4]],
        norms,
        trust,
    )


def solution(mesh):
    in_specs = (
        P(None, "dp", "tensor", None),
        P(None, "dp", "tensor", None),
        P(None, "dp", None),
        P(None, None, "dp", None),
        P(None, "dp", None),
        P(None, "dp", None),
        P("dp", None, "tensor"),
        P("tensor", "dp"),
        P("dp", "tensor"),
        P("tensor", "dp"),
        P(None, "tensor"),
        P("tensor"),
        P(),
        P(None, "dp", None, "tensor"),
        P(None, "tensor", "dp"),
        P(None, "dp", "tensor"),
        P(None, "tensor", "dp"),
        P(None, None, "tensor"),
        P(None, "tensor"),
        P(),
    )
    out_specs = (
        P(None, "dp", "tensor", None),
        P(None, "dp", "tensor", None),
        P("dp", None, "tensor"),
        P("tensor", "dp"),
        P("dp", "tensor"),
        P("tensor", "dp"),
        P(None, "tensor"),
        P("tensor"),
        P(),
        P(None, "dp", None, "tensor"),
        P(None, "tensor", "dp"),
        P(None, "dp", "tensor"),
        P(None, "tensor", "dp"),
        P(None, None, "tensor"),
        P(None, "tensor"),
        P(),
        P("dp", None, "tensor"),
        P("tensor", "dp"),
        P("dp", "tensor"),
        P("tensor", "dp"),
        P(),
        P(),
    )
    return jax.shard_map(body, mesh=mesh, in_specs=in_specs, out_specs=out_specs, check_vma=False)
```

```python
import jax
import jax.numpy as jnp
from jax import lax
from jax.experimental import pallas as pl
from jax.experimental.pallas import tpu as pltpu
from jax.sharding import PartitionSpec as P

HD = 80
SLOTS = 4
LEN = 576


NEGATIVE = -1e30
EPS_NORM = 1e-06
EPS_ADAM = 1e-06
WEIGHT_DECAY = 0.01
LEARN_RATE = 0.5
GELU_SLOPE = 1.702
F32 = jnp.float32
LOW = jnp.bfloat16


def norm_parts(values):
    center = values - jnp.mean(values, -1, keepdims=True)
    inverse = lax.rsqrt(jnp.mean(center * center, -1, keepdims=True) + EPS_NORM)
    return (center * inverse, inverse)


def norm_back(out_grad, normed, inverse, gain):
    scaled = out_grad * gain
    return inverse * (
        scaled
        - jnp.mean(scaled, -1, keepdims=True)
        - normed * jnp.mean(scaled * normed, -1, keepdims=True)
    )


def rotary_tables(rows_at, cols_at):
    quarter = HD // 4
    frequency = 10000.0 ** (-jnp.arange(quarter, dtype=F32) / quarter)
    halves = jnp.concatenate(
        [
            rows_at.astype(F32)[:, None] * frequency,
            cols_at.astype(F32)[:, None] * frequency,
        ],
        -1,
    )
    angles = jnp.concatenate([halves, halves], -1)
    return (jnp.cos(angles), jnp.sin(angles))


def dot(left, right):
    return lax.dot_general(left, right, (((1,), (0,)), ((), ())), preferred_element_type=F32)


def dot_t(left, right):
    return lax.dot_general(left, right, (((1,), (1,)), ((), ())), preferred_element_type=F32)


def outer(left, right):
    return lax.dot_general(left, right, (((0,), (0,)), ((), ())), preferred_element_type=F32)


def lamb_parts(master, moments, gradient):
    first = 0.5 * moments[0] + 0.5 * gradient
    second = 0.5 * moments[1] + 0.5 * gradient * gradient
    update = first / (jnp.sqrt(second) + EPS_ADAM) + WEIGHT_DECAY * master
    return (first, second, update)


VMEM_LIMIT = 56 * 1024 * 1024
COST = int(8 * 1.15e9)


class Order:
    def __init__(self):
        self.last = None


ORDER = Order()


def call(
    kernel, grid, in_specs, out_specs, out_shape, scratch=(), us=2.4, after=()
):
    if ORDER.last is not None:
        after = [*after, ORDER.last]
    count, extra = len(in_specs), len(after)

    def ordered(*refs):
        kernel(*refs[:count], *refs[count + extra :])

    run = pl.pallas_call(
        ordered,
        grid=grid,
        in_specs=list(in_specs) + [pl.BlockSpec(memory_space=pl.ANY)] * extra,
        out_specs=out_specs,
        out_shape=out_shape,
        scratch_shapes=list(scratch),
        compiler_params=pltpu.CompilerParams(
            dimension_semantics=("arbitrary",) * len(grid), vmem_limit_bytes=VMEM_LIMIT
        ),
        cost_estimate=pl.CostEstimate(
            flops=int(COST * us), bytes_accessed=0, transcendentals=0
        ),
    )

    def start(*operands):
        result = run(*operands, *after)
        ORDER.last = result[0] if isinstance(result, (list, tuple)) else result
        return result

    return start


def whole(shape):
    return pl.BlockSpec(shape, lambda *_: (0,) * len(shape))


def lookup(table):
    def column(j):
        found = table[0]
        for k in range(1, len(table)):
            found = jnp.where(j == k, table[k], found)
        return found

    return column


class Parts:
    def __init__(self, sets, block):
        self.sets, self.block = sets, block
        self.steps = sum(s[2] for s in sets)
        self.width = sum(piece.shape[0] for piece, _ in sets[0][0])
        self.arrays, self.specs = [], []
        base = 0
        for pieces, _, count in sets:
            for piece, first in pieces:
                self.arrays.append(piece)
                self.specs.append(
                    pl.BlockSpec(
                        (piece.shape[0], block),
                        lambda j, first=first, base=base, count=count: (
                            0,
                            first + jnp.clip(j - base, 0, count - 1),
                        ),
                    )
                )
            base += count

    def each(self, refs, work):
        j = pl.program_id(0)
        base, at = 0, 0
        for pieces, cuts, count in self.sets:
            mine = refs[at : at + len(pieces)]

            @pl.when((j >= base) & (j < base + count))
            def _(mine=mine, cuts=cuts):
                if cuts is None:
                    values = [r[...] for r in mine]
                else:
                    values = [mine[p][r : r + n, :] for p, r, n in cuts]
                work(values[0] if len(values) == 1 else jnp.concatenate(values, 0))

            base += count
            at += len(pieces)


def row_loop(rows, work):
    work(pl.ds(0, rows))


def times_weight(left, parts, table, ins, in_specs, outs, out_specs, finish, us, after=()):
    count = len(parts.arrays)

    def kernel(*refs):
        left_ref, w_refs, rest = refs[0], refs[1 : 1 + count], refs[1 + count :]

        def work(w):
            y = jnp.dot(left_ref[...], w, preferred_element_type=F32)
            finish(y, rest[: len(ins)], rest[len(ins) :])

        parts.each(w_refs, work)

    return call(
        kernel,
        (parts.steps,),
        [whole(left.shape)] + parts.specs + in_specs,
        out_specs,
        outs,
        us=us,
        after=after,
    )(left, *parts.arrays, *ins)


def times_turned(left, parts, table, ins, in_specs, outs, out_specs, finish, us, after=()):
    count = len(parts.arrays)
    rows, width = left.shape[0], parts.width
    column = lookup(table)

    def kernel(*refs):
        left_ref, w_refs, rest = refs[0], refs[1 : 1 + count], refs[1 + count :]
        acc = rest[-1]
        rest = rest[:-1]

        def work(w):
            y = lax.dot_general(
                left_ref[...], w, (((1,), (1,)), ((), ())), preferred_element_type=F32
            )

            @pl.when(pl.program_id(0) == 0)
            def _():
                acc[...] = y

            @pl.when(pl.program_id(0) > 0)
            def _():
                acc[...] += y

        parts.each(w_refs, work)

        @pl.when(pl.program_id(0) == parts.steps - 1)
        def _():
            finish(acc, rest[: len(ins)], rest[len(ins) :])

    return call(
        kernel,
        (parts.steps,),
        [pl.BlockSpec((rows, parts.block), lambda j: (0, column(j)))] + parts.specs + in_specs,
        out_specs,
        outs,
        scratch=[pltpu.VMEM((rows, width), F32)],
        us=us,
        after=after,
    )(left, *parts.arrays, *ins)


def qkv_forward(first_in, parts, bias, table, after=()):
    column = lookup(table)
    block = parts.block

    def finish(y, ins, outs):
        outs[0][...] = y + ins[0][...]

    total_columns = parts.steps * block
    return times_weight(
        first_in,
        parts,
        table,
        [bias],
        [pl.BlockSpec((1, block), lambda j: (0, column(j)))],
        [jax.ShapeDtypeStruct((first_in.shape[0], total_columns), F32)],
        [pl.BlockSpec((first_in.shape[0], block), lambda j: (0, column(j)))],
        finish,
        14,
        after,
    )[0]


def proj_forward(attended, parts, row_low, vec, after=()):
    rows, width = row_low.shape

    def finish(acc, ins, outs):
        row_ref, vec_ref = ins
        hidden_ref, second_ref = outs

        def work(cut):
            hidden = row_ref[cut, :].astype(F32) + (acc[cut, :] + vec_ref[2:3, :])
            hidden_ref[cut, :] = hidden
            normed, _ = norm_parts(hidden)
            second_ref[cut, :] = (normed * vec_ref[3:4, :] + vec_ref[4:5, :]).astype(LOW)

        row_loop(rows, work)

    return times_turned(
        attended,
        parts,
        list(range(parts.steps)),
        [row_low, vec],
        [whole(row_low.shape), whole(vec.shape)],
        [jax.ShapeDtypeStruct((rows, width), F32), jax.ShapeDtypeStruct((rows, width), LOW)],
        [whole((rows, width))] * 2,
        finish,
        9.8,
        after,
    )


def up_forward(second_in, parts, bias, after=()):
    rows, block = second_in.shape[0], parts.block
    total_columns = parts.steps * block

    def finish(y, ins, outs):
        outs[0][...] = y + ins[0][...]

        def work(cut):
            u = outs[0][cut, :]
            outs[1][cut, :] = (u * jax.nn.sigmoid(GELU_SLOPE * u)).astype(LOW)

        row_loop(rows, work)

    spec = pl.BlockSpec((rows, block), lambda j: (0, j))
    return times_weight(
        second_in,
        parts,
        None,
        [bias],
        [pl.BlockSpec((1, block), lambda j: (0, j))],
        [
            jax.ShapeDtypeStruct((rows, total_columns), F32),
            jax.ShapeDtypeStruct((rows, total_columns), LOW),
        ],
        [spec, spec],
        finish,
        17.8,
        after,
    )


def down_forward(activated, parts, hidden1, vec, after=()):
    rows, width = hidden1.shape

    def finish(acc, ins, outs):
        def work(cut):
            outs[0][cut, :] = (ins[0][cut, :] + (acc[cut, :] + ins[1][5:6, :])).astype(LOW)

        row_loop(rows, work)

    return times_turned(
        activated,
        parts,
        list(range(parts.steps)),
        [hidden1, vec],
        [whole(hidden1.shape), whole(vec.shape)],
        [jax.ShapeDtypeStruct((rows, width), LOW)],
        [whole((rows, width))],
        finish,
        15,
        after,
    )[0]


def down_backward(down_grad, parts, upward, after=()):
    rows, block = down_grad.shape[0], parts.block
    total_columns = parts.steps * block

    def finish(y, ins, outs):
        total_ref = outs[1]
        total_ref[...] = jnp.zeros_like(total_ref)
        scratch = outs[2]
        scratch[...] = y

        def work(cut):
            u = ins[0][cut, :]
            sigma = jax.nn.sigmoid(GELU_SLOPE * u)
            g = (scratch[cut, :] * (sigma + GELU_SLOPE * u * sigma * (1.0 - sigma))).astype(LOW)
            outs[0][cut, :] = g
            total_ref[...] += jnp.sum(g.astype(F32), 0, keepdims=True)

        row_loop(rows, work)

    count = len(parts.arrays)

    def kernel(*refs):
        left_ref, w_refs, rest = refs[0], refs[1 : 1 + count], refs[1 + count :]

        def work(w):
            y = jnp.dot(left_ref[...], w, preferred_element_type=F32)
            finish(y, rest[:1], rest[1:])

        parts.each(w_refs, work)

    spec = pl.BlockSpec((rows, block), lambda j: (0, j))
    return call(
        kernel,
        (parts.steps,),
        [whole(down_grad.shape)] + parts.specs + [spec],
        [spec, pl.BlockSpec((1, block), lambda j: (0, j))],
        [
            jax.ShapeDtypeStruct((rows, total_columns), LOW),
            jax.ShapeDtypeStruct((1, total_columns), F32),
        ],
        scratch=[pltpu.VMEM((rows, block), F32)],
        us=19,
        after=after,
    )(down_grad, *parts.arrays, upward)


def up_backward(up_grad, parts, hidden1, cot_low, token_weight, vec, after=()):
    rows, width = hidden1.shape

    def finish(acc, ins, outs):
        hidden_ref, cot_ref, weight_ref, vec_ref = ins
        grad_ref, branch_ref, sums_ref = outs
        sums_ref[...] = jnp.zeros_like(sums_ref)

        def work(cut):
            e = acc[cut, :]
            normed, inverse = norm_parts(hidden_ref[cut, :])
            grad_y = cot_ref[cut, :].astype(F32) * weight_ref[cut, :]
            grad = grad_y + norm_back(e, normed, inverse, vec_ref[3:4, :])
            branch = grad.astype(LOW)
            grad_ref[cut, :] = grad
            branch_ref[cut, :] = branch
            sums_ref[0:1, :] += jnp.sum(e * normed, 0, keepdims=True)
            sums_ref[1:2, :] += jnp.sum(e, 0, keepdims=True)
            sums_ref[2:3, :] += jnp.sum(branch.astype(F32), 0, keepdims=True)
            sums_ref[3:4, :] += jnp.sum(grad_y.astype(LOW).astype(F32), 0, keepdims=True)

        row_loop(rows, work)

    return times_turned(
        up_grad,
        parts,
        list(range(parts.steps)),
        [hidden1, cot_low, token_weight, vec],
        [whole(hidden1.shape), whole(cot_low.shape), whole(token_weight.shape), whole(vec.shape)],
        [
            jax.ShapeDtypeStruct((rows, width), F32),
            jax.ShapeDtypeStruct((rows, width), LOW),
            jax.ShapeDtypeStruct((8, width), F32),
        ],
        [whole((rows, width)), whole((rows, width)), whole((8, width))],
        finish,
        21.7,
        after,
    )


def proj_backward(branch_grad, parts, after=()):
    rows, block = branch_grad.shape[0], parts.block

    def finish(y, ins, outs):
        outs[0][...] = y.astype(LOW)

    return times_weight(
        branch_grad,
        parts,
        None,
        [],
        [],
        [jax.ShapeDtypeStruct((rows, parts.steps * block), LOW)],
        [pl.BlockSpec((rows, block), lambda j: (0, j))],
        finish,
        6,
        after,
    )[0]


def qkv_backward(mixed_grad, parts, table, row_low, hidden1_grad, vec, after=()):
    rows, width = row_low.shape

    def finish(acc, ins, outs):
        row_ref, grad_ref, vec_ref = ins
        sums_ref = outs[1]
        sums_ref[...] = jnp.zeros_like(sums_ref)

        def work(cut):
            e = acc[cut, :]
            normed, inverse = norm_parts(row_ref[cut, :].astype(F32))
            grad = grad_ref[cut, :] + norm_back(e, normed, inverse, vec_ref[0:1, :])
            outs[0][cut, :] = grad.astype(LOW)
            sums_ref[0:1, :] += jnp.sum(e * normed, 0, keepdims=True)
            sums_ref[1:2, :] += jnp.sum(e, 0, keepdims=True)

        row_loop(rows, work)

    return times_turned(
        mixed_grad,
        parts,
        table,
        [row_low, hidden1_grad, vec],
        [whole(row_low.shape), whole(hidden1_grad.shape), whole(vec.shape)],
        [jax.ShapeDtypeStruct((rows, width), LOW), jax.ShapeDtypeStruct((8, width), F32)],
        [whole((rows, width)), whole((8, width))],
        finish,
        18,
        after,
    )


def grad_kernel(pairs, block, kind, half, came=None, part=None, us=10, after=()):
    rows, width = pairs[0][0].shape
    middle = width // 2
    low = middle // 2
    steps = len(kind)
    near = steps // 2
    count = len(pairs)

    def kernel(*refs):
        lefts, rights = refs[:count], refs[count : 2 * count]
        rest = refs[2 * count :]
        turned = rest[-count:]
        j = pl.program_id(0)

        @pl.when(j == 0)
        def _():
            for k in range(count):
                turned[k][...] = lefts[k][:, half * middle : (half + 1) * middle].T

        for k in range(count):
            hits = [s for s in range(steps) if kind[s][0] == k]
            hit = j == hits[0]
            for s in hits[1:]:
                hit = hit | (j == s)

            @pl.when(hit)
            def _(k=k):
                right = rights[k][...]
                if came is None:
                    rest[0][...] = jnp.dot(
                        turned[k][...], right, preferred_element_type=F32
                    ).astype(LOW)
                    return
                came_ref, out0, out1, out2 = rest[:4]
                y0 = jnp.dot(turned[k][:low, :], right, preferred_element_type=F32)
                y0 = (y0 + came_ref[:low, :].astype(F32)).astype(LOW)
                y1 = jnp.dot(turned[k][low:, :], right, preferred_element_type=F32)
                y1 = (y1 + came_ref[low:, :].astype(F32)).astype(LOW)

                @pl.when(j < near)
                def _():
                    out0[...] = y0
                    out1[...] = y1

                @pl.when(j >= near)
                def _():
                    if part == "a":
                        out2[...] = y0
                        out1[...] = y1
                    else:
                        out2[:low, :] = y0
                        out2[low:, :] = y1

    right_specs = []
    for k in range(count):
        table, last = [], 0
        for s in range(steps):
            if kind[s][0] == k:
                last = kind[s][1]
            table.append(last)
        column = lookup(table)
        right_specs.append(pl.BlockSpec((rows, block), lambda j, column=column: (0, column(j))))

    def clipped(base, number, height):
        spec = pl.BlockSpec((height, block), lambda j: (0, jnp.clip(j - base, 0, number - 1)))
        return spec, jax.ShapeDtypeStruct((height, number * block), LOW)

    extra, extra_specs = [], []
    if came is None:
        outs = [clipped(0, steps, middle)]
    else:
        extra = [came[0]]
        column = lookup(came[1])
        extra_specs = [pl.BlockSpec((middle, block), lambda j: (0, column(j)))]
        if part == "a":
            both = pl.BlockSpec((low, block), lambda j: (j // near, j % near))
            outs = [
                clipped(0, near, low),
                (both, jax.ShapeDtypeStruct((middle, near * block), LOW)),
                clipped(near, near, low),
            ]
        else:
            outs = [clipped(0, near, low), clipped(0, near, low), clipped(near, near, middle)]
    return call(
        kernel,
        (steps,),
        [whole(left.shape) for left, _ in pairs] + right_specs + extra_specs,
        [s for s, _ in outs],
        [s for _, s in outs],
        scratch=[pltpu.VMEM((middle, rows), LOW) for _ in pairs],
        us=us,
        after=after,
    )(*[left for left, _ in pairs], *[right for _, right in pairs], *extra)


def add_second(other_a, own_b, from_y, from_x):
    rows, columns = other_a.shape

    def kernel(a_ref, b_ref, y_ref, x_ref, to_x, to_y):
        to_x[...] = (a_ref[...].astype(F32) + y_ref[...].astype(F32)).astype(LOW)
        to_y[...] = (b_ref[...].astype(F32) + x_ref[...].astype(F32)).astype(LOW)

    shape = jax.ShapeDtypeStruct((rows, columns), LOW)
    block = columns // 2
    spec = pl.BlockSpec((rows, block), lambda j: (0, j))
    later = pl.BlockSpec((rows, block), lambda j: (1, j))
    return call(
        kernel,
        (2,),
        [spec, spec, later, later],
        [spec, spec],
        [shape, shape],
    )(other_a, own_b, from_y, from_x)


def add_ring(own_a, own_b, from_y, from_x, second_x, second_y, came, place, rows, kind):
    half = own_a.shape[1]
    columns = 2 * half

    def kernel(*refs):
        own_a, own_b, y, x, x2, y2 = refs[:6]
        out = refs[-1]
        a = own_a[...].astype(F32) + y[...].astype(F32) + x2[...].astype(F32)
        b = own_b[...].astype(F32) + x[...].astype(F32) + y2[...].astype(F32)
        if came is not None:
            a = a + refs[6][:, :half].astype(F32)
            b = b + refs[6][:, half:].astype(F32)
        out[:, :half] = a.astype(kind)
        out[:, half:] = b.astype(kind)

    side = pl.BlockSpec((rows, half), lambda j: (place, 0))
    extra = [] if came is None else [came]
    return call(
        kernel,
        (1,),
        [side] * 6
        + [whole(v.shape) for v in extra],
        whole((rows, columns)),
        jax.ShapeDtypeStruct((rows, columns), kind),
    )(own_a, own_b, from_y, from_x, second_x, second_y, *extra)


def cut_far(side, across, split):
    rows, columns = side.shape

    def kernel(a, b, out_a, out_b):
        out_a[...] = a[:, :split]
        out_b[...] = b[:, split:]

    return call(
        kernel,
        (1,),
        [whole(side.shape)] * 2,
        [whole((rows, split)), whole((rows, columns - split))],
        [
            jax.ShapeDtypeStruct((rows, split), side.dtype),
            jax.ShapeDtypeStruct((rows, columns - split), side.dtype),
        ],
    )(side, across)


def unshuffle(values, shuffle):
    rows, width = values.shape
    half = rows // 2

    def kernel(in_ref, s_ref, first, second):
        y = lax.dot_general(
            in_ref[...], s_ref[...], (((1,), (1,)), ((), ())), preferred_element_type=F32
        ).astype(LOW)
        first[...] = y[:half]
        second[...] = y[half:]

    shape = jax.ShapeDtypeStruct((half, width), LOW)
    return call(
        kernel,
        (1,),
        [whole(values.shape), whole(shuffle.shape)],
        [whole((half, width))] * 2,
        [shape, shape],
        us=5,
    )(values, shuffle)


def lamb_row(index, master_sq, update_sq):
    lane = lax.broadcasted_iota(jnp.int32, (1, 128), 1)
    row = jnp.where(lane == index, master_sq, 0.0)
    return row + jnp.where(lane == 7 + index, update_sq, 0.0)


def lamb_first(master, moments, grad, column, turned, index, factor):
    shape = master.shape

    def kernel(p_ref, m_ref, g_ref, new_ref, u_ref, row_ref):
        if len(shape) == 2:
            g = g_ref[...]
            g = (g.T if turned else g) * factor
            p = p_ref[...]
            first, second, update = lamb_parts(p, (m_ref[0], m_ref[1]), g)
            new_ref[0] = first
            new_ref[1] = second
            u_ref[...] = update
            row_ref[...] = lamb_row(index, jnp.sum(p * p), jnp.sum(update * update))
            return
        row = jnp.zeros((1, 128), F32)
        for k in range(shape[1]):
            g = g_ref[:, k * shape[2] : (k + 1) * shape[2]] * factor
            p = p_ref[:, k, :]
            first, second, update = lamb_parts(p, (m_ref[0, :, k, :], m_ref[1, :, k, :]), g)
            new_ref[0, :, k, :] = first
            new_ref[1, :, k, :] = second
            u_ref[:, k, :] = update
            row = row + lamb_row(index, jnp.sum(p * p), jnp.sum(update * update))
        row_ref[...] = row

    if turned:
        columns = shape[0]
    else:
        columns = shape[-1] * (shape[1] if len(shape) == 3 else 1)
    rows = shape[1] if turned else shape[0]
    return call(
        kernel,
        (1,),
        [
            whole(shape),
            whole(moments.shape),
            pl.BlockSpec((rows, columns), lambda j: (0, column)),
        ],
        [whole(moments.shape), whole(shape), whole((1, 128))],
        [
            jax.ShapeDtypeStruct(moments.shape, F32),
            jax.ShapeDtypeStruct(shape, F32),
            jax.ShapeDtypeStruct((1, 128), F32),
        ],
        us=4,
    )(master, moments, grad)


def lamb_small(masters, moments, grads, shares, factor):
    count = len(masters)

    def kernel(*refs):
        p_refs, m_refs, g_refs = refs[:count], refs[count : 2 * count], refs[2 * count : 3 * count]
        share_ref = refs[3 * count]
        outs = refs[3 * count + 1 :]
        row = jnp.zeros((1, 128), F32)
        for k in range(count):
            p = p_refs[k][...]
            if len(m_refs[k].shape) == 2:
                old = (m_refs[k][0:1, :], m_refs[k][1:2, :])
            else:
                old = (m_refs[k][0], m_refs[k][1])
            first, second, update = lamb_parts(p, old, g_refs[k][...] * factor)
            if len(m_refs[k].shape) == 2:
                outs[k][0:1, :] = first
                outs[k][1:2, :] = second
            else:
                outs[k][0] = first
                outs[k][1] = second
            outs[count + k][...] = update
            row = row + lamb_row(4 + k, jnp.sum(p * p), jnp.sum(update * update))
        outs[2 * count][...] = row * share_ref[...]

    operands = [*masters, *moments, *grads, shares]
    shapes = [v.shape for v in (*moments, *masters)] + [(1, 128)]
    return call(
        kernel,
        (1,),
        [whole(v.shape) for v in operands],
        [whole(v) for v in shapes],
        [jax.ShapeDtypeStruct(v, F32) for v in shapes],
    )(*operands)


def lamb_last(masters, updates, rows, copies):
    count = len(masters)

    def kernel(*refs):
        p_refs, u_refs, row_ref = refs[:count], refs[count : 2 * count], refs[2 * count]
        outs = refs[2 * count + 1 :]
        row = row_ref[...]
        stats = outs[count + copies]
        stats[0:1, :] = jnp.sqrt(row)
        for k in range(count):
            master_sq, update_sq = row[:, k : k + 1], row[:, 7 + k : 8 + k]
            trust = jnp.sqrt(master_sq) / jnp.sqrt(update_sq + 1e-12)
            stats[1:2, k : k + 1] = trust
            if len(p_refs[k].shape) == 3:
                trust = trust[:, :, None]
            new = p_refs[k][...] - LEARN_RATE * trust * u_refs[k][...]
            outs[k][...] = new
            if k < copies:
                outs[count + k][...] = new.astype(LOW)

    shapes = [jax.ShapeDtypeStruct(v.shape, F32) for v in masters]
    shapes += [jax.ShapeDtypeStruct(v.shape, LOW) for v in masters[:copies]]
    shapes += [jax.ShapeDtypeStruct((2, 128), F32)]
    operands = [*masters, *updates, rows]
    return call(
        kernel,
        (1,),
        [whole(v.shape) for v in operands],
        [whole(v.shape) for v in shapes],
        shapes,
        us=8,
    )(*operands)


def hold(values):
    def kernel(in_ref, out_ref):
        out_ref[...] = in_ref[...]

    return call(
        kernel,
        (1,),
        [whole(values.shape)],
        whole(values.shape),
        jax.ShapeDtypeStruct(values.shape, values.dtype),
        us=1,
    )(values)


def stack_early(shard, side, across, far, after=()):
    rows, columns = shard.shape

    def kernel(a, b, c, d, out):
        out[:rows, :columns] = a[...]
        out[:rows, columns:] = b[...]
        out[rows:, :columns] = c[...]
        out[rows:, columns:] = d[...]

    return call(
        kernel,
        (1,),
        [whole(shard.shape)] * 4,
        whole((2 * rows, 2 * columns)),
        jax.ShapeDtypeStruct((2 * rows, 2 * columns), shard.dtype),
        after=after,
    )(shard, side, across, far)


def stack_rows(pieces, after=()):
    rows, columns = pieces[0].shape
    count = len(pieces)
    block = columns // (columns // 640)

    def kernel(*refs):
        for k in range(count):
            refs[-1][k * rows : (k + 1) * rows, :] = refs[k][...]

    return call(
        kernel,
        (columns // block,),
        [pl.BlockSpec((rows, block), lambda j: (0, j))] * count,
        pl.BlockSpec((count * rows, block), lambda j: (0, j)),
        jax.ShapeDtypeStruct((count * rows, columns), pieces[0].dtype),
        after=after,
    )(*pieces)


def turn_pairs(v, heads_lanes):
    middle = HD // 2
    lanes = lax.broadcasted_iota(jnp.int32, v.shape, 1)
    early = lanes % HD < middle
    width = v.shape[1]
    return jnp.where(early, -pltpu.roll(v, width - middle, 1), pltpu.roll(v, middle, 1))


def head_cut(h):
    return slice(h * HD, (h + 1) * HD)


def attention_forward(mixed, cosine, sine, key_code, query_code, groups, after=()):
    rows, columns = mixed.shape
    lanes = columns // (3 * groups)
    heads = lanes // HD
    scale = HD ** (-0.5)

    def kernel(mixed_ref, cos_ref, sin_ref, key_ref, query_ref, qkv_ref, att_ref, lse_ref, out_t):
        cos, sin = cos_ref[...], sin_ref[...]
        for part in range(2):
            cut = slice(part * lanes, (part + 1) * lanes)
            v = mixed_ref[:, cut]
            qkv_ref[:, cut] = (v * cos + turn_pairs(v, lanes) * sin).astype(LOW)
        qkv_ref[:, 2 * lanes :] = mixed_ref[:, 2 * lanes :].astype(LOW)
        query_t = qkv_ref[:, :lanes].T
        keys = qkv_ref[:, lanes : 2 * lanes]
        value_t = qkv_ref[:, 2 * lanes :].T
        allowed = key_ref[...] == query_ref[...]
        for h in range(heads):
            cut = head_cut(h)
            logits = jnp.dot(keys[:, cut], query_t[cut, :], preferred_element_type=F32)
            logits = jnp.where(allowed, logits * scale, NEGATIVE)
            top = jnp.max(logits, 0, keepdims=True)
            exponent = jnp.exp(logits - top)
            total_ = jnp.sum(exponent, 0, keepdims=True)
            prob = (exponent / total_).astype(LOW)
            out_t[cut, :] = jnp.dot(value_t[cut, :], prob, preferred_element_type=F32)
            lse_ref[0, h : h + 1, :] = top + jnp.log(total_)
        att_ref[...] = out_t[...].T.astype(LOW)

    return call(
        kernel,
        (groups,),
        [
            pl.BlockSpec((rows, 3 * lanes), lambda g: (0, g)),
            whole(cosine.shape),
            whole(sine.shape),
            whole(key_code.shape),
            whole(query_code.shape),
        ],
        [
            pl.BlockSpec((rows, 3 * lanes), lambda g: (0, g)),
            pl.BlockSpec((rows, lanes), lambda g: (0, g)),
            pl.BlockSpec((1, heads, rows), lambda g: (g, 0, 0)),
        ],
        [
            jax.ShapeDtypeStruct((rows, columns), LOW),
            jax.ShapeDtypeStruct((rows, groups * lanes), LOW),
            jax.ShapeDtypeStruct((groups, heads, rows), F32),
        ],
        scratch=[pltpu.VMEM((lanes, rows), F32)],
        us=19.6,
        after=after,
    )(mixed, cosine, sine, key_code, query_code)


def attention_backward(qkv, lse, attn_grad, cosine, sine, key_code, query_code, groups, after=()):
    rows, columns = qkv.shape
    lanes = columns // (3 * groups)
    heads = lanes // HD
    scale = HD ** (-0.5)

    def kernel(
        qkv_ref, lse_ref, grad_ref, cos_ref, sin_ref, key_ref, query_ref, out_ref, sum_ref, q_t, k_n, v_n
    ):
        query_t = qkv_ref[:, :lanes].T
        key_t = qkv_ref[:, lanes : 2 * lanes].T
        grad_t = grad_ref[...].T
        queries = qkv_ref[:, :lanes]
        keys = qkv_ref[:, lanes : 2 * lanes]
        values = qkv_ref[:, 2 * lanes :]
        grads = grad_ref[...]
        allowed = key_ref[...] == query_ref[...]
        for h in range(heads):
            cut = head_cut(h)
            logits = jnp.dot(keys[:, cut], query_t[cut, :], preferred_element_type=F32)
            logits = jnp.where(allowed, logits * scale, NEGATIVE)
            prob = jnp.exp(logits - lse_ref[0, h : h + 1, :])
            prob_grad = jnp.dot(values[:, cut], grad_t[cut, :], preferred_element_type=F32)
            inner = jnp.sum(prob * prob_grad, 0, keepdims=True)
            score_grad = (scale * prob * (prob_grad - inner)).astype(LOW)
            q_t[cut, :] = jnp.dot(key_t[cut, :], score_grad, preferred_element_type=F32)
            k_n[:, cut] = jnp.dot(score_grad, queries[:, cut], preferred_element_type=F32)
            v_n[:, cut] = jnp.dot(prob.astype(LOW), grads[:, cut], preferred_element_type=F32)
        cos, sin = cos_ref[...], sin_ref[...]
        for part, w in enumerate((q_t[...].T, k_n[...], v_n[...])):
            cut = slice(part * lanes, (part + 1) * lanes)
            if part < 2:
                w = w * cos - turn_pairs(w, lanes) * sin
            w = w.astype(LOW)
            out_ref[:, cut] = w
            sum_ref[:, cut] = jnp.sum(w.astype(F32), 0, keepdims=True)

    return call(
        kernel,
        (groups,),
        [
            pl.BlockSpec((rows, 3 * lanes), lambda g: (0, g)),
            pl.BlockSpec((1, heads, rows), lambda g: (g, 0, 0)),
            pl.BlockSpec((rows, lanes), lambda g: (0, g)),
            whole(cosine.shape),
            whole(sine.shape),
            whole(key_code.shape),
            whole(query_code.shape),
        ],
        [
            pl.BlockSpec((rows, 3 * lanes), lambda g: (0, g)),
            pl.BlockSpec((1, 3 * lanes), lambda g: (0, g)),
        ],
        [
            jax.ShapeDtypeStruct((rows, columns), LOW),
            jax.ShapeDtypeStruct((1, columns), F32),
        ],
        scratch=[
            pltpu.VMEM((lanes, rows), F32),
            pltpu.VMEM((rows, lanes), F32),
            pltpu.VMEM((rows, lanes), F32),
        ],
        us=27.3,
        after=after,
    )(qkv, lse, attn_grad, cosine, sine, key_code, query_code)
class Lanes:
    def __init__(self, dp):
        self.dp = dp
        self.ring = dp // 4

    def over_x(self, v):
        return lax.ppermute(v, "tensor", [(0, 1), (1, 0)])

    def over_core(self, v):
        return lax.ppermute(v, "dp", [(i, i ^ 1) for i in range(self.dp)])

    def over_y(self, v):
        return lax.ppermute(v, "dp", [(i, i ^ 2) for i in range(self.dp)])

    def down_z(self, v):
        return lax.ppermute(v, "dp", [(i, (i - 4) % self.dp) for i in range(self.dp)])

    def up_z(self, v):
        return lax.ppermute(v, "dp", [(i, (i + 4) % self.dp) for i in range(self.dp)])

    def order(self):
        i = lax.axis_index("dp")
        z, y, c = i // 4, (i // 2) % 2, i % 2
        blocks = []
        for dc in range(2):
            for dy in range(2):
                for dz in range(self.ring):
                    blocks.append(((z + dz) % self.ring) * 4 + (y ^ dy) * 2 + (c ^ dc))
        return jnp.stack(blocks)

    def ring_down(self, v):
        held = [v]
        for _ in range(self.ring - 1):
            held.append(self.down_z(held[-1]))
        return held

    def far(self, side, across, split):
        a, b = cut_far(side, across, split)
        return self.over_y(a), self.over_x(b)

    def gathered(self, held, side, across, far_a, far_b):
        core = self.over_core
        side_core = core(side)
        return Gathered(
            [held, across, core(held), core(across)],
            [side, far_a, side_core, core(far_a)],
            [side, far_b, side_core, core(far_b)],
            far_a.shape[1],
        )

    def stacked(self, held):
        rows = held[0].shape[0] // 2
        held = held + [self.over_core(v) for v in held]
        cuts = [
            (dc * self.ring + dz, dy * rows, rows)
            for dc in range(2)
            for dy in range(2)
            for dz in range(self.ring)
        ]
        return Stacked(held, cuts)


class Gathered:
    def __init__(self, own, other_a, other_b, split):
        self.own, self.other_a, self.other_b, self.split = own, other_a, other_b, split

    def parts(self, block, first, count):
        columns = self.own[0].shape[1]
        split = self.split // block
        sets = [([(v, first) for v in self.own], None, count)]
        count_a = max(0, min(first + count, split) - first)
        if count_a:
            sets.append(([(v, first) for v in self.other_a], None, count_a))
        if count > count_a:
            start = max(first, split)
            pieces = [(v, start if v.shape[1] == columns else start - split) for v in self.other_b]
            sets.append((pieces, None, count - count_a))
        return Parts(sets, block)


class Stacked:
    def __init__(self, pieces, cuts):
        self.pieces, self.cuts = pieces, cuts

    def parts(self, block):
        count = self.pieces[0].shape[1] // block
        return Parts([([(v, 0) for v in self.pieces], self.cuts, count)], block)


def butterfly(value, dp):
    if dp & (dp - 1):
        return lax.psum(value, ("dp", "tensor"))
    value = value + lax.ppermute(value, "tensor", [(0, 1), (1, 0)])
    bit = 1
    while bit < dp:
        value = value + lax.ppermute(value, "dp", [(i, i ^ bit) for i in range(dp)])
        bit *= 2
    return value


def body(
    block_input,
    out_cotangent,
    picture_ids,
    patch_positions,
    picture_lengths,
    pad_mask,
    qkv_weight,
    proj_weight,
    fc1_weight,
    fc2_weight,
    qkv_bias,
    fc1_bias,
    vectors,
    qkv_moments,
    proj_moments,
    fc1_moments,
    fc2_moments,
    qkv_bias_moments,
    fc1_bias_moments,
    vector_moments,
):
    ORDER.last = None
    dp = lax.axis_size("dp")
    relative = dp == 16
    lanes = Lanes(dp)
    slot = lax.axis_index("tensor")
    lead_dp = (lax.axis_index("dp") == 0).astype(F32)
    lead_all = lead_dp * (slot == 0).astype(F32)
    width = block_input.shape[3]
    rows_own = width // dp
    lane_columns = qkv_weight.shape[2]
    hidden = fc1_weight.shape[1]
    grad_factor = float(block_input.shape[0] * block_input.shape[1] * dp * LEN) ** (-0.5)

    shard_1 = qkv_weight.astype(LOW).reshape(rows_own, 3 * lane_columns)
    shard_2 = jnp.concatenate([fc1_weight.astype(LOW), proj_weight.astype(LOW).T], 1)
    shard_3 = fc2_weight.astype(LOW).T
    half = hidden // 2
    if relative:
        ring_1 = lanes.ring_down(shard_1)
        side_3, across_3 = lanes.over_x(shard_3), lanes.over_y(shard_3)
        far_3 = lanes.over_y(side_3)
        late_3 = [stack_early(shard_3, side_3, across_3, far_3, after=[ring_1[2]])]
        held_1 = stack_rows(ring_1)
        sides_w1 = lanes.over_x(held_1), lanes.over_y(held_1)
        fars_w1 = lanes.far(*sides_w1, 2 * lane_columns)
        w1 = lanes.gathered(held_1, *sides_w1, *fars_w1)
        for _ in range(3):
            late_3.append(lanes.down_z(late_3[-1]))
        ring_2 = lanes.ring_down(shard_2)
        held_2 = stack_rows(ring_2, after=[*fars_w1, late_3[1]])
        sides_w2 = lanes.over_x(held_2), lanes.over_y(held_2)
        w3 = lanes.stacked(late_3)
        w_down = w3.parts(half)
    else:

        def plain(shard):
            held = lax.all_gather(shard, "dp", axis=0, tiled=True)
            side = lanes.over_x(held)
            return Gathered([held], [side], [side], half)

        w1, w2, w3 = plain(shard_1), plain(shard_2), plain(shard_3)
        w_down = w3.parts(half, 0, 2)
    w_qkv = w1.parts(lane_columns, 0, 3)

    def own_row(both):
        mine = lax.dynamic_index_in_dim(both[:, 0], slot, 0, keepdims=False)
        theirs = lax.dynamic_index_in_dim(both[:, 0], 1 - slot, 0, keepdims=False)
        return jnp.concatenate([mine, lanes.over_x(theirs)], 0)

    local_rows = block_input.shape[2]
    biases = jnp.concatenate([qkv_bias.reshape(-1), fc1_bias])
    other_biases = lanes.over_x(biases)
    cut = qkv_bias.size
    bias_qkv = jnp.concatenate([biases[:cut], other_biases[:cut]])[None]
    bias_up = jnp.concatenate([biases[cut:], other_biases[cut:]])[None]

    def pick(array, axis=0):
        return lax.dynamic_index_in_dim(array, slot, axis, keepdims=False)

    def turn(values):
        return jnp.roll(values, -slot * local_rows, axis=-1)

    ids_row = turn(pick(picture_ids[:, 0]))
    rows_at = turn(pick(patch_positions[0, :, 0]))
    cols_at = turn(pick(patch_positions[1, :, 0]))
    mask_row = turn(pick(pad_mask[:, 0]))
    length_row = pick(picture_lengths[:, 0])
    cosine, sine = rotary_tables(rows_at, cols_at)
    groups = 2
    heads = lane_columns // HD
    cosine, sine = jnp.tile(cosine, (1, heads)), jnp.tile(sine, (1, heads))
    key_code = jnp.where(mask_row == 1, ids_row, -1)[:, None]
    query_code = ids_row[None, :]
    slot_hit = (ids_row[:, None] == jnp.arange(SLOTS, dtype=jnp.int32)[None, :]).astype(F32)
    picture_size = jnp.sum(slot_hit * length_row.astype(F32)[None, :], -1)
    token_weight = (mask_row.astype(F32) * jnp.sqrt(LEN / picture_size))[:, None]

    if relative:
        order = lanes.order()
        column = (order[:, None] * rows_own + jnp.arange(rows_own)[None, :]).reshape(-1)
        shuffle = (jnp.arange(width)[:, None] == column[None, :]).astype(LOW)
        vec = lax.dot_general(
            vectors,
            shuffle.astype(F32),
            (((1,), (0,)), ((), ())),
            precision=lax.Precision.HIGHEST,
            preferred_element_type=F32,
        )
        row_low = dot(own_row(block_input), shuffle).astype(LOW)
        cot_low = dot(own_row(out_cotangent), shuffle).astype(LOW)
    else:
        vec = vectors
        row_low = own_row(block_input)
        cot_low = own_row(out_cotangent)

    def give_back(values_low):
        if relative:
            mine, theirs = unshuffle(values_low, shuffle)
        else:
            mine, theirs = values_low[:local_rows], values_low[local_rows:]
        theirs = lanes.over_x(theirs)
        swap = slot == 0
        return jnp.stack([jnp.where(swap, mine, theirs), jnp.where(swap, theirs, mine)])[:, None]

    wide_kind = [(0, j) for j in range(4)]
    first_kind = [(0, 0), (0, 1), (0, 2), (1, 0), (0, 3), (0, 4), (0, 5), (1, 1)]

    def send_grads(pairs, block, kind, us):
        (sent,) = grad_kernel(pairs, block, kind, 1, us=us)
        return lanes.over_core(sent)

    def wide_grads(pairs, came):
        a = grad_kernel(pairs, half, [(0, 0), (0, 2)], 0, (came, [0, 2]), "a", 7)
        from_y = lanes.over_y(a[1])
        b = grad_kernel(pairs, half, [(0, 1), (0, 3)], 0, (came, [1, 3]), "b", 7)
        return (a[0], b[0]), (a[2], b[1]), (from_y, lanes.over_x(b[2]))

    def send_second(kept, first):
        to_x, to_y = add_second(*kept, *first)
        return (*first, lanes.over_x(to_x), lanes.over_y(to_y))

    def ring_step(own, sides, came, place):
        kind = LOW if place else F32
        total = add_ring(*own, *sides, came, place, rows_own, kind)
        return lanes.up_z(total) if place else total

    def plain_grads(pairs, block, kind):
        whole_grad = jnp.concatenate(
            [
                outer(pairs[p][0], pairs[p][1][:, c * block : (c + 1) * block])
                for p, c in kind
            ],
            1,
        )
        both = whole_grad[:, :hidden] + lanes.over_x(whole_grad[:, hidden:])
        return lax.psum_scatter(both, "dp", scatter_dimension=0, tiled=True)

    normed1, _ = norm_parts(row_low.astype(F32))
    first_in = (normed1 * vec[0] + vec[1]).astype(LOW)
    down_grad = (cot_low.astype(F32) * token_weight).astype(LOW)
    mixed = qkv_forward(first_in, w_qkv, bias_qkv, list(range(6)))
    qkv, attended, lse = attention_forward(mixed, cosine, sine, key_code, query_code, groups)
    before_proj = []
    if relative:
        fars_w2 = lanes.far(*sides_w2, half)
        w2 = lanes.gathered(held_2, *sides_w2, *fars_w2)
        before_proj = [late_3[2]]
    w_proj = w2.parts(lane_columns, hidden // lane_columns, 1)
    w_up = w2.parts(half, 0, 2)
    hidden1, second_in = proj_forward(attended, w_proj, row_low, vec, after=before_proj)
    upward, activated = up_forward(second_in, w_up, bias_up)
    pair_3 = [(down_grad, activated)]
    if relative:
        came_3 = send_grads(pair_3, half, wide_kind, 10)
    result = down_forward(activated, w_down, hidden1, vec)

    if relative:
        own_3, later_3, first_3 = wide_grads(pair_3, came_3)
    up_grad, sum_up = down_backward(down_grad, w_down, upward)
    pair_2 = [(second_in, up_grad)]
    if relative:
        came_2 = send_grads(pair_2, half, wide_kind, 10)
        sides_3 = send_second(later_3, first_3)
    block_output = give_back(result)
    hidden1_grad, branch_grad, sums_2 = up_backward(
        up_grad, w_up, hidden1, cot_low, token_weight, vec
    )
    if relative:
        ring_3 = ring_step(own_3, sides_3, None, 3)
        own_2, later_2, first_2 = wide_grads(pair_2, came_2)
    attn_grad = proj_backward(branch_grad, w_proj)
    if relative:
        ring_3 = ring_step(own_3, sides_3, ring_3, 2)
    mixed_grad, sum_qkv = attention_backward(
        qkv, lse, attn_grad, cosine, sine, key_code, query_code, groups
    )
    pair_q, pair_p = (first_in, mixed_grad), (branch_grad, attended)
    factor = grad_factor
    if relative:
        kind_a = [(0, 0), (0, 1), (0, 3), (0, 4)]
        kind_b = [(0, 2), (1, 0), (0, 5), (1, 1)]
        sides_2 = send_second(later_2, first_2)
        ring_3 = ring_step(own_3, sides_3, ring_3, 1)
        came_a = send_grads([pair_q], lane_columns, kind_a, 7)
        came_b = send_grads([pair_q, pair_p], lane_columns, kind_b, 7)
        part_a = grad_kernel([pair_q], lane_columns, kind_a, 0, (came_a, [0, 1, 2, 3]), "a", 8)
        first_y = lanes.over_y(part_a[1])
        ring_2 = ring_step(own_2, sides_2, None, 3)
        part_b = grad_kernel(
            [pair_q, pair_p], lane_columns, kind_b, 0, (came_b, [0, 1, 2, 3]), "b", 8
        )
        own_1, later_1 = (part_a[0], part_b[0]), (part_a[2], part_b[1])
        first_1 = first_y, lanes.over_x(part_b[2])
        grad_3 = ring_step(own_3, sides_3, ring_3, 0)
        lamb_3 = lamb_first(fc2_weight, fc2_moments, grad_3, 0, True, 3, factor)
        ring_2 = ring_step(own_2, sides_2, ring_2, 2)
    input_low, sums_1 = qkv_backward(
        mixed_grad, w_qkv, list(range(6)), row_low, hidden1_grad, vec
    )
    if relative:
        ring_2 = ring_step(own_2, sides_2, ring_2, 1)
        sides_1 = send_second(later_1, first_1)
        input_grad = give_back(input_low)
        grad_2 = ring_step(own_2, sides_2, ring_2, 0)
        lamb_2 = lamb_first(fc1_weight, fc1_moments, grad_2, 0, False, 2, factor)
        sums_1 = hold(sums_1)
        ring_1 = ring_step(own_1, sides_1, None, 3)
        ring_1 = ring_step(own_1, sides_1, ring_1, 2)
        ring_1 = ring_step(own_1, sides_1, ring_1, 1)
    else:
        input_grad = give_back(input_low)
        grad_3 = plain_grads(pair_3, half, wide_kind).T
        lamb_3 = lamb_first(fc2_weight, fc2_moments, grad_3, 0, False, 3, factor)
        grad_2 = plain_grads(pair_2, half, wide_kind)
        lamb_2 = lamb_first(fc1_weight, fc1_moments, grad_2, 0, False, 2, factor)

    vector_terms = jnp.concatenate([sums_1[0:2], sums_2[2:3], sums_2[0:2], sums_2[3:4]], 0)
    if relative:
        vector_terms = lax.dot_general(
            vector_terms,
            shuffle.astype(F32),
            (((1,), (1,)), ((), ())),
            precision=lax.Precision.HIGHEST,
            preferred_element_type=F32,
        )
    qkv_columns = 3 * lane_columns
    own_small = jnp.concatenate([sum_qkv[0, :qkv_columns], sum_up[0, :hidden]])
    other_small = jnp.concatenate([sum_qkv[0, qkv_columns:], sum_up[0, hidden:]])
    first_half = slot == 0
    small = jnp.concatenate(
        [
            jnp.where(first_half, own_small, other_small),
            jnp.where(first_half, other_small, own_small),
            vector_terms.reshape(-1),
        ]
    )
    small = butterfly(small.reshape(-1, 128), dp).reshape(-1)
    size = own_small.shape[0]
    bias_sum = jnp.where(first_half, small[:size], small[size : 2 * size])
    small_grads = [
        bias_sum[:qkv_columns].reshape(qkv_bias.shape),
        bias_sum[None, qkv_columns:],
        small[2 * size :].reshape(vectors.shape),
    ]
    small_masters = [qkv_bias, fc1_bias[None], vectors]
    lane = jnp.arange(128)
    is_bias = (lane == 4) | (lane == 5) | (lane == 11) | (lane == 12)
    shares = jnp.where(is_bias, lead_dp, lead_all)[None]
    *small_lamb, small_row = lamb_small(
        small_masters,
        [qkv_bias_moments, fc1_bias_moments, vector_moments],
        small_grads,
        shares,
        factor,
    )

    if relative:
        grad_1 = ring_step(own_1, sides_1, ring_1, 0)
        lamb_p = lamb_first(proj_weight, proj_moments, grad_1, 3, True, 1, factor)
    else:
        grad_1 = plain_grads([pair_q, pair_p], lane_columns, first_kind)
        lamb_p = lamb_first(
            proj_weight, proj_moments, grad_1[:, qkv_columns:].T, 0, False, 1, factor
        )
    lamb_q = lamb_first(qkv_weight, qkv_moments, grad_1, 0, False, 0, factor)
    rows = lamb_q[2] + lamb_p[2] + lamb_2[2] + lamb_3[2] + small_row
    rows = butterfly(rows, dp)
    last = lamb_last(
        [qkv_weight, proj_weight, fc1_weight, fc2_weight, *small_masters],
        [lamb_q[1], lamb_p[1], lamb_2[1], lamb_3[1], *small_lamb[3:]],
        rows,
        4,
    )
    new_params, copies, stats = last[:7], last[7:11], last[11]
    return (
        block_output,
        input_grad,
        *new_params[:5],
        new_params[5][0],
        new_params[6],
        lamb_q[0],
        lamb_p[0],
        lamb_2[0],
        lamb_3[0],
        *small_lamb[:3],
        *copies,
        jnp.concatenate([stats[0:1, :7], stats[0:1, 7:14]], 0),
        stats[1, :7],
    )


def solution(mesh):
    in_specs = (
        P(None, "dp", "tensor", None),
        P(None, "dp", "tensor", None),
        P(None, "dp", None),
        P(None, None, "dp", None),
        P(None, "dp", None),
        P(None, "dp", None),
        P("dp", None, "tensor"),
        P("tensor", "dp"),
        P("dp", "tensor"),
        P("tensor", "dp"),
        P(None, "tensor"),
        P("tensor"),
        P(),
        P(None, "dp", None, "tensor"),
        P(None, "tensor", "dp"),
        P(None, "dp", "tensor"),
        P(None, "tensor", "dp"),
        P(None, None, "tensor"),
        P(None, "tensor"),
        P(),
    )
    out_specs = (
        P(None, "dp", "tensor", None),
        P(None, "dp", "tensor", None),
        P("dp", None, "tensor"),
        P("tensor", "dp"),
        P("dp", "tensor"),
        P("tensor", "dp"),
        P(None, "tensor"),
        P("tensor"),
        P(),
        P(None, "dp", None, "tensor"),
        P(None, "tensor", "dp"),
        P(None, "dp", "tensor"),
        P(None, "tensor", "dp"),
        P(None, None, "tensor"),
        P(None, "tensor"),
        P(),
        P("dp", None, "tensor"),
        P("tensor", "dp"),
        P("dp", "tensor"),
        P("tensor", "dp"),
        P(),
        P(),
    )
    return jax.shard_map(body, mesh=mesh, in_specs=in_specs, out_specs=out_specs, check_vma=False)
```

```python
import jax
import jax.numpy as jnp
from jax import lax
from jax.experimental import pallas as pl
from jax.experimental.pallas import tpu as pltpu
from jax.sharding import PartitionSpec as P

HD = 80
SLOTS = 4
LEN = 576


NEGATIVE = -1e30
EPS_NORM = 1e-06
EPS_ADAM = 1e-06
WEIGHT_DECAY = 0.01
LEARN_RATE = 0.5
GELU_SLOPE = 1.702
F32 = jnp.float32
LOW = jnp.bfloat16


def norm_parts(values):
    center = values - jnp.mean(values, -1, keepdims=True)
    inverse = lax.rsqrt(jnp.mean(center * center, -1, keepdims=True) + EPS_NORM)
    return (center * inverse, inverse)


def norm_back(out_grad, normed, inverse, gain):
    scaled = out_grad * gain
    return inverse * (
        scaled
        - jnp.mean(scaled, -1, keepdims=True)
        - normed * jnp.mean(scaled * normed, -1, keepdims=True)
    )


def rotary_tables(rows_at, cols_at):
    quarter = HD // 4
    frequency = 10000.0 ** (-jnp.arange(quarter, dtype=F32) / quarter)
    halves = jnp.concatenate(
        [
            rows_at.astype(F32)[:, None] * frequency,
            cols_at.astype(F32)[:, None] * frequency,
        ],
        -1,
    )
    angles = jnp.concatenate([halves, halves], -1)
    return (jnp.cos(angles), jnp.sin(angles))


def dot(left, right):
    return lax.dot_general(left, right, (((1,), (0,)), ((), ())), preferred_element_type=F32)


def dot_t(left, right):
    return lax.dot_general(left, right, (((1,), (1,)), ((), ())), preferred_element_type=F32)


def outer(left, right):
    return lax.dot_general(left, right, (((0,), (0,)), ((), ())), preferred_element_type=F32)


def lamb_parts(master, moments, gradient):
    first = 0.5 * moments[0] + 0.5 * gradient
    second = 0.5 * moments[1] + 0.5 * gradient * gradient
    update = first / (jnp.sqrt(second) + EPS_ADAM) + WEIGHT_DECAY * master
    return (first, second, update)


VMEM_LIMIT = 56 * 1024 * 1024
COST = int(8 * 1.15e9)


class Order:
    def __init__(self):
        self.last = None


ORDER = Order()


def call(
    kernel, grid, in_specs, out_specs, out_shape, scratch=(), us=2.4, after=()
):
    if ORDER.last is not None:
        after = [*after, ORDER.last]
    count, extra = len(in_specs), len(after)

    def ordered(*refs):
        kernel(*refs[:count], *refs[count + extra :])

    run = pl.pallas_call(
        ordered,
        grid=grid,
        in_specs=list(in_specs) + [pl.BlockSpec(memory_space=pl.ANY)] * extra,
        out_specs=out_specs,
        out_shape=out_shape,
        scratch_shapes=list(scratch),
        compiler_params=pltpu.CompilerParams(
            dimension_semantics=("arbitrary",) * len(grid), vmem_limit_bytes=VMEM_LIMIT
        ),
        cost_estimate=pl.CostEstimate(
            flops=int(COST * us), bytes_accessed=0, transcendentals=0
        ),
    )

    def start(*operands):
        result = run(*operands, *after)
        ORDER.last = result[0] if isinstance(result, (list, tuple)) else result
        return result

    return start


def whole(shape):
    return pl.BlockSpec(shape, lambda *_: (0,) * len(shape))


def lookup(table):
    def column(j):
        found = table[0]
        for k in range(1, len(table)):
            found = jnp.where(j == k, table[k], found)
        return found

    return column


class Parts:
    def __init__(self, sets, block):
        self.sets, self.block = sets, block
        self.steps = sum(s[2] for s in sets)
        self.width = sum(piece.shape[0] for piece, _ in sets[0][0])
        self.arrays, self.specs = [], []
        base = 0
        for pieces, _, count in sets:
            for piece, first in pieces:
                self.arrays.append(piece)
                self.specs.append(
                    pl.BlockSpec(
                        (piece.shape[0], block),
                        lambda j, first=first, base=base, count=count: (
                            0,
                            first + jnp.clip(j - base, 0, count - 1),
                        ),
                    )
                )
            base += count

    def each(self, refs, work):
        j = pl.program_id(0)
        base, at = 0, 0
        for pieces, cuts, count in self.sets:
            mine = refs[at : at + len(pieces)]

            @pl.when((j >= base) & (j < base + count))
            def _(mine=mine, cuts=cuts):
                if cuts is None:
                    values = [r[...] for r in mine]
                else:
                    values = [mine[p][r : r + n, :] for p, r, n in cuts]
                work(values[0] if len(values) == 1 else jnp.concatenate(values, 0))

            base += count
            at += len(pieces)


def row_loop(rows, work):
    work(pl.ds(0, rows))


def times_weight(left, parts, table, ins, in_specs, outs, out_specs, finish, us, after=()):
    count = len(parts.arrays)

    def kernel(*refs):
        left_ref, w_refs, rest = refs[0], refs[1 : 1 + count], refs[1 + count :]

        def work(w):
            y = jnp.dot(left_ref[...], w, preferred_element_type=F32)
            finish(y, rest[: len(ins)], rest[len(ins) :])

        parts.each(w_refs, work)

    return call(
        kernel,
        (parts.steps,),
        [whole(left.shape)] + parts.specs + in_specs,
        out_specs,
        outs,
        us=us,
        after=after,
    )(left, *parts.arrays, *ins)


def times_turned(left, parts, table, ins, in_specs, outs, out_specs, finish, us, after=()):
    count = len(parts.arrays)
    rows, width = left.shape[0], parts.width
    column = lookup(table)

    def kernel(*refs):
        left_ref, w_refs, rest = refs[0], refs[1 : 1 + count], refs[1 + count :]
        acc = rest[-1]
        rest = rest[:-1]

        def work(w):
            y = lax.dot_general(
                left_ref[...], w, (((1,), (1,)), ((), ())), preferred_element_type=F32
            )

            @pl.when(pl.program_id(0) == 0)
            def _():
                acc[...] = y

            @pl.when(pl.program_id(0) > 0)
            def _():
                acc[...] += y

        parts.each(w_refs, work)

        @pl.when(pl.program_id(0) == parts.steps - 1)
        def _():
            finish(acc, rest[: len(ins)], rest[len(ins) :])

    return call(
        kernel,
        (parts.steps,),
        [pl.BlockSpec((rows, parts.block), lambda j: (0, column(j)))] + parts.specs + in_specs,
        out_specs,
        outs,
        scratch=[pltpu.VMEM((rows, width), F32)],
        us=us,
        after=after,
    )(left, *parts.arrays, *ins)


def qkv_forward(first_in, parts, bias, table, after=()):
    column = lookup(table)
    block = parts.block

    def finish(y, ins, outs):
        outs[0][...] = y + ins[0][...]

    total_columns = parts.steps * block
    return times_weight(
        first_in,
        parts,
        table,
        [bias],
        [pl.BlockSpec((1, block), lambda j: (0, column(j)))],
        [jax.ShapeDtypeStruct((first_in.shape[0], total_columns), F32)],
        [pl.BlockSpec((first_in.shape[0], block), lambda j: (0, column(j)))],
        finish,
        14,
        after,
    )[0]


def proj_forward(attended, parts, row_low, vec, after=()):
    rows, width = row_low.shape

    def finish(acc, ins, outs):
        row_ref, vec_ref = ins
        hidden_ref, second_ref = outs

        def work(cut):
            hidden = row_ref[cut, :].astype(F32) + (acc[cut, :] + vec_ref[2:3, :])
            hidden_ref[cut, :] = hidden
            normed, _ = norm_parts(hidden)
            second_ref[cut, :] = (normed * vec_ref[3:4, :] + vec_ref[4:5, :]).astype(LOW)

        row_loop(rows, work)

    return times_turned(
        attended,
        parts,
        list(range(parts.steps)),
        [row_low, vec],
        [whole(row_low.shape), whole(vec.shape)],
        [jax.ShapeDtypeStruct((rows, width), F32), jax.ShapeDtypeStruct((rows, width), LOW)],
        [whole((rows, width))] * 2,
        finish,
        9.8,
        after,
    )


def up_forward(second_in, parts, bias, after=()):
    rows, block = second_in.shape[0], parts.block
    total_columns = parts.steps * block

    def finish(y, ins, outs):
        outs[0][...] = y + ins[0][...]

        def work(cut):
            u = outs[0][cut, :]
            outs[1][cut, :] = (u * jax.nn.sigmoid(GELU_SLOPE * u)).astype(LOW)

        row_loop(rows, work)

    spec = pl.BlockSpec((rows, block), lambda j: (0, j))
    return times_weight(
        second_in,
        parts,
        None,
        [bias],
        [pl.BlockSpec((1, block), lambda j: (0, j))],
        [
            jax.ShapeDtypeStruct((rows, total_columns), F32),
            jax.ShapeDtypeStruct((rows, total_columns), LOW),
        ],
        [spec, spec],
        finish,
        17.8,
        after,
    )


def down_forward(activated, parts, hidden1, vec, after=()):
    rows, width = hidden1.shape

    def finish(acc, ins, outs):
        def work(cut):
            outs[0][cut, :] = (ins[0][cut, :] + (acc[cut, :] + ins[1][5:6, :])).astype(LOW)

        row_loop(rows, work)

    return times_turned(
        activated,
        parts,
        list(range(parts.steps)),
        [hidden1, vec],
        [whole(hidden1.shape), whole(vec.shape)],
        [jax.ShapeDtypeStruct((rows, width), LOW)],
        [whole((rows, width))],
        finish,
        15,
        after,
    )[0]


def down_backward(down_grad, parts, upward, after=()):
    rows, block = down_grad.shape[0], parts.block
    total_columns = parts.steps * block

    def finish(y, ins, outs):
        total_ref = outs[1]
        total_ref[...] = jnp.zeros_like(total_ref)
        scratch = outs[2]
        scratch[...] = y

        def work(cut):
            u = ins[0][cut, :]
            sigma = jax.nn.sigmoid(GELU_SLOPE * u)
            g = (scratch[cut, :] * (sigma + GELU_SLOPE * u * sigma * (1.0 - sigma))).astype(LOW)
            outs[0][cut, :] = g
            total_ref[...] += jnp.sum(g.astype(F32), 0, keepdims=True)

        row_loop(rows, work)

    count = len(parts.arrays)

    def kernel(*refs):
        left_ref, w_refs, rest = refs[0], refs[1 : 1 + count], refs[1 + count :]

        def work(w):
            y = jnp.dot(left_ref[...], w, preferred_element_type=F32)
            finish(y, rest[:1], rest[1:])

        parts.each(w_refs, work)

    spec = pl.BlockSpec((rows, block), lambda j: (0, j))
    return call(
        kernel,
        (parts.steps,),
        [whole(down_grad.shape)] + parts.specs + [spec],
        [spec, pl.BlockSpec((1, block), lambda j: (0, j))],
        [
            jax.ShapeDtypeStruct((rows, total_columns), LOW),
            jax.ShapeDtypeStruct((1, total_columns), F32),
        ],
        scratch=[pltpu.VMEM((rows, block), F32)],
        us=19,
        after=after,
    )(down_grad, *parts.arrays, upward)


def up_backward(up_grad, parts, hidden1, cot_low, token_weight, vec, after=()):
    rows, width = hidden1.shape

    def finish(acc, ins, outs):
        hidden_ref, cot_ref, weight_ref, vec_ref = ins
        grad_ref, branch_ref, sums_ref = outs
        sums_ref[...] = jnp.zeros_like(sums_ref)

        def work(cut):
            e = acc[cut, :]
            normed, inverse = norm_parts(hidden_ref[cut, :])
            grad_y = cot_ref[cut, :].astype(F32) * weight_ref[cut, :]
            grad = grad_y + norm_back(e, normed, inverse, vec_ref[3:4, :])
            branch = grad.astype(LOW)
            grad_ref[cut, :] = grad
            branch_ref[cut, :] = branch
            sums_ref[0:1, :] += jnp.sum(e * normed, 0, keepdims=True)
            sums_ref[1:2, :] += jnp.sum(e, 0, keepdims=True)
            sums_ref[2:3, :] += jnp.sum(branch.astype(F32), 0, keepdims=True)
            sums_ref[3:4, :] += jnp.sum(grad_y.astype(LOW).astype(F32), 0, keepdims=True)

        row_loop(rows, work)

    return times_turned(
        up_grad,
        parts,
        list(range(parts.steps)),
        [hidden1, cot_low, token_weight, vec],
        [whole(hidden1.shape), whole(cot_low.shape), whole(token_weight.shape), whole(vec.shape)],
        [
            jax.ShapeDtypeStruct((rows, width), F32),
            jax.ShapeDtypeStruct((rows, width), LOW),
            jax.ShapeDtypeStruct((8, width), F32),
        ],
        [whole((rows, width)), whole((rows, width)), whole((8, width))],
        finish,
        21.7,
        after,
    )


def proj_backward(branch_grad, parts, after=()):
    rows, block = branch_grad.shape[0], parts.block

    def finish(y, ins, outs):
        outs[0][...] = y.astype(LOW)

    return times_weight(
        branch_grad,
        parts,
        None,
        [],
        [],
        [jax.ShapeDtypeStruct((rows, parts.steps * block), LOW)],
        [pl.BlockSpec((rows, block), lambda j: (0, j))],
        finish,
        6,
        after,
    )[0]


def qkv_backward(mixed_grad, parts, table, row_low, hidden1_grad, vec, after=()):
    rows, width = row_low.shape

    def finish(acc, ins, outs):
        row_ref, grad_ref, vec_ref = ins
        sums_ref = outs[1]
        sums_ref[...] = jnp.zeros_like(sums_ref)

        def work(cut):
            e = acc[cut, :]
            normed, inverse = norm_parts(row_ref[cut, :].astype(F32))
            grad = grad_ref[cut, :] + norm_back(e, normed, inverse, vec_ref[0:1, :])
            outs[0][cut, :] = grad.astype(LOW)
            sums_ref[0:1, :] += jnp.sum(e * normed, 0, keepdims=True)
            sums_ref[1:2, :] += jnp.sum(e, 0, keepdims=True)

        row_loop(rows, work)

    return times_turned(
        mixed_grad,
        parts,
        table,
        [row_low, hidden1_grad, vec],
        [whole(row_low.shape), whole(hidden1_grad.shape), whole(vec.shape)],
        [jax.ShapeDtypeStruct((rows, width), LOW), jax.ShapeDtypeStruct((8, width), F32)],
        [whole((rows, width)), whole((8, width))],
        finish,
        18,
        after,
    )


def grad_kernel(pairs, block, kind, half, came=None, part=None, us=10, after=()):
    rows, width = pairs[0][0].shape
    middle = width // 2
    low = middle // 2
    steps = len(kind)
    near = steps // 2
    count = len(pairs)

    def kernel(*refs):
        lefts, rights = refs[:count], refs[count : 2 * count]
        rest = refs[2 * count :]
        turned = rest[-count:]
        j = pl.program_id(0)

        @pl.when(j == 0)
        def _():
            for k in range(count):
                turned[k][...] = lefts[k][:, half * middle : (half + 1) * middle].T

        for k in range(count):
            hits = [s for s in range(steps) if kind[s][0] == k]
            hit = j == hits[0]
            for s in hits[1:]:
                hit = hit | (j == s)

            @pl.when(hit)
            def _(k=k):
                right = rights[k][...]
                if came is None:
                    rest[0][...] = jnp.dot(
                        turned[k][...], right, preferred_element_type=F32
                    ).astype(LOW)
                    return
                came_ref, out0, out1, out2 = rest[:4]
                y0 = jnp.dot(turned[k][:low, :], right, preferred_element_type=F32)
                y0 = (y0 + came_ref[:low, :].astype(F32)).astype(LOW)
                y1 = jnp.dot(turned[k][low:, :], right, preferred_element_type=F32)
                y1 = (y1 + came_ref[low:, :].astype(F32)).astype(LOW)

                @pl.when(j < near)
                def _():
                    out0[...] = y0
                    out1[...] = y1

                @pl.when(j >= near)
                def _():
                    if part == "a":
                        out2[...] = y0
                        out1[...] = y1
                    else:
                        out2[:low, :] = y0
                        out2[low:, :] = y1

    right_specs = []
    for k in range(count):
        table, last = [], 0
        for s in range(steps):
            if kind[s][0] == k:
                last = kind[s][1]
            table.append(last)
        column = lookup(table)
        right_specs.append(pl.BlockSpec((rows, block), lambda j, column=column: (0, column(j))))

    def clipped(base, number, height):
        spec = pl.BlockSpec((height, block), lambda j: (0, jnp.clip(j - base, 0, number - 1)))
        return spec, jax.ShapeDtypeStruct((height, number * block), LOW)

    extra, extra_specs = [], []
    if came is None:
        outs = [clipped(0, steps, middle)]
    else:
        extra = [came[0]]
        column = lookup(came[1])
        extra_specs = [pl.BlockSpec((middle, block), lambda j: (0, column(j)))]
        if part == "a":
            both = pl.BlockSpec((low, block), lambda j: (j // near, j % near))
            outs = [
                clipped(0, near, low),
                (both, jax.ShapeDtypeStruct((middle, near * block), LOW)),
                clipped(near, near, low),
            ]
        else:
            outs = [clipped(0, near, low), clipped(0, near, low), clipped(near, near, middle)]
    return call(
        kernel,
        (steps,),
        [whole(left.shape) for left, _ in pairs] + right_specs + extra_specs,
        [s for s, _ in outs],
        [s for _, s in outs],
        scratch=[pltpu.VMEM((middle, rows), LOW) for _ in pairs],
        us=us,
        after=after,
    )(*[left for left, _ in pairs], *[right for _, right in pairs], *extra)


def add_second(other_a, own_b, from_y, from_x):
    rows, columns = other_a.shape

    def kernel(a_ref, b_ref, y_ref, x_ref, to_x, to_y):
        to_x[...] = (a_ref[...].astype(F32) + y_ref[...].astype(F32)).astype(LOW)
        to_y[...] = (b_ref[...].astype(F32) + x_ref[...].astype(F32)).astype(LOW)

    shape = jax.ShapeDtypeStruct((rows, columns), LOW)
    block = columns // 2
    spec = pl.BlockSpec((rows, block), lambda j: (0, j))
    later = pl.BlockSpec((rows, block), lambda j: (1, j))
    return call(
        kernel,
        (2,),
        [spec, spec, later, later],
        [spec, spec],
        [shape, shape],
    )(other_a, own_b, from_y, from_x)


def add_ring(own_a, own_b, from_y, from_x, second_x, second_y, came, place, rows, kind):
    half = own_a.shape[1]
    columns = 2 * half

    def kernel(*refs):
        own_a, own_b, y, x, x2, y2 = refs[:6]
        out = refs[-1]
        a = own_a[...].astype(F32) + y[...].astype(F32) + x2[...].astype(F32)
        b = own_b[...].astype(F32) + x[...].astype(F32) + y2[...].astype(F32)
        if came is not None:
            a = a + refs[6][:, :half].astype(F32)
            b = b + refs[6][:, half:].astype(F32)
        out[:, :half] = a.astype(kind)
        out[:, half:] = b.astype(kind)

    side = pl.BlockSpec((rows, half), lambda j: (place, 0))
    extra = [] if came is None else [came]
    return call(
        kernel,
        (1,),
        [side] * 6
        + [whole(v.shape) for v in extra],
        whole((rows, columns)),
        jax.ShapeDtypeStruct((rows, columns), kind),
    )(own_a, own_b, from_y, from_x, second_x, second_y, *extra)


def cut_far(side, across, near, after=()):
    rows, columns = side.shape
    far, at = [], 0
    for start, stop in near:
        if start > at:
            far.append((at, start))
        at = stop
    if at < columns:
        far.append((at, columns))

    def kernel(a, b, out_a, out_b):
        for source, out, ranges in ((a, out_a, near), (b, out_b, far)):
            at = 0
            for start, stop in ranges:
                out[:, at : at + stop - start] = source[:, start:stop]
                at += stop - start

    widths = [sum(stop - start for start, stop in ranges) for ranges in (near, far)]
    return call(
        kernel,
        (1,),
        [whole(side.shape)] * 2,
        [whole((rows, w)) for w in widths],
        [jax.ShapeDtypeStruct((rows, w), side.dtype) for w in widths],
        after=after,
    )(side, across)


def pack_columns(values, after=()):
    rows = values[0].shape[0]
    columns = sum(v.shape[1] for v in values)

    def kernel(*refs):
        at = 0
        for ref in refs[:-1]:
            n = ref.shape[1]
            refs[-1][:, at : at + n] = ref[...].astype(LOW)
            at += n

    return call(
        kernel,
        (1,),
        [whole(v.shape) for v in values],
        whole((rows, columns)),
        jax.ShapeDtypeStruct((rows, columns), LOW),
        after=after,
    )(*values)


def hold(*values, after=()):
    def kernel(*refs):
        total = refs[0][...]
        for ref in refs[1:-1]:
            total = total + ref[...]
        refs[-1][...] = total

    shape = values[0].shape
    return call(
        kernel,
        (1,),
        [whole(shape)] * len(values),
        whole(shape),
        jax.ShapeDtypeStruct(shape, values[0].dtype),
        us=1,
        after=after,
    )(*values)


def place_halves(mine, theirs, slot, after=()):
    shape = (2, 1, *mine.shape)

    def kernel(slot_ref, mine_ref, their_ref, out_ref):
        for k in range(2):

            @pl.when(slot_ref[0] == k)
            def _(k=k):
                out_ref[k, 0] = mine_ref[...]
                out_ref[1 - k, 0] = their_ref[...]

    return call(
        kernel,
        (1,),
        [pl.BlockSpec(memory_space=pltpu.SMEM), whole(mine.shape), whole(theirs.shape)],
        whole(shape),
        jax.ShapeDtypeStruct(shape, mine.dtype),
        after=after,
    )(slot.reshape(1), mine, theirs)


def unshuffle(values, shuffle):
    rows, width = values.shape
    half = rows // 2

    def kernel(in_ref, s_ref, first, second):
        y = lax.dot_general(
            in_ref[...], s_ref[...], (((1,), (1,)), ((), ())), preferred_element_type=F32
        ).astype(LOW)
        first[...] = y[:half]
        second[...] = y[half:]

    shape = jax.ShapeDtypeStruct((half, width), LOW)
    return call(
        kernel,
        (1,),
        [whole(values.shape), whole(shuffle.shape)],
        [whole((half, width))] * 2,
        [shape, shape],
        us=5,
    )(values, shuffle)


def lamb_row(index, master_sq, update_sq):
    lane = lax.broadcasted_iota(jnp.int32, (1, 128), 1)
    row = jnp.where(lane == index, master_sq, 0.0)
    return row + jnp.where(lane == 7 + index, update_sq, 0.0)


def lamb_first(items, grad, factor, rows=()):
    count = len(items)

    def kernel(*refs):
        p_refs, m_refs = refs[:count], refs[count : 2 * count]
        g_ref = refs[2 * count]
        row_refs = refs[2 * count + 1 : 2 * count + 1 + len(rows)]
        outs = refs[2 * count + 1 + len(rows) :]
        row = jnp.zeros((1, 128), F32)
        for ref in row_refs:
            row = row + ref[...]
        for n, (place, master, _, at) in enumerate(items):
            width = master.shape[-1]
            for k in range(1 if master.ndim == 2 else master.shape[0]):
                cut = () if master.ndim == 2 else (k,)
                g = g_ref[:, at + k * width : at + (k + 1) * width] * factor
                p = p_refs[n][(*cut, ...)]
                old = (m_refs[n][(0, *cut, ...)], m_refs[n][(1, *cut, ...)])
                first, second, update = lamb_parts(p, old, g)
                outs[n][(0, *cut, ...)] = first
                outs[n][(1, *cut, ...)] = second
                outs[count + n][(*cut, ...)] = update
                row = row + lamb_row(place, jnp.sum(p * p), jnp.sum(update * update))
        outs[2 * count][...] = row

    operands = [*[i[1] for i in items], *[i[2] for i in items], grad, *rows]
    shapes = [i[2].shape for i in items] + [i[1].shape for i in items] + [(1, 128)]
    return call(
        kernel,
        (1,),
        [whole(v.shape) for v in operands],
        [whole(v) for v in shapes],
        [jax.ShapeDtypeStruct(v, F32) for v in shapes],
        us=4,
    )(*operands)


def lamb_small(masters, moments, grads, shares, factor):
    count = len(masters)

    def kernel(*refs):
        p_refs, m_refs, g_refs = refs[:count], refs[count : 2 * count], refs[2 * count : 3 * count]
        share_ref = refs[3 * count]
        outs = refs[3 * count + 1 :]
        row = jnp.zeros((1, 128), F32)
        for k in range(count):
            p = p_refs[k][...]
            if len(m_refs[k].shape) == 2:
                old = (m_refs[k][0:1, :], m_refs[k][1:2, :])
            else:
                old = (m_refs[k][:, 0, :], m_refs[k][:, 1, :])
            first, second, update = lamb_parts(p, old, g_refs[k][...] * factor)
            if len(m_refs[k].shape) == 2:
                outs[k][0:1, :] = first
                outs[k][1:2, :] = second
            else:
                outs[k][:, 0, :] = first
                outs[k][:, 1, :] = second
            outs[count + k][...] = update
            row = row + lamb_row(4 + k, jnp.sum(p * p), jnp.sum(update * update))
        outs[2 * count][...] = row * share_ref[...]

    operands = [*masters, *moments, *grads, shares]
    shapes = [v.shape for v in (*moments, *masters)] + [(1, 128)]
    return call(
        kernel,
        (1,),
        [whole(v.shape) for v in operands],
        [whole(v) for v in shapes],
        [jax.ShapeDtypeStruct(v, F32) for v in shapes],
    )(*operands)


def lamb_last(masters, updates, row, copies):
    count = len(masters)

    def kernel(*refs):
        p_refs, u_refs, row_ref = refs[:count], refs[count : 2 * count], refs[2 * count]
        outs = refs[2 * count + 1 :]
        norms, trust_ref = outs[count + copies :]
        master_sq, update_sq = row_ref[:, :count], row_ref[:, count : 2 * count]
        trust = jnp.sqrt(master_sq) / jnp.sqrt(update_sq + 1e-12)
        norms[0:1, :] = jnp.sqrt(master_sq)
        norms[1:2, :] = jnp.sqrt(update_sq)
        trust_ref[...] = trust
        for k in range(count):
            for c in range(1 if len(p_refs[k].shape) == 2 else p_refs[k].shape[0]):
                cut = (...,) if len(p_refs[k].shape) == 2 else (c, ...)
                new = p_refs[k][cut] - LEARN_RATE * trust[:, k : k + 1] * u_refs[k][cut]
                outs[k][cut] = new
                if k < copies:
                    outs[count + k][cut] = new.astype(LOW)

    shapes = [jax.ShapeDtypeStruct(v.shape, F32) for v in masters]
    shapes += [jax.ShapeDtypeStruct(v.shape, LOW) for v in masters[:copies]]
    shapes += [jax.ShapeDtypeStruct((2, count), F32), jax.ShapeDtypeStruct((1, count), F32)]
    operands = [*masters, *updates, row]
    return call(
        kernel,
        (1,),
        [whole(v.shape) for v in operands],
        [whole(v.shape) for v in shapes],
        shapes,
        us=8,
    )(*operands)


def stack_early(shard, side, across, far, after=()):
    rows, columns = shard.shape

    def kernel(a, b, c, d, out):
        out[:rows, :columns] = a[...]
        out[:rows, columns:] = b[...]
        out[rows:, :columns] = c[...]
        out[rows:, columns:] = d[...]

    return call(
        kernel,
        (1,),
        [whole(shard.shape)] * 4,
        whole((2 * rows, 2 * columns)),
        jax.ShapeDtypeStruct((2 * rows, 2 * columns), shard.dtype),
        after=after,
    )(shard, side, across, far)


def stack_rows(pieces, after=()):
    rows, columns = pieces[0].shape
    count = len(pieces)
    block = columns // (columns // 640)

    def kernel(*refs):
        for k in range(count):
            refs[-1][k * rows : (k + 1) * rows, :] = refs[k][...]

    return call(
        kernel,
        (columns // block,),
        [pl.BlockSpec((rows, block), lambda j: (0, j))] * count,
        pl.BlockSpec((count * rows, block), lambda j: (0, j)),
        jax.ShapeDtypeStruct((count * rows, columns), pieces[0].dtype),
        after=after,
    )(*pieces)


def turn_pairs(v, heads_lanes):
    middle = HD // 2
    lanes = lax.broadcasted_iota(jnp.int32, v.shape, 1)
    early = lanes % HD < middle
    width = v.shape[1]
    return jnp.where(early, -pltpu.roll(v, width - middle, 1), pltpu.roll(v, middle, 1))


def head_cut(h):
    return slice(h * HD, (h + 1) * HD)


def attention_forward(mixed, cosine, sine, key_code, query_code, groups, after=()):
    rows, columns = mixed.shape
    lanes = columns // (3 * groups)
    heads = lanes // HD
    scale = HD ** (-0.5)

    def kernel(mixed_ref, cos_ref, sin_ref, key_ref, query_ref, qkv_ref, att_ref, lse_ref, out_t):
        cos, sin = cos_ref[...], sin_ref[...]
        for part in range(2):
            cut = slice(part * lanes, (part + 1) * lanes)
            v = mixed_ref[:, cut]
            qkv_ref[:, cut] = (v * cos + turn_pairs(v, lanes) * sin).astype(LOW)
        qkv_ref[:, 2 * lanes :] = mixed_ref[:, 2 * lanes :].astype(LOW)
        query_t = qkv_ref[:, :lanes].T
        keys = qkv_ref[:, lanes : 2 * lanes]
        value_t = qkv_ref[:, 2 * lanes :].T
        allowed = key_ref[...] == query_ref[...]
        for h in range(heads):
            cut = head_cut(h)
            logits = jnp.dot(keys[:, cut], query_t[cut, :], preferred_element_type=F32)
            logits = jnp.where(allowed, logits * scale, NEGATIVE)
            top = jnp.max(logits, 0, keepdims=True)
            exponent = jnp.exp(logits - top)
            total_ = jnp.sum(exponent, 0, keepdims=True)
            prob = (exponent / total_).astype(LOW)
            out_t[cut, :] = jnp.dot(value_t[cut, :], prob, preferred_element_type=F32)
            lse_ref[0, h : h + 1, :] = top + jnp.log(total_)
        att_ref[...] = out_t[...].T.astype(LOW)

    return call(
        kernel,
        (groups,),
        [
            pl.BlockSpec((rows, 3 * lanes), lambda g: (0, g)),
            whole(cosine.shape),
            whole(sine.shape),
            whole(key_code.shape),
            whole(query_code.shape),
        ],
        [
            pl.BlockSpec((rows, 3 * lanes), lambda g: (0, g)),
            pl.BlockSpec((rows, lanes), lambda g: (0, g)),
            pl.BlockSpec((1, heads, rows), lambda g: (g, 0, 0)),
        ],
        [
            jax.ShapeDtypeStruct((rows, columns), LOW),
            jax.ShapeDtypeStruct((rows, groups * lanes), LOW),
            jax.ShapeDtypeStruct((groups, heads, rows), F32),
        ],
        scratch=[pltpu.VMEM((lanes, rows), F32)],
        us=19.6,
        after=after,
    )(mixed, cosine, sine, key_code, query_code)


def attention_backward(qkv, lse, attn_grad, cosine, sine, key_code, query_code, groups, after=()):
    rows, columns = qkv.shape
    lanes = columns // (3 * groups)
    heads = lanes // HD
    scale = HD ** (-0.5)

    def kernel(
        qkv_ref, lse_ref, grad_ref, cos_ref, sin_ref, key_ref, query_ref, out_ref, sum_ref, q_t, k_n, v_n
    ):
        query_t = qkv_ref[:, :lanes].T
        key_t = qkv_ref[:, lanes : 2 * lanes].T
        grad_t = grad_ref[...].T
        queries = qkv_ref[:, :lanes]
        keys = qkv_ref[:, lanes : 2 * lanes]
        values = qkv_ref[:, 2 * lanes :]
        grads = grad_ref[...]
        allowed = key_ref[...] == query_ref[...]
        for h in range(heads):
            cut = head_cut(h)
            logits = jnp.dot(keys[:, cut], query_t[cut, :], preferred_element_type=F32)
            logits = jnp.where(allowed, logits * scale, NEGATIVE)
            prob = jnp.exp(logits - lse_ref[0, h : h + 1, :])
            prob_grad = jnp.dot(values[:, cut], grad_t[cut, :], preferred_element_type=F32)
            inner = jnp.sum(prob * prob_grad, 0, keepdims=True)
            score_grad = (scale * prob * (prob_grad - inner)).astype(LOW)
            q_t[cut, :] = jnp.dot(key_t[cut, :], score_grad, preferred_element_type=F32)
            k_n[:, cut] = jnp.dot(score_grad, queries[:, cut], preferred_element_type=F32)
            v_n[:, cut] = jnp.dot(prob.astype(LOW), grads[:, cut], preferred_element_type=F32)
        cos, sin = cos_ref[...], sin_ref[...]
        for part, w in enumerate((q_t[...].T, k_n[...], v_n[...])):
            cut = slice(part * lanes, (part + 1) * lanes)
            if part < 2:
                w = w * cos - turn_pairs(w, lanes) * sin
            w = w.astype(LOW)
            out_ref[:, cut] = w
            sum_ref[:, cut] = jnp.sum(w.astype(F32), 0, keepdims=True)

    return call(
        kernel,
        (groups,),
        [
            pl.BlockSpec((rows, 3 * lanes), lambda g: (0, g)),
            pl.BlockSpec((1, heads, rows), lambda g: (g, 0, 0)),
            pl.BlockSpec((rows, lanes), lambda g: (0, g)),
            whole(cosine.shape),
            whole(sine.shape),
            whole(key_code.shape),
            whole(query_code.shape),
        ],
        [
            pl.BlockSpec((rows, 3 * lanes), lambda g: (0, g)),
            pl.BlockSpec((1, 3 * lanes), lambda g: (0, g)),
        ],
        [
            jax.ShapeDtypeStruct((rows, columns), LOW),
            jax.ShapeDtypeStruct((1, columns), F32),
        ],
        scratch=[
            pltpu.VMEM((lanes, rows), F32),
            pltpu.VMEM((rows, lanes), F32),
            pltpu.VMEM((rows, lanes), F32),
        ],
        us=27.3,
        after=after,
    )(qkv, lse, attn_grad, cosine, sine, key_code, query_code)
class Lanes:
    def __init__(self, dp):
        self.dp = dp
        self.ring = dp // 4

    def over_x(self, v):
        return lax.ppermute(v, "tensor", [(0, 1), (1, 0)])

    def over_core(self, v):
        return lax.ppermute(v, "dp", [(i, i ^ 1) for i in range(self.dp)])

    def over_y(self, v):
        return lax.ppermute(v, "dp", [(i, i ^ 2) for i in range(self.dp)])

    def down_z(self, v):
        return lax.ppermute(v, "dp", [(i, (i - 4) % self.dp) for i in range(self.dp)])

    def up_z(self, v):
        return lax.ppermute(v, "dp", [(i, (i + 4) % self.dp) for i in range(self.dp)])

    def exchange(self, v, bit):
        return lax.ppermute(v, "dp", [(i, i ^ bit) for i in range(self.dp)])

    def order(self):
        i = lax.axis_index("dp")
        z, y, c = i // 4, (i // 2) % 2, i % 2
        blocks = []
        for dc in range(2):
            for dy in range(2):
                for dz in range(self.ring):
                    blocks.append(((z + dz) % self.ring) * 4 + (y ^ dy) * 2 + (c ^ dc))
        return jnp.stack(blocks)

    def ring_down(self, v):
        held = [v]
        for _ in range(self.ring - 1):
            held.append(self.down_z(held[-1]))
        return held

    def far(self, side, across, near, after=()):
        a, b = cut_far(side, across, near, after)
        return self.over_y(a), self.over_x(b)

    def both_cores(self, values):
        return [(v, self.over_core(v)) for v in values]

    def stacked(self, pairs):
        rows = pairs[0][0].shape[0] // 2
        cuts = [
            (dc * self.ring + dz, dy * rows, rows)
            for dc in range(2)
            for dy in range(2)
            for dz in range(self.ring)
        ]
        return Stacked([p[0] for p in pairs] + [p[1] for p in pairs], cuts)


class Gathered:
    def __init__(self, own, other, far=None, near=()):
        self.own, self.other, self.far, self.near = own, other, far, near

    def pieces(self, column):
        if self.far is None:
            return [(v, column) for v in self.other]
        side, side_core = self.other
        place, spent, before = 1, column, 0
        for start, stop in self.near:
            if start <= column < stop:
                place, spent = 0, before + column - start
            before += stop - start
            if place and stop <= column:
                spent -= stop - start
        a, a_core = self.far[place]
        return [(side, column), (a, spent), (side_core, column), (a_core, spent)]

    def parts(self, block, first, count):
        sets = [([(v, first) for v in self.own], None, count)]
        last = None
        for b in range(first, first + count):
            here = [(v, c // block) for v, c in self.pieces(b * block)]
            if last is not None and all(
                v is w and c == d + sets[-1][2] for (v, c), (w, d) in zip(here, last)
            ):
                sets[-1] = (last, None, sets[-1][2] + 1)
            else:
                last = here
                sets.append((here, None, 1))
        return Parts(sets, block)


class Stacked:
    def __init__(self, pieces, cuts):
        self.pieces, self.cuts = pieces, cuts

    def parts(self, block):
        count = self.pieces[0].shape[1] // block
        return Parts([([(v, 0) for v in self.pieces], self.cuts, count)], block)


def butterfly(value, dp):
    if dp & (dp - 1):
        return lax.psum(value, ("dp", "tensor"))
    value = value + lax.ppermute(value, "tensor", [(0, 1), (1, 0)])
    bit = 1
    while bit < dp:
        value = value + lax.ppermute(value, "dp", [(i, i ^ bit) for i in range(dp)])
        bit *= 2
    return value


def body(
    block_input,
    out_cotangent,
    picture_ids,
    patch_positions,
    picture_lengths,
    pad_mask,
    qkv_weight,
    proj_weight,
    fc1_weight,
    fc2_weight,
    qkv_bias,
    fc1_bias,
    vectors,
    qkv_moments,
    proj_moments,
    fc1_moments,
    fc2_moments,
    qkv_bias_moments,
    fc1_bias_moments,
    vector_moments,
):
    ORDER.last = None
    dp = lax.axis_size("dp")
    relative = dp == 16
    lanes = Lanes(dp)
    slot = lax.axis_index("tensor")
    lead_dp = (lax.axis_index("dp") == 0).astype(F32)
    lead_all = lead_dp * (slot == 0).astype(F32)
    width = block_input.shape[3]
    rows_own = width // dp
    lane_columns = qkv_weight.shape[2]
    hidden = fc1_weight.shape[1]
    grad_factor = float(block_input.shape[0] * block_input.shape[1] * dp * LEN) ** (-0.5)

    def row_view(v):
        return jnp.swapaxes(v, -1, -2)

    qkv_view, qkv_moments_view = jnp.swapaxes(qkv_weight, 0, 1), jnp.swapaxes(qkv_moments, 1, 2)
    proj_view, proj_moments_view = row_view(proj_weight), row_view(proj_moments)
    fc2_view, fc2_moments_view = row_view(fc2_weight), row_view(fc2_moments)

    local_rows = block_input.shape[2]

    def half_of(both, place):
        return lax.dynamic_index_in_dim(both[:, 0], place, 0, keepdims=False)

    input_came = lanes.over_x(half_of(block_input, 1 - slot))
    cot_came = lanes.over_x(half_of(out_cotangent, 1 - slot))

    shard_1 = jnp.concatenate([qkv_view[k].astype(LOW) for k in range(3)], 1)
    shard_3 = fc2_view.astype(LOW)
    half = hidden // 2
    if relative:
        ring_1 = lanes.ring_down(shard_1)
        side_3, across_3 = lanes.over_x(shard_3), lanes.over_y(shard_3)
        far_3 = lanes.over_y(side_3)
        shard_2 = pack_columns([fc1_weight, proj_view], after=[ring_1[2]])
        held_1 = stack_rows(ring_1, after=[input_came, cot_came, side_3, across_3, far_3])
        ring_2 = lanes.ring_down(shard_2)
        core_held_1 = lanes.over_core(held_1)
        sides_1 = lanes.over_x(held_1), lanes.over_y(held_1)
        near_1 = [(0, 2 * lane_columns)]
        fars_1 = lanes.far(*sides_1, near_1, after=[core_held_1])
        late_3 = [stack_early(shard_3, side_3, across_3, far_3, after=[ring_2[3]])]
        late_came = lanes.down_z(late_3[0])
        core_late = lanes.over_core(late_3[0])
        cores_1 = lanes.both_cores(sides_1)
        held_2 = stack_rows(ring_2, after=[*fars_1, cores_1[0][1], cores_1[1][1]])
        sides_2 = lanes.over_x(held_2), lanes.over_y(held_2)
        core_held_2 = lanes.over_core(held_2)
        w1 = Gathered(
            [held_1, sides_1[1], core_held_1, cores_1[1][1]],
            cores_1[0],
            lanes.both_cores(fars_1),
            near_1,
        )
    else:

        def plain(shard):
            held = lax.all_gather(shard, "dp", axis=0, tiled=True)
            return Gathered([held], [lanes.over_x(held)])

        shard_2 = jnp.concatenate([fc1_weight.astype(LOW), proj_view.astype(LOW)], 1)
        w1, w2, w3 = plain(shard_1), plain(shard_2), plain(shard_3)
        w_down = w3.parts(half, 0, 2)
    w_qkv = w1.parts(lane_columns, 0, 3)

    def own_row(both, came):
        return jnp.concatenate([half_of(both, slot), came], 0)

    biases = jnp.concatenate([qkv_bias.reshape(-1), fc1_bias])
    other_biases = lanes.over_x(biases)
    cut = qkv_bias.size
    bias_qkv = jnp.concatenate([biases[:cut], other_biases[:cut]])[None]
    bias_up = jnp.concatenate([biases[cut:], other_biases[cut:]])[None]

    def pick(array, axis=0):
        return lax.dynamic_index_in_dim(array, slot, axis, keepdims=False)

    def turn(values):
        return jnp.roll(values, -slot * local_rows, axis=-1)

    ids_row = turn(pick(picture_ids[:, 0]))
    rows_at = turn(pick(patch_positions[0, :, 0]))
    cols_at = turn(pick(patch_positions[1, :, 0]))
    mask_row = turn(pick(pad_mask[:, 0]))
    length_row = pick(picture_lengths[:, 0])
    cosine, sine = rotary_tables(rows_at, cols_at)
    groups = 2
    heads = lane_columns // HD
    cosine, sine = jnp.tile(cosine, (1, heads)), jnp.tile(sine, (1, heads))
    key_code = jnp.where(mask_row == 1, ids_row, -1)[:, None]
    query_code = ids_row[None, :]
    slot_hit = (ids_row[:, None] == jnp.arange(SLOTS, dtype=jnp.int32)[None, :]).astype(F32)
    picture_size = jnp.sum(slot_hit * length_row.astype(F32)[None, :], -1)
    token_weight = (mask_row.astype(F32) * jnp.sqrt(LEN / picture_size))[:, None]

    if relative:
        order = lanes.order()
        column = (order[:, None] * rows_own + jnp.arange(rows_own)[None, :]).reshape(-1)
        shuffle = (jnp.arange(width)[:, None] == column[None, :]).astype(LOW)
        vec = lax.dot_general(
            vectors,
            shuffle.astype(F32),
            (((1,), (0,)), ((), ())),
            precision=lax.Precision.HIGHEST,
            preferred_element_type=F32,
        )
        row_low = dot(own_row(block_input, input_came), shuffle).astype(LOW)
        cot_low = dot(own_row(out_cotangent, cot_came), shuffle).astype(LOW)
    else:
        vec = vectors
        row_low = own_row(block_input, input_came)
        cot_low = own_row(out_cotangent, cot_came)

    def give_back(values_low):
        if relative:
            mine, theirs = unshuffle(values_low, shuffle)
        else:
            mine, theirs = values_low[:local_rows], values_low[local_rows:]
        return mine, lanes.over_x(theirs)

    wide_kind = [(0, j) for j in range(4)]
    first_kind = [(0, 0), (0, 1), (0, 2), (1, 0), (0, 3), (0, 4), (0, 5), (1, 1)]

    def send_grads(pairs, block, kind, us):
        (sent,) = grad_kernel(pairs, block, kind, 1, us=us)
        return lanes.over_core(sent)

    def wide_grads(pairs, came):
        a = grad_kernel(pairs, half, [(0, 0), (0, 2)], 0, (came, [0, 2]), "a", 7)
        from_y = lanes.over_y(a[1])
        b = grad_kernel(pairs, half, [(0, 1), (0, 3)], 0, (came, [1, 3]), "b", 7)
        return (a[0], b[0]), (a[2], b[1]), (from_y, lanes.over_x(b[2]))

    def send_second(kept, first):
        to_x, to_y = add_second(*kept, *first)
        return (*first, lanes.over_x(to_x), lanes.over_y(to_y))

    def ring_step(own, sides, came, place):
        kind = LOW if place else F32
        total = add_ring(*own, *sides, came, place, rows_own, kind)
        return lanes.up_z(total) if place else total

    def plain_grads(pairs, block, kind):
        whole_grad = jnp.concatenate(
            [
                outer(pairs[p][0], pairs[p][1][:, c * block : (c + 1) * block])
                for p, c in kind
            ],
            1,
        )
        both = whole_grad[:, :hidden] + lanes.over_x(whole_grad[:, hidden:])
        return lax.psum_scatter(both, "dp", scatter_dimension=0, tiled=True)

    qkv_columns = 3 * lane_columns

    def small_sums(sums_1, sums_2, sum_qkv, sum_up):
        terms = jnp.concatenate([sums_1[0:2], sums_2[2:3], sums_2[0:2], sums_2[3:4]], 0)
        if relative:
            terms = lax.dot_general(
                terms,
                shuffle.astype(F32),
                (((1,), (1,)), ((), ())),
                precision=lax.Precision.HIGHEST,
                preferred_element_type=F32,
            )
        own = jnp.concatenate([sum_qkv[0, :qkv_columns], sum_up[0, :hidden]])
        other = jnp.concatenate([sum_qkv[0, qkv_columns:], sum_up[0, hidden:]])
        first_half = slot == 0
        return jnp.concatenate(
            [
                jnp.where(first_half, own, other),
                jnp.where(first_half, other, own),
                terms.reshape(-1),
            ]
        ).reshape(-1, 128)

    normed1, _ = norm_parts(row_low.astype(F32))
    first_in = (normed1 * vec[0] + vec[1]).astype(LOW)
    down_grad = (cot_low.astype(F32) * token_weight).astype(LOW)
    mixed = qkv_forward(first_in, w_qkv, bias_qkv, list(range(6)))
    before_attention = [core_held_2, core_late, cot_came] if relative else []
    qkv, attended, lse = attention_forward(
        mixed, cosine, sine, key_code, query_code, groups, after=before_attention
    )
    if relative:
        late_3.append(hold(late_came))
        late_3.append(lanes.down_z(late_3[1]))
        late_came = lanes.down_z(late_3[2])
        late_cores = [(late_3[0], core_late), *lanes.both_cores(late_3[1:])]
        before_far = [late_cores[1][1]]
        near_2 = [(0, half), (hidden, hidden + lane_columns)]
        fars_2 = lanes.far(*sides_2, near_2, after=before_far)
        hold(query_code, after=fars_2)
        cores_2 = lanes.both_cores(sides_2)
        w2 = Gathered(
            [held_2, sides_2[1], core_held_2, cores_2[1][1]],
            cores_2[0],
            lanes.both_cores(fars_2),
            near_2,
        )
    w_proj = w2.parts(lane_columns, hidden // lane_columns, 1)
    w_up = w2.parts(half, 0, 2)
    hidden1, second_in = proj_forward(attended, w_proj, row_low, vec)
    upward, activated = up_forward(second_in, w_up, bias_up)
    pair_3 = [(down_grad, activated)]
    if relative:
        late_cores += lanes.both_cores([hold(late_came)])
        w_down = lanes.stacked(late_cores).parts(half)
        came_3 = send_grads(pair_3, half, wide_kind, 60)
    result = down_forward(activated, w_down, hidden1, vec)

    if relative:
        own_3, later_3, first_3 = wide_grads(pair_3, came_3)
    up_grad, sum_up = down_backward(down_grad, w_down, upward)
    pair_2 = [(second_in, up_grad)]
    output_halves = give_back(result)
    if relative:
        came_2 = send_grads(pair_2, half, wide_kind, 10)
        sides_3 = send_second(later_3, first_3)
    hidden1_grad, branch_grad, sums_2 = up_backward(
        up_grad, w_up, hidden1, cot_low, token_weight, vec
    )
    if relative:
        ring_3 = ring_step(own_3, sides_3, None, 3)
        own_2, later_2, first_2 = wide_grads(pair_2, came_2)
    attn_grad = proj_backward(branch_grad, w_proj)
    if relative:
        ring_3 = ring_step(own_3, sides_3, ring_3, 2)
    block_output = place_halves(*output_halves, slot)
    mixed_grad, sum_qkv = attention_backward(
        qkv, lse, attn_grad, cosine, sine, key_code, query_code, groups
    )
    pair_q, pair_p = (first_in, mixed_grad), (branch_grad, attended)
    factor = grad_factor
    if relative:
        kind_a = [(0, 0), (0, 1), (0, 3), (0, 4)]
        kind_b = [(0, 2), (1, 0), (0, 5), (1, 1)]
        sides_2 = send_second(later_2, first_2)
        ring_3 = ring_step(own_3, sides_3, ring_3, 1)
        came_a = send_grads([pair_q], lane_columns, kind_a, 7)
        came_b = send_grads([pair_q, pair_p], lane_columns, kind_b, 7)
        part_a = grad_kernel([pair_q], lane_columns, kind_a, 0, (came_a, [0, 1, 2, 3]), "a", 8)
        first_y = lanes.over_y(part_a[1])
        ring_2 = ring_step(own_2, sides_2, None, 3)
        part_b = grad_kernel(
            [pair_q, pair_p], lane_columns, kind_b, 0, (came_b, [0, 1, 2, 3]), "b", 8
        )
        own_1, later_1 = (part_a[0], part_b[0]), (part_a[2], part_b[1])
        first_1 = first_y, lanes.over_x(part_b[2])
        grad_3 = ring_step(own_3, sides_3, ring_3, 0)
        lamb_3 = lamb_first([(3, fc2_view, fc2_moments_view, 0)], grad_3, factor)
        ring_2 = ring_step(own_2, sides_2, ring_2, 2)
    input_low, sums_1 = qkv_backward(
        mixed_grad, w_qkv, list(range(6)), row_low, hidden1_grad, vec
    )
    input_halves = give_back(input_low)
    small = small_sums(sums_1, sums_2, sum_qkv, sum_up)
    if relative:
        small = hold(small)
        came = lanes.over_x(small)
        ring_2 = ring_step(own_2, sides_2, ring_2, 1)
        small = hold(small, came)
        came = lanes.over_core(small)
        sides_1 = send_second(later_1, first_1)
        small = hold(small, came)
        came = lanes.over_y(small)
        grad_2 = ring_step(own_2, sides_2, ring_2, 0)
        small = hold(small, came)
        came = lanes.exchange(small, 4)
    else:
        grad_3 = plain_grads(pair_3, half, wide_kind)
        lamb_3 = lamb_first([(3, fc2_view, fc2_moments_view, 0)], grad_3, factor)
        grad_2 = plain_grads(pair_2, half, wide_kind)
    lamb_2 = lamb_first([(2, fc1_weight, fc1_moments, 0)], grad_2, factor)
    if relative:
        small = hold(small, came)
        came = lanes.exchange(small, 8)
        ring_1 = ring_step(own_1, sides_1, None, 3)
        small = hold(small, came)
        ring_1 = ring_step(own_1, sides_1, ring_1, 2)
        ring_1 = ring_step(own_1, sides_1, ring_1, 1)

    if not relative:
        small = butterfly(small, dp)
    small = small.reshape(-1)
    first_half = slot == 0
    size = qkv_columns + hidden
    bias_sum = jnp.where(first_half, small[:size], small[size : 2 * size])
    small_grads = [
        bias_sum[:qkv_columns].reshape(qkv_bias.shape),
        bias_sum[None, qkv_columns:],
        small[2 * size :].reshape(vectors.shape),
    ]
    small_masters = [qkv_bias, fc1_bias[None], vectors]
    lane = jnp.arange(128)
    is_bias = (lane == 4) | (lane == 5) | (lane == 11) | (lane == 12)
    shares = jnp.where(is_bias, lead_dp, lead_all)[None]
    *small_lamb, small_row = lamb_small(
        small_masters,
        [
            jnp.swapaxes(qkv_bias_moments, 0, 1),
            fc1_bias_moments,
            jnp.swapaxes(vector_moments, 0, 1),
        ],
        small_grads,
        shares,
        factor,
    )

    if relative:
        input_grad = place_halves(*input_halves, slot)
        grad_1 = ring_step(own_1, sides_1, ring_1, 0)
    else:
        input_grad = place_halves(*input_halves, slot)
        grad_1 = plain_grads([pair_q, pair_p], lane_columns, first_kind)
    q_moments, p_moments, q_update, p_update, row = lamb_first(
        [(0, qkv_view, qkv_moments_view, 0), (1, proj_view, proj_moments_view, qkv_columns)],
        grad_1,
        factor,
        [lamb_2[2], lamb_3[2], small_row],
    )
    row = butterfly(row, dp)
    last = lamb_last(
        [qkv_view, proj_view, fc1_weight, fc2_view, *small_masters],
        [q_update, p_update, lamb_2[1], lamb_3[1], *small_lamb[3:]],
        row,
        4,
    )
    new_params, copies, norms, trust = last[:7], last[7:11], last[11], last[12]
    new_weights, copies = [
        [jnp.swapaxes(v[0], 0, 1), row_view(v[1]), v[2], row_view(v[3])]
        for v in (new_params, copies)
    ]
    return (
        block_output,
        input_grad,
        *new_weights,
        new_params[4],
        new_params[5][0],
        new_params[6],
        jnp.swapaxes(q_moments, 1, 2),
        row_view(p_moments),
        lamb_2[0],
        row_view(lamb_3[0]),
        jnp.swapaxes(small_lamb[0], 0, 1),
        small_lamb[1],
        jnp.swapaxes(small_lamb[2], 0, 1),
        *copies,
        norms,
        trust[0],
    )


def solution(mesh):
    in_specs = (
        P(None, "dp", "tensor", None),
        P(None, "dp", "tensor", None),
        P(None, "dp", None),
        P(None, None, "dp", None),
        P(None, "dp", None),
        P(None, "dp", None),
        P("dp", None, "tensor"),
        P("tensor", "dp"),
        P("dp", "tensor"),
        P("tensor", "dp"),
        P(None, "tensor"),
        P("tensor"),
        P(),
        P(None, "dp", None, "tensor"),
        P(None, "tensor", "dp"),
        P(None, "dp", "tensor"),
        P(None, "tensor", "dp"),
        P(None, None, "tensor"),
        P(None, "tensor"),
        P(),
    )
    out_specs = (
        P(None, "dp", "tensor", None),
        P(None, "dp", "tensor", None),
        P("dp", None, "tensor"),
        P("tensor", "dp"),
        P("dp", "tensor"),
        P("tensor", "dp"),
        P(None, "tensor"),
        P("tensor"),
        P(),
        P(None, "dp", None, "tensor"),
        P(None, "tensor", "dp"),
        P(None, "dp", "tensor"),
        P(None, "tensor", "dp"),
        P(None, None, "tensor"),
        P(None, "tensor"),
        P(),
        P("dp", None, "tensor"),
        P("tensor", "dp"),
        P("dp", "tensor"),
        P("tensor", "dp"),
        P(),
        P(),
    )
    return jax.shard_map(body, mesh=mesh, in_specs=in_specs, out_specs=out_specs, check_vma=False)
```

```python
import math

import jax
import jax.numpy as jnp
from jax import lax
from jax.experimental import pallas as pl
from jax.experimental.pallas import tpu as pltpu
from jax.sharding import PartitionSpec as P

HD = 80
SLOTS = 4
LEN = 576


NEGATIVE = -1e30
EPS_NORM = 1e-06
EPS_ADAM = 1e-06
WEIGHT_DECAY = 0.01
LEARN_RATE = 0.5
GELU_SLOPE = 1.702
F32 = jnp.float32
LOW = jnp.bfloat16


def norm_parts(values):
    center = values - jnp.mean(values, -1, keepdims=True)
    inverse = lax.rsqrt(jnp.mean(center * center, -1, keepdims=True) + EPS_NORM)
    return (center * inverse, inverse)


def norm_back(out_grad, normed, inverse, gain):
    scaled = out_grad * gain
    return inverse * (
        scaled
        - jnp.mean(scaled, -1, keepdims=True)
        - normed * jnp.mean(scaled * normed, -1, keepdims=True)
    )


def rotary_tables(rows_at, cols_at):
    quarter = HD // 4
    frequency = 10000.0 ** (-jnp.arange(quarter, dtype=F32) / quarter)
    halves = jnp.concatenate(
        [
            rows_at.astype(F32)[:, None] * frequency,
            cols_at.astype(F32)[:, None] * frequency,
        ],
        -1,
    )
    angles = jnp.concatenate([halves, halves], -1)
    return (jnp.cos(angles), jnp.sin(angles))


def dot(left, right):
    return lax.dot_general(left, right, (((1,), (0,)), ((), ())), preferred_element_type=F32)


def dot_t(left, right):
    return lax.dot_general(left, right, (((1,), (1,)), ((), ())), preferred_element_type=F32)


def outer(left, right):
    return lax.dot_general(left, right, (((0,), (0,)), ((), ())), preferred_element_type=F32)


def lamb_parts(master, moments, gradient):
    first = 0.5 * moments[0] + 0.5 * gradient
    second = 0.5 * moments[1] + 0.5 * gradient * gradient
    update = first / (jnp.sqrt(second) + EPS_ADAM) + WEIGHT_DECAY * master
    return (first, second, update)


VMEM_MOST = 56 * 1024 * 1024
VMEM_SPARE = 14 * 1024 * 1024
COST = int(8 * 1.15e9)


class Order:
    def __init__(self):
        self.last = None


ORDER = Order()


def call(
    kernel, grid, in_specs, out_specs, out_shape, scratch=(), us=2.4, after=()
):
    if ORDER.last is not None:
        after = [*after, ORDER.last]
    count, extra = len(in_specs), len(after)
    shapes = out_shape if isinstance(out_shape, (list, tuple)) else [out_shape]
    outs = out_specs if isinstance(out_specs, (list, tuple)) else [out_specs]
    out_bytes = sum(
        2 * math.prod(o.block_shape) * v.dtype.itemsize for o, v in zip(outs, shapes)
    )
    scratch_bytes = sum(math.prod(v.shape) * v.dtype.itemsize for v in scratch)

    def room(operands):
        in_bytes = sum(
            2 * math.prod(i.block_shape) * v.dtype.itemsize
            for i, v in zip(in_specs, operands)
            if i.block_shape is not None
        )
        return min(VMEM_MOST, in_bytes + out_bytes + scratch_bytes + VMEM_SPARE)

    def ordered(*refs):
        kernel(*refs[:count], *refs[count + extra :])

    def run(*operands):
        return pl.pallas_call(
            ordered,
            grid=grid,
            in_specs=list(in_specs) + [pl.BlockSpec(memory_space=pl.ANY)] * extra,
            out_specs=out_specs,
            out_shape=out_shape,
            scratch_shapes=list(scratch),
            compiler_params=pltpu.CompilerParams(
                dimension_semantics=("arbitrary",) * len(grid), vmem_limit_bytes=room(operands)
            ),
            cost_estimate=pl.CostEstimate(
                flops=int(COST * us), bytes_accessed=0, transcendentals=0
            ),
        )(*operands, *after)

    def start(*operands):
        result = run(*operands)
        ORDER.last = result[0] if isinstance(result, (list, tuple)) else result
        return result

    return start


def whole(shape):
    return pl.BlockSpec(shape, lambda *_: (0,) * len(shape))


def lookup(table):
    def column(j):
        found = table[0]
        for k in range(1, len(table)):
            found = jnp.where(j == k, table[k], found)
        return found

    return column


class Parts:
    def __init__(self, sets, block):
        self.sets, self.block = sets, block
        self.steps = sum(s[2] for s in sets)
        self.width = sum(piece.shape[0] for piece, _ in sets[0][0])
        self.arrays, self.specs = [], []
        base = 0
        for pieces, _, count in sets:
            for piece, first in pieces:
                self.arrays.append(piece)
                self.specs.append(
                    pl.BlockSpec(
                        (piece.shape[0], block),
                        lambda j, first=first, base=base, count=count: (
                            0,
                            first + jnp.clip(j - base, 0, count - 1),
                        ),
                    )
                )
            base += count

    def each(self, refs, work):
        j = pl.program_id(0)
        base, at = 0, 0
        for pieces, cuts, count in self.sets:
            mine = refs[at : at + len(pieces)]

            @pl.when((j >= base) & (j < base + count))
            def _(mine=mine, cuts=cuts):
                if cuts is None:
                    values = [r[...] for r in mine]
                else:
                    values = [mine[p][r : r + n, :] for p, r, n in cuts]
                work(values[0] if len(values) == 1 else jnp.concatenate(values, 0))

            base += count
            at += len(pieces)


def row_loop(rows, work):
    work(pl.ds(0, rows))


def times_weight(left, parts, table, ins, in_specs, outs, out_specs, finish, us, after=()):
    count = len(parts.arrays)

    def kernel(*refs):
        left_ref, w_refs, rest = refs[0], refs[1 : 1 + count], refs[1 + count :]

        def work(w):
            y = jnp.dot(left_ref[...], w, preferred_element_type=F32)
            finish(y, rest[: len(ins)], rest[len(ins) :])

        parts.each(w_refs, work)

    return call(
        kernel,
        (parts.steps,),
        [whole(left.shape)] + parts.specs + in_specs,
        out_specs,
        outs,
        us=us,
        after=after,
    )(left, *parts.arrays, *ins)


def times_turned(left, parts, table, ins, in_specs, outs, out_specs, finish, us, after=()):
    count = len(parts.arrays)
    rows, width = left.shape[0], parts.width
    column = lookup(table)

    def kernel(*refs):
        left_ref, w_refs, rest = refs[0], refs[1 : 1 + count], refs[1 + count :]
        acc = rest[-1]
        rest = rest[:-1]

        def work(w):
            y = lax.dot_general(
                left_ref[...], w, (((1,), (1,)), ((), ())), preferred_element_type=F32
            )

            @pl.when(pl.program_id(0) == 0)
            def _():
                acc[...] = y

            @pl.when(pl.program_id(0) > 0)
            def _():
                acc[...] += y

        parts.each(w_refs, work)

        @pl.when(pl.program_id(0) == parts.steps - 1)
        def _():
            finish(acc, rest[: len(ins)], rest[len(ins) :])

    return call(
        kernel,
        (parts.steps,),
        [pl.BlockSpec((rows, parts.block), lambda j: (0, column(j)))] + parts.specs + in_specs,
        out_specs,
        outs,
        scratch=[pltpu.VMEM((rows, width), F32)],
        us=us,
        after=after,
    )(left, *parts.arrays, *ins)


def qkv_forward(first_in, parts, bias, table, after=()):
    column = lookup(table)
    block = parts.block

    def finish(y, ins, outs):
        outs[0][...] = y + ins[0][...]

    total_columns = parts.steps * block
    return times_weight(
        first_in,
        parts,
        table,
        [bias],
        [pl.BlockSpec((1, block), lambda j: (0, column(j)))],
        [jax.ShapeDtypeStruct((first_in.shape[0], total_columns), F32)],
        [pl.BlockSpec((first_in.shape[0], block), lambda j: (0, column(j)))],
        finish,
        14,
        after,
    )[0]


def proj_forward(attended, parts, row_low, vec, after=()):
    rows, width = row_low.shape

    def finish(acc, ins, outs):
        row_ref, vec_ref = ins
        hidden_ref, second_ref = outs

        def work(cut):
            hidden = row_ref[cut, :].astype(F32) + (acc[cut, :] + vec_ref[2:3, :])
            hidden_ref[cut, :] = hidden
            normed, _ = norm_parts(hidden)
            second_ref[cut, :] = (normed * vec_ref[3:4, :] + vec_ref[4:5, :]).astype(LOW)

        row_loop(rows, work)

    return times_turned(
        attended,
        parts,
        list(range(parts.steps)),
        [row_low, vec],
        [whole(row_low.shape), whole(vec.shape)],
        [jax.ShapeDtypeStruct((rows, width), F32), jax.ShapeDtypeStruct((rows, width), LOW)],
        [whole((rows, width))] * 2,
        finish,
        9.8,
        after,
    )


def up_forward(second_in, parts, bias, after=()):
    rows, block = second_in.shape[0], parts.block
    total_columns = parts.steps * block

    def finish(y, ins, outs):
        outs[0][...] = y + ins[0][...]

        def work(cut):
            u = outs[0][cut, :]
            outs[1][cut, :] = (u * jax.nn.sigmoid(GELU_SLOPE * u)).astype(LOW)

        row_loop(rows, work)

    spec = pl.BlockSpec((rows, block), lambda j: (0, j))
    return times_weight(
        second_in,
        parts,
        None,
        [bias],
        [pl.BlockSpec((1, block), lambda j: (0, j))],
        [
            jax.ShapeDtypeStruct((rows, total_columns), F32),
            jax.ShapeDtypeStruct((rows, total_columns), LOW),
        ],
        [spec, spec],
        finish,
        17.8,
        after,
    )


def down_forward(activated, parts, hidden1, vec, after=()):
    rows, width = hidden1.shape

    def finish(acc, ins, outs):
        def work(cut):
            outs[0][cut, :] = (ins[0][cut, :] + (acc[cut, :] + ins[1][5:6, :])).astype(LOW)

        row_loop(rows, work)

    return times_turned(
        activated,
        parts,
        list(range(parts.steps)),
        [hidden1, vec],
        [whole(hidden1.shape), whole(vec.shape)],
        [jax.ShapeDtypeStruct((rows, width), LOW)],
        [whole((rows, width))],
        finish,
        15,
        after,
    )[0]


def down_backward(down_grad, parts, upward, after=()):
    rows, block = down_grad.shape[0], parts.block
    total_columns = parts.steps * block

    def finish(y, ins, outs):
        total_ref = outs[1]
        total_ref[...] = jnp.zeros_like(total_ref)
        scratch = outs[2]
        scratch[...] = y

        def work(cut):
            u = ins[0][cut, :]
            sigma = jax.nn.sigmoid(GELU_SLOPE * u)
            g = (scratch[cut, :] * (sigma + GELU_SLOPE * u * sigma * (1.0 - sigma))).astype(LOW)
            outs[0][cut, :] = g
            total_ref[...] += jnp.sum(g.astype(F32), 0, keepdims=True)

        row_loop(rows, work)

    count = len(parts.arrays)

    def kernel(*refs):
        left_ref, w_refs, rest = refs[0], refs[1 : 1 + count], refs[1 + count :]

        def work(w):
            y = jnp.dot(left_ref[...], w, preferred_element_type=F32)
            finish(y, rest[:1], rest[1:])

        parts.each(w_refs, work)

    spec = pl.BlockSpec((rows, block), lambda j: (0, j))
    return call(
        kernel,
        (parts.steps,),
        [whole(down_grad.shape)] + parts.specs + [spec],
        [spec, pl.BlockSpec((1, block), lambda j: (0, j))],
        [
            jax.ShapeDtypeStruct((rows, total_columns), LOW),
            jax.ShapeDtypeStruct((1, total_columns), F32),
        ],
        scratch=[pltpu.VMEM((rows, block), F32)],
        us=0.1,
        after=after,
    )(down_grad, *parts.arrays, upward)


def up_backward(up_grad, parts, hidden1, cot_low, token_weight, vec, after=()):
    rows, width = hidden1.shape

    def finish(acc, ins, outs):
        hidden_ref, cot_ref, weight_ref, vec_ref = ins
        grad_ref, branch_ref, sums_ref = outs
        sums_ref[...] = jnp.zeros_like(sums_ref)

        def work(cut):
            e = acc[cut, :]
            normed, inverse = norm_parts(hidden_ref[cut, :])
            grad_y = cot_ref[cut, :].astype(F32) * weight_ref[cut, :]
            grad = grad_y + norm_back(e, normed, inverse, vec_ref[3:4, :])
            branch = grad.astype(LOW)
            grad_ref[cut, :] = grad
            branch_ref[cut, :] = branch
            sums_ref[0:1, :] += jnp.sum(e * normed, 0, keepdims=True)
            sums_ref[1:2, :] += jnp.sum(e, 0, keepdims=True)
            sums_ref[2:3, :] += jnp.sum(branch.astype(F32), 0, keepdims=True)
            sums_ref[3:4, :] += jnp.sum(grad_y.astype(LOW).astype(F32), 0, keepdims=True)

        row_loop(rows, work)

    return times_turned(
        up_grad,
        parts,
        list(range(parts.steps)),
        [hidden1, cot_low, token_weight, vec],
        [whole(hidden1.shape), whole(cot_low.shape), whole(token_weight.shape), whole(vec.shape)],
        [
            jax.ShapeDtypeStruct((rows, width), F32),
            jax.ShapeDtypeStruct((rows, width), LOW),
            jax.ShapeDtypeStruct((8, width), F32),
        ],
        [whole((rows, width)), whole((rows, width)), whole((8, width))],
        finish,
        0.1,
        after,
    )


def proj_backward(branch_grad, parts, after=()):
    rows, block = branch_grad.shape[0], parts.block

    def finish(y, ins, outs):
        outs[0][...] = y.astype(LOW)

    return times_weight(
        branch_grad,
        parts,
        None,
        [],
        [],
        [jax.ShapeDtypeStruct((rows, parts.steps * block), LOW)],
        [pl.BlockSpec((rows, block), lambda j: (0, j))],
        finish,
        250,
        after,
    )[0]


def qkv_backward(mixed_grad, parts, table, row_low, hidden1_grad, vec, after=()):
    rows, width = row_low.shape

    def finish(acc, ins, outs):
        row_ref, grad_ref, vec_ref = ins
        sums_ref = outs[1]
        sums_ref[...] = jnp.zeros_like(sums_ref)

        def work(cut):
            e = acc[cut, :]
            normed, inverse = norm_parts(row_ref[cut, :].astype(F32))
            grad = grad_ref[cut, :] + norm_back(e, normed, inverse, vec_ref[0:1, :])
            outs[0][cut, :] = grad.astype(LOW)
            sums_ref[0:1, :] += jnp.sum(e * normed, 0, keepdims=True)
            sums_ref[1:2, :] += jnp.sum(e, 0, keepdims=True)

        row_loop(rows, work)

    return times_turned(
        mixed_grad,
        parts,
        table,
        [row_low, hidden1_grad, vec],
        [whole(row_low.shape), whole(hidden1_grad.shape), whole(vec.shape)],
        [jax.ShapeDtypeStruct((rows, width), LOW), jax.ShapeDtypeStruct((8, width), F32)],
        [whole((rows, width)), whole((8, width))],
        finish,
        18,
        after,
    )


def grad_kernel(pairs, block, kind, half, came=None, part=None, us=10, after=()):
    rows, width = pairs[0][0].shape
    middle = width // 2
    low = middle // 2
    steps = len(kind)
    near = steps // 2
    count = len(pairs)

    def kernel(*refs):
        lefts, rights = refs[:count], refs[count : 2 * count]
        rest = refs[2 * count :]
        j = pl.program_id(0)

        for k in range(count):
            hits = [s for s in range(steps) if kind[s][0] == k]
            hit = j == hits[0]
            for s in hits[1:]:
                hit = hit | (j == s)

            @pl.when(hit)
            def _(k=k):
                right = rights[k][...]
                if came is None:
                    rest[0][...] = outer(lefts[k][...], right).astype(LOW)
                    return
                came_ref, out0, out1, out2 = rest[:4]
                y = outer(lefts[k][...], right)
                y0 = y[:low]
                y0 = (y0 + came_ref[:low, :].astype(F32)).astype(LOW)
                y1 = y[low:]
                y1 = (y1 + came_ref[low:, :].astype(F32)).astype(LOW)

                @pl.when(j < near)
                def _():
                    out0[...] = y0
                    out1[...] = y1

                @pl.when(j >= near)
                def _():
                    if part == "a":
                        out2[...] = y0
                        out1[...] = y1
                    else:
                        out2[:low, :] = y0
                        out2[low:, :] = y1

    right_specs = []
    for k in range(count):
        table, last = [], 0
        for s in range(steps):
            if kind[s][0] == k:
                last = kind[s][1]
            table.append(last)
        column = lookup(table)
        right_specs.append(pl.BlockSpec((rows, block), lambda j, column=column: (0, column(j))))

    def clipped(base, number, height):
        spec = pl.BlockSpec((height, block), lambda j: (0, jnp.clip(j - base, 0, number - 1)))
        return spec, jax.ShapeDtypeStruct((height, number * block), LOW)

    extra, extra_specs = [], []
    if came is None:
        outs = [clipped(0, steps, middle)]
    else:
        extra = [came[0]]
        column = lookup(came[1])
        extra_specs = [pl.BlockSpec((middle, block), lambda j: (0, column(j)))]
        if part == "a":
            both = pl.BlockSpec((low, block), lambda j: (j // near, j % near))
            outs = [
                clipped(0, near, low),
                (both, jax.ShapeDtypeStruct((middle, near * block), LOW)),
                clipped(near, near, low),
            ]
        else:
            outs = [clipped(0, near, low), clipped(0, near, low), clipped(near, near, middle)]
    return call(
        kernel,
        (steps,),
        [pl.BlockSpec((rows, middle), lambda j: (0, half)) for _ in pairs]
        + right_specs
        + extra_specs,
        [s for s, _ in outs],
        [s for _, s in outs],
        us=us,
        after=after,
    )(*[left for left, _ in pairs], *[right for _, right in pairs], *extra)


def add_second(other_a, own_b, from_y, from_x):
    rows, columns = other_a.shape

    def kernel(a_ref, b_ref, y_ref, x_ref, to_x, to_y):
        to_x[...] = (a_ref[...].astype(F32) + y_ref[...].astype(F32)).astype(LOW)
        to_y[...] = (b_ref[...].astype(F32) + x_ref[...].astype(F32)).astype(LOW)

    shape = jax.ShapeDtypeStruct((rows, columns), LOW)
    block = columns // 2
    spec = pl.BlockSpec((rows, block), lambda j: (0, j))
    later = pl.BlockSpec((rows, block), lambda j: (1, j))
    return call(
        kernel,
        (2,),
        [spec, spec, later, later],
        [spec, spec],
        [shape, shape],
    )(other_a, own_b, from_y, from_x)


def add_ring(own_a, own_b, from_y, from_x, second_x, second_y, came, place, rows, kind):
    half = own_a.shape[1]
    columns = 2 * half

    def kernel(*refs):
        own_a, own_b, y, x, x2, y2 = refs[:6]
        out = refs[-1]
        a = own_a[...].astype(F32) + y[...].astype(F32) + x2[...].astype(F32)
        b = own_b[...].astype(F32) + x[...].astype(F32) + y2[...].astype(F32)
        if came is not None:
            a = a + refs[6][:, :half].astype(F32)
            b = b + refs[6][:, half:].astype(F32)
        out[:, :half] = a.astype(kind)
        out[:, half:] = b.astype(kind)

    side = pl.BlockSpec((rows, half), lambda j: (place, 0))
    extra = [] if came is None else [came]
    return call(
        kernel,
        (1,),
        [side] * 6
        + [whole(v.shape) for v in extra],
        whole((rows, columns)),
        jax.ShapeDtypeStruct((rows, columns), kind),
    )(own_a, own_b, from_y, from_x, second_x, second_y, *extra)


def cut_far(side, across, near, after=()):
    rows, columns = side.shape
    far, at = [], 0
    for start, stop in near:
        if start > at:
            far.append((at, start))
        at = stop
    if at < columns:
        far.append((at, columns))

    def kernel(a, b, out_a, out_b):
        for source, out, ranges in ((a, out_a, near), (b, out_b, far)):
            at = 0
            for start, stop in ranges:
                out[:, at : at + stop - start] = source[:, start:stop]
                at += stop - start

    widths = [sum(stop - start for start, stop in ranges) for ranges in (near, far)]
    return call(
        kernel,
        (1,),
        [whole(side.shape)] * 2,
        [whole((rows, w)) for w in widths],
        [jax.ShapeDtypeStruct((rows, w), side.dtype) for w in widths],
        after=after,
    )(side, across)


def pack_columns(values, after=()):
    rows = values[0].shape[0]
    columns = sum(v.shape[1] for v in values)

    def kernel(*refs):
        at = 0
        for ref in refs[:-1]:
            n = ref.shape[1]
            refs[-1][:, at : at + n] = ref[...].astype(LOW)
            at += n

    return call(
        kernel,
        (1,),
        [whole(v.shape) for v in values],
        whole((rows, columns)),
        jax.ShapeDtypeStruct((rows, columns), LOW),
        after=after,
    )(*values)


def hold(*values, after=()):
    def kernel(*refs):
        total = refs[0][...]
        for ref in refs[1:-1]:
            total = total + ref[...]
        refs[-1][...] = total

    shape = values[0].shape
    return call(
        kernel,
        (1,),
        [whole(shape)] * len(values),
        whole(shape),
        jax.ShapeDtypeStruct(shape, values[0].dtype),
        us=1,
        after=after,
    )(*values)


def enter_input(mine, came, shuffle, vec):
    half, width = mine.shape
    rows = 2 * half

    def kernel(mine_ref, came_ref, s_ref, vec_ref, row_ref, first_ref):
        row_ref[:half, :] = jnp.dot(
            mine_ref[...], s_ref[...], preferred_element_type=F32
        ).astype(LOW)
        row_ref[half:, :] = jnp.dot(
            came_ref[0], s_ref[...], preferred_element_type=F32
        ).astype(LOW)
        normed, _ = norm_parts(row_ref[...].astype(F32))
        first_ref[...] = (normed * vec_ref[0:1, :] + vec_ref[1:2, :]).astype(LOW)

    shape = jax.ShapeDtypeStruct((rows, width), LOW)
    return call(
        kernel,
        (1,),
        [
            whole(mine.shape),
            pl.BlockSpec((1, half, width), lambda j: (0, 0, 0)),
            whole(shuffle.shape),
            whole(vec.shape),
        ],
        [whole((rows, width))] * 2,
        [shape, shape],
        us=7,
    )(mine, came, shuffle, vec)


def enter_cotangent(mine, came, shuffle, token_weight):
    half, width = mine.shape
    rows = 2 * half

    def kernel(mine_ref, came_ref, s_ref, weight_ref, row_ref, grad_ref):
        for k, part in enumerate((mine_ref[...], came_ref[0])):
            cut = slice(k * half, (k + 1) * half)
            y = jnp.dot(part, s_ref[...], preferred_element_type=F32)
            row_ref[cut, :] = y.astype(LOW)
            grad_ref[cut, :] = (y * weight_ref[cut, :]).astype(LOW)

    shape = jax.ShapeDtypeStruct((rows, width), LOW)
    return call(
        kernel,
        (1,),
        [
            whole(mine.shape),
            pl.BlockSpec((1, half, width), lambda j: (1, 0, 0)),
            whole(shuffle.shape),
            whole(token_weight.shape),
        ],
        [whole((rows, width))] * 2,
        [shape, shape],
        us=7,
    )(mine, came, shuffle, token_weight)


def place_halves(mine, theirs, slot, after=()):
    shape = (2, 1, *mine.shape)

    def kernel(slot_ref, mine_ref, their_ref, out_ref):
        for k in range(2):

            @pl.when(slot_ref[0] == k)
            def _(k=k):
                out_ref[k, 0] = mine_ref[...]
                out_ref[1 - k, 0] = their_ref[...]

    return call(
        kernel,
        (1,),
        [pl.BlockSpec(memory_space=pltpu.SMEM), whole(mine.shape), whole(theirs.shape)],
        whole(shape),
        jax.ShapeDtypeStruct(shape, mine.dtype),
        after=after,
    )(slot.reshape(1), mine, theirs)


def unshuffle(values, shuffle):
    rows, width = values.shape
    half = rows // 2

    def kernel(in_ref, s_ref, first, second):
        y = lax.dot_general(
            in_ref[...], s_ref[...], (((1,), (1,)), ((), ())), preferred_element_type=F32
        ).astype(LOW)
        first[...] = y[:half]
        second[...] = y[half:]

    shape = jax.ShapeDtypeStruct((half, width), LOW)
    return call(
        kernel,
        (1,),
        [whole(values.shape), whole(shuffle.shape)],
        [whole((half, width))] * 2,
        [shape, shape],
        us=0.1,
    )(values, shuffle)


def lamb_row(index, master_sq, update_sq):
    lane = lax.broadcasted_iota(jnp.int32, (1, 128), 1)
    row = jnp.where(lane == index, master_sq, 0.0)
    return row + jnp.where(lane == 7 + index, update_sq, 0.0)


def lamb_first(items, grad, factor, rows=()):
    count = len(items)

    def kernel(*refs):
        p_refs, m_refs = refs[:count], refs[count : 2 * count]
        g_ref = refs[2 * count]
        row_refs = refs[2 * count + 1 : 2 * count + 1 + len(rows)]
        outs = refs[2 * count + 1 + len(rows) :]
        row = jnp.zeros((1, 128), F32)
        for ref in row_refs:
            row = row + ref[...]
        for n, (place, master, _, at) in enumerate(items):
            width = master.shape[-1]
            for k in range(1 if master.ndim == 2 else master.shape[0]):
                cut = () if master.ndim == 2 else (k,)
                g = g_ref[:, at + k * width : at + (k + 1) * width] * factor
                p = p_refs[n][(*cut, ...)]
                old = (m_refs[n][(0, *cut, ...)], m_refs[n][(1, *cut, ...)])
                first, second, update = lamb_parts(p, old, g)
                outs[n][(0, *cut, ...)] = first
                outs[n][(1, *cut, ...)] = second
                outs[count + n][(*cut, ...)] = update
                row = row + lamb_row(place, jnp.sum(p * p), jnp.sum(update * update))
        outs[2 * count][...] = row

    operands = [*[i[1] for i in items], *[i[2] for i in items], grad, *rows]
    shapes = [i[2].shape for i in items] + [i[1].shape for i in items] + [(1, 128)]
    return call(
        kernel,
        (1,),
        [whole(v.shape) for v in operands],
        [whole(v) for v in shapes],
        [jax.ShapeDtypeStruct(v, F32) for v in shapes],
        us=4,
    )(*operands)


def lamb_small(masters, moments, grads, shares, factor):
    count = len(masters)

    def kernel(*refs):
        p_refs, m_refs, g_refs = refs[:count], refs[count : 2 * count], refs[2 * count : 3 * count]
        share_ref = refs[3 * count]
        outs = refs[3 * count + 1 :]
        row = jnp.zeros((1, 128), F32)
        for k in range(count):
            p = p_refs[k][...]
            if len(m_refs[k].shape) == 2:
                old = (m_refs[k][0:1, :], m_refs[k][1:2, :])
            else:
                old = (m_refs[k][:, 0, :], m_refs[k][:, 1, :])
            first, second, update = lamb_parts(p, old, g_refs[k][...] * factor)
            if len(m_refs[k].shape) == 2:
                outs[k][0:1, :] = first
                outs[k][1:2, :] = second
            else:
                outs[k][:, 0, :] = first
                outs[k][:, 1, :] = second
            outs[count + k][...] = update
            row = row + lamb_row(4 + k, jnp.sum(p * p), jnp.sum(update * update))
        outs[2 * count][...] = row * share_ref[...]

    operands = [*masters, *moments, *grads, shares]
    shapes = [v.shape for v in (*moments, *masters)] + [(1, 128)]
    return call(
        kernel,
        (1,),
        [whole(v.shape) for v in operands],
        [whole(v) for v in shapes],
        [jax.ShapeDtypeStruct(v, F32) for v in shapes],
    )(*operands)


def lamb_last(masters, updates, row, copies):
    count = len(masters)

    def kernel(*refs):
        p_refs, u_refs, row_ref = refs[:count], refs[count : 2 * count], refs[2 * count]
        outs = refs[2 * count + 1 :]
        norms, trust_ref = outs[count + copies :]
        master_sq, update_sq = row_ref[:, :count], row_ref[:, count : 2 * count]
        trust = jnp.sqrt(master_sq) / jnp.sqrt(update_sq + 1e-12)
        norms[0:1, :] = jnp.sqrt(master_sq)
        norms[1:2, :] = jnp.sqrt(update_sq)
        trust_ref[...] = trust
        for k in range(count):
            for c in range(1 if len(p_refs[k].shape) == 2 else p_refs[k].shape[0]):
                cut = (...,) if len(p_refs[k].shape) == 2 else (c, ...)
                new = p_refs[k][cut] - LEARN_RATE * trust[:, k : k + 1] * u_refs[k][cut]
                outs[k][cut] = new
                if k < copies:
                    outs[count + k][cut] = new.astype(LOW)

    shapes = [jax.ShapeDtypeStruct(v.shape, F32) for v in masters]
    shapes += [jax.ShapeDtypeStruct(v.shape, LOW) for v in masters[:copies]]
    shapes += [jax.ShapeDtypeStruct((2, count), F32), jax.ShapeDtypeStruct((1, count), F32)]
    operands = [*masters, *updates, row]
    return call(
        kernel,
        (1,),
        [whole(v.shape) for v in operands],
        [whole(v.shape) for v in shapes],
        shapes,
        us=8,
    )(*operands)


def stack_early(shard, side, across, far, after=()):
    rows, columns = shard.shape

    def kernel(a, b, c, d, out):
        out[:rows, :columns] = a[...]
        out[:rows, columns:] = b[...]
        out[rows:, :columns] = c[...]
        out[rows:, columns:] = d[...]

    return call(
        kernel,
        (1,),
        [whole(shard.shape)] * 4,
        whole((2 * rows, 2 * columns)),
        jax.ShapeDtypeStruct((2 * rows, 2 * columns), shard.dtype),
        after=after,
    )(shard, side, across, far)


def stack_rows(pieces, after=()):
    rows, columns = pieces[0].shape
    count = len(pieces)
    block = columns // (columns // 640)

    def kernel(*refs):
        for k in range(count):
            refs[-1][k * rows : (k + 1) * rows, :] = refs[k][...]

    return call(
        kernel,
        (columns // block,),
        [pl.BlockSpec((rows, block), lambda j: (0, j))] * count,
        pl.BlockSpec((count * rows, block), lambda j: (0, j)),
        jax.ShapeDtypeStruct((count * rows, columns), pieces[0].dtype),
        after=after,
    )(*pieces)


def turn_pairs(v, heads_lanes):
    middle = HD // 2
    lanes = lax.broadcasted_iota(jnp.int32, v.shape, 1)
    early = lanes % HD < middle
    width = v.shape[1]
    return jnp.where(early, -pltpu.roll(v, width - middle, 1), pltpu.roll(v, middle, 1))


def head_cut(h):
    return slice(h * HD, (h + 1) * HD)


def attention_forward(mixed, cosine, sine, key_code, query_code, groups, after=()):
    rows, columns = mixed.shape
    lanes = columns // (3 * groups)
    heads = lanes // HD
    scale = HD ** (-0.5)

    def kernel(mixed_ref, cos_ref, sin_ref, key_ref, query_ref, qkv_ref, att_ref, lse_ref, out_t):
        cos, sin = cos_ref[...], sin_ref[...]
        for part in range(2):
            cut = slice(part * lanes, (part + 1) * lanes)
            v = mixed_ref[:, cut]
            qkv_ref[:, cut] = (v * cos + turn_pairs(v, lanes) * sin).astype(LOW)
        qkv_ref[:, 2 * lanes :] = mixed_ref[:, 2 * lanes :].astype(LOW)
        query_t = qkv_ref[:, :lanes].T
        keys = qkv_ref[:, lanes : 2 * lanes]
        value_t = qkv_ref[:, 2 * lanes :].T
        allowed = key_ref[...] == query_ref[...]
        for h in range(heads):
            cut = head_cut(h)
            logits = jnp.dot(keys[:, cut], query_t[cut, :], preferred_element_type=F32)
            logits = jnp.where(allowed, logits * scale, NEGATIVE)
            top = jnp.max(logits, 0, keepdims=True)
            exponent = jnp.exp(logits - top)
            total_ = jnp.sum(exponent, 0, keepdims=True)
            prob = (exponent / total_).astype(LOW)
            out_t[cut, :] = jnp.dot(value_t[cut, :], prob, preferred_element_type=F32)
            lse_ref[0, h : h + 1, :] = top + jnp.log(total_)
        att_ref[...] = out_t[...].T.astype(LOW)

    return call(
        kernel,
        (groups,),
        [
            pl.BlockSpec((rows, 3 * lanes), lambda g: (0, g)),
            whole(cosine.shape),
            whole(sine.shape),
            whole(key_code.shape),
            whole(query_code.shape),
        ],
        [
            pl.BlockSpec((rows, 3 * lanes), lambda g: (0, g)),
            pl.BlockSpec((rows, lanes), lambda g: (0, g)),
            pl.BlockSpec((1, heads, rows), lambda g: (g, 0, 0)),
        ],
        [
            jax.ShapeDtypeStruct((rows, columns), LOW),
            jax.ShapeDtypeStruct((rows, groups * lanes), LOW),
            jax.ShapeDtypeStruct((groups, heads, rows), F32),
        ],
        scratch=[pltpu.VMEM((lanes, rows), F32)],
        us=19.6,
        after=after,
    )(mixed, cosine, sine, key_code, query_code)


def attention_backward(qkv, lse, attn_grad, cosine, sine, key_code, query_code, groups, after=()):
    rows, columns = qkv.shape
    lanes = columns // (3 * groups)
    heads = lanes // HD
    scale = HD ** (-0.5)

    def kernel(
        qkv_ref, lse_ref, grad_ref, cos_ref, sin_ref, key_ref, query_ref, out_ref, sum_ref, q_t, k_n, v_n
    ):
        query_t = qkv_ref[:, :lanes].T
        key_t = qkv_ref[:, lanes : 2 * lanes].T
        grad_t = grad_ref[...].T
        queries = qkv_ref[:, :lanes]
        keys = qkv_ref[:, lanes : 2 * lanes]
        values = qkv_ref[:, 2 * lanes :]
        grads = grad_ref[...]
        allowed = key_ref[...] == query_ref[...]
        for h in range(heads):
            cut = head_cut(h)
            logits = jnp.dot(keys[:, cut], query_t[cut, :], preferred_element_type=F32)
            logits = jnp.where(allowed, logits * scale, NEGATIVE)
            prob = jnp.exp(logits - lse_ref[0, h : h + 1, :])
            prob_grad = jnp.dot(values[:, cut], grad_t[cut, :], preferred_element_type=F32)
            inner = jnp.sum(prob * prob_grad, 0, keepdims=True)
            score_grad = (scale * prob * (prob_grad - inner)).astype(LOW)
            q_t[cut, :] = jnp.dot(key_t[cut, :], score_grad, preferred_element_type=F32)
            k_n[:, cut] = jnp.dot(score_grad, queries[:, cut], preferred_element_type=F32)
            v_n[:, cut] = jnp.dot(prob.astype(LOW), grads[:, cut], preferred_element_type=F32)
        cos, sin = cos_ref[...], sin_ref[...]
        for part, w in enumerate((q_t[...].T, k_n[...], v_n[...])):
            cut = slice(part * lanes, (part + 1) * lanes)
            if part < 2:
                w = w * cos - turn_pairs(w, lanes) * sin
            w = w.astype(LOW)
            out_ref[:, cut] = w
            sum_ref[:, cut] = jnp.sum(w.astype(F32), 0, keepdims=True)

    return call(
        kernel,
        (groups,),
        [
            pl.BlockSpec((rows, 3 * lanes), lambda g: (0, g)),
            pl.BlockSpec((1, heads, rows), lambda g: (g, 0, 0)),
            pl.BlockSpec((rows, lanes), lambda g: (0, g)),
            whole(cosine.shape),
            whole(sine.shape),
            whole(key_code.shape),
            whole(query_code.shape),
        ],
        [
            pl.BlockSpec((rows, 3 * lanes), lambda g: (0, g)),
            pl.BlockSpec((1, 3 * lanes), lambda g: (0, g)),
        ],
        [
            jax.ShapeDtypeStruct((rows, columns), LOW),
            jax.ShapeDtypeStruct((1, columns), F32),
        ],
        scratch=[
            pltpu.VMEM((lanes, rows), F32),
            pltpu.VMEM((rows, lanes), F32),
            pltpu.VMEM((rows, lanes), F32),
        ],
        us=27.3,
        after=after,
    )(qkv, lse, attn_grad, cosine, sine, key_code, query_code)
class Lanes:
    def __init__(self, dp):
        self.dp = dp
        self.ring = dp // 4

    def over_x(self, v):
        return lax.ppermute(v, "tensor", [(0, 1), (1, 0)])

    def over_core(self, v):
        return lax.ppermute(v, "dp", [(i, i ^ 1) for i in range(self.dp)])

    def over_y(self, v):
        return lax.ppermute(v, "dp", [(i, i ^ 2) for i in range(self.dp)])

    def down_z(self, v):
        return lax.ppermute(v, "dp", [(i, (i - 4) % self.dp) for i in range(self.dp)])

    def up_z(self, v):
        return lax.ppermute(v, "dp", [(i, (i + 4) % self.dp) for i in range(self.dp)])

    def exchange(self, v, bit):
        return lax.ppermute(v, "dp", [(i, i ^ bit) for i in range(self.dp)])

    def order(self):
        i = lax.axis_index("dp")
        z, y, c = i // 4, (i // 2) % 2, i % 2
        blocks = []
        for dc in range(2):
            for dy in range(2):
                for dz in range(self.ring):
                    blocks.append(((z + dz) % self.ring) * 4 + (y ^ dy) * 2 + (c ^ dc))
        return jnp.stack(blocks)

    def ring_down(self, v):
        held = [v]
        for _ in range(self.ring - 1):
            held.append(self.down_z(held[-1]))
        return held

    def far(self, side, across, near, after=()):
        a, b = cut_far(side, across, near, after)
        return self.over_y(a), self.over_x(b)

    def both_cores(self, values):
        return [(v, self.over_core(v)) for v in values]

    def stacked(self, pairs):
        rows = pairs[0][0].shape[0] // 2
        cuts = [
            (dc * self.ring + dz, dy * rows, rows)
            for dc in range(2)
            for dy in range(2)
            for dz in range(self.ring)
        ]
        return Stacked([p[0] for p in pairs] + [p[1] for p in pairs], cuts)


class Gathered:
    def __init__(self, own, other, far=None, near=()):
        self.own, self.other, self.far, self.near = own, other, far, near

    def pieces(self, column):
        if self.far is None:
            return [(v, column) for v in self.other]
        side, side_core = self.other
        place, spent, before = 1, column, 0
        for start, stop in self.near:
            if start <= column < stop:
                place, spent = 0, before + column - start
            before += stop - start
            if place and stop <= column:
                spent -= stop - start
        a, a_core = self.far[place]
        return [(side, column), (a, spent), (side_core, column), (a_core, spent)]

    def parts(self, block, first, count):
        sets = [([(v, first) for v in self.own], None, count)]
        last = None
        for b in range(first, first + count):
            here = [(v, c // block) for v, c in self.pieces(b * block)]
            if last is not None and all(
                v is w and c == d + sets[-1][2] for (v, c), (w, d) in zip(here, last)
            ):
                sets[-1] = (last, None, sets[-1][2] + 1)
            else:
                last = here
                sets.append((here, None, 1))
        return Parts(sets, block)


class Stacked:
    def __init__(self, pieces, cuts):
        self.pieces, self.cuts = pieces, cuts

    def parts(self, block):
        count = self.pieces[0].shape[1] // block
        return Parts([([(v, 0) for v in self.pieces], self.cuts, count)], block)


def butterfly(value, dp):
    if dp & (dp - 1):
        return lax.psum(value, ("dp", "tensor"))
    value = value + lax.ppermute(value, "tensor", [(0, 1), (1, 0)])
    bit = 1
    while bit < dp:
        value = value + lax.ppermute(value, "dp", [(i, i ^ bit) for i in range(dp)])
        bit *= 2
    return value


def body(
    block_input,
    out_cotangent,
    picture_ids,
    patch_positions,
    picture_lengths,
    pad_mask,
    qkv_weight,
    proj_weight,
    fc1_weight,
    fc2_weight,
    qkv_bias,
    fc1_bias,
    vectors,
    qkv_moments,
    proj_moments,
    fc1_moments,
    fc2_moments,
    qkv_bias_moments,
    fc1_bias_moments,
    vector_moments,
):
    ORDER.last = None
    dp = lax.axis_size("dp")
    relative = dp == 16
    lanes = Lanes(dp)
    slot = lax.axis_index("tensor")
    lead_dp = (lax.axis_index("dp") == 0).astype(F32)
    lead_all = lead_dp * (slot == 0).astype(F32)
    width = block_input.shape[3]
    rows_own = width // dp
    lane_columns = qkv_weight.shape[2]
    hidden = fc1_weight.shape[1]
    grad_factor = float(block_input.shape[0] * block_input.shape[1] * dp * LEN) ** (-0.5)

    biases = jnp.concatenate([qkv_bias.reshape(-1), fc1_bias]).reshape(-1, 128)

    def row_view(v):
        return jnp.swapaxes(v, -1, -2)

    qkv_view, qkv_moments_view = jnp.swapaxes(qkv_weight, 0, 1), jnp.swapaxes(qkv_moments, 1, 2)
    proj_view, proj_moments_view = row_view(proj_weight), row_view(proj_moments)
    fc2_view, fc2_moments_view = row_view(fc2_weight), row_view(fc2_moments)

    local_rows = block_input.shape[2]

    def half_of(both, place):
        return lax.dynamic_index_in_dim(both[:, 0], place, 0, keepdims=False)

    both_came = lanes.over_x(
        jnp.stack([half_of(block_input, 1 - slot), half_of(out_cotangent, 1 - slot)])
    )
    input_mine, cot_mine = half_of(block_input, slot), half_of(out_cotangent, slot)

    shard_1 = jnp.concatenate([qkv_view[k].astype(LOW) for k in range(3)], 1)
    shard_3 = fc2_view.astype(LOW)
    half = hidden // 2
    if relative:
        ring_1 = lanes.ring_down(shard_1)
        side_3, across_3 = lanes.over_x(shard_3), lanes.over_y(shard_3)
        far_3 = lanes.over_y(side_3)
        shard_2 = pack_columns([fc1_weight, proj_view])
        ring_2 = [shard_2, lanes.down_z(shard_2)]
        held_1 = stack_rows(ring_1, after=[side_3, across_3, far_3, both_came])
        ring_2[1] = hold(ring_2[1])
        for _ in range(2):
            ring_2.append(lanes.down_z(ring_2[-1]))
    else:

        def plain(shard):
            held = lax.all_gather(shard, "dp", axis=0, tiled=True)
            return Gathered([held], [lanes.over_x(held)])

        shard_2 = jnp.concatenate([fc1_weight.astype(LOW), proj_view.astype(LOW)], 1)
        w1, w2, w3 = plain(shard_1), plain(shard_2), plain(shard_3)
        w_down = w3.parts(half, 0, 2)
    def pick(array, axis=0):
        return lax.dynamic_index_in_dim(array, slot, axis, keepdims=False)

    def turn(values):
        return jnp.roll(values, -slot * local_rows, axis=-1)

    ids_row = turn(pick(picture_ids[:, 0]))
    rows_at = turn(pick(patch_positions[0, :, 0]))
    cols_at = turn(pick(patch_positions[1, :, 0]))
    mask_row = turn(pick(pad_mask[:, 0]))
    length_row = pick(picture_lengths[:, 0])
    cosine, sine = rotary_tables(rows_at, cols_at)
    groups = 2
    heads = lane_columns // HD
    cosine, sine = jnp.tile(cosine, (1, heads)), jnp.tile(sine, (1, heads))
    key_code = jnp.where(mask_row == 1, ids_row, -1)[:, None]
    query_code = ids_row[None, :]
    slot_hit = (ids_row[:, None] == jnp.arange(SLOTS, dtype=jnp.int32)[None, :]).astype(F32)
    picture_size = jnp.sum(slot_hit * length_row.astype(F32)[None, :], -1)
    token_weight = (mask_row.astype(F32) * jnp.sqrt(LEN / picture_size))[:, None]

    if relative:
        order = lanes.order()
        column = (order[:, None] * rows_own + jnp.arange(rows_own)[None, :]).reshape(-1)
        shuffle = (jnp.arange(width)[:, None] == column[None, :]).astype(LOW)
        vec = lax.dot_general(
            vectors,
            shuffle.astype(F32),
            (((1,), (0,)), ((), ())),
            precision=lax.Precision.HIGHEST,
            preferred_element_type=F32,
        )
        core_held_1 = lanes.over_core(held_1)
        sides_1 = lanes.over_x(held_1), lanes.over_y(held_1)
        row_low, first_in = enter_input(input_mine, both_came, shuffle, vec)
        biases = hold(biases)
        near_1 = [(0, 2 * lane_columns)]
        fars_1 = lanes.far(*sides_1, near_1, after=[core_held_1])
        late_3 = [stack_early(shard_3, side_3, across_3, far_3, after=[ring_2[3]])]
        late_came = lanes.down_z(late_3[0])
        core_late = lanes.over_core(late_3[0])
        cores_1 = lanes.both_cores(sides_1)
        held_2 = stack_rows(ring_2, after=[*fars_1, cores_1[0][1], cores_1[1][1]])
        sides_2 = lanes.over_x(held_2), lanes.over_y(held_2)
        core_held_2 = lanes.over_core(held_2)
        w1 = Gathered(
            [held_1, sides_1[1], core_held_1, cores_1[1][1]],
            cores_1[0],
            lanes.both_cores(fars_1),
            near_1,
        )
    else:
        vec = vectors
        row_low = jnp.concatenate([input_mine, both_came[0]], 0)
        cot_low = jnp.concatenate([cot_mine, both_came[1]], 0)
        normed1, _ = norm_parts(row_low.astype(F32))
        first_in = (normed1 * vec[0] + vec[1]).astype(LOW)
        down_grad = (cot_low.astype(F32) * token_weight).astype(LOW)
    w_qkv = w1.parts(lane_columns, 0, 3)
    other_biases = lanes.over_x(biases).reshape(-1)
    biases = biases.reshape(-1)
    cut = qkv_bias.size
    bias_qkv = jnp.concatenate([biases[:cut], other_biases[:cut]])[None]
    bias_up = jnp.concatenate([biases[cut:], other_biases[cut:]])[None]

    def give_back(values_low):
        if relative:
            mine, theirs = unshuffle(values_low, shuffle)
        else:
            mine, theirs = values_low[:local_rows], values_low[local_rows:]
        return mine, lanes.over_x(theirs)

    wide_kind = [(0, j) for j in range(4)]
    first_kind = [(0, 0), (0, 1), (0, 2), (1, 0), (0, 3), (0, 4), (0, 5), (1, 1)]

    def send_grads(pairs, block, kind, us):
        (sent,) = grad_kernel(pairs, block, kind, 1, us=us)
        return lanes.over_core(sent)

    def wide_grads(pairs, came):
        a = grad_kernel(pairs, half, [(0, 0), (0, 2)], 0, (came, [0, 2]), "a", 7)
        from_y = lanes.over_y(a[1])
        b = grad_kernel(pairs, half, [(0, 1), (0, 3)], 0, (came, [1, 3]), "b", 7)
        return (a[0], b[0]), (a[2], b[1]), (from_y, lanes.over_x(b[2]))

    def send_second(kept, first):
        to_x, to_y = add_second(*kept, *first)
        return (*first, lanes.over_x(to_x), lanes.over_y(to_y))

    def ring_step(own, sides, came, place):
        kind = LOW if place else F32
        total = add_ring(*own, *sides, came, place, rows_own, kind)
        return lanes.up_z(total) if place else total

    def plain_grads(pairs, block, kind):
        whole_grad = jnp.concatenate(
            [
                outer(pairs[p][0], pairs[p][1][:, c * block : (c + 1) * block])
                for p, c in kind
            ],
            1,
        )
        both = whole_grad[:, :hidden] + lanes.over_x(whole_grad[:, hidden:])
        return lax.psum_scatter(both, "dp", scatter_dimension=0, tiled=True)

    qkv_columns = 3 * lane_columns

    def small_sums(sums_1, sums_2, sum_qkv, sum_up):
        terms = jnp.concatenate([sums_1[0:2], sums_2[2:3], sums_2[0:2], sums_2[3:4]], 0)
        if relative:
            terms = lax.dot_general(
                terms,
                shuffle.astype(F32),
                (((1,), (1,)), ((), ())),
                precision=lax.Precision.HIGHEST,
                preferred_element_type=F32,
            )
        own = jnp.concatenate([sum_qkv[0, :qkv_columns], sum_up[0, :hidden]])
        other = jnp.concatenate([sum_qkv[0, qkv_columns:], sum_up[0, hidden:]])
        first_half = slot == 0
        return jnp.concatenate(
            [
                jnp.where(first_half, own, other),
                jnp.where(first_half, other, own),
                terms.reshape(-1),
            ]
        ).reshape(-1, 128)

    mixed = qkv_forward(first_in, w_qkv, bias_qkv, list(range(6)))
    if relative:
        late_3.append(hold(late_came))
    before_attention = [core_held_2, core_late] if relative else []
    qkv, attended, lse = attention_forward(
        mixed, cosine, sine, key_code, query_code, groups, after=before_attention
    )
    if relative:
        late_3.append(lanes.down_z(late_3[1]))
        late_came = lanes.down_z(late_3[2])
        late_cores = [(late_3[0], core_late), *lanes.both_cores(late_3[1:])]
        before_far = [late_cores[1][1]]
        near_2 = [(0, half), (hidden, hidden + lane_columns)]
        fars_2 = lanes.far(*sides_2, near_2, after=before_far)
        cot_low, down_grad = enter_cotangent(cot_mine, both_came, shuffle, token_weight)
        hold(query_code, after=fars_2)
        cores_2 = lanes.both_cores(sides_2)
        w2 = Gathered(
            [held_2, sides_2[1], core_held_2, cores_2[1][1]],
            cores_2[0],
            lanes.both_cores(fars_2),
            near_2,
        )
    w_proj = w2.parts(lane_columns, hidden // lane_columns, 1)
    w_up = w2.parts(half, 0, 2)
    hidden1, second_in = proj_forward(attended, w_proj, row_low, vec)
    upward, activated = up_forward(second_in, w_up, bias_up)
    pair_3 = [(down_grad, activated)]
    if relative:
        came_3 = send_grads(pair_3, half, wide_kind, 60)
        late_cores += lanes.both_cores([hold(late_came)])
        w_down = lanes.stacked(late_cores).parts(half)
    result = down_forward(activated, w_down, hidden1, vec)

    if relative:
        own_3, later_3, first_3 = wide_grads(pair_3, came_3)
    up_grad, sum_up = down_backward(down_grad, w_down, upward)
    pair_2 = [(second_in, up_grad)]
    output_halves = give_back(result)
    if relative:
        came_2 = send_grads(pair_2, half, wide_kind, 0.1)
    hidden1_grad, branch_grad, sums_2 = up_backward(
        up_grad, w_up, hidden1, cot_low, token_weight, vec
    )
    if relative:
        sides_3 = send_second(later_3, first_3)
    attn_grad = proj_backward(branch_grad, w_proj)
    if relative:
        own_2, later_2, first_2 = wide_grads(pair_2, came_2)
        ring_3 = ring_step(own_3, sides_3, None, 3)
    block_output = place_halves(*output_halves, slot)
    mixed_grad, sum_qkv = attention_backward(
        qkv, lse, attn_grad, cosine, sine, key_code, query_code, groups
    )
    pair_q, pair_p = (first_in, mixed_grad), (branch_grad, attended)
    factor = grad_factor
    if relative:
        kind_a = [(0, 0), (0, 1), (0, 3), (0, 4)]
        kind_b = [(0, 2), (1, 0), (0, 5), (1, 1)]
        sides_2 = send_second(later_2, first_2)
        ring_3 = ring_step(own_3, sides_3, ring_3, 2)
        came_a = send_grads([pair_q], lane_columns, kind_a, 1)
        came_b = send_grads([pair_q, pair_p], lane_columns, kind_b, 1)
        part_a = grad_kernel([pair_q], lane_columns, kind_a, 0, (came_a, [0, 1, 2, 3]), "a", 8)
        first_y = lanes.over_y(part_a[1])
        ring_3 = ring_step(own_3, sides_3, ring_3, 1)
        ring_2 = ring_step(own_2, sides_2, None, 3)
        part_b = grad_kernel(
            [pair_q, pair_p], lane_columns, kind_b, 0, (came_b, [0, 1, 2, 3]), "b", 8
        )
        own_1, later_1 = (part_a[0], part_b[0]), (part_a[2], part_b[1])
        first_1 = first_y, lanes.over_x(part_b[2])
        grad_3 = ring_step(own_3, sides_3, ring_3, 0)
        lamb_3 = lamb_first([(3, fc2_view, fc2_moments_view, 0)], grad_3, factor)
    input_low, sums_1 = qkv_backward(
        mixed_grad, w_qkv, list(range(6)), row_low, hidden1_grad, vec
    )
    if relative:
        ring_2 = ring_step(own_2, sides_2, ring_2, 2)
        sides_1 = send_second(later_1, first_1)
        ring_2 = ring_step(own_2, sides_2, ring_2, 1)
        small = hold(small_sums(sums_1, sums_2, sum_qkv, sum_up))
        came = lanes.over_core(small)
        grad_2 = ring_step(own_2, sides_2, ring_2, 0)
        small = hold(small, came)
        came = lanes.exchange(small, 4)
    else:
        input_halves = give_back(input_low)
        small = small_sums(sums_1, sums_2, sum_qkv, sum_up)
        grad_3 = plain_grads(pair_3, half, wide_kind)
        lamb_3 = lamb_first([(3, fc2_view, fc2_moments_view, 0)], grad_3, factor)
        grad_2 = plain_grads(pair_2, half, wide_kind)
    lamb_2 = lamb_first([(2, fc1_weight, fc1_moments, 0)], grad_2, factor)
    if relative:
        small = hold(small, came)
        came = lanes.exchange(small, 8)
        ring_1 = ring_step(own_1, sides_1, None, 3)
        input_halves = give_back(input_low)
        small = hold(small, came)
        came = lanes.over_y(small)
        ring_1 = ring_step(own_1, sides_1, ring_1, 2)
        small = hold(small, came)
        came = lanes.over_x(small)
        ring_1 = ring_step(own_1, sides_1, ring_1, 1)
        small = hold(small, came)

    if not relative:
        small = butterfly(small, dp)
    small = small.reshape(-1)
    first_half = slot == 0
    size = qkv_columns + hidden
    bias_sum = jnp.where(first_half, small[:size], small[size : 2 * size])
    small_grads = [
        bias_sum[:qkv_columns].reshape(qkv_bias.shape),
        bias_sum[None, qkv_columns:],
        small[2 * size :].reshape(vectors.shape),
    ]
    small_masters = [qkv_bias, fc1_bias[None], vectors]
    lane = jnp.arange(128)
    is_bias = (lane == 4) | (lane == 5) | (lane == 11) | (lane == 12)
    shares = jnp.where(is_bias, lead_dp, lead_all)[None]
    *small_lamb, small_row = lamb_small(
        small_masters,
        [
            jnp.swapaxes(qkv_bias_moments, 0, 1),
            fc1_bias_moments,
            jnp.swapaxes(vector_moments, 0, 1),
        ],
        small_grads,
        shares,
        factor,
    )

    if relative:
        input_grad = place_halves(*input_halves, slot)
        grad_1 = ring_step(own_1, sides_1, ring_1, 0)
    else:
        input_grad = place_halves(*input_halves, slot)
        grad_1 = plain_grads([pair_q, pair_p], lane_columns, first_kind)
    q_moments, p_moments, q_update, p_update, row = lamb_first(
        [(0, qkv_view, qkv_moments_view, 0), (1, proj_view, proj_moments_view, qkv_columns)],
        grad_1,
        factor,
        [lamb_2[2], lamb_3[2], small_row],
    )
    row = butterfly(row, dp)
    last = lamb_last(
        [qkv_view, proj_view, fc1_weight, fc2_view, *small_masters],
        [q_update, p_update, lamb_2[1], lamb_3[1], *small_lamb[3:]],
        row,
        4,
    )
    new_params, copies, norms, trust = last[:7], last[7:11], last[11], last[12]
    new_weights, copies = [
        [jnp.swapaxes(v[0], 0, 1), row_view(v[1]), v[2], row_view(v[3])]
        for v in (new_params, copies)
    ]
    return (
        block_output,
        input_grad,
        *new_weights,
        new_params[4],
        new_params[5][0],
        new_params[6],
        jnp.swapaxes(q_moments, 1, 2),
        row_view(p_moments),
        lamb_2[0],
        row_view(lamb_3[0]),
        jnp.swapaxes(small_lamb[0], 0, 1),
        small_lamb[1],
        jnp.swapaxes(small_lamb[2], 0, 1),
        *copies,
        norms,
        trust[0],
    )


def solution(mesh):
    in_specs = (
        P(None, "dp", "tensor", None),
        P(None, "dp", "tensor", None),
        P(None, "dp", None),
        P(None, None, "dp", None),
        P(None, "dp", None),
        P(None, "dp", None),
        P("dp", None, "tensor"),
        P("tensor", "dp"),
        P("dp", "tensor"),
        P("tensor", "dp"),
        P(None, "tensor"),
        P("tensor"),
        P(),
        P(None, "dp", None, "tensor"),
        P(None, "tensor", "dp"),
        P(None, "dp", "tensor"),
        P(None, "tensor", "dp"),
        P(None, None, "tensor"),
        P(None, "tensor"),
        P(),
    )
    out_specs = (
        P(None, "dp", "tensor", None),
        P(None, "dp", "tensor", None),
        P("dp", None, "tensor"),
        P("tensor", "dp"),
        P("dp", "tensor"),
        P("tensor", "dp"),
        P(None, "tensor"),
        P("tensor"),
        P(),
        P(None, "dp", None, "tensor"),
        P(None, "tensor", "dp"),
        P(None, "dp", "tensor"),
        P(None, "tensor", "dp"),
        P(None, None, "tensor"),
        P(None, "tensor"),
        P(),
        P("dp", None, "tensor"),
        P("tensor", "dp"),
        P("dp", "tensor"),
        P("tensor", "dp"),
        P(),
        P(),
    )
    return jax.shard_map(body, mesh=mesh, in_specs=in_specs, out_specs=out_specs, check_vma=False)
```

```python
import math

import jax
import jax.numpy as jnp
from jax import lax
from jax.experimental import pallas as pl
from jax.experimental.pallas import tpu as pltpu
from jax.sharding import PartitionSpec as P

HD = 80
SLOTS = 4
LEN = 576


NEGATIVE = -1e30
EPS_NORM = 1e-06
EPS_ADAM = 1e-06
WEIGHT_DECAY = 0.01
LEARN_RATE = 0.5
GELU_SLOPE = 1.702
F32 = jnp.float32
LOW = jnp.bfloat16


def norm_parts(values):
    center = values - jnp.mean(values, -1, keepdims=True)
    inverse = lax.rsqrt(jnp.mean(center * center, -1, keepdims=True) + EPS_NORM)
    return (center * inverse, inverse)


def norm_back(out_grad, normed, inverse, gain):
    scaled = out_grad * gain
    return inverse * (
        scaled
        - jnp.mean(scaled, -1, keepdims=True)
        - normed * jnp.mean(scaled * normed, -1, keepdims=True)
    )


def rotary_tables(rows_at, cols_at):
    quarter = HD // 4
    frequency = 10000.0 ** (-jnp.arange(quarter, dtype=F32) / quarter)
    halves = jnp.concatenate(
        [
            rows_at.astype(F32)[:, None] * frequency,
            cols_at.astype(F32)[:, None] * frequency,
        ],
        -1,
    )
    angles = jnp.concatenate([halves, halves], -1)
    return (jnp.cos(angles), jnp.sin(angles))


def dot(left, right):
    return lax.dot_general(left, right, (((1,), (0,)), ((), ())), preferred_element_type=F32)


def dot_t(left, right):
    return lax.dot_general(left, right, (((1,), (1,)), ((), ())), preferred_element_type=F32)


def outer(left, right):
    return lax.dot_general(left, right, (((0,), (0,)), ((), ())), preferred_element_type=F32)


def lamb_parts(master, moments, gradient):
    first = 0.5 * moments[0] + 0.5 * gradient
    second = 0.5 * moments[1] + 0.5 * gradient * gradient
    update = first / (jnp.sqrt(second) + EPS_ADAM) + WEIGHT_DECAY * master
    return (first, second, update)


VMEM_MOST = 56 * 1024 * 1024
VMEM_SPARE = 6 * 1024 * 1024
COST = int(8 * 1.15e9)


class Order:
    def __init__(self):
        self.last = None


ORDER = Order()


def call(
    kernel, grid, in_specs, out_specs, out_shape, scratch=(), us=2.4, after=()
):
    if ORDER.last is not None:
        after = [*after, ORDER.last]
    count, extra = len(in_specs), len(after)
    shapes = out_shape if isinstance(out_shape, (list, tuple)) else [out_shape]
    outs = out_specs if isinstance(out_specs, (list, tuple)) else [out_specs]
    out_bytes = sum(
        2 * math.prod(o.block_shape) * v.dtype.itemsize for o, v in zip(outs, shapes)
    )
    scratch_bytes = sum(math.prod(v.shape) * v.dtype.itemsize for v in scratch)

    def room(operands):
        in_bytes = sum(
            2 * math.prod(i.block_shape) * v.dtype.itemsize
            for i, v in zip(in_specs, operands)
            if i.block_shape is not None
        )
        return min(VMEM_MOST, in_bytes + out_bytes + scratch_bytes + VMEM_SPARE)

    def ordered(*refs):
        kernel(*refs[:count], *refs[count + extra :])

    def run(*operands):
        return pl.pallas_call(
            ordered,
            grid=grid,
            in_specs=list(in_specs) + [pl.BlockSpec(memory_space=pl.ANY)] * extra,
            out_specs=out_specs,
            out_shape=out_shape,
            scratch_shapes=list(scratch),
            compiler_params=pltpu.CompilerParams(
                dimension_semantics=("arbitrary",) * len(grid), vmem_limit_bytes=room(operands)
            ),
            cost_estimate=pl.CostEstimate(
                flops=int(COST * us), bytes_accessed=0, transcendentals=0
            ),
        )(*operands, *after)

    def start(*operands):
        result = run(*operands)
        ORDER.last = result[0] if isinstance(result, (list, tuple)) else result
        return result

    return start


def whole(shape):
    return pl.BlockSpec(shape, lambda *_: (0,) * len(shape))


def lookup(table):
    def column(j):
        found = table[0]
        for k in range(1, len(table)):
            found = jnp.where(j == k, table[k], found)
        return found

    return column


class Parts:
    def __init__(self, sets, block):
        self.sets, self.block = sets, block
        self.steps = sum(s[2] for s in sets)
        self.width = sum(piece.shape[0] for piece, _ in sets[0][0])
        self.arrays, self.specs = [], []
        base = 0
        for pieces, _, count in sets:
            for piece, first in pieces:
                self.arrays.append(piece)
                self.specs.append(
                    pl.BlockSpec(
                        (piece.shape[0], block),
                        lambda j, first=first, base=base, count=count: (
                            0,
                            first + jnp.clip(j - base, 0, count - 1),
                        ),
                    )
                )
            base += count

    def each(self, refs, work):
        j = pl.program_id(0)
        base, at = 0, 0
        for pieces, cuts, count in self.sets:
            mine = refs[at : at + len(pieces)]

            @pl.when((j >= base) & (j < base + count))
            def _(mine=mine, cuts=cuts):
                if cuts is None:
                    values = [r[...] for r in mine]
                else:
                    values = [mine[p][r : r + n, :] for p, r, n in cuts]
                work(values[0] if len(values) == 1 else jnp.concatenate(values, 0))

            base += count
            at += len(pieces)


def row_loop(rows, work):
    work(pl.ds(0, rows))


def times_weight(left, parts, table, ins, in_specs, outs, out_specs, finish, us, after=()):
    count = len(parts.arrays)

    def kernel(*refs):
        left_ref, w_refs, rest = refs[0], refs[1 : 1 + count], refs[1 + count :]

        def work(w):
            y = jnp.dot(left_ref[...], w, preferred_element_type=F32)
            finish(y, rest[: len(ins)], rest[len(ins) :])

        parts.each(w_refs, work)

    return call(
        kernel,
        (parts.steps,),
        [whole(left.shape)] + parts.specs + in_specs,
        out_specs,
        outs,
        us=us,
        after=after,
    )(left, *parts.arrays, *ins)


def times_turned(left, parts, table, ins, in_specs, outs, out_specs, finish, us, after=()):
    count = len(parts.arrays)
    rows, width = left.shape[0], parts.width
    column = lookup(table)

    def kernel(*refs):
        left_ref, w_refs, rest = refs[0], refs[1 : 1 + count], refs[1 + count :]
        acc = rest[-1]
        rest = rest[:-1]

        def work(w):
            y = lax.dot_general(
                left_ref[...], w, (((1,), (1,)), ((), ())), preferred_element_type=F32
            )

            @pl.when(pl.program_id(0) == 0)
            def _():
                acc[...] = y

            @pl.when(pl.program_id(0) > 0)
            def _():
                acc[...] += y

        parts.each(w_refs, work)

        @pl.when(pl.program_id(0) == parts.steps - 1)
        def _():
            finish(acc, rest[: len(ins)], rest[len(ins) :])

    return call(
        kernel,
        (parts.steps,),
        [pl.BlockSpec((rows, parts.block), lambda j: (0, column(j)))] + parts.specs + in_specs,
        out_specs,
        outs,
        scratch=[pltpu.VMEM((rows, width), F32)],
        us=us,
        after=after,
    )(left, *parts.arrays, *ins)


def qkv_forward(first_in, parts, bias, table, after=()):
    column = lookup(table)
    block = parts.block

    def finish(y, ins, outs):
        outs[0][...] = y + ins[0][...]

    total_columns = parts.steps * block
    return times_weight(
        first_in,
        parts,
        table,
        [bias],
        [pl.BlockSpec((1, block), lambda j: (0, column(j)))],
        [jax.ShapeDtypeStruct((first_in.shape[0], total_columns), F32)],
        [pl.BlockSpec((first_in.shape[0], block), lambda j: (0, column(j)))],
        finish,
        14,
        after,
    )[0]


def proj_forward(attended, parts, row_low, vec, after=()):
    rows, width = row_low.shape

    def finish(acc, ins, outs):
        row_ref, vec_ref = ins
        hidden_ref, second_ref = outs

        def work(cut):
            hidden = row_ref[cut, :].astype(F32) + (acc[cut, :] + vec_ref[2:3, :])
            hidden_ref[cut, :] = hidden
            normed, _ = norm_parts(hidden)
            second_ref[cut, :] = (normed * vec_ref[3:4, :] + vec_ref[4:5, :]).astype(LOW)

        row_loop(rows, work)

    return times_turned(
        attended,
        parts,
        list(range(parts.steps)),
        [row_low, vec],
        [whole(row_low.shape), whole(vec.shape)],
        [jax.ShapeDtypeStruct((rows, width), F32), jax.ShapeDtypeStruct((rows, width), LOW)],
        [whole((rows, width))] * 2,
        finish,
        9.8,
        after,
    )


def up_forward(second_in, parts, bias, after=()):
    rows, block = second_in.shape[0], parts.block
    total_columns = parts.steps * block

    def finish(y, ins, outs):
        outs[0][...] = y + ins[0][...]

        def work(cut):
            u = outs[0][cut, :]
            outs[1][cut, :] = (u * jax.nn.sigmoid(GELU_SLOPE * u)).astype(LOW)

        row_loop(rows, work)

    spec = pl.BlockSpec((rows, block), lambda j: (0, j))
    return times_weight(
        second_in,
        parts,
        None,
        [bias],
        [pl.BlockSpec((1, block), lambda j: (0, j))],
        [
            jax.ShapeDtypeStruct((rows, total_columns), F32),
            jax.ShapeDtypeStruct((rows, total_columns), LOW),
        ],
        [spec, spec],
        finish,
        17.8,
        after,
    )


def down_forward(activated, parts, hidden1, vec, after=()):
    rows, width = hidden1.shape

    def finish(acc, ins, outs):
        def work(cut):
            outs[0][cut, :] = (ins[0][cut, :] + (acc[cut, :] + ins[1][5:6, :])).astype(LOW)

        row_loop(rows, work)

    return times_turned(
        activated,
        parts,
        list(range(parts.steps)),
        [hidden1, vec],
        [whole(hidden1.shape), whole(vec.shape)],
        [jax.ShapeDtypeStruct((rows, width), LOW)],
        [whole((rows, width))],
        finish,
        15,
        after,
    )[0]


def down_backward(down_grad, parts, upward, after=()):
    rows, block = down_grad.shape[0], parts.block
    total_columns = parts.steps * block

    def finish(y, ins, outs):
        total_ref = outs[1]
        total_ref[...] = jnp.zeros_like(total_ref)
        scratch = outs[2]
        scratch[...] = y

        def work(cut):
            u = ins[0][cut, :]
            sigma = jax.nn.sigmoid(GELU_SLOPE * u)
            g = (scratch[cut, :] * (sigma + GELU_SLOPE * u * sigma * (1.0 - sigma))).astype(LOW)
            outs[0][cut, :] = g
            total_ref[...] += jnp.sum(g.astype(F32), 0, keepdims=True)

        row_loop(rows, work)

    count = len(parts.arrays)

    def kernel(*refs):
        left_ref, w_refs, rest = refs[0], refs[1 : 1 + count], refs[1 + count :]

        def work(w):
            y = jnp.dot(left_ref[...], w, preferred_element_type=F32)
            finish(y, rest[:1], rest[1:])

        parts.each(w_refs, work)

    spec = pl.BlockSpec((rows, block), lambda j: (0, j))
    return call(
        kernel,
        (parts.steps,),
        [whole(down_grad.shape)] + parts.specs + [spec],
        [spec, pl.BlockSpec((1, block), lambda j: (0, j))],
        [
            jax.ShapeDtypeStruct((rows, total_columns), LOW),
            jax.ShapeDtypeStruct((1, total_columns), F32),
        ],
        scratch=[pltpu.VMEM((rows, block), F32)],
        us=0.1,
        after=after,
    )(down_grad, *parts.arrays, upward)


def up_backward(up_grad, parts, hidden1, cot_low, token_weight, vec, after=()):
    rows, width = hidden1.shape

    def finish(acc, ins, outs):
        hidden_ref, cot_ref, weight_ref, vec_ref = ins
        grad_ref, branch_ref, sums_ref = outs
        sums_ref[...] = jnp.zeros_like(sums_ref)

        def work(cut):
            e = acc[cut, :]
            normed, inverse = norm_parts(hidden_ref[cut, :])
            grad_y = cot_ref[cut, :].astype(F32) * weight_ref[cut, :]
            grad = grad_y + norm_back(e, normed, inverse, vec_ref[3:4, :])
            branch = grad.astype(LOW)
            grad_ref[cut, :] = grad
            branch_ref[cut, :] = branch
            sums_ref[0:1, :] += jnp.sum(e * normed, 0, keepdims=True)
            sums_ref[1:2, :] += jnp.sum(e, 0, keepdims=True)
            sums_ref[2:3, :] += jnp.sum(branch.astype(F32), 0, keepdims=True)
            sums_ref[3:4, :] += jnp.sum(grad_y.astype(LOW).astype(F32), 0, keepdims=True)

        row_loop(rows, work)

    return times_turned(
        up_grad,
        parts,
        list(range(parts.steps)),
        [hidden1, cot_low, token_weight, vec],
        [whole(hidden1.shape), whole(cot_low.shape), whole(token_weight.shape), whole(vec.shape)],
        [
            jax.ShapeDtypeStruct((rows, width), F32),
            jax.ShapeDtypeStruct((rows, width), LOW),
            jax.ShapeDtypeStruct((8, width), F32),
        ],
        [whole((rows, width)), whole((rows, width)), whole((8, width))],
        finish,
        0.1,
        after,
    )


def proj_backward(branch_grad, parts, after=()):
    rows, block = branch_grad.shape[0], parts.block

    def finish(y, ins, outs):
        outs[0][...] = y.astype(LOW)

    return times_weight(
        branch_grad,
        parts,
        None,
        [],
        [],
        [jax.ShapeDtypeStruct((rows, parts.steps * block), LOW)],
        [pl.BlockSpec((rows, block), lambda j: (0, j))],
        finish,
        250,
        after,
    )[0]


def qkv_backward(mixed_grad, parts, table, row_low, hidden1_grad, vec, after=()):
    rows, width = row_low.shape

    def finish(acc, ins, outs):
        row_ref, grad_ref, vec_ref = ins
        sums_ref = outs[1]
        sums_ref[...] = jnp.zeros_like(sums_ref)

        def work(cut):
            e = acc[cut, :]
            normed, inverse = norm_parts(row_ref[cut, :].astype(F32))
            grad = grad_ref[cut, :] + norm_back(e, normed, inverse, vec_ref[0:1, :])
            outs[0][cut, :] = grad.astype(LOW)
            sums_ref[0:1, :] += jnp.sum(e * normed, 0, keepdims=True)
            sums_ref[1:2, :] += jnp.sum(e, 0, keepdims=True)

        row_loop(rows, work)

    return times_turned(
        mixed_grad,
        parts,
        table,
        [row_low, hidden1_grad, vec],
        [whole(row_low.shape), whole(hidden1_grad.shape), whole(vec.shape)],
        [jax.ShapeDtypeStruct((rows, width), LOW), jax.ShapeDtypeStruct((8, width), F32)],
        [whole((rows, width)), whole((8, width))],
        finish,
        18,
        after,
    )


def grad_kernel(pairs, block, kind, half, came=None, part=None, us=10, after=()):
    rows, width = pairs[0][0].shape
    middle = width // 2
    low = middle // 2
    steps = len(kind)
    near = steps // 2
    count = len(pairs)

    def kernel(*refs):
        lefts, rights = refs[:count], refs[count : 2 * count]
        rest = refs[2 * count :]
        j = pl.program_id(0)

        for k in range(count):
            hits = [s for s in range(steps) if kind[s][0] == k]
            hit = j == hits[0]
            for s in hits[1:]:
                hit = hit | (j == s)

            @pl.when(hit)
            def _(k=k):
                right = rights[k][...]
                if came is None:
                    rest[0][...] = outer(lefts[k][...], right).astype(LOW)
                    return
                came_ref, out0, out1, out2 = rest[:4]
                y = outer(lefts[k][...], right)
                y0 = y[:low]
                y0 = (y0 + came_ref[:low, :].astype(F32)).astype(LOW)
                y1 = y[low:]
                y1 = (y1 + came_ref[low:, :].astype(F32)).astype(LOW)

                @pl.when(j < near)
                def _():
                    out0[...] = y0
                    out1[...] = y1

                @pl.when(j >= near)
                def _():
                    if part == "a":
                        out2[...] = y0
                        out1[...] = y1
                    else:
                        out2[:low, :] = y0
                        out2[low:, :] = y1

    right_specs = []
    for k in range(count):
        table, last = [], 0
        for s in range(steps):
            if kind[s][0] == k:
                last = kind[s][1]
            table.append(last)
        column = lookup(table)
        right_specs.append(pl.BlockSpec((rows, block), lambda j, column=column: (0, column(j))))

    def clipped(base, number, height):
        spec = pl.BlockSpec((height, block), lambda j: (0, jnp.clip(j - base, 0, number - 1)))
        return spec, jax.ShapeDtypeStruct((height, number * block), LOW)

    extra, extra_specs = [], []
    if came is None:
        outs = [clipped(0, steps, middle)]
    else:
        extra = [came[0]]
        column = lookup(came[1])
        extra_specs = [pl.BlockSpec((middle, block), lambda j: (0, column(j)))]
        if part == "a":
            both = pl.BlockSpec((low, block), lambda j: (j // near, j % near))
            outs = [
                clipped(0, near, low),
                (both, jax.ShapeDtypeStruct((middle, near * block), LOW)),
                clipped(near, near, low),
            ]
        else:
            outs = [clipped(0, near, low), clipped(0, near, low), clipped(near, near, middle)]
    return call(
        kernel,
        (steps,),
        [pl.BlockSpec((rows, middle), lambda j: (0, half)) for _ in pairs]
        + right_specs
        + extra_specs,
        [s for s, _ in outs],
        [s for _, s in outs],
        us=us,
        after=after,
    )(*[left for left, _ in pairs], *[right for _, right in pairs], *extra)


def add_second(other_a, own_b, from_y, from_x):
    rows, columns = other_a.shape

    def kernel(a_ref, b_ref, y_ref, x_ref, to_x, to_y):
        to_x[...] = (a_ref[...].astype(F32) + y_ref[...].astype(F32)).astype(LOW)
        to_y[...] = (b_ref[...].astype(F32) + x_ref[...].astype(F32)).astype(LOW)

    shape = jax.ShapeDtypeStruct((rows, columns), LOW)
    block = columns // 2
    spec = pl.BlockSpec((rows, block), lambda j: (0, j))
    later = pl.BlockSpec((rows, block), lambda j: (1, j))
    return call(
        kernel,
        (2,),
        [spec, spec, later, later],
        [spec, spec],
        [shape, shape],
    )(other_a, own_b, from_y, from_x)


def add_ring(own_a, own_b, from_y, from_x, second_x, second_y, came, place, rows, kind):
    half = own_a.shape[1]
    columns = 2 * half

    def kernel(*refs):
        own_a, own_b, y, x, x2, y2 = refs[:6]
        out = refs[-1]
        a = own_a[...].astype(F32) + y[...].astype(F32) + x2[...].astype(F32)
        b = own_b[...].astype(F32) + x[...].astype(F32) + y2[...].astype(F32)
        if came is not None:
            a = a + refs[6][:, :half].astype(F32)
            b = b + refs[6][:, half:].astype(F32)
        out[:, :half] = a.astype(kind)
        out[:, half:] = b.astype(kind)

    side = pl.BlockSpec((rows, half), lambda j: (place, 0))
    extra = [] if came is None else [came]
    return call(
        kernel,
        (1,),
        [side] * 6
        + [whole(v.shape) for v in extra],
        whole((rows, columns)),
        jax.ShapeDtypeStruct((rows, columns), kind),
    )(own_a, own_b, from_y, from_x, second_x, second_y, *extra)


def cut_far(side, across, near, after=()):
    rows, columns = side.shape
    far, at = [], 0
    for start, stop in near:
        if start > at:
            far.append((at, start))
        at = stop
    if at < columns:
        far.append((at, columns))

    def kernel(a, b, out_a, out_b):
        for source, out, ranges in ((a, out_a, near), (b, out_b, far)):
            at = 0
            for start, stop in ranges:
                out[:, at : at + stop - start] = source[:, start:stop]
                at += stop - start

    widths = [sum(stop - start for start, stop in ranges) for ranges in (near, far)]
    return call(
        kernel,
        (1,),
        [whole(side.shape)] * 2,
        [whole((rows, w)) for w in widths],
        [jax.ShapeDtypeStruct((rows, w), side.dtype) for w in widths],
        after=after,
    )(side, across)


def pack_columns(values, after=()):
    rows = values[0].shape[0]
    columns = sum(v.shape[1] for v in values)

    def kernel(*refs):
        at = 0
        for ref in refs[:-1]:
            n = ref.shape[1]
            refs[-1][:, at : at + n] = ref[...].astype(LOW)
            at += n

    return call(
        kernel,
        (1,),
        [whole(v.shape) for v in values],
        whole((rows, columns)),
        jax.ShapeDtypeStruct((rows, columns), LOW),
        after=after,
    )(*values)


def hold(*values, after=()):
    def kernel(*refs):
        total = refs[0][...]
        for ref in refs[1:-1]:
            total = total + ref[...]
        refs[-1][...] = total

    shape = values[0].shape
    return call(
        kernel,
        (1,),
        [whole(shape)] * len(values),
        whole(shape),
        jax.ShapeDtypeStruct(shape, values[0].dtype),
        us=1,
        after=after,
    )(*values)


def enter_input(mine, came, shuffle, vec):
    half, width = mine.shape
    rows = 2 * half

    def kernel(mine_ref, came_ref, s_ref, vec_ref, row_ref, first_ref):
        row_ref[:half, :] = jnp.dot(
            mine_ref[...], s_ref[...], preferred_element_type=F32
        ).astype(LOW)
        row_ref[half:, :] = jnp.dot(
            came_ref[0], s_ref[...], preferred_element_type=F32
        ).astype(LOW)
        normed, _ = norm_parts(row_ref[...].astype(F32))
        first_ref[...] = (normed * vec_ref[0:1, :] + vec_ref[1:2, :]).astype(LOW)

    shape = jax.ShapeDtypeStruct((rows, width), LOW)
    return call(
        kernel,
        (1,),
        [
            whole(mine.shape),
            pl.BlockSpec((1, half, width), lambda j: (0, 0, 0)),
            whole(shuffle.shape),
            whole(vec.shape),
        ],
        [whole((rows, width))] * 2,
        [shape, shape],
        us=7,
    )(mine, came, shuffle, vec)


def enter_cotangent(mine, came, shuffle, token_weight):
    half, width = mine.shape
    rows = 2 * half

    def kernel(mine_ref, came_ref, s_ref, weight_ref, row_ref, grad_ref):
        for k, part in enumerate((mine_ref[...], came_ref[0])):
            cut = slice(k * half, (k + 1) * half)
            y = jnp.dot(part, s_ref[...], preferred_element_type=F32)
            row_ref[cut, :] = y.astype(LOW)
            grad_ref[cut, :] = (y * weight_ref[cut, :]).astype(LOW)

    shape = jax.ShapeDtypeStruct((rows, width), LOW)
    return call(
        kernel,
        (1,),
        [
            whole(mine.shape),
            pl.BlockSpec((1, half, width), lambda j: (1, 0, 0)),
            whole(shuffle.shape),
            whole(token_weight.shape),
        ],
        [whole((rows, width))] * 2,
        [shape, shape],
        us=7,
    )(mine, came, shuffle, token_weight)


def place_halves(mine, theirs, slot, after=()):
    shape = (2, 1, *mine.shape)

    def kernel(slot_ref, mine_ref, their_ref, out_ref):
        for k in range(2):

            @pl.when(slot_ref[0] == k)
            def _(k=k):
                out_ref[k, 0] = mine_ref[...]
                out_ref[1 - k, 0] = their_ref[...]

    return call(
        kernel,
        (1,),
        [pl.BlockSpec(memory_space=pltpu.SMEM), whole(mine.shape), whole(theirs.shape)],
        whole(shape),
        jax.ShapeDtypeStruct(shape, mine.dtype),
        after=after,
    )(slot.reshape(1), mine, theirs)


def unshuffle(values, shuffle):
    rows, width = values.shape
    half = rows // 2

    def kernel(in_ref, s_ref, first, second):
        y = lax.dot_general(
            in_ref[...], s_ref[...], (((1,), (1,)), ((), ())), preferred_element_type=F32
        ).astype(LOW)
        first[...] = y[:half]
        second[...] = y[half:]

    shape = jax.ShapeDtypeStruct((half, width), LOW)
    return call(
        kernel,
        (1,),
        [whole(values.shape), whole(shuffle.shape)],
        [whole((half, width))] * 2,
        [shape, shape],
        us=0.1,
    )(values, shuffle)


def lamb_row(index, master_sq, update_sq):
    lane = lax.broadcasted_iota(jnp.int32, (1, 128), 1)
    row = jnp.where(lane == index, master_sq, 0.0)
    return row + jnp.where(lane == 7 + index, update_sq, 0.0)


def lamb_first(items, grad, factor, rows=()):
    count = len(items)

    def kernel(*refs):
        p_refs, m_refs = refs[:count], refs[count : 2 * count]
        g_ref = refs[2 * count]
        row_refs = refs[2 * count + 1 : 2 * count + 1 + len(rows)]
        outs = refs[2 * count + 1 + len(rows) :]
        row = jnp.zeros((1, 128), F32)
        for ref in row_refs:
            row = row + ref[...]
        for n, (place, master, _, at) in enumerate(items):
            width = master.shape[-1]
            for k in range(1 if master.ndim == 2 else master.shape[0]):
                cut = () if master.ndim == 2 else (k,)
                g = g_ref[:, at + k * width : at + (k + 1) * width] * factor
                p = p_refs[n][(*cut, ...)]
                old = (m_refs[n][(0, *cut, ...)], m_refs[n][(1, *cut, ...)])
                first, second, update = lamb_parts(p, old, g)
                outs[n][(0, *cut, ...)] = first
                outs[n][(1, *cut, ...)] = second
                outs[count + n][(*cut, ...)] = update
                row = row + lamb_row(place, jnp.sum(p * p), jnp.sum(update * update))
        outs[2 * count][...] = row

    operands = [*[i[1] for i in items], *[i[2] for i in items], grad, *rows]
    shapes = [i[2].shape for i in items] + [i[1].shape for i in items] + [(1, 128)]
    return call(
        kernel,
        (1,),
        [whole(v.shape) for v in operands],
        [whole(v) for v in shapes],
        [jax.ShapeDtypeStruct(v, F32) for v in shapes],
        us=4,
    )(*operands)


def lamb_small(masters, moments, grads, shares, factor):
    count = len(masters)

    def kernel(*refs):
        p_refs, m_refs, g_refs = refs[:count], refs[count : 2 * count], refs[2 * count : 3 * count]
        share_ref = refs[3 * count]
        outs = refs[3 * count + 1 :]
        row = jnp.zeros((1, 128), F32)
        for k in range(count):
            p = p_refs[k][...]
            if len(m_refs[k].shape) == 2:
                old = (m_refs[k][0:1, :], m_refs[k][1:2, :])
            else:
                old = (m_refs[k][:, 0, :], m_refs[k][:, 1, :])
            first, second, update = lamb_parts(p, old, g_refs[k][...] * factor)
            if len(m_refs[k].shape) == 2:
                outs[k][0:1, :] = first
                outs[k][1:2, :] = second
            else:
                outs[k][:, 0, :] = first
                outs[k][:, 1, :] = second
            outs[count + k][...] = update
            row = row + lamb_row(4 + k, jnp.sum(p * p), jnp.sum(update * update))
        outs[2 * count][...] = row * share_ref[...]

    operands = [*masters, *moments, *grads, shares]
    shapes = [v.shape for v in (*moments, *masters)] + [(1, 128)]
    return call(
        kernel,
        (1,),
        [whole(v.shape) for v in operands],
        [whole(v) for v in shapes],
        [jax.ShapeDtypeStruct(v, F32) for v in shapes],
    )(*operands)


def lamb_last(masters, updates, row, copies):
    count = len(masters)

    def kernel(*refs):
        p_refs, u_refs, row_ref = refs[:count], refs[count : 2 * count], refs[2 * count]
        outs = refs[2 * count + 1 :]
        norms, trust_ref = outs[count + copies :]
        master_sq, update_sq = row_ref[:, :count], row_ref[:, count : 2 * count]
        trust = jnp.sqrt(master_sq) / jnp.sqrt(update_sq + 1e-12)
        norms[0:1, :] = jnp.sqrt(master_sq)
        norms[1:2, :] = jnp.sqrt(update_sq)
        trust_ref[...] = trust
        for k in range(count):
            for c in range(1 if len(p_refs[k].shape) == 2 else p_refs[k].shape[0]):
                cut = (...,) if len(p_refs[k].shape) == 2 else (c, ...)
                new = p_refs[k][cut] - LEARN_RATE * trust[:, k : k + 1] * u_refs[k][cut]
                outs[k][cut] = new
                if k < copies:
                    outs[count + k][cut] = new.astype(LOW)

    shapes = [jax.ShapeDtypeStruct(v.shape, F32) for v in masters]
    shapes += [jax.ShapeDtypeStruct(v.shape, LOW) for v in masters[:copies]]
    shapes += [jax.ShapeDtypeStruct((2, count), F32), jax.ShapeDtypeStruct((1, count), F32)]
    operands = [*masters, *updates, row]
    return call(
        kernel,
        (1,),
        [whole(v.shape) for v in operands],
        [whole(v.shape) for v in shapes],
        shapes,
        us=8,
    )(*operands)


def stack_early(shard, side, across, far, after=()):
    rows, columns = shard.shape

    def kernel(a, b, c, d, out):
        out[:rows, :columns] = a[...]
        out[:rows, columns:] = b[...]
        out[rows:, :columns] = c[...]
        out[rows:, columns:] = d[...]

    return call(
        kernel,
        (1,),
        [whole(shard.shape)] * 4,
        whole((2 * rows, 2 * columns)),
        jax.ShapeDtypeStruct((2 * rows, 2 * columns), shard.dtype),
        after=after,
    )(shard, side, across, far)


def stack_rows(pieces, after=()):
    rows, columns = pieces[0].shape
    count = len(pieces)
    block = columns // (columns // 640)

    def kernel(*refs):
        for k in range(count):
            refs[-1][k * rows : (k + 1) * rows, :] = refs[k][...]

    return call(
        kernel,
        (columns // block,),
        [pl.BlockSpec((rows, block), lambda j: (0, j))] * count,
        pl.BlockSpec((count * rows, block), lambda j: (0, j)),
        jax.ShapeDtypeStruct((count * rows, columns), pieces[0].dtype),
        after=after,
    )(*pieces)


def turn_pairs(v, heads_lanes):
    middle = HD // 2
    lanes = lax.broadcasted_iota(jnp.int32, v.shape, 1)
    early = lanes % HD < middle
    width = v.shape[1]
    return jnp.where(early, -pltpu.roll(v, width - middle, 1), pltpu.roll(v, middle, 1))


def head_cut(h):
    return slice(h * HD, (h + 1) * HD)


def attention_forward(mixed, cosine, sine, key_code, query_code, groups, after=()):
    rows, columns = mixed.shape
    lanes = columns // (3 * groups)
    heads = lanes // HD
    scale = HD ** (-0.5)

    def kernel(mixed_ref, cos_ref, sin_ref, key_ref, query_ref, qkv_ref, att_ref, lse_ref, out_t):
        cos, sin = cos_ref[...], sin_ref[...]
        for part in range(2):
            cut = slice(part * lanes, (part + 1) * lanes)
            v = mixed_ref[:, cut]
            qkv_ref[:, cut] = (v * cos + turn_pairs(v, lanes) * sin).astype(LOW)
        qkv_ref[:, 2 * lanes :] = mixed_ref[:, 2 * lanes :].astype(LOW)
        query_t = qkv_ref[:, :lanes].T
        keys = qkv_ref[:, lanes : 2 * lanes]
        value_t = qkv_ref[:, 2 * lanes :].T
        allowed = key_ref[...] == query_ref[...]
        for h in range(heads):
            cut = head_cut(h)
            logits = jnp.dot(keys[:, cut], query_t[cut, :], preferred_element_type=F32)
            logits = jnp.where(allowed, logits * scale, NEGATIVE)
            top = jnp.max(logits, 0, keepdims=True)
            exponent = jnp.exp(logits - top)
            total_ = jnp.sum(exponent, 0, keepdims=True)
            prob = (exponent / total_).astype(LOW)
            out_t[cut, :] = jnp.dot(value_t[cut, :], prob, preferred_element_type=F32)
            lse_ref[0, h : h + 1, :] = top + jnp.log(total_)
        att_ref[...] = out_t[...].T.astype(LOW)

    return call(
        kernel,
        (groups,),
        [
            pl.BlockSpec((rows, 3 * lanes), lambda g: (0, g)),
            whole(cosine.shape),
            whole(sine.shape),
            whole(key_code.shape),
            whole(query_code.shape),
        ],
        [
            pl.BlockSpec((rows, 3 * lanes), lambda g: (0, g)),
            pl.BlockSpec((rows, lanes), lambda g: (0, g)),
            pl.BlockSpec((1, heads, rows), lambda g: (g, 0, 0)),
        ],
        [
            jax.ShapeDtypeStruct((rows, columns), LOW),
            jax.ShapeDtypeStruct((rows, groups * lanes), LOW),
            jax.ShapeDtypeStruct((groups, heads, rows), F32),
        ],
        scratch=[pltpu.VMEM((lanes, rows), F32)],
        us=19.6,
        after=after,
    )(mixed, cosine, sine, key_code, query_code)


def attention_backward(qkv, lse, attn_grad, cosine, sine, key_code, query_code, groups, after=()):
    rows, columns = qkv.shape
    lanes = columns // (3 * groups)
    heads = lanes // HD
    scale = HD ** (-0.5)

    def kernel(
        qkv_ref, lse_ref, grad_ref, cos_ref, sin_ref, key_ref, query_ref, out_ref, sum_ref, q_t, k_n, v_n
    ):
        query_t = qkv_ref[:, :lanes].T
        key_t = qkv_ref[:, lanes : 2 * lanes].T
        grad_t = grad_ref[...].T
        queries = qkv_ref[:, :lanes]
        keys = qkv_ref[:, lanes : 2 * lanes]
        values = qkv_ref[:, 2 * lanes :]
        grads = grad_ref[...]
        allowed = key_ref[...] == query_ref[...]
        for h in range(heads):
            cut = head_cut(h)
            logits = jnp.dot(keys[:, cut], query_t[cut, :], preferred_element_type=F32)
            logits = jnp.where(allowed, logits * scale, NEGATIVE)
            prob = jnp.exp(logits - lse_ref[0, h : h + 1, :])
            prob_grad = jnp.dot(values[:, cut], grad_t[cut, :], preferred_element_type=F32)
            inner = jnp.sum(prob * prob_grad, 0, keepdims=True)
            score_grad = (scale * prob * (prob_grad - inner)).astype(LOW)
            q_t[cut, :] = jnp.dot(key_t[cut, :], score_grad, preferred_element_type=F32)
            k_n[:, cut] = jnp.dot(score_grad, queries[:, cut], preferred_element_type=F32)
            v_n[:, cut] = jnp.dot(prob.astype(LOW), grads[:, cut], preferred_element_type=F32)
        cos, sin = cos_ref[...], sin_ref[...]
        for part, w in enumerate((q_t[...].T, k_n[...], v_n[...])):
            cut = slice(part * lanes, (part + 1) * lanes)
            if part < 2:
                w = w * cos - turn_pairs(w, lanes) * sin
            w = w.astype(LOW)
            out_ref[:, cut] = w
            sum_ref[:, cut] = jnp.sum(w.astype(F32), 0, keepdims=True)

    return call(
        kernel,
        (groups,),
        [
            pl.BlockSpec((rows, 3 * lanes), lambda g: (0, g)),
            pl.BlockSpec((1, heads, rows), lambda g: (g, 0, 0)),
            pl.BlockSpec((rows, lanes), lambda g: (0, g)),
            whole(cosine.shape),
            whole(sine.shape),
            whole(key_code.shape),
            whole(query_code.shape),
        ],
        [
            pl.BlockSpec((rows, 3 * lanes), lambda g: (0, g)),
            pl.BlockSpec((1, 3 * lanes), lambda g: (0, g)),
        ],
        [
            jax.ShapeDtypeStruct((rows, columns), LOW),
            jax.ShapeDtypeStruct((1, columns), F32),
        ],
        scratch=[
            pltpu.VMEM((lanes, rows), F32),
            pltpu.VMEM((rows, lanes), F32),
            pltpu.VMEM((rows, lanes), F32),
        ],
        us=27.3,
        after=after,
    )(qkv, lse, attn_grad, cosine, sine, key_code, query_code)
class Lanes:
    def __init__(self, dp):
        self.dp = dp
        self.ring = dp // 4

    def over_x(self, v):
        return lax.ppermute(v, "tensor", [(0, 1), (1, 0)])

    def over_core(self, v):
        return lax.ppermute(v, "dp", [(i, i ^ 1) for i in range(self.dp)])

    def over_y(self, v):
        return lax.ppermute(v, "dp", [(i, i ^ 2) for i in range(self.dp)])

    def down_z(self, v):
        return lax.ppermute(v, "dp", [(i, (i - 4) % self.dp) for i in range(self.dp)])

    def up_z(self, v):
        return lax.ppermute(v, "dp", [(i, (i + 4) % self.dp) for i in range(self.dp)])

    def exchange(self, v, bit):
        return lax.ppermute(v, "dp", [(i, i ^ bit) for i in range(self.dp)])

    def order(self):
        i = lax.axis_index("dp")
        z, y, c = i // 4, (i // 2) % 2, i % 2
        blocks = []
        for dc in range(2):
            for dy in range(2):
                for dz in range(self.ring):
                    blocks.append(((z + dz) % self.ring) * 4 + (y ^ dy) * 2 + (c ^ dc))
        return jnp.stack(blocks)

    def ring_down(self, v):
        held = [v]
        for _ in range(self.ring - 1):
            held.append(self.down_z(held[-1]))
        return held

    def far(self, side, across, near, after=()):
        a, b = cut_far(side, across, near, after)
        return self.over_y(a), self.over_x(b)

    def both_cores(self, values):
        return [(v, self.over_core(v)) for v in values]

    def stacked(self, pairs):
        rows = pairs[0][0].shape[0] // 2
        cuts = [
            (dc * self.ring + dz, dy * rows, rows)
            for dc in range(2)
            for dy in range(2)
            for dz in range(self.ring)
        ]
        return Stacked([p[0] for p in pairs] + [p[1] for p in pairs], cuts)


class Gathered:
    def __init__(self, own, other, far=None, near=()):
        self.own, self.other, self.far, self.near = own, other, far, near

    def pieces(self, column):
        if self.far is None:
            return [(v, column) for v in self.other]
        side, side_core = self.other
        place, spent, before = 1, column, 0
        for start, stop in self.near:
            if start <= column < stop:
                place, spent = 0, before + column - start
            before += stop - start
            if place and stop <= column:
                spent -= stop - start
        a, a_core = self.far[place]
        return [(side, column), (a, spent), (side_core, column), (a_core, spent)]

    def parts(self, block, first, count):
        sets = [([(v, first) for v in self.own], None, count)]
        last = None
        for b in range(first, first + count):
            here = [(v, c // block) for v, c in self.pieces(b * block)]
            if last is not None and all(
                v is w and c == d + sets[-1][2] for (v, c), (w, d) in zip(here, last)
            ):
                sets[-1] = (last, None, sets[-1][2] + 1)
            else:
                last = here
                sets.append((here, None, 1))
        return Parts(sets, block)


class Stacked:
    def __init__(self, pieces, cuts):
        self.pieces, self.cuts = pieces, cuts

    def parts(self, block):
        count = self.pieces[0].shape[1] // block
        return Parts([([(v, 0) for v in self.pieces], self.cuts, count)], block)


def butterfly(value, dp):
    if dp & (dp - 1):
        return lax.psum(value, ("dp", "tensor"))
    value = value + lax.ppermute(value, "tensor", [(0, 1), (1, 0)])
    bit = 1
    while bit < dp:
        value = value + lax.ppermute(value, "dp", [(i, i ^ bit) for i in range(dp)])
        bit *= 2
    return value


def body(
    block_input,
    out_cotangent,
    picture_ids,
    patch_positions,
    picture_lengths,
    pad_mask,
    qkv_weight,
    proj_weight,
    fc1_weight,
    fc2_weight,
    qkv_bias,
    fc1_bias,
    vectors,
    qkv_moments,
    proj_moments,
    fc1_moments,
    fc2_moments,
    qkv_bias_moments,
    fc1_bias_moments,
    vector_moments,
):
    ORDER.last = None
    dp = lax.axis_size("dp")
    relative = dp == 16
    lanes = Lanes(dp)
    slot = lax.axis_index("tensor")
    lead_dp = (lax.axis_index("dp") == 0).astype(F32)
    lead_all = lead_dp * (slot == 0).astype(F32)
    width = block_input.shape[3]
    rows_own = width // dp
    lane_columns = qkv_weight.shape[2]
    hidden = fc1_weight.shape[1]
    grad_factor = float(block_input.shape[0] * block_input.shape[1] * dp * LEN) ** (-0.5)

    biases = jnp.concatenate([qkv_bias.reshape(-1), fc1_bias]).reshape(-1, 128)

    def row_view(v):
        return jnp.swapaxes(v, -1, -2)

    qkv_view, qkv_moments_view = jnp.swapaxes(qkv_weight, 0, 1), jnp.swapaxes(qkv_moments, 1, 2)
    proj_view, proj_moments_view = row_view(proj_weight), row_view(proj_moments)
    fc2_view, fc2_moments_view = row_view(fc2_weight), row_view(fc2_moments)

    local_rows = block_input.shape[2]

    def half_of(both, place):
        return lax.dynamic_index_in_dim(both[:, 0], place, 0, keepdims=False)

    both_came = lanes.over_x(
        jnp.stack([half_of(block_input, 1 - slot), half_of(out_cotangent, 1 - slot)])
    )
    input_mine, cot_mine = half_of(block_input, slot), half_of(out_cotangent, slot)

    shard_1 = jnp.concatenate([qkv_view[k].astype(LOW) for k in range(3)], 1)
    shard_3 = fc2_view.astype(LOW)
    half = hidden // 2
    if relative:
        ring_1 = lanes.ring_down(shard_1)
        side_3, across_3 = lanes.over_x(shard_3), lanes.over_y(shard_3)
        far_3 = lanes.over_y(side_3)
        shard_2 = pack_columns([fc1_weight, proj_view])
        ring_2 = [shard_2, lanes.down_z(shard_2)]
        held_1 = stack_rows(ring_1, after=[side_3, across_3, far_3, both_came])
        ring_2[1] = hold(ring_2[1])
        for _ in range(2):
            ring_2.append(lanes.down_z(ring_2[-1]))
    else:

        def plain(shard):
            held = lax.all_gather(shard, "dp", axis=0, tiled=True)
            return Gathered([held], [lanes.over_x(held)])

        shard_2 = jnp.concatenate([fc1_weight.astype(LOW), proj_view.astype(LOW)], 1)
        w1, w2, w3 = plain(shard_1), plain(shard_2), plain(shard_3)
        w_down = w3.parts(half, 0, 2)
    def pick(array, axis=0):
        return lax.dynamic_index_in_dim(array, slot, axis, keepdims=False)

    def turn(values):
        return jnp.roll(values, -slot * local_rows, axis=-1)

    ids_row = turn(pick(picture_ids[:, 0]))
    rows_at = turn(pick(patch_positions[0, :, 0]))
    cols_at = turn(pick(patch_positions[1, :, 0]))
    mask_row = turn(pick(pad_mask[:, 0]))
    length_row = pick(picture_lengths[:, 0])
    cosine, sine = rotary_tables(rows_at, cols_at)
    groups = 2
    heads = lane_columns // HD
    cosine, sine = jnp.tile(cosine, (1, heads)), jnp.tile(sine, (1, heads))
    key_code = jnp.where(mask_row == 1, ids_row, -1)[:, None]
    query_code = ids_row[None, :]
    slot_hit = (ids_row[:, None] == jnp.arange(SLOTS, dtype=jnp.int32)[None, :]).astype(F32)
    picture_size = jnp.sum(slot_hit * length_row.astype(F32)[None, :], -1)
    token_weight = (mask_row.astype(F32) * jnp.sqrt(LEN / picture_size))[:, None]

    if relative:
        order = lanes.order()
        column = (order[:, None] * rows_own + jnp.arange(rows_own)[None, :]).reshape(-1)
        shuffle = (jnp.arange(width)[:, None] == column[None, :]).astype(LOW)
        vec = lax.dot_general(
            vectors,
            shuffle.astype(F32),
            (((1,), (0,)), ((), ())),
            precision=lax.Precision.HIGHEST,
            preferred_element_type=F32,
        )
        core_held_1 = lanes.over_core(held_1)
        sides_1 = lanes.over_x(held_1), lanes.over_y(held_1)
        row_low, first_in = enter_input(input_mine, both_came, shuffle, vec)
        biases = hold(biases)
        near_1 = [(0, 2 * lane_columns)]
        fars_1 = lanes.far(*sides_1, near_1, after=[core_held_1])
        late_3 = [stack_early(shard_3, side_3, across_3, far_3, after=[ring_2[3]])]
        late_came = lanes.down_z(late_3[0])
        core_late = lanes.over_core(late_3[0])
        cores_1 = lanes.both_cores(sides_1)
        held_2 = stack_rows(ring_2, after=[*fars_1, cores_1[0][1], cores_1[1][1]])
        sides_2 = lanes.over_x(held_2), lanes.over_y(held_2)
        core_held_2 = lanes.over_core(held_2)
        w1 = Gathered(
            [held_1, sides_1[1], core_held_1, cores_1[1][1]],
            cores_1[0],
            lanes.both_cores(fars_1),
            near_1,
        )
    else:
        vec = vectors
        row_low = jnp.concatenate([input_mine, both_came[0]], 0)
        cot_low = jnp.concatenate([cot_mine, both_came[1]], 0)
        normed1, _ = norm_parts(row_low.astype(F32))
        first_in = (normed1 * vec[0] + vec[1]).astype(LOW)
        down_grad = (cot_low.astype(F32) * token_weight).astype(LOW)
    w_qkv = w1.parts(lane_columns, 0, 3)
    other_biases = lanes.over_x(biases).reshape(-1)
    biases = biases.reshape(-1)
    cut = qkv_bias.size
    bias_qkv = jnp.concatenate([biases[:cut], other_biases[:cut]])[None]
    bias_up = jnp.concatenate([biases[cut:], other_biases[cut:]])[None]

    def give_back(values_low):
        if relative:
            mine, theirs = unshuffle(values_low, shuffle)
        else:
            mine, theirs = values_low[:local_rows], values_low[local_rows:]
        return mine, lanes.over_x(theirs)

    wide_kind = [(0, j) for j in range(4)]
    first_kind = [(0, 0), (0, 1), (0, 2), (1, 0), (0, 3), (0, 4), (0, 5), (1, 1)]

    def send_grads(pairs, block, kind, us):
        (sent,) = grad_kernel(pairs, block, kind, 1, us=us)
        return lanes.over_core(sent)

    def wide_grads(pairs, came):
        a = grad_kernel(pairs, half, [(0, 0), (0, 2)], 0, (came, [0, 2]), "a", 7)
        from_y = lanes.over_y(a[1])
        b = grad_kernel(pairs, half, [(0, 1), (0, 3)], 0, (came, [1, 3]), "b", 7)
        return (a[0], b[0]), (a[2], b[1]), (from_y, lanes.over_x(b[2]))

    def send_second(kept, first):
        to_x, to_y = add_second(*kept, *first)
        return (*first, lanes.over_x(to_x), lanes.over_y(to_y))

    def ring_step(own, sides, came, place):
        kind = LOW if place else F32
        total = add_ring(*own, *sides, came, place, rows_own, kind)
        return lanes.up_z(total) if place else total

    def plain_grads(pairs, block, kind):
        whole_grad = jnp.concatenate(
            [
                outer(pairs[p][0], pairs[p][1][:, c * block : (c + 1) * block])
                for p, c in kind
            ],
            1,
        )
        both = whole_grad[:, :hidden] + lanes.over_x(whole_grad[:, hidden:])
        return lax.psum_scatter(both, "dp", scatter_dimension=0, tiled=True)

    qkv_columns = 3 * lane_columns

    def small_sums(sums_1, sums_2, sum_qkv, sum_up):
        terms = jnp.concatenate([sums_1[0:2], sums_2[2:3], sums_2[0:2], sums_2[3:4]], 0)
        if relative:
            terms = lax.dot_general(
                terms,
                shuffle.astype(F32),
                (((1,), (1,)), ((), ())),
                precision=lax.Precision.HIGHEST,
                preferred_element_type=F32,
            )
        own = jnp.concatenate([sum_qkv[0, :qkv_columns], sum_up[0, :hidden]])
        other = jnp.concatenate([sum_qkv[0, qkv_columns:], sum_up[0, hidden:]])
        first_half = slot == 0
        return jnp.concatenate(
            [
                jnp.where(first_half, own, other),
                jnp.where(first_half, other, own),
                terms.reshape(-1),
            ]
        ).reshape(-1, 128)

    mixed = qkv_forward(first_in, w_qkv, bias_qkv, list(range(6)))
    if relative:
        late_3.append(hold(late_came))
    before_attention = [core_held_2, core_late] if relative else []
    qkv, attended, lse = attention_forward(
        mixed, cosine, sine, key_code, query_code, groups, after=before_attention
    )
    if relative:
        late_3.append(lanes.down_z(late_3[1]))
        late_came = lanes.down_z(late_3[2])
        late_cores = [(late_3[0], core_late), *lanes.both_cores(late_3[1:])]
        before_far = [late_cores[1][1]]
        near_2 = [(0, half), (hidden, hidden + lane_columns)]
        fars_2 = lanes.far(*sides_2, near_2, after=before_far)
        cot_low, down_grad = enter_cotangent(cot_mine, both_came, shuffle, token_weight)
        hold(query_code, after=fars_2)
        cores_2 = lanes.both_cores(sides_2)
        w2 = Gathered(
            [held_2, sides_2[1], core_held_2, cores_2[1][1]],
            cores_2[0],
            lanes.both_cores(fars_2),
            near_2,
        )
    w_proj = w2.parts(lane_columns, hidden // lane_columns, 1)
    w_up = w2.parts(half, 0, 2)
    hidden1, second_in = proj_forward(attended, w_proj, row_low, vec)
    upward, activated = up_forward(second_in, w_up, bias_up)
    pair_3 = [(down_grad, activated)]
    if relative:
        came_3 = send_grads(pair_3, half, wide_kind, 60)
        late_cores += lanes.both_cores([hold(late_came)])
        w_down = lanes.stacked(late_cores).parts(half)
    result = down_forward(activated, w_down, hidden1, vec)

    if relative:
        own_3, later_3, first_3 = wide_grads(pair_3, came_3)
    up_grad, sum_up = down_backward(down_grad, w_down, upward)
    pair_2 = [(second_in, up_grad)]
    output_halves = give_back(result)
    if relative:
        came_2 = send_grads(pair_2, half, wide_kind, 0.1)
    hidden1_grad, branch_grad, sums_2 = up_backward(
        up_grad, w_up, hidden1, cot_low, token_weight, vec
    )
    if relative:
        sides_3 = send_second(later_3, first_3)
    attn_grad = proj_backward(branch_grad, w_proj)
    if relative:
        own_2, later_2, first_2 = wide_grads(pair_2, came_2)
        ring_3 = ring_step(own_3, sides_3, None, 3)
    block_output = place_halves(*output_halves, slot)
    mixed_grad, sum_qkv = attention_backward(
        qkv, lse, attn_grad, cosine, sine, key_code, query_code, groups
    )
    pair_q, pair_p = (first_in, mixed_grad), (branch_grad, attended)
    factor = grad_factor
    if relative:
        kind_a = [(0, 0), (0, 1), (0, 3), (0, 4)]
        kind_b = [(0, 2), (1, 0), (0, 5), (1, 1)]
        sides_2 = send_second(later_2, first_2)
        ring_3 = ring_step(own_3, sides_3, ring_3, 2)
        came_a = send_grads([pair_q], lane_columns, kind_a, 1)
        came_b = send_grads([pair_q, pair_p], lane_columns, kind_b, 1)
        part_a = grad_kernel([pair_q], lane_columns, kind_a, 0, (came_a, [0, 1, 2, 3]), "a", 8)
        first_y = lanes.over_y(part_a[1])
        ring_3 = ring_step(own_3, sides_3, ring_3, 1)
        ring_2 = ring_step(own_2, sides_2, None, 3)
        part_b = grad_kernel(
            [pair_q, pair_p], lane_columns, kind_b, 0, (came_b, [0, 1, 2, 3]), "b", 8
        )
        own_1, later_1 = (part_a[0], part_b[0]), (part_a[2], part_b[1])
        first_1 = first_y, lanes.over_x(part_b[2])
        grad_3 = ring_step(own_3, sides_3, ring_3, 0)
        lamb_3 = lamb_first([(3, fc2_view, fc2_moments_view, 0)], grad_3, factor)
    input_low, sums_1 = qkv_backward(
        mixed_grad, w_qkv, list(range(6)), row_low, hidden1_grad, vec
    )
    if relative:
        ring_2 = ring_step(own_2, sides_2, ring_2, 2)
        sides_1 = send_second(later_1, first_1)
        ring_2 = ring_step(own_2, sides_2, ring_2, 1)
        small = hold(small_sums(sums_1, sums_2, sum_qkv, sum_up))
        came = lanes.over_core(small)
        grad_2 = ring_step(own_2, sides_2, ring_2, 0)
        small = hold(small, came)
        came = lanes.exchange(small, 4)
    else:
        input_halves = give_back(input_low)
        small = small_sums(sums_1, sums_2, sum_qkv, sum_up)
        grad_3 = plain_grads(pair_3, half, wide_kind)
        lamb_3 = lamb_first([(3, fc2_view, fc2_moments_view, 0)], grad_3, factor)
        grad_2 = plain_grads(pair_2, half, wide_kind)
    lamb_2 = lamb_first([(2, fc1_weight, fc1_moments, 0)], grad_2, factor)
    if relative:
        small = hold(small, came)
        came = lanes.exchange(small, 8)
        ring_1 = ring_step(own_1, sides_1, None, 3)
        input_halves = give_back(input_low)
        small = hold(small, came)
        came = lanes.over_y(small)
        ring_1 = ring_step(own_1, sides_1, ring_1, 2)
        small = hold(small, came)
        came = lanes.over_x(small)
        ring_1 = ring_step(own_1, sides_1, ring_1, 1)
        small = hold(small, came)

    if not relative:
        small = butterfly(small, dp)
    small = small.reshape(-1)
    first_half = slot == 0
    size = qkv_columns + hidden
    bias_sum = jnp.where(first_half, small[:size], small[size : 2 * size])
    small_grads = [
        bias_sum[:qkv_columns].reshape(qkv_bias.shape),
        bias_sum[None, qkv_columns:],
        small[2 * size :].reshape(vectors.shape),
    ]
    small_masters = [qkv_bias, fc1_bias[None], vectors]
    lane = jnp.arange(128)
    is_bias = (lane == 4) | (lane == 5) | (lane == 11) | (lane == 12)
    shares = jnp.where(is_bias, lead_dp, lead_all)[None]
    *small_lamb, small_row = lamb_small(
        small_masters,
        [
            jnp.swapaxes(qkv_bias_moments, 0, 1),
            fc1_bias_moments,
            jnp.swapaxes(vector_moments, 0, 1),
        ],
        small_grads,
        shares,
        factor,
    )

    if relative:
        input_grad = place_halves(*input_halves, slot)
        grad_1 = ring_step(own_1, sides_1, ring_1, 0)
    else:
        input_grad = place_halves(*input_halves, slot)
        grad_1 = plain_grads([pair_q, pair_p], lane_columns, first_kind)
    q_moments, p_moments, q_update, p_update, row = lamb_first(
        [(0, qkv_view, qkv_moments_view, 0), (1, proj_view, proj_moments_view, qkv_columns)],
        grad_1,
        factor,
        [lamb_2[2], lamb_3[2], small_row],
    )
    row = butterfly(row, dp)
    last = lamb_last(
        [qkv_view, proj_view, fc1_weight, fc2_view, *small_masters],
        [q_update, p_update, lamb_2[1], lamb_3[1], *small_lamb[3:]],
        row,
        4,
    )
    new_params, copies, norms, trust = last[:7], last[7:11], last[11], last[12]
    new_weights, copies = [
        [jnp.swapaxes(v[0], 0, 1), row_view(v[1]), v[2], row_view(v[3])]
        for v in (new_params, copies)
    ]
    return (
        block_output,
        input_grad,
        *new_weights,
        new_params[4],
        new_params[5][0],
        new_params[6],
        jnp.swapaxes(q_moments, 1, 2),
        row_view(p_moments),
        lamb_2[0],
        row_view(lamb_3[0]),
        jnp.swapaxes(small_lamb[0], 0, 1),
        small_lamb[1],
        jnp.swapaxes(small_lamb[2], 0, 1),
        *copies,
        norms,
        trust[0],
    )


def solution(mesh):
    in_specs = (
        P(None, "dp", "tensor", None),
        P(None, "dp", "tensor", None),
        P(None, "dp", None),
        P(None, None, "dp", None),
        P(None, "dp", None),
        P(None, "dp", None),
        P("dp", None, "tensor"),
        P("tensor", "dp"),
        P("dp", "tensor"),
        P("tensor", "dp"),
        P(None, "tensor"),
        P("tensor"),
        P(),
        P(None, "dp", None, "tensor"),
        P(None, "tensor", "dp"),
        P(None, "dp", "tensor"),
        P(None, "tensor", "dp"),
        P(None, None, "tensor"),
        P(None, "tensor"),
        P(),
    )
    out_specs = (
        P(None, "dp", "tensor", None),
        P(None, "dp", "tensor", None),
        P("dp", None, "tensor"),
        P("tensor", "dp"),
        P("dp", "tensor"),
        P("tensor", "dp"),
        P(None, "tensor"),
        P("tensor"),
        P(),
        P(None, "dp", None, "tensor"),
        P(None, "tensor", "dp"),
        P(None, "dp", "tensor"),
        P(None, "tensor", "dp"),
        P(None, None, "tensor"),
        P(None, "tensor"),
        P(),
        P("dp", None, "tensor"),
        P("tensor", "dp"),
        P("dp", "tensor"),
        P("tensor", "dp"),
        P(),
        P(),
    )
    return jax.shard_map(body, mesh=mesh, in_specs=in_specs, out_specs=out_specs, check_vma=False)
```

```python
import math

import jax
import jax.numpy as jnp
from jax import lax
from jax.experimental import pallas as pl
from jax.experimental.pallas import tpu as pltpu
from jax.sharding import PartitionSpec as P

HD = 80
SLOTS = 4
LEN = 576


NEGATIVE = -1e30
EPS_NORM = 1e-06
EPS_ADAM = 1e-06
WEIGHT_DECAY = 0.01
LEARN_RATE = 0.5
GELU_SLOPE = 1.702
F32 = jnp.float32
LOW = jnp.bfloat16


def norm_parts(values):
    center = values - jnp.mean(values, -1, keepdims=True)
    inverse = lax.rsqrt(jnp.mean(center * center, -1, keepdims=True) + EPS_NORM)
    return (center * inverse, inverse)


def norm_back(out_grad, normed, inverse, gain):
    scaled = out_grad * gain
    return inverse * (
        scaled
        - jnp.mean(scaled, -1, keepdims=True)
        - normed * jnp.mean(scaled * normed, -1, keepdims=True)
    )


def rotary_tables(rows_at, cols_at):
    quarter = HD // 4
    frequency = 10000.0 ** (-jnp.arange(quarter, dtype=F32) / quarter)
    halves = jnp.concatenate(
        [
            rows_at.astype(F32)[:, None] * frequency,
            cols_at.astype(F32)[:, None] * frequency,
        ],
        -1,
    )
    angles = jnp.concatenate([halves, halves], -1)
    return (jnp.cos(angles), jnp.sin(angles))


def dot(left, right):
    return lax.dot_general(left, right, (((1,), (0,)), ((), ())), preferred_element_type=F32)


def dot_t(left, right):
    return lax.dot_general(left, right, (((1,), (1,)), ((), ())), preferred_element_type=F32)


def outer(left, right):
    return lax.dot_general(left, right, (((0,), (0,)), ((), ())), preferred_element_type=F32)


def lamb_parts(master, moments, gradient):
    first = 0.5 * moments[0] + 0.5 * gradient
    second = 0.5 * moments[1] + 0.5 * gradient * gradient
    update = first / (jnp.sqrt(second) + EPS_ADAM) + WEIGHT_DECAY * master
    return (first, second, update)


VMEM_MOST = 56 * 1024 * 1024
VMEM_SPARE = 6 * 1024 * 1024
COST = int(8 * 1.15e9)


class Order:
    def __init__(self):
        self.last = None


ORDER = Order()


def call(
    kernel, grid, in_specs, out_specs, out_shape, scratch=(), us=2.4, after=()
):
    if ORDER.last is not None:
        after = [*after, ORDER.last]
    count, extra = len(in_specs), len(after)
    shapes = out_shape if isinstance(out_shape, (list, tuple)) else [out_shape]
    outs = out_specs if isinstance(out_specs, (list, tuple)) else [out_specs]
    out_bytes = sum(
        2 * math.prod(o.block_shape) * v.dtype.itemsize for o, v in zip(outs, shapes)
    )
    scratch_bytes = sum(math.prod(v.shape) * v.dtype.itemsize for v in scratch)

    def room(operands):
        in_bytes = sum(
            2 * math.prod(i.block_shape) * v.dtype.itemsize
            for i, v in zip(in_specs, operands)
            if i.block_shape is not None
        )
        return min(VMEM_MOST, in_bytes + out_bytes + scratch_bytes + VMEM_SPARE)

    def ordered(*refs):
        kernel(*refs[:count], *refs[count + extra :])

    def run(*operands):
        return pl.pallas_call(
            ordered,
            grid=grid,
            in_specs=list(in_specs) + [pl.BlockSpec(memory_space=pl.ANY)] * extra,
            out_specs=out_specs,
            out_shape=out_shape,
            scratch_shapes=list(scratch),
            compiler_params=pltpu.CompilerParams(
                dimension_semantics=("arbitrary",) * len(grid), vmem_limit_bytes=room(operands)
            ),
            cost_estimate=pl.CostEstimate(
                flops=int(COST * us), bytes_accessed=0, transcendentals=0
            ),
        )(*operands, *after)

    def start(*operands):
        result = run(*operands)
        ORDER.last = result[0] if isinstance(result, (list, tuple)) else result
        return result

    return start


def whole(shape):
    return pl.BlockSpec(shape, lambda *_: (0,) * len(shape))


def lookup(table):
    def column(j):
        found = table[0]
        for k in range(1, len(table)):
            found = jnp.where(j == k, table[k], found)
        return found

    return column


class Parts:
    def __init__(self, sets, block):
        self.sets, self.block = sets, block
        self.steps = sum(s[2] for s in sets)
        self.width = sum(piece.shape[0] for piece, _ in sets[0][0])
        self.arrays, self.specs = [], []
        base = 0
        for pieces, _, count in sets:
            for piece, first in pieces:
                self.arrays.append(piece)
                self.specs.append(
                    pl.BlockSpec(
                        (piece.shape[0], block),
                        lambda j, first=first, base=base, count=count: (
                            0,
                            first + jnp.clip(j - base, 0, count - 1),
                        ),
                    )
                )
            base += count

    def each(self, refs, work):
        j = pl.program_id(0)
        base, at = 0, 0
        for pieces, cuts, count in self.sets:
            mine = refs[at : at + len(pieces)]

            @pl.when((j >= base) & (j < base + count))
            def _(mine=mine, cuts=cuts):
                if cuts is None:
                    values = [r[...] for r in mine]
                else:
                    values = [mine[p][r : r + n, :] for p, r, n in cuts]
                work(values[0] if len(values) == 1 else jnp.concatenate(values, 0))

            base += count
            at += len(pieces)


def row_loop(rows, work):
    work(pl.ds(0, rows))


def times_weight(left, parts, table, ins, in_specs, outs, out_specs, finish, us, after=()):
    count = len(parts.arrays)

    def kernel(*refs):
        left_ref, w_refs, rest = refs[0], refs[1 : 1 + count], refs[1 + count :]

        def work(w):
            y = jnp.dot(left_ref[...], w, preferred_element_type=F32)
            finish(y, rest[: len(ins)], rest[len(ins) :])

        parts.each(w_refs, work)

    return call(
        kernel,
        (parts.steps,),
        [whole(left.shape)] + parts.specs + in_specs,
        out_specs,
        outs,
        us=us,
        after=after,
    )(left, *parts.arrays, *ins)


def times_turned(left, parts, table, ins, in_specs, outs, out_specs, finish, us, after=()):
    count = len(parts.arrays)
    rows, width = left.shape[0], parts.width
    column = lookup(table)

    def kernel(*refs):
        left_ref, w_refs, rest = refs[0], refs[1 : 1 + count], refs[1 + count :]
        acc = rest[-1]
        rest = rest[:-1]

        def work(w):
            y = lax.dot_general(
                left_ref[...], w, (((1,), (1,)), ((), ())), preferred_element_type=F32
            )

            @pl.when(pl.program_id(0) == 0)
            def _():
                acc[...] = y

            @pl.when(pl.program_id(0) > 0)
            def _():
                acc[...] += y

        parts.each(w_refs, work)

        @pl.when(pl.program_id(0) == parts.steps - 1)
        def _():
            finish(acc, rest[: len(ins)], rest[len(ins) :])

    return call(
        kernel,
        (parts.steps,),
        [pl.BlockSpec((rows, parts.block), lambda j: (0, column(j)))] + parts.specs + in_specs,
        out_specs,
        outs,
        scratch=[pltpu.VMEM((rows, width), F32)],
        us=us,
        after=after,
    )(left, *parts.arrays, *ins)


def qkv_forward(first_in, parts, bias, table, after=()):
    column = lookup(table)
    block = parts.block

    def finish(y, ins, outs):
        outs[0][...] = y + ins[0][...]

    total_columns = parts.steps * block
    return times_weight(
        first_in,
        parts,
        table,
        [bias],
        [pl.BlockSpec((1, block), lambda j: (0, column(j)))],
        [jax.ShapeDtypeStruct((first_in.shape[0], total_columns), F32)],
        [pl.BlockSpec((first_in.shape[0], block), lambda j: (0, column(j)))],
        finish,
        14,
        after,
    )[0]


def proj_forward(attended, parts, row_low, vec, after=()):
    rows, width = row_low.shape

    def finish(acc, ins, outs):
        row_ref, vec_ref = ins
        hidden_ref, second_ref = outs

        def work(cut):
            hidden = row_ref[cut, :].astype(F32) + (acc[cut, :] + vec_ref[2:3, :])
            hidden_ref[cut, :] = hidden
            normed, _ = norm_parts(hidden)
            second_ref[cut, :] = (normed * vec_ref[3:4, :] + vec_ref[4:5, :]).astype(LOW)

        row_loop(rows, work)

    return times_turned(
        attended,
        parts,
        list(range(parts.steps)),
        [row_low, vec],
        [whole(row_low.shape), whole(vec.shape)],
        [jax.ShapeDtypeStruct((rows, width), F32), jax.ShapeDtypeStruct((rows, width), LOW)],
        [whole((rows, width))] * 2,
        finish,
        9.8,
        after,
    )


def up_forward(second_in, parts, bias, after=()):
    rows, block = second_in.shape[0], parts.block
    total_columns = parts.steps * block

    def finish(y, ins, outs):
        outs[0][...] = y + ins[0][...]

        def work(cut):
            u = outs[0][cut, :]
            outs[1][cut, :] = (u * jax.nn.sigmoid(GELU_SLOPE * u)).astype(LOW)

        row_loop(rows, work)

    spec = pl.BlockSpec((rows, block), lambda j: (0, j))
    return times_weight(
        second_in,
        parts,
        None,
        [bias],
        [pl.BlockSpec((1, block), lambda j: (0, j))],
        [
            jax.ShapeDtypeStruct((rows, total_columns), F32),
            jax.ShapeDtypeStruct((rows, total_columns), LOW),
        ],
        [spec, spec],
        finish,
        17.8,
        after,
    )


def down_forward(activated, parts, hidden1, vec, after=()):
    rows, width = hidden1.shape

    def finish(acc, ins, outs):
        def work(cut):
            outs[0][cut, :] = (ins[0][cut, :] + (acc[cut, :] + ins[1][5:6, :])).astype(LOW)

        row_loop(rows, work)

    return times_turned(
        activated,
        parts,
        list(range(parts.steps)),
        [hidden1, vec],
        [whole(hidden1.shape), whole(vec.shape)],
        [jax.ShapeDtypeStruct((rows, width), LOW)],
        [whole((rows, width))],
        finish,
        15,
        after,
    )[0]


def down_backward(down_grad, parts, upward, after=()):
    rows, block = down_grad.shape[0], parts.block
    total_columns = parts.steps * block

    def finish(y, ins, outs):
        total_ref = outs[1]
        total_ref[...] = jnp.zeros_like(total_ref)
        scratch = outs[2]
        scratch[...] = y

        def work(cut):
            u = ins[0][cut, :]
            sigma = jax.nn.sigmoid(GELU_SLOPE * u)
            g = (scratch[cut, :] * (sigma + GELU_SLOPE * u * sigma * (1.0 - sigma))).astype(LOW)
            outs[0][cut, :] = g
            total_ref[...] += jnp.sum(g.astype(F32), 0, keepdims=True)

        row_loop(rows, work)

    count = len(parts.arrays)

    def kernel(*refs):
        left_ref, w_refs, rest = refs[0], refs[1 : 1 + count], refs[1 + count :]

        def work(w):
            y = jnp.dot(left_ref[...], w, preferred_element_type=F32)
            finish(y, rest[:1], rest[1:])

        parts.each(w_refs, work)

    spec = pl.BlockSpec((rows, block), lambda j: (0, j))
    return call(
        kernel,
        (parts.steps,),
        [whole(down_grad.shape)] + parts.specs + [spec],
        [spec, pl.BlockSpec((1, block), lambda j: (0, j))],
        [
            jax.ShapeDtypeStruct((rows, total_columns), LOW),
            jax.ShapeDtypeStruct((1, total_columns), F32),
        ],
        scratch=[pltpu.VMEM((rows, block), F32)],
        us=0.1,
        after=after,
    )(down_grad, *parts.arrays, upward)


def up_backward(up_grad, parts, hidden1, cot_low, token_weight, vec, after=()):
    rows, width = hidden1.shape

    def finish(acc, ins, outs):
        hidden_ref, cot_ref, weight_ref, vec_ref = ins
        grad_ref, branch_ref, sums_ref = outs
        sums_ref[...] = jnp.zeros_like(sums_ref)

        def work(cut):
            e = acc[cut, :]
            normed, inverse = norm_parts(hidden_ref[cut, :])
            grad_y = cot_ref[cut, :].astype(F32) * weight_ref[cut, :]
            grad = grad_y + norm_back(e, normed, inverse, vec_ref[3:4, :])
            branch = grad.astype(LOW)
            grad_ref[cut, :] = grad
            branch_ref[cut, :] = branch
            sums_ref[0:1, :] += jnp.sum(e * normed, 0, keepdims=True)
            sums_ref[1:2, :] += jnp.sum(e, 0, keepdims=True)
            sums_ref[2:3, :] += jnp.sum(branch.astype(F32), 0, keepdims=True)
            sums_ref[3:4, :] += jnp.sum(grad_y.astype(LOW).astype(F32), 0, keepdims=True)

        row_loop(rows, work)

    return times_turned(
        up_grad,
        parts,
        list(range(parts.steps)),
        [hidden1, cot_low, token_weight, vec],
        [whole(hidden1.shape), whole(cot_low.shape), whole(token_weight.shape), whole(vec.shape)],
        [
            jax.ShapeDtypeStruct((rows, width), F32),
            jax.ShapeDtypeStruct((rows, width), LOW),
            jax.ShapeDtypeStruct((8, width), F32),
        ],
        [whole((rows, width)), whole((rows, width)), whole((8, width))],
        finish,
        0.1,
        after,
    )


def proj_backward(branch_grad, parts, after=()):
    rows, block = branch_grad.shape[0], parts.block

    def finish(y, ins, outs):
        outs[0][...] = y.astype(LOW)

    return times_weight(
        branch_grad,
        parts,
        None,
        [],
        [],
        [jax.ShapeDtypeStruct((rows, parts.steps * block), LOW)],
        [pl.BlockSpec((rows, block), lambda j: (0, j))],
        finish,
        250,
        after,
    )[0]


def qkv_backward(mixed_grad, parts, table, row_low, hidden1_grad, vec, after=()):
    rows, width = row_low.shape

    def finish(acc, ins, outs):
        row_ref, grad_ref, vec_ref = ins
        sums_ref = outs[1]
        sums_ref[...] = jnp.zeros_like(sums_ref)

        def work(cut):
            e = acc[cut, :]
            normed, inverse = norm_parts(row_ref[cut, :].astype(F32))
            grad = grad_ref[cut, :] + norm_back(e, normed, inverse, vec_ref[0:1, :])
            outs[0][cut, :] = grad.astype(LOW)
            sums_ref[0:1, :] += jnp.sum(e * normed, 0, keepdims=True)
            sums_ref[1:2, :] += jnp.sum(e, 0, keepdims=True)

        row_loop(rows, work)

    return times_turned(
        mixed_grad,
        parts,
        table,
        [row_low, hidden1_grad, vec],
        [whole(row_low.shape), whole(hidden1_grad.shape), whole(vec.shape)],
        [jax.ShapeDtypeStruct((rows, width), LOW), jax.ShapeDtypeStruct((8, width), F32)],
        [whole((rows, width)), whole((8, width))],
        finish,
        18,
        after,
    )


def grad_kernel(pairs, block, kind, half, came=None, part=None, us=10, after=()):
    rows, width = pairs[0][0].shape
    middle = width // 2
    low = middle // 2
    steps = len(kind)
    near = steps // 2
    count = len(pairs)

    def kernel(*refs):
        lefts, rights = refs[:count], refs[count : 2 * count]
        rest = refs[2 * count :]
        j = pl.program_id(0)

        for k in range(count):
            hits = [s for s in range(steps) if kind[s][0] == k]
            hit = j == hits[0]
            for s in hits[1:]:
                hit = hit | (j == s)

            @pl.when(hit)
            def _(k=k):
                right = rights[k][...]
                if came is None:
                    rest[0][...] = outer(lefts[k][...], right).astype(LOW)
                    return
                came_ref, out0, out1, out2 = rest[:4]
                y = outer(lefts[k][...], right)
                y0 = y[:low]
                y0 = (y0 + came_ref[:low, :].astype(F32)).astype(LOW)
                y1 = y[low:]
                y1 = (y1 + came_ref[low:, :].astype(F32)).astype(LOW)

                @pl.when(j < near)
                def _():
                    out0[...] = y0
                    out1[...] = y1

                @pl.when(j >= near)
                def _():
                    if part == "a":
                        out2[...] = y0
                        out1[...] = y1
                    else:
                        out2[:low, :] = y0
                        out2[low:, :] = y1

    right_specs = []
    for k in range(count):
        table, last = [], 0
        for s in range(steps):
            if kind[s][0] == k:
                last = kind[s][1]
            table.append(last)
        column = lookup(table)
        right_specs.append(pl.BlockSpec((rows, block), lambda j, column=column: (0, column(j))))

    def clipped(base, number, height):
        spec = pl.BlockSpec((height, block), lambda j: (0, jnp.clip(j - base, 0, number - 1)))
        return spec, jax.ShapeDtypeStruct((height, number * block), LOW)

    extra, extra_specs = [], []
    if came is None:
        outs = [clipped(0, steps, middle)]
    else:
        extra = [came[0]]
        column = lookup(came[1])
        extra_specs = [pl.BlockSpec((middle, block), lambda j: (0, column(j)))]
        if part == "a":
            both = pl.BlockSpec((low, block), lambda j: (j // near, j % near))
            outs = [
                clipped(0, near, low),
                (both, jax.ShapeDtypeStruct((middle, near * block), LOW)),
                clipped(near, near, low),
            ]
        else:
            outs = [clipped(0, near, low), clipped(0, near, low), clipped(near, near, middle)]
    return call(
        kernel,
        (steps,),
        [pl.BlockSpec((rows, middle), lambda j: (0, half)) for _ in pairs]
        + right_specs
        + extra_specs,
        [s for s, _ in outs],
        [s for _, s in outs],
        us=us,
        after=after,
    )(*[left for left, _ in pairs], *[right for _, right in pairs], *extra)


def add_second(other_a, own_b, from_y, from_x):
    rows, columns = other_a.shape

    def kernel(a_ref, b_ref, y_ref, x_ref, to_x, to_y):
        to_x[...] = (a_ref[...].astype(F32) + y_ref[...].astype(F32)).astype(LOW)
        to_y[...] = (b_ref[...].astype(F32) + x_ref[...].astype(F32)).astype(LOW)

    shape = jax.ShapeDtypeStruct((rows, columns), LOW)
    block = columns // 2
    spec = pl.BlockSpec((rows, block), lambda j: (0, j))
    later = pl.BlockSpec((rows, block), lambda j: (1, j))
    return call(
        kernel,
        (2,),
        [spec, spec, later, later],
        [spec, spec],
        [shape, shape],
    )(other_a, own_b, from_y, from_x)


def add_ring(own_a, own_b, from_y, from_x, second_x, second_y, came, place, rows, kind):
    half = own_a.shape[1]
    columns = 2 * half

    def kernel(*refs):
        own_a, own_b, y, x, x2, y2 = refs[:6]
        out = refs[-1]
        a = own_a[...].astype(F32) + y[...].astype(F32) + x2[...].astype(F32)
        b = own_b[...].astype(F32) + x[...].astype(F32) + y2[...].astype(F32)
        if came is not None:
            a = a + refs[6][:, :half].astype(F32)
            b = b + refs[6][:, half:].astype(F32)
        out[:, :half] = a.astype(kind)
        out[:, half:] = b.astype(kind)

    side = pl.BlockSpec((rows, half), lambda j: (place, 0))
    extra = [] if came is None else [came]
    return call(
        kernel,
        (1,),
        [side] * 6
        + [whole(v.shape) for v in extra],
        whole((rows, columns)),
        jax.ShapeDtypeStruct((rows, columns), kind),
    )(own_a, own_b, from_y, from_x, second_x, second_y, *extra)


def cut_far(side, across, near, after=()):
    rows, columns = side.shape
    far, at = [], 0
    for start, stop in near:
        if start > at:
            far.append((at, start))
        at = stop
    if at < columns:
        far.append((at, columns))

    def kernel(a, b, out_a, out_b):
        for source, out, ranges in ((a, out_a, near), (b, out_b, far)):
            at = 0
            for start, stop in ranges:
                out[:, at : at + stop - start] = source[:, start:stop]
                at += stop - start

    widths = [sum(stop - start for start, stop in ranges) for ranges in (near, far)]
    return call(
        kernel,
        (1,),
        [whole(side.shape)] * 2,
        [whole((rows, w)) for w in widths],
        [jax.ShapeDtypeStruct((rows, w), side.dtype) for w in widths],
        after=after,
    )(side, across)


def pack_columns(values, after=()):
    rows = values[0].shape[0]
    columns = sum(v.shape[1] for v in values)

    def kernel(*refs):
        at = 0
        for ref in refs[:-1]:
            n = ref.shape[1]
            refs[-1][:, at : at + n] = ref[...].astype(LOW)
            at += n

    return call(
        kernel,
        (1,),
        [whole(v.shape) for v in values],
        whole((rows, columns)),
        jax.ShapeDtypeStruct((rows, columns), LOW),
        after=after,
    )(*values)


def hold(*values, us=1, after=()):
    def kernel(*refs):
        total = refs[0][...]
        for ref in refs[1:-1]:
            total = total + ref[...]
        refs[-1][...] = total

    shape = values[0].shape
    return call(
        kernel,
        (1,),
        [whole(shape)] * len(values),
        whole(shape),
        jax.ShapeDtypeStruct(shape, values[0].dtype),
        us=us,
        after=after,
    )(*values)


def enter_input(mine, came, shuffle, vec):
    half, width = mine.shape
    rows = 2 * half

    def kernel(mine_ref, came_ref, s_ref, vec_ref, row_ref, first_ref):
        row_ref[:half, :] = jnp.dot(
            mine_ref[...], s_ref[...], preferred_element_type=F32
        ).astype(LOW)
        row_ref[half:, :] = jnp.dot(
            came_ref[0], s_ref[...], preferred_element_type=F32
        ).astype(LOW)
        normed, _ = norm_parts(row_ref[...].astype(F32))
        first_ref[...] = (normed * vec_ref[0:1, :] + vec_ref[1:2, :]).astype(LOW)

    shape = jax.ShapeDtypeStruct((rows, width), LOW)
    return call(
        kernel,
        (1,),
        [
            whole(mine.shape),
            pl.BlockSpec((1, half, width), lambda j: (0, 0, 0)),
            whole(shuffle.shape),
            whole(vec.shape),
        ],
        [whole((rows, width))] * 2,
        [shape, shape],
        us=7,
    )(mine, came, shuffle, vec)


def enter_cotangent(mine, came, shuffle, token_weight):
    half, width = mine.shape
    rows = 2 * half

    def kernel(mine_ref, came_ref, s_ref, weight_ref, row_ref, grad_ref):
        for k, part in enumerate((mine_ref[...], came_ref[0])):
            cut = slice(k * half, (k + 1) * half)
            y = jnp.dot(part, s_ref[...], preferred_element_type=F32)
            row_ref[cut, :] = y.astype(LOW)
            grad_ref[cut, :] = (y * weight_ref[cut, :]).astype(LOW)

    shape = jax.ShapeDtypeStruct((rows, width), LOW)
    return call(
        kernel,
        (1,),
        [
            whole(mine.shape),
            pl.BlockSpec((1, half, width), lambda j: (1, 0, 0)),
            whole(shuffle.shape),
            whole(token_weight.shape),
        ],
        [whole((rows, width))] * 2,
        [shape, shape],
        us=7,
    )(mine, came, shuffle, token_weight)


def place_halves(mine, theirs, slot, after=()):
    shape = (2, 1, *mine.shape)

    def kernel(slot_ref, mine_ref, their_ref, out_ref):
        for k in range(2):

            @pl.when(slot_ref[0] == k)
            def _(k=k):
                out_ref[k, 0] = mine_ref[...]
                out_ref[1 - k, 0] = their_ref[...]

    return call(
        kernel,
        (1,),
        [pl.BlockSpec(memory_space=pltpu.SMEM), whole(mine.shape), whole(theirs.shape)],
        whole(shape),
        jax.ShapeDtypeStruct(shape, mine.dtype),
        after=after,
    )(slot.reshape(1), mine, theirs)


def unshuffle(values, shuffle):
    rows, width = values.shape
    half = rows // 2

    def kernel(in_ref, s_ref, first, second):
        y = lax.dot_general(
            in_ref[...], s_ref[...], (((1,), (1,)), ((), ())), preferred_element_type=F32
        ).astype(LOW)
        first[...] = y[:half]
        second[...] = y[half:]

    shape = jax.ShapeDtypeStruct((half, width), LOW)
    return call(
        kernel,
        (1,),
        [whole(values.shape), whole(shuffle.shape)],
        [whole((half, width))] * 2,
        [shape, shape],
        us=0.1,
    )(values, shuffle)


def lamb_row(index, master_sq, update_sq):
    lane = lax.broadcasted_iota(jnp.int32, (1, 128), 1)
    row = jnp.where(lane == index, master_sq, 0.0)
    return row + jnp.where(lane == 7 + index, update_sq, 0.0)


def lamb_first(items, grad, factor, rows=()):
    count = len(items)

    def kernel(*refs):
        p_refs, m_refs = refs[:count], refs[count : 2 * count]
        g_ref = refs[2 * count]
        row_refs = refs[2 * count + 1 : 2 * count + 1 + len(rows)]
        outs = refs[2 * count + 1 + len(rows) :]
        row = jnp.zeros((1, 128), F32)
        for ref in row_refs:
            row = row + ref[...]
        for n, (place, master, _, at) in enumerate(items):
            width = master.shape[-1]
            for k in range(1 if master.ndim == 2 else master.shape[0]):
                cut = () if master.ndim == 2 else (k,)
                g = g_ref[:, at + k * width : at + (k + 1) * width] * factor
                p = p_refs[n][(*cut, ...)]
                old = (m_refs[n][(0, *cut, ...)], m_refs[n][(1, *cut, ...)])
                first, second, update = lamb_parts(p, old, g)
                outs[n][(0, *cut, ...)] = first
                outs[n][(1, *cut, ...)] = second
                outs[count + n][(*cut, ...)] = update
                row = row + lamb_row(place, jnp.sum(p * p), jnp.sum(update * update))
        outs[2 * count][...] = row

    operands = [*[i[1] for i in items], *[i[2] for i in items], grad, *rows]
    shapes = [i[2].shape for i in items] + [i[1].shape for i in items] + [(1, 128)]
    return call(
        kernel,
        (1,),
        [whole(v.shape) for v in operands],
        [whole(v) for v in shapes],
        [jax.ShapeDtypeStruct(v, F32) for v in shapes],
        us=4,
    )(*operands)


def lamb_small(masters, moments, grads, shares, factor):
    count = len(masters)

    def kernel(*refs):
        p_refs, m_refs, g_refs = refs[:count], refs[count : 2 * count], refs[2 * count : 3 * count]
        share_ref = refs[3 * count]
        outs = refs[3 * count + 1 :]
        row = jnp.zeros((1, 128), F32)
        for k in range(count):
            p = p_refs[k][...]
            if len(m_refs[k].shape) == 2:
                old = (m_refs[k][0:1, :], m_refs[k][1:2, :])
            else:
                old = (m_refs[k][:, 0, :], m_refs[k][:, 1, :])
            first, second, update = lamb_parts(p, old, g_refs[k][...] * factor)
            if len(m_refs[k].shape) == 2:
                outs[k][0:1, :] = first
                outs[k][1:2, :] = second
            else:
                outs[k][:, 0, :] = first
                outs[k][:, 1, :] = second
            outs[count + k][...] = update
            row = row + lamb_row(4 + k, jnp.sum(p * p), jnp.sum(update * update))
        outs[2 * count][...] = row * share_ref[...]

    operands = [*masters, *moments, *grads, shares]
    shapes = [v.shape for v in (*moments, *masters)] + [(1, 128)]
    return call(
        kernel,
        (1,),
        [whole(v.shape) for v in operands],
        [whole(v) for v in shapes],
        [jax.ShapeDtypeStruct(v, F32) for v in shapes],
    )(*operands)


def lamb_last(masters, updates, row, copies):
    count = len(masters)

    def kernel(*refs):
        p_refs, u_refs, row_ref = refs[:count], refs[count : 2 * count], refs[2 * count]
        outs = refs[2 * count + 1 :]
        norms, trust_ref = outs[count + copies :]
        master_sq, update_sq = row_ref[:, :count], row_ref[:, count : 2 * count]
        trust = jnp.sqrt(master_sq) / jnp.sqrt(update_sq + 1e-12)
        norms[0:1, :] = jnp.sqrt(master_sq)
        norms[1:2, :] = jnp.sqrt(update_sq)
        trust_ref[...] = trust
        for k in range(count):
            for c in range(1 if len(p_refs[k].shape) == 2 else p_refs[k].shape[0]):
                cut = (...,) if len(p_refs[k].shape) == 2 else (c, ...)
                new = p_refs[k][cut] - LEARN_RATE * trust[:, k : k + 1] * u_refs[k][cut]
                outs[k][cut] = new
                if k < copies:
                    outs[count + k][cut] = new.astype(LOW)

    shapes = [jax.ShapeDtypeStruct(v.shape, F32) for v in masters]
    shapes += [jax.ShapeDtypeStruct(v.shape, LOW) for v in masters[:copies]]
    shapes += [jax.ShapeDtypeStruct((2, count), F32), jax.ShapeDtypeStruct((1, count), F32)]
    operands = [*masters, *updates, row]
    return call(
        kernel,
        (1,),
        [whole(v.shape) for v in operands],
        [whole(v.shape) for v in shapes],
        shapes,
        us=8,
    )(*operands)


def stack_early(shard, side, across, far, after=()):
    rows, columns = shard.shape

    def kernel(a, b, c, d, out):
        out[:rows, :columns] = a[...]
        out[:rows, columns:] = b[...]
        out[rows:, :columns] = c[...]
        out[rows:, columns:] = d[...]

    return call(
        kernel,
        (1,),
        [whole(shard.shape)] * 4,
        whole((2 * rows, 2 * columns)),
        jax.ShapeDtypeStruct((2 * rows, 2 * columns), shard.dtype),
        after=after,
    )(shard, side, across, far)


def stack_rows(pieces, after=()):
    rows, columns = pieces[0].shape
    count = len(pieces)
    block = columns // (columns // 640)

    def kernel(*refs):
        for k in range(count):
            refs[-1][k * rows : (k + 1) * rows, :] = refs[k][...]

    return call(
        kernel,
        (columns // block,),
        [pl.BlockSpec((rows, block), lambda j: (0, j))] * count,
        pl.BlockSpec((count * rows, block), lambda j: (0, j)),
        jax.ShapeDtypeStruct((count * rows, columns), pieces[0].dtype),
        after=after,
    )(*pieces)


def turn_pairs(v, heads_lanes):
    middle = HD // 2
    lanes = lax.broadcasted_iota(jnp.int32, v.shape, 1)
    early = lanes % HD < middle
    width = v.shape[1]
    return jnp.where(early, -pltpu.roll(v, width - middle, 1), pltpu.roll(v, middle, 1))


def head_cut(h):
    return slice(h * HD, (h + 1) * HD)


def attention_forward(mixed, cosine, sine, key_code, query_code, groups, after=()):
    rows, columns = mixed.shape
    lanes = columns // (3 * groups)
    heads = lanes // HD
    scale = HD ** (-0.5)

    def kernel(mixed_ref, cos_ref, sin_ref, key_ref, query_ref, qkv_ref, att_ref, lse_ref, out_t):
        cos, sin = cos_ref[...], sin_ref[...]
        for part in range(2):
            cut = slice(part * lanes, (part + 1) * lanes)
            v = mixed_ref[:, cut]
            qkv_ref[:, cut] = (v * cos + turn_pairs(v, lanes) * sin).astype(LOW)
        qkv_ref[:, 2 * lanes :] = mixed_ref[:, 2 * lanes :].astype(LOW)
        query_t = qkv_ref[:, :lanes].T
        keys = qkv_ref[:, lanes : 2 * lanes]
        value_t = qkv_ref[:, 2 * lanes :].T
        allowed = key_ref[...] == query_ref[...]
        for h in range(heads):
            cut = head_cut(h)
            logits = jnp.dot(keys[:, cut], query_t[cut, :], preferred_element_type=F32)
            logits = jnp.where(allowed, logits * scale, NEGATIVE)
            top = jnp.max(logits, 0, keepdims=True)
            exponent = jnp.exp(logits - top)
            total_ = jnp.sum(exponent, 0, keepdims=True)
            prob = (exponent * (1.0 / total_)).astype(LOW)
            out_t[cut, :] = jnp.dot(value_t[cut, :], prob, preferred_element_type=F32)
            lse_ref[0, h : h + 1, :] = top + jnp.log(total_)
        att_ref[...] = out_t[...].T.astype(LOW)

    return call(
        kernel,
        (groups,),
        [
            pl.BlockSpec((rows, 3 * lanes), lambda g: (0, g)),
            whole(cosine.shape),
            whole(sine.shape),
            whole(key_code.shape),
            whole(query_code.shape),
        ],
        [
            pl.BlockSpec((rows, 3 * lanes), lambda g: (0, g)),
            pl.BlockSpec((rows, lanes), lambda g: (0, g)),
            pl.BlockSpec((1, heads, rows), lambda g: (g, 0, 0)),
        ],
        [
            jax.ShapeDtypeStruct((rows, columns), LOW),
            jax.ShapeDtypeStruct((rows, groups * lanes), LOW),
            jax.ShapeDtypeStruct((groups, heads, rows), F32),
        ],
        scratch=[pltpu.VMEM((lanes, rows), F32)],
        us=19.6,
        after=after,
    )(mixed, cosine, sine, key_code, query_code)


def attention_backward(qkv, lse, attn_grad, cosine, sine, key_code, query_code, groups, after=()):
    rows, columns = qkv.shape
    lanes = columns // (3 * groups)
    heads = lanes // HD
    scale = HD ** (-0.5)

    def kernel(
        qkv_ref, lse_ref, grad_ref, cos_ref, sin_ref, key_ref, query_ref, out_ref, sum_ref, q_t, k_n, v_n
    ):
        query_t = qkv_ref[:, :lanes].T
        key_t = qkv_ref[:, lanes : 2 * lanes].T
        grad_t = grad_ref[...].T
        queries = qkv_ref[:, :lanes]
        keys = qkv_ref[:, lanes : 2 * lanes]
        values = qkv_ref[:, 2 * lanes :]
        grads = grad_ref[...]
        allowed = key_ref[...] == query_ref[...]
        for h in range(heads):
            cut = head_cut(h)
            logits = jnp.dot(keys[:, cut], query_t[cut, :], preferred_element_type=F32)
            logits = jnp.where(allowed, logits * scale, NEGATIVE)
            prob = jnp.exp(logits - lse_ref[0, h : h + 1, :])
            prob_grad = jnp.dot(values[:, cut], grad_t[cut, :], preferred_element_type=F32)
            inner = jnp.sum(prob * prob_grad, 0, keepdims=True)
            score_grad = (scale * prob * (prob_grad - inner)).astype(LOW)
            q_t[cut, :] = jnp.dot(key_t[cut, :], score_grad, preferred_element_type=F32)
            k_n[:, cut] = jnp.dot(score_grad, queries[:, cut], preferred_element_type=F32)
            v_n[:, cut] = jnp.dot(prob.astype(LOW), grads[:, cut], preferred_element_type=F32)
        cos, sin = cos_ref[...], sin_ref[...]
        for part, w in enumerate((q_t[...].T, k_n[...], v_n[...])):
            cut = slice(part * lanes, (part + 1) * lanes)
            if part < 2:
                w = w * cos - turn_pairs(w, lanes) * sin
            w = w.astype(LOW)
            out_ref[:, cut] = w
            sum_ref[:, cut] = jnp.sum(w.astype(F32), 0, keepdims=True)

    return call(
        kernel,
        (groups,),
        [
            pl.BlockSpec((rows, 3 * lanes), lambda g: (0, g)),
            pl.BlockSpec((1, heads, rows), lambda g: (g, 0, 0)),
            pl.BlockSpec((rows, lanes), lambda g: (0, g)),
            whole(cosine.shape),
            whole(sine.shape),
            whole(key_code.shape),
            whole(query_code.shape),
        ],
        [
            pl.BlockSpec((rows, 3 * lanes), lambda g: (0, g)),
            pl.BlockSpec((1, 3 * lanes), lambda g: (0, g)),
        ],
        [
            jax.ShapeDtypeStruct((rows, columns), LOW),
            jax.ShapeDtypeStruct((1, columns), F32),
        ],
        scratch=[
            pltpu.VMEM((lanes, rows), F32),
            pltpu.VMEM((rows, lanes), F32),
            pltpu.VMEM((rows, lanes), F32),
        ],
        us=27.3,
        after=after,
    )(qkv, lse, attn_grad, cosine, sine, key_code, query_code)
class Lanes:
    def __init__(self, dp):
        self.dp = dp
        self.ring = dp // 4

    def over_x(self, v):
        return lax.ppermute(v, "tensor", [(0, 1), (1, 0)])

    def over_core(self, v):
        return lax.ppermute(v, "dp", [(i, i ^ 1) for i in range(self.dp)])

    def over_y(self, v):
        return lax.ppermute(v, "dp", [(i, i ^ 2) for i in range(self.dp)])

    def down_z(self, v):
        return lax.ppermute(v, "dp", [(i, (i - 4) % self.dp) for i in range(self.dp)])

    def up_z(self, v):
        return lax.ppermute(v, "dp", [(i, (i + 4) % self.dp) for i in range(self.dp)])

    def exchange(self, v, bit):
        return lax.ppermute(v, "dp", [(i, i ^ bit) for i in range(self.dp)])

    def order(self):
        i = lax.axis_index("dp")
        z, y, c = i // 4, (i // 2) % 2, i % 2
        blocks = []
        for dc in range(2):
            for dy in range(2):
                for dz in range(self.ring):
                    blocks.append(((z + dz) % self.ring) * 4 + (y ^ dy) * 2 + (c ^ dc))
        return jnp.stack(blocks)

    def ring_down(self, v):
        held = [v]
        for _ in range(self.ring - 1):
            held.append(self.down_z(held[-1]))
        return held

    def far(self, side, across, near, after=()):
        a, b = cut_far(side, across, near, after)
        return self.over_y(a), self.over_x(b)

    def both_cores(self, values):
        return [(v, self.over_core(v)) for v in values]

    def stacked(self, pairs):
        rows = pairs[0][0].shape[0] // 2
        cuts = [
            (dc * self.ring + dz, dy * rows, rows)
            for dc in range(2)
            for dy in range(2)
            for dz in range(self.ring)
        ]
        return Stacked([p[0] for p in pairs] + [p[1] for p in pairs], cuts)


class Gathered:
    def __init__(self, own, other, far=None, near=()):
        self.own, self.other, self.far, self.near = own, other, far, near

    def pieces(self, column):
        if self.far is None:
            return [(v, column) for v in self.other]
        side, side_core = self.other
        place, spent, before = 1, column, 0
        for start, stop in self.near:
            if start <= column < stop:
                place, spent = 0, before + column - start
            before += stop - start
            if place and stop <= column:
                spent -= stop - start
        a, a_core = self.far[place]
        return [(side, column), (a, spent), (side_core, column), (a_core, spent)]

    def parts(self, block, first, count):
        sets = [([(v, first) for v in self.own], None, count)]
        last = None
        for b in range(first, first + count):
            here = [(v, c // block) for v, c in self.pieces(b * block)]
            if last is not None and all(
                v is w and c == d + sets[-1][2] for (v, c), (w, d) in zip(here, last)
            ):
                sets[-1] = (last, None, sets[-1][2] + 1)
            else:
                last = here
                sets.append((here, None, 1))
        return Parts(sets, block)


class Stacked:
    def __init__(self, pieces, cuts):
        self.pieces, self.cuts = pieces, cuts

    def parts(self, block):
        count = self.pieces[0].shape[1] // block
        return Parts([([(v, 0) for v in self.pieces], self.cuts, count)], block)


def butterfly(value, dp):
    if dp & (dp - 1):
        return lax.psum(value, ("dp", "tensor"))
    value = value + lax.ppermute(value, "tensor", [(0, 1), (1, 0)])
    bit = 1
    while bit < dp:
        value = value + lax.ppermute(value, "dp", [(i, i ^ bit) for i in range(dp)])
        bit *= 2
    return value


def body(
    block_input,
    out_cotangent,
    picture_ids,
    patch_positions,
    picture_lengths,
    pad_mask,
    qkv_weight,
    proj_weight,
    fc1_weight,
    fc2_weight,
    qkv_bias,
    fc1_bias,
    vectors,
    qkv_moments,
    proj_moments,
    fc1_moments,
    fc2_moments,
    qkv_bias_moments,
    fc1_bias_moments,
    vector_moments,
):
    ORDER.last = None
    dp = lax.axis_size("dp")
    relative = dp == 16
    lanes = Lanes(dp)
    slot = lax.axis_index("tensor")
    lead_dp = (lax.axis_index("dp") == 0).astype(F32)
    lead_all = lead_dp * (slot == 0).astype(F32)
    width = block_input.shape[3]
    rows_own = width // dp
    lane_columns = qkv_weight.shape[2]
    hidden = fc1_weight.shape[1]
    grad_factor = float(block_input.shape[0] * block_input.shape[1] * dp * LEN) ** (-0.5)

    biases = jnp.concatenate([qkv_bias.reshape(-1), fc1_bias]).reshape(-1, 128)

    def row_view(v):
        return jnp.swapaxes(v, -1, -2)

    qkv_view, qkv_moments_view = jnp.swapaxes(qkv_weight, 0, 1), jnp.swapaxes(qkv_moments, 1, 2)
    proj_view, proj_moments_view = row_view(proj_weight), row_view(proj_moments)
    fc2_view, fc2_moments_view = row_view(fc2_weight), row_view(fc2_moments)

    local_rows = block_input.shape[2]

    def half_of(both, place):
        return lax.dynamic_index_in_dim(both[:, 0], place, 0, keepdims=False)

    both_came = lanes.over_x(
        jnp.stack([half_of(block_input, 1 - slot), half_of(out_cotangent, 1 - slot)])
    )
    input_mine, cot_mine = half_of(block_input, slot), half_of(out_cotangent, slot)

    shard_1 = jnp.concatenate([qkv_view[k].astype(LOW) for k in range(3)], 1)
    shard_3 = fc2_view.astype(LOW)
    half = hidden // 2
    if relative:
        ring_1 = lanes.ring_down(shard_1)
        side_3, across_3 = lanes.over_x(shard_3), lanes.over_y(shard_3)
        far_3 = lanes.over_y(side_3)
        shard_2 = pack_columns([fc1_weight, proj_view])
        ring_2 = [shard_2, lanes.down_z(shard_2)]
        held_1 = stack_rows(ring_1, after=[side_3, across_3, far_3, both_came])
        ring_2[1] = hold(ring_2[1])
        for _ in range(2):
            ring_2.append(lanes.down_z(ring_2[-1]))
    else:

        def plain(shard):
            held = lax.all_gather(shard, "dp", axis=0, tiled=True)
            return Gathered([held], [lanes.over_x(held)])

        shard_2 = jnp.concatenate([fc1_weight.astype(LOW), proj_view.astype(LOW)], 1)
        w1, w2, w3 = plain(shard_1), plain(shard_2), plain(shard_3)
        w_down = w3.parts(half, 0, 2)
    def pick(array, axis=0):
        return lax.dynamic_index_in_dim(array, slot, axis, keepdims=False)

    def turn(values):
        return jnp.roll(values, -slot * local_rows, axis=-1)

    ids_row = turn(pick(picture_ids[:, 0]))
    rows_at = turn(pick(patch_positions[0, :, 0]))
    cols_at = turn(pick(patch_positions[1, :, 0]))
    mask_row = turn(pick(pad_mask[:, 0]))
    length_row = pick(picture_lengths[:, 0])
    cosine, sine = rotary_tables(rows_at, cols_at)
    groups = 2
    heads = lane_columns // HD
    cosine, sine = jnp.tile(cosine, (1, heads)), jnp.tile(sine, (1, heads))
    key_code = jnp.where(mask_row == 1, ids_row, -1)[:, None]
    query_code = ids_row[None, :]
    slot_hit = (ids_row[:, None] == jnp.arange(SLOTS, dtype=jnp.int32)[None, :]).astype(F32)
    picture_size = jnp.sum(slot_hit * length_row.astype(F32)[None, :], -1)
    token_weight = (mask_row.astype(F32) * jnp.sqrt(LEN / picture_size))[:, None]

    if relative:
        order = lanes.order()
        column = (order[:, None] * rows_own + jnp.arange(rows_own)[None, :]).reshape(-1)
        shuffle = (jnp.arange(width)[:, None] == column[None, :]).astype(LOW)
        vec = lax.dot_general(
            vectors,
            shuffle.astype(F32),
            (((1,), (0,)), ((), ())),
            precision=lax.Precision.HIGHEST,
            preferred_element_type=F32,
        )
        core_held_1 = lanes.over_core(held_1)
        sides_1 = lanes.over_x(held_1), lanes.over_y(held_1)
        row_low, first_in = enter_input(input_mine, both_came, shuffle, vec)
        cot_low, down_grad = enter_cotangent(cot_mine, both_came, shuffle, token_weight)
        biases = hold(biases)
        near_1 = [(0, 2 * lane_columns)]
        fars_1 = lanes.far(*sides_1, near_1, after=[core_held_1])
        late_3 = [stack_early(shard_3, side_3, across_3, far_3, after=[ring_2[3]])]
        late_came = lanes.down_z(late_3[0])
        core_late = lanes.over_core(late_3[0])
        cores_1 = lanes.both_cores(sides_1)
        held_2 = stack_rows(ring_2, after=[*fars_1, cores_1[0][1], cores_1[1][1]])
        sides_2 = lanes.over_x(held_2), lanes.over_y(held_2)
        core_held_2 = lanes.over_core(held_2)
        w1 = Gathered(
            [held_1, sides_1[1], core_held_1, cores_1[1][1]],
            cores_1[0],
            lanes.both_cores(fars_1),
            near_1,
        )
    else:
        vec = vectors
        row_low = jnp.concatenate([input_mine, both_came[0]], 0)
        cot_low = jnp.concatenate([cot_mine, both_came[1]], 0)
        normed1, _ = norm_parts(row_low.astype(F32))
        first_in = (normed1 * vec[0] + vec[1]).astype(LOW)
        down_grad = (cot_low.astype(F32) * token_weight).astype(LOW)
    w_qkv = w1.parts(lane_columns, 0, 3)
    other_biases = lanes.over_x(biases).reshape(-1)
    biases = biases.reshape(-1)
    cut = qkv_bias.size
    bias_qkv = jnp.concatenate([biases[:cut], other_biases[:cut]])[None]
    bias_up = jnp.concatenate([biases[cut:], other_biases[cut:]])[None]

    def give_back(values_low):
        if relative:
            mine, theirs = unshuffle(values_low, shuffle)
        else:
            mine, theirs = values_low[:local_rows], values_low[local_rows:]
        return mine, lanes.over_x(theirs)

    wide_kind = [(0, j) for j in range(4)]
    first_kind = [(0, 0), (0, 1), (0, 2), (1, 0), (0, 3), (0, 4), (0, 5), (1, 1)]

    def send_grads(pairs, block, kind, us):
        (sent,) = grad_kernel(pairs, block, kind, 1, us=us)
        return lanes.over_core(sent)

    def wide_grads(pairs, came):
        a = grad_kernel(pairs, half, [(0, 0), (0, 2)], 0, (came, [0, 2]), "a", 7)
        from_y = lanes.over_y(a[1])
        b = grad_kernel(pairs, half, [(0, 1), (0, 3)], 0, (came, [1, 3]), "b", 7)
        return (a[0], b[0]), (a[2], b[1]), (from_y, lanes.over_x(b[2]))

    def send_second(kept, first):
        to_x, to_y = add_second(*kept, *first)
        return (*first, lanes.over_x(to_x), lanes.over_y(to_y))

    def ring_step(own, sides, came, place):
        kind = LOW if place else F32
        total = add_ring(*own, *sides, came, place, rows_own, kind)
        return lanes.up_z(total) if place else total

    def plain_grads(pairs, block, kind):
        whole_grad = jnp.concatenate(
            [
                outer(pairs[p][0], pairs[p][1][:, c * block : (c + 1) * block])
                for p, c in kind
            ],
            1,
        )
        both = whole_grad[:, :hidden] + lanes.over_x(whole_grad[:, hidden:])
        return lax.psum_scatter(both, "dp", scatter_dimension=0, tiled=True)

    qkv_columns = 3 * lane_columns

    def small_sums(sums_1, sums_2, sum_qkv, sum_up):
        terms = jnp.concatenate([sums_1[0:2], sums_2[2:3], sums_2[0:2], sums_2[3:4]], 0)
        if relative:
            terms = lax.dot_general(
                terms,
                shuffle.astype(F32),
                (((1,), (1,)), ((), ())),
                precision=lax.Precision.HIGHEST,
                preferred_element_type=F32,
            )
        own = jnp.concatenate([sum_qkv[0, :qkv_columns], sum_up[0, :hidden]])
        other = jnp.concatenate([sum_qkv[0, qkv_columns:], sum_up[0, hidden:]])
        first_half = slot == 0
        return jnp.concatenate(
            [
                jnp.where(first_half, own, other),
                jnp.where(first_half, other, own),
                terms.reshape(-1),
            ]
        ).reshape(-1, 128)

    mixed = qkv_forward(first_in, w_qkv, bias_qkv, list(range(6)))
    if relative:
        late_3.append(hold(late_came))
    before_attention = [core_held_2, core_late] if relative else []
    qkv, attended, lse = attention_forward(
        mixed, cosine, sine, key_code, query_code, groups, after=before_attention
    )
    if relative:
        late_3.append(lanes.down_z(late_3[1]))
        late_came = lanes.down_z(late_3[2])
        late_cores = [(late_3[0], core_late), *lanes.both_cores(late_3[1:])]
        before_far = [late_cores[1][1]]
        near_2 = [(0, half), (hidden, hidden + lane_columns)]
        fars_2 = lanes.far(*sides_2, near_2, after=before_far)
        hold(query_code, us=8, after=fars_2)
        cores_2 = lanes.both_cores(sides_2)
        w2 = Gathered(
            [held_2, sides_2[1], core_held_2, cores_2[1][1]],
            cores_2[0],
            lanes.both_cores(fars_2),
            near_2,
        )
    w_proj = w2.parts(lane_columns, hidden // lane_columns, 1)
    w_up = w2.parts(half, 0, 2)
    hidden1, second_in = proj_forward(attended, w_proj, row_low, vec)
    upward, activated = up_forward(second_in, w_up, bias_up)
    pair_3 = [(down_grad, activated)]
    if relative:
        came_3 = send_grads(pair_3, half, wide_kind, 60)
        late_cores += lanes.both_cores([hold(late_came)])
        w_down = lanes.stacked(late_cores).parts(half)
    result = down_forward(activated, w_down, hidden1, vec)

    if relative:
        own_3, later_3, first_3 = wide_grads(pair_3, came_3)
    up_grad, sum_up = down_backward(down_grad, w_down, upward)
    pair_2 = [(second_in, up_grad)]
    output_halves = give_back(result)
    if relative:
        came_2 = send_grads(pair_2, half, wide_kind, 0.1)
    hidden1_grad, branch_grad, sums_2 = up_backward(
        up_grad, w_up, hidden1, cot_low, token_weight, vec
    )
    if relative:
        sides_3 = send_second(later_3, first_3)
    attn_grad = proj_backward(branch_grad, w_proj)
    if relative:
        own_2, later_2, first_2 = wide_grads(pair_2, came_2)
        ring_3 = ring_step(own_3, sides_3, None, 3)
    block_output = place_halves(*output_halves, slot)
    mixed_grad, sum_qkv = attention_backward(
        qkv, lse, attn_grad, cosine, sine, key_code, query_code, groups
    )
    pair_q, pair_p = (first_in, mixed_grad), (branch_grad, attended)
    factor = grad_factor
    if relative:
        kind_a = [(0, 0), (0, 1), (0, 3), (0, 4)]
        kind_b = [(0, 2), (1, 0), (0, 5), (1, 1)]
        sides_2 = send_second(later_2, first_2)
        ring_3 = ring_step(own_3, sides_3, ring_3, 2)
        came_a = send_grads([pair_q], lane_columns, kind_a, 1)
        came_b = send_grads([pair_q, pair_p], lane_columns, kind_b, 1)
        part_a = grad_kernel([pair_q], lane_columns, kind_a, 0, (came_a, [0, 1, 2, 3]), "a", 8)
        first_y = lanes.over_y(part_a[1])
        ring_3 = ring_step(own_3, sides_3, ring_3, 1)
        ring_2 = ring_step(own_2, sides_2, None, 3)
        part_b = grad_kernel(
            [pair_q, pair_p], lane_columns, kind_b, 0, (came_b, [0, 1, 2, 3]), "b", 8
        )
        own_1, later_1 = (part_a[0], part_b[0]), (part_a[2], part_b[1])
        first_1 = first_y, lanes.over_x(part_b[2])
        grad_3 = ring_step(own_3, sides_3, ring_3, 0)
        lamb_3 = lamb_first([(3, fc2_view, fc2_moments_view, 0)], grad_3, factor)
    input_low, sums_1 = qkv_backward(
        mixed_grad, w_qkv, list(range(6)), row_low, hidden1_grad, vec
    )
    if relative:
        ring_2 = ring_step(own_2, sides_2, ring_2, 2)
        sides_1 = send_second(later_1, first_1)
        ring_2 = ring_step(own_2, sides_2, ring_2, 1)
        small = hold(small_sums(sums_1, sums_2, sum_qkv, sum_up))
        came = lanes.over_core(small)
        grad_2 = ring_step(own_2, sides_2, ring_2, 0)
        small = hold(small, came)
        came = lanes.exchange(small, 4)
    else:
        input_halves = give_back(input_low)
        small = small_sums(sums_1, sums_2, sum_qkv, sum_up)
        grad_3 = plain_grads(pair_3, half, wide_kind)
        lamb_3 = lamb_first([(3, fc2_view, fc2_moments_view, 0)], grad_3, factor)
        grad_2 = plain_grads(pair_2, half, wide_kind)
    lamb_2 = lamb_first([(2, fc1_weight, fc1_moments, 0)], grad_2, factor)
    if relative:
        small = hold(small, came)
        came = lanes.exchange(small, 8)
        ring_1 = ring_step(own_1, sides_1, None, 3)
        input_halves = give_back(input_low)
        small = hold(small, came)
        came = lanes.over_y(small)
        ring_1 = ring_step(own_1, sides_1, ring_1, 2)
        small = hold(small, came)
        came = lanes.over_x(small)
        ring_1 = ring_step(own_1, sides_1, ring_1, 1)
        small = hold(small, came)

    if not relative:
        small = butterfly(small, dp)
    small = small.reshape(-1)
    first_half = slot == 0
    size = qkv_columns + hidden
    bias_sum = jnp.where(first_half, small[:size], small[size : 2 * size])
    small_grads = [
        bias_sum[:qkv_columns].reshape(qkv_bias.shape),
        bias_sum[None, qkv_columns:],
        small[2 * size :].reshape(vectors.shape),
    ]
    small_masters = [qkv_bias, fc1_bias[None], vectors]
    lane = jnp.arange(128)
    is_bias = (lane == 4) | (lane == 5) | (lane == 11) | (lane == 12)
    shares = jnp.where(is_bias, lead_dp, lead_all)[None]
    *small_lamb, small_row = lamb_small(
        small_masters,
        [
            jnp.swapaxes(qkv_bias_moments, 0, 1),
            fc1_bias_moments,
            jnp.swapaxes(vector_moments, 0, 1),
        ],
        small_grads,
        shares,
        factor,
    )

    if relative:
        input_grad = place_halves(*input_halves, slot)
        grad_1 = ring_step(own_1, sides_1, ring_1, 0)
    else:
        input_grad = place_halves(*input_halves, slot)
        grad_1 = plain_grads([pair_q, pair_p], lane_columns, first_kind)
    q_moments, p_moments, q_update, p_update, row = lamb_first(
        [(0, qkv_view, qkv_moments_view, 0), (1, proj_view, proj_moments_view, qkv_columns)],
        grad_1,
        factor,
        [lamb_2[2], lamb_3[2], small_row],
    )
    row = butterfly(row, dp)
    last = lamb_last(
        [qkv_view, proj_view, fc1_weight, fc2_view, *small_masters],
        [q_update, p_update, lamb_2[1], lamb_3[1], *small_lamb[3:]],
        row,
        4,
    )
    new_params, copies, norms, trust = last[:7], last[7:11], last[11], last[12]
    new_weights, copies = [
        [jnp.swapaxes(v[0], 0, 1), row_view(v[1]), v[2], row_view(v[3])]
        for v in (new_params, copies)
    ]
    return (
        block_output,
        input_grad,
        *new_weights,
        new_params[4],
        new_params[5][0],
        new_params[6],
        jnp.swapaxes(q_moments, 1, 2),
        row_view(p_moments),
        lamb_2[0],
        row_view(lamb_3[0]),
        jnp.swapaxes(small_lamb[0], 0, 1),
        small_lamb[1],
        jnp.swapaxes(small_lamb[2], 0, 1),
        *copies,
        norms,
        trust[0],
    )


def solution(mesh):
    in_specs = (
        P(None, "dp", "tensor", None),
        P(None, "dp", "tensor", None),
        P(None, "dp", None),
        P(None, None, "dp", None),
        P(None, "dp", None),
        P(None, "dp", None),
        P("dp", None, "tensor"),
        P("tensor", "dp"),
        P("dp", "tensor"),
        P("tensor", "dp"),
        P(None, "tensor"),
        P("tensor"),
        P(),
        P(None, "dp", None, "tensor"),
        P(None, "tensor", "dp"),
        P(None, "dp", "tensor"),
        P(None, "tensor", "dp"),
        P(None, None, "tensor"),
        P(None, "tensor"),
        P(),
    )
    out_specs = (
        P(None, "dp", "tensor", None),
        P(None, "dp", "tensor", None),
        P("dp", None, "tensor"),
        P("tensor", "dp"),
        P("dp", "tensor"),
        P("tensor", "dp"),
        P(None, "tensor"),
        P("tensor"),
        P(),
        P(None, "dp", None, "tensor"),
        P(None, "tensor", "dp"),
        P(None, "dp", "tensor"),
        P(None, "tensor", "dp"),
        P(None, None, "tensor"),
        P(None, "tensor"),
        P(),
        P("dp", None, "tensor"),
        P("tensor", "dp"),
        P("dp", "tensor"),
        P("tensor", "dp"),
        P(),
        P(),
    )
    return jax.shard_map(body, mesh=mesh, in_specs=in_specs, out_specs=out_specs, check_vma=False)
```
